32 devices in a mesh: node: 4 (over y, x), local: 2 (over core), edata: 4 (over z).
Axes of the slice: x: 2, y: 2, z: 4, core: 2. Of those that a mesh axis runs over, the one named last changes fastest.
Arguments:
- tokens: bfloat16 [2048, 4096], P(('node', 'local'), 'edata'), may hold values from -6 to 6
- grad_out: bfloat16 [2048, 4096], P(('node', 'local'), 'edata'), may hold values from -0.59765625 to 0.59765625
- routes: int32 [2048, 2], P(('node', 'local')), may hold values from 0 to 63, all different within a row
- gates: bfloat16 [2048, 2], P(('node', 'local')), may hold values from 0.099609375 to 1
- w_in: bfloat16 [4096, 2048], P('edata', ('node', 'local')), may hold values from -0.09375 to 0.09375
- w_out: bfloat16 [2048, 4096], P(('node', 'local'), 'edata'), may hold values from -0.09375 to 0.09375
Outputs:
- grad_tokens: bfloat16 [2048, 4096], P(('node', 'local'), 'edata')
- grad_gates: float32 [2048, 2], P(('node', 'local'))
- grad_w_in: float32 [4096, 2048], P('edata', ('node', 'local'))
- grad_w_out: float32 [2048, 4096], P(('node', 'local'), 'edata')
The draws below stay inside these ranges and needn't reach their ends.
Inputs may be any that keep to these rules, and one draw needn't show every extreme that they name: `routes`: each token names two different experts.
All inputs are finite; a program needn't handle non-finite values.
Results may differ from the reference program's by a relative error of at most 0.0049.
Values may be sent and summed in bfloat16 or wider, within the bound.
No kernel may reach another device: no remote copies, remote signals or barrier semaphores. Data moves between devices by JAX's collectives and lax.ppermute only.
A program may use at most 64 MiB of HBM per device.

```python
import jax
import jax.numpy as jnp
from jax import lax

D = 4096
EXPERTS = 64
WINDOW = 2
TOK_DEV = 256
FFW = 1024
CAP = 8
TOKENS = 2048
N_NODE = 4
N_LOCAL = 2


def level_of(own_key, extent, pieces, smallest, high):
    def one(dim, blocks):
        draws = jax.random.uniform(jax.random.fold_in(jax.random.fold_in(own_key, 6), dim), (blocks,), jnp.float32, smallest / len(pieces), high / len(pieces))
        return jnp.repeat(jnp.exp(draws), extent[dim] // blocks).reshape((-1,) + (1,) * (len(extent) - dim - 1))

    factor_of = one(*pieces[0])
    for cut in pieces[1:]:
        factor_of = factor_of * one(*cut)
    return factor_of


def picks_of(own_key, rows, amount, top, lift):
    ranking = jax.random.permutation(jax.random.fold_in(own_key, 1), amount)
    boost = ranking
    for power in range(3):
        boost = boost * boost // amount
    boost = boost * lift // amount
    tickets = jax.random.randint(jax.random.fold_in(own_key, 2), (rows, amount), 0, 4096) + boost
    fixed_rows = jax.random.permutation(jax.random.fold_in(own_key, 3), rows)[jnp.arange(amount) % rows]
    tickets = jnp.where(jnp.arange(rows)[:, None] == fixed_rows[None, :], 1 << 14, tickets)
    priority = tickets * amount + jnp.arange(amount)
    return lax.top_k(priority.astype(jnp.int32), top)[1].astype(jnp.int32)


def scatter_about(stream_key, dims, deviation, most, cuts=(), kind=jnp.bfloat16):
    result = deviation * jax.random.normal(stream_key, dims, jnp.float32)
    if cuts:
        result = result * level_of(stream_key, dims, cuts, -0.22, 0.18)
    return jnp.clip(result, -most, most).astype(kind)


def setup_inputs(seed: int = 0) -> dict:
    key_of = jax.random.split(jax.random.key(seed), 7)
    tokens = scatter_about(key_of[0], (TOKENS, D), 1.0, 6.0, ((0, 8), (1, 4)))
    grad_out = scatter_about(key_of[1], (TOKENS, D), 0.1, 0.59765625, ((0, 8), (1, 4)))
    routes = picks_of(key_of[2], TOKENS, EXPERTS, 2, 0)
    gates = jnp.clip(0.099609375 + 0.9003906 * jax.random.uniform(key_of[3], (TOKENS, 2), jnp.float32) ** level_of(key_of[3], (TOKENS, 2), ((0, 8),), -0.2, 0.2), 0.099609375, 1.0).astype(jnp.bfloat16)
    w_in = scatter_about(key_of[4], (D, WINDOW * FFW), D ** -0.5, 0.09375, ((0, 4), (1, 8)))
    w_out = scatter_about(key_of[5], (WINDOW * FFW, D), D ** -0.5, 0.09375, ((0, 8), (1, 4)))
    return dict(tokens=tokens, grad_out=grad_out, routes=routes, gates=gates, w_in=w_in, w_out=w_out)


def gelu_pair(pre_act):
    coefficient = 0.7978845608028654
    inner_arg = coefficient * (pre_act + 0.044715 * pre_act * pre_act * pre_act)
    tanh_val = jnp.tanh(inner_arg)
    activation = 0.5 * pre_act * (1.0 + tanh_val)
    slopes = 0.5 * (1.0 + tanh_val) + 0.5 * pre_act * (1.0 - tanh_val * tanh_val) * coefficient * (1.0 + 3.0 * 0.044715 * pre_act * pre_act)
    return activation, slopes


def reference(tokens, grad_out, routes, gates, w_in, w_out):
    groups = N_NODE * N_LOCAL
    pairs = routes.reshape(groups, TOK_DEV * 2)
    onehot = (pairs[:, :, None] == jnp.arange(WINDOW, dtype=jnp.int32)[None, None, :]).astype(jnp.int32)
    before = jnp.cumsum(onehot, axis=1) - onehot
    position = jnp.sum(before * onehot, axis=2).astype(jnp.int32)
    live_pair = (pairs < WINDOW) & (position < CAP)
    slot_index = jnp.where(live_pair, pairs * CAP + position, -1).astype(jnp.int32)
    matches = slot_index[:, :, None] == jnp.arange(WINDOW * CAP, dtype=jnp.int32)[None, None, :]
    token_ids = jnp.arange(TOK_DEV * 2, dtype=jnp.int32) // 2
    token_of = jnp.sum(jnp.where(matches, token_ids[None, :, None], 0), axis=1).astype(jnp.int32)
    filled = jnp.any(matches, axis=1)
    gate_pairs = gates.reshape(groups, TOK_DEV * 2).astype(jnp.float32)
    gate_of = jnp.sum(jnp.where(matches, gate_pairs[:, :, None], jnp.zeros((), jnp.float32)), axis=1)
    group_base = (jnp.arange(groups, dtype=jnp.int32) * TOK_DEV)[:, None]
    in_grads = []
    out_grads = []
    slot_grads = []
    gate_parts = []
    for expert in range(WINDOW):
        local_ids = token_of[:, expert * CAP:(expert + 1) * CAP]
        live_rows = filled[:, expert * CAP:(expert + 1) * CAP].reshape(-1)
        gate_rows = gate_of[:, expert * CAP:(expert + 1) * CAP].reshape(-1)
        row_ids = (group_base + local_ids).reshape(-1).astype(jnp.int32)
        x_rows = jnp.where(live_rows[:, None], tokens[row_ids], jnp.zeros((), tokens.dtype))
        dy_rows = jnp.where(live_rows[:, None], grad_out[row_ids], jnp.zeros((), grad_out.dtype))
        w_in_e = w_in[:, expert * FFW:(expert + 1) * FFW]
        w_out_e = w_out[expert * FFW:(expert + 1) * FFW, :]
        pre_act = jnp.dot(x_rows, w_in_e, preferred_element_type=jnp.float32)
        back_grad = jnp.dot(dy_rows, w_out_e.T, preferred_element_type=jnp.float32)
        activation, slopes = gelu_pair(pre_act)
        scaled = (gate_rows[:, None] * activation).astype(jnp.bfloat16)
        out_grads.append(jnp.dot(scaled.T, dy_rows, preferred_element_type=jnp.float32))
        pre_grad = (gate_rows[:, None] * back_grad * slopes).astype(jnp.bfloat16)
        in_grads.append(jnp.dot(x_rows.T, pre_grad, preferred_element_type=jnp.float32))
        slot_grads.append(jnp.dot(pre_grad, w_in_e.T, preferred_element_type=jnp.float32))
        gate_parts.append(jnp.sum(activation * back_grad, axis=1))
    grad_w_in = jnp.concatenate(in_grads, axis=1)
    grad_w_out = jnp.concatenate(out_grads, axis=0)
    slot_flat = jnp.concatenate(slot_grads, axis=0)
    gate_flat = jnp.concatenate(gate_parts, axis=0)
    safe_expert = jnp.where(live_pair, pairs, 0)
    safe_pos = jnp.where(live_pair, position, 0)
    index = ((safe_expert * groups + jnp.arange(groups, dtype=jnp.int32)[:, None]) * CAP + safe_pos).reshape(-1).astype(jnp.int32)
    picked = slot_flat[index].reshape(groups * TOK_DEV, 2, tokens.shape[1])
    keep_pair = live_pair.reshape(groups * TOK_DEV, 2)
    grad_tokens = jnp.sum(jnp.where(keep_pair[:, :, None], picked, jnp.zeros((), picked.dtype)), axis=1).astype(jnp.bfloat16)
    grad_gates = jnp.where(keep_pair, gate_flat[index].reshape(groups * TOK_DEV, 2), jnp.zeros((), gate_flat.dtype))
    return grad_tokens, grad_gates, grad_w_in, grad_w_out
```

```python
import functools

import jax
import jax.numpy as jnp
from jax import lax
from jax.experimental import pallas as pl
from jax.experimental.pallas import tpu as pltpu
from jax.sharding import PartitionSpec as P

EXPERTS = 64
WINDOW = 2
GATE_LANES = 128
VMEM_LIMIT = 40 * 1024 * 1024

BF16 = jnp.bfloat16
F32 = jnp.float32


def gelu_pair(pre_act):
    coefficient = 0.7978845608028654
    square = pre_act * pre_act
    tanh_val = jnp.tanh(coefficient * (pre_act + 0.044715 * pre_act * square))
    half = 0.5 * (1.0 + tanh_val)
    activation = pre_act * half
    slopes = half + 0.5 * pre_act * (1.0 - tanh_val * tanh_val) * coefficient * (
        1.0 + 3.0 * 0.044715 * square
    )
    return (activation, slopes)


def call(kernel, out_shape, flops, moved):
    return pl.pallas_call(
        kernel,
        out_shape=out_shape,
        compiler_params=pltpu.CompilerParams(vmem_limit_bytes=VMEM_LIMIT),
        cost_estimate=pl.CostEstimate(flops=flops, bytes_accessed=moved, transcendentals=0),
    )


def gather_kernel(copies, routes_ref, gates_ref, tokens_ref, grads_ref, send_ref, place_ref):
    tok_rows = tokens_ref.shape[0]
    slots = place_ref.shape[0]
    capacity = slots // WINDOW
    routes = routes_ref[...]
    gates = gates_ref[...].astype(F32)
    named = []
    weight = []
    for expert in range(WINDOW):
        hit = (routes == expert).astype(F32)
        named.append(hit[0:1] + hit[1:2])
        scaled = hit * gates
        weight.append(scaled[0:1] + scaled[1:2])
    row_of = lax.broadcasted_iota(jnp.int32, (8, tok_rows), 0)
    names = jnp.where(row_of == 0, named[0], jnp.where(row_of == 1, named[1], 0.0)).astype(BF16)
    earlier = lax.broadcasted_iota(jnp.int32, (tok_rows, tok_rows), 0) < lax.broadcasted_iota(
        jnp.int32, (tok_rows, tok_rows), 1
    )
    before = jnp.dot(names, earlier.astype(F32).astype(BF16), preferred_element_type=F32)
    slot_of = lax.broadcasted_iota(jnp.int32, (capacity, tok_rows), 0).astype(F32)
    parts = [
        jnp.where(before[e : e + 1] == slot_of, named[e], 0.0) for e in range(WINDOW)
    ]
    place = jnp.concatenate(parts, axis=0)
    gated = jnp.concatenate([parts[e] * weight[e] for e in range(WINDOW)], axis=0)
    place_ref[...] = place.astype(BF16)
    rows_x = jnp.dot(place.astype(BF16), tokens_ref[...], preferred_element_type=F32)
    rows_dy = jnp.dot(gated.astype(BF16), grads_ref[...], preferred_element_type=F32)
    for expert in range(WINDOW):
        own = slice(expert * capacity, (expert + 1) * capacity)
        chunk = jnp.concatenate([rows_x[own], rows_dy[own]], axis=0).astype(BF16)
        for copy in range(copies):
            send_ref[expert * copies + copy] = chunk


def part_kernel(rows_ref, w_in_ref, w_out_ref, part_ref):
    groups, pair, feats = rows_ref.shape
    capacity = pair // 2
    hidden = w_in_ref.shape[1]
    rows = rows_ref[...].reshape(groups * pair, feats)
    pre = jnp.dot(rows, w_in_ref[...], preferred_element_type=F32)
    back = lax.dot_general(
        rows, w_out_ref[...], (((1,), (1,)), ((), ())), preferred_element_type=F32
    )
    pre = pre.reshape(groups, pair, hidden)[:, :capacity].reshape(groups * capacity, hidden)
    back = back.reshape(groups, pair, hidden)[:, capacity:].reshape(groups * capacity, hidden)
    part_ref[:, :hidden] = pre.astype(BF16)
    part_ref[:, hidden:] = back.astype(BF16)


def hidden_kernel(groups, parts_ref, w_in_ref, slot_ref, dpre_ref, act_ref):
    feats, hidden = w_in_ref.shape
    total = parts_ref[0].astype(F32)
    for index in range(1, parts_ref.shape[0]):
        total = total + parts_ref[index].astype(F32)
    pre, back = total[:, :hidden], total[:, hidden:]
    activation, slopes = gelu_pair(pre)
    dpre = back * slopes
    slot_ref[:, :feats] = lax.dot_general(
        dpre.astype(BF16), w_in_ref[...], (((1,), (1,)), ((), ())), preferred_element_type=F32
    ).astype(BF16)
    gate = jnp.sum(activation * back, axis=1, keepdims=True)
    high = gate.astype(BF16).astype(F32)
    lane = lax.broadcasted_iota(jnp.int32, (gate.shape[0], GATE_LANES), 1)
    slot_ref[:, feats:] = jnp.where(lane == 0, high, jnp.where(lane == 1, gate - high, 0.0)).astype(
        BF16
    )
    rows = dpre.shape[0]
    capacity = rows // groups
    dpre = dpre.reshape(groups, capacity, hidden)
    activation = activation.reshape(groups, capacity, hidden)
    blank = jnp.zeros_like(dpre)
    dpre_ref[...] = (
        jnp.concatenate([dpre, blank], axis=1).reshape(2 * rows, hidden).astype(BF16)
    )
    act_ref[...] = (
        jnp.concatenate([blank, activation], axis=1).reshape(2 * rows, hidden).astype(BF16)
    )


def combine_kernel(copies, came_ref, place_ref, routes_ref, gates_ref, tokens_ref, gate_out_ref):
    feats = tokens_ref.shape[1]
    slots = place_ref.shape[0]
    capacity = slots // WINDOW
    place = place_ref[...].astype(F32)
    spread = []
    for expert in range(WINDOW):
        own = place[expert * capacity : (expert + 1) * capacity]
        spread.append(jnp.concatenate([own] * copies, axis=0).astype(BF16))
    contract = (((0,), (0,)), ((), ()))
    tokens_ref[...] = lax.dot_general(
        jnp.concatenate(spread, axis=0), came_ref[:, :feats], contract, preferred_element_type=F32
    ).astype(BF16)
    routes = routes_ref[...]
    gates = gates_ref[...].astype(F32)
    result = jnp.zeros(gates.shape, F32)
    half = copies * capacity
    for expert in range(WINDOW):
        sums = lax.dot_general(
            came_ref[expert * half : (expert + 1) * half, feats:],
            spread[expert],
            contract,
            preferred_element_type=F32,
        )
        result = result + jnp.where(routes == expert, sums[0:1] + sums[1:2], 0.0)
    gate_out_ref[...] = result / gates


def body(tokens, grad_out, routes, gates, w_in, w_out):
    groups = lax.axis_size("node") * lax.axis_size("local")
    copies = groups // WINDOW
    tok_rows, feats = tokens.shape
    hidden = w_in.shape[1]
    capacity = 2 * tok_rows // EXPERTS
    slots = WINDOW * capacity
    rows = groups * capacity
    routes_t, gates_t = routes.T, gates.T
    send, place = call(
        functools.partial(gather_kernel, copies),
        (
            jax.ShapeDtypeStruct((groups, 2 * capacity, feats), BF16),
            jax.ShapeDtypeStruct((slots, tok_rows), BF16),
        ),
        4 * slots * tok_rows * feats,
        4 * tok_rows * feats + 4 * rows * feats,
    )(routes_t, gates_t, tokens, grad_out)
    got = lax.all_to_all(send, ("node", "local"), split_axis=0, concat_axis=0, tiled=True)
    part = call(
        part_kernel,
        jax.ShapeDtypeStruct((rows, 2 * hidden), BF16),
        8 * rows * feats * hidden,
        4 * rows * feats + 4 * feats * hidden,
    )(got, w_in, w_out)
    parts = lax.all_gather(part, "edata", axis=0)
    slot, dpre, act = call(
        functools.partial(hidden_kernel, groups),
        (
            jax.ShapeDtypeStruct((rows, feats + GATE_LANES), BF16),
            jax.ShapeDtypeStruct((2 * rows, hidden), BF16),
            jax.ShapeDtypeStruct((2 * rows, hidden), BF16),
        ),
        2 * rows * feats * hidden,
        2 * feats * hidden + 2 * rows * feats,
    )(parts, w_in)
    came = lax.all_to_all(
        slot.reshape(groups, capacity, feats + GATE_LANES),
        ("node", "local"),
        split_axis=0,
        concat_axis=0,
        tiled=True,
    )
    got_rows = got.reshape(2 * rows, feats)
    contract = (((0,), (0,)), ((), ()))
    grad_w_in = lax.dot_general(got_rows, dpre, contract, preferred_element_type=F32)
    grad_w_out = lax.dot_general(act, got_rows, contract, preferred_element_type=F32)
    grad_tokens, grad_gates = call(
        functools.partial(combine_kernel, copies),
        (
            jax.ShapeDtypeStruct((tok_rows, feats), BF16),
            jax.ShapeDtypeStruct((2, tok_rows), F32),
        ),
        2 * rows * tok_rows * feats,
        2 * rows * feats + 2 * tok_rows * feats,
    )(came.reshape(rows, feats + GATE_LANES), place, routes_t, gates_t)
    return (grad_tokens, grad_gates.T, grad_w_in, grad_w_out)


def solution(mesh):
    in_specs = (
        P(("node", "local"), "edata"),
        P(("node", "local"), "edata"),
        P(("node", "local"), None),
        P(("node", "local"), None),
        P("edata", ("node", "local")),
        P(("node", "local"), "edata"),
    )
    out_specs = (
        P(("node", "local"), "edata"),
        P(("node", "local"), None),
        P("edata", ("node", "local")),
        P(("node", "local"), "edata"),
    )
    return jax.shard_map(body, mesh=mesh, in_specs=in_specs, out_specs=out_specs, check_vma=False)
```

```python
import functools

import jax
import jax.numpy as jnp
from jax import lax
from jax.experimental import pallas as pl
from jax.experimental.pallas import tpu as pltpu
from jax.sharding import PartitionSpec as P

EXPERTS = 64
WINDOW = 2
GATE_LANES = 128
MOST_PERMUTES = 16
VMEM_LIMIT = 40 * 1024 * 1024

BF16 = jnp.bfloat16
F32 = jnp.float32
ROWS_BY_ROWS = (((0,), (0,)), ((), ()))
COLS_BY_COLS = (((1,), (1,)), ((), ()))


def gelu_pair(pre_act):
    coefficient = 0.7978845608028654
    square = pre_act * pre_act
    tanh_val = jnp.tanh(coefficient * (pre_act + 0.044715 * pre_act * square))
    half = 0.5 * (1.0 + tanh_val)
    activation = pre_act * half
    slopes = half + 0.5 * pre_act * (1.0 - tanh_val * tanh_val) * coefficient * (
        1.0 + 3.0 * 0.044715 * square
    )
    return (activation, slopes)


def call(kernel, out_shape, flops, moved, **more):
    return pl.pallas_call(
        kernel,
        out_shape=out_shape,
        compiler_params=pltpu.CompilerParams(vmem_limit_bytes=VMEM_LIMIT),
        cost_estimate=pl.CostEstimate(flops=flops, bytes_accessed=moved, transcendentals=0),
        **more,
    )


def own_expert():
    half_nodes = lax.axis_size("node") // WINDOW
    return lax.axis_index("node") // half_nodes


def gather_kernel(routes_hbm, gates_hbm, tokens_hbm, grads_hbm, own_ref, other_ref, place_ref,
                  routes_ref, gates_ref, tokens_ref, grads_ref, sems):
    tok_rows, feats = tokens_ref.shape
    slots = place_ref.shape[0]
    capacity = slots // WINDOW
    pairs = (
        (routes_hbm, routes_ref),
        (gates_hbm, gates_ref),
        (tokens_hbm, tokens_ref),
        (grads_hbm, grads_ref),
    )
    copies = [
        pltpu.make_async_copy(source, target, sems.at[index])
        for index, (source, target) in enumerate(pairs)
    ]
    for copy in copies:
        copy.start()
    earlier = lax.broadcasted_iota(jnp.int32, (tok_rows, tok_rows), 0) < lax.broadcasted_iota(
        jnp.int32, (tok_rows, tok_rows), 1
    )
    earlier = earlier.astype(F32).astype(BF16)
    slot_of = lax.broadcasted_iota(jnp.int32, (capacity, tok_rows), 0).astype(F32)
    row_of = lax.broadcasted_iota(jnp.int32, (8, tok_rows), 0)
    own = own_expert()
    copies[0].wait()
    copies[1].wait()
    routes = routes_ref[...]
    gates = gates_ref[...].astype(F32)
    named = []
    weight = []
    for expert in (own, 1 - own):
        hit = (routes == expert).astype(F32)
        named.append(hit[0:1] + hit[1:2])
        scaled = hit * gates
        weight.append(scaled[0:1] + scaled[1:2])
    names = jnp.where(row_of == 0, named[0], jnp.where(row_of == 1, named[1], 0.0)).astype(BF16)
    before = jnp.dot(names, earlier, preferred_element_type=F32)
    parts = [jnp.where(before[e : e + 1] == slot_of, named[e], 0.0) for e in range(WINDOW)]
    place = jnp.concatenate(parts, axis=0).astype(BF16)
    place_ref[...] = place
    copies[2].wait()
    rows_x = jnp.dot(place, tokens_ref[...], preferred_element_type=F32)
    copies[3].wait()
    rows_dy = jnp.dot(place, grads_ref[...], preferred_element_type=F32)
    for expert, out_ref in ((0, own_ref), (1, other_ref)):
        span = slice(expert * capacity, (expert + 1) * capacity)
        out_ref[:, :feats] = jnp.concatenate([rows_x[span], rows_dy[span]], axis=0).astype(BF16)
        gate = jnp.sum(parts[expert] * weight[expert], axis=1, keepdims=True)
        gate = jnp.concatenate([gate, gate], axis=0)
        out_ref[:, feats:] = jnp.broadcast_to(gate, (2 * capacity, GATE_LANES)).astype(BF16)


def part_kernel(capacity, pieces, edatas, *refs):
    rows_refs, (w_in_ref, w_out_ref), part_refs = (
        refs[:pieces],
        refs[pieces : pieces + 2],
        refs[pieces + 2 : pieces + 2 + edatas],
    )
    gate_ref, sums_ref = refs[pieces + 2 + edatas :]
    feats, hidden = w_in_ref.shape
    rows = jnp.concatenate([ref[...] for ref in rows_refs], axis=0)
    groups = rows.shape[0] // (2 * capacity)
    gate = rows[:, feats:].astype(F32).reshape(groups, 2 * capacity, GATE_LANES)
    gate_ref[...] = gate[:, :capacity].reshape(groups * capacity, GATE_LANES)
    rows = rows[:, :feats]
    pre = jnp.dot(rows, w_in_ref[...], preferred_element_type=F32)
    back = lax.dot_general(rows, w_out_ref[...], COLS_BY_COLS, preferred_element_type=F32)
    pre = pre.reshape(groups, 2 * capacity, hidden)[:, :capacity]
    back = back.reshape(groups, 2 * capacity, hidden)[:, capacity:]
    sums_ref[:, :hidden] = pre.reshape(groups * capacity, hidden)
    sums_ref[:, hidden:] = back.reshape(groups * capacity, hidden)
    chunk = groups * capacity // edatas
    mine = lax.axis_index("edata")
    for step in range(edatas):
        start = pl.multiple_of((mine ^ step) * chunk, chunk)
        part_refs[step][...] = sums_ref[pl.ds(start, chunk), :]


def hidden_kernel(edatas, *refs):
    part_refs, gate_ref, pack_ref = refs[:edatas], refs[edatas], refs[edatas + 1]
    total = part_refs[0][...]
    for ref in part_refs[1:]:
        total = total + ref[...]
    chunk = total.shape[0]
    hidden = total.shape[1] // 2
    pre, back = total[:, :hidden], total[:, hidden:]
    start = pl.multiple_of(lax.axis_index("edata") * chunk, chunk)
    gate = gate_ref[pl.ds(start, chunk), :][:, :1]
    activation, slopes = gelu_pair(pre)
    pack_ref[:, :hidden] = (gate * back * slopes).astype(BF16)
    pack_ref[:, hidden : 2 * hidden] = (gate * activation).astype(BF16)
    slot_gate = jnp.sum(activation * back, axis=1, keepdims=True)
    high = slot_gate.astype(BF16).astype(F32)
    lane = lax.broadcasted_iota(jnp.int32, (chunk, GATE_LANES), 1)
    pack_ref[:, 2 * hidden :] = jnp.where(
        lane == 0, high, jnp.where(lane == 1, slot_gate - high, 0.0)
    ).astype(BF16)


def slot_kernel(capacity, pieces, edatas, *refs):
    pack_refs, w_in_ref, slot_refs = (
        refs[:edatas],
        refs[edatas],
        refs[edatas + 1 : edatas + 1 + pieces],
    )
    dpre_ref, act_ref, all_ref = refs[edatas + 1 + pieces :]
    feats, hidden = w_in_ref.shape
    chunk = pack_refs[0].shape[0]
    mine = lax.axis_index("edata")
    for step in range(edatas):
        start = pl.multiple_of((mine ^ step) * chunk, chunk)
        all_ref[pl.ds(start, chunk), :] = pack_refs[step][...]
    packed = all_ref[...]
    rows = packed.shape[0]
    dpre = packed[:, :hidden]
    slot = lax.dot_general(dpre, w_in_ref[...], COLS_BY_COLS, preferred_element_type=F32)
    each = rows // pieces
    for index in range(pieces):
        span = slice(index * each, (index + 1) * each)
        slot_refs[index][:, :feats] = slot[span].astype(BF16)
        slot_refs[index][:, feats:] = packed[span, 2 * hidden :]
    groups = rows // capacity
    dpre = dpre.astype(F32).reshape(groups, capacity, hidden)
    act = packed[:, hidden : 2 * hidden].astype(F32).reshape(groups, capacity, hidden)
    blank = jnp.zeros_like(dpre)
    dpre_ref[...] = jnp.concatenate([dpre, blank], axis=1).reshape(2 * rows, hidden).astype(BF16)
    act_ref[...] = jnp.concatenate([blank, act], axis=1).reshape(2 * rows, hidden).astype(BF16)


def weight_kernel(pieces, *refs):
    rows_refs = refs[:pieces]
    dpre_ref, act_ref, w_in_ref, w_out_ref = refs[pieces:]
    feats = w_in_ref.shape[0]
    rows = jnp.concatenate([ref[:, :feats] for ref in rows_refs], axis=0)
    w_in_ref[...] = lax.dot_general(rows, dpre_ref[...], ROWS_BY_ROWS, preferred_element_type=F32)
    w_out_ref[...] = lax.dot_general(act_ref[...], rows, ROWS_BY_ROWS, preferred_element_type=F32)


def combine_kernel(pieces, *refs):
    came_refs = refs[:pieces]
    place_ref, routes_ref, gates_ref, tokens_ref, gate_out_ref = refs[pieces:]
    feats = tokens_ref.shape[1]
    came = jnp.concatenate([ref[...] for ref in came_refs], axis=0)
    capacity = place_ref.shape[0] // WINDOW
    half = came.shape[0] // WINDOW
    place = place_ref[...].astype(F32)
    spread = []
    for expert in range(WINDOW):
        own = place[expert * capacity : (expert + 1) * capacity]
        spread.append(jnp.concatenate([own] * (half // capacity), axis=0).astype(BF16))
    tokens_ref[...] = lax.dot_general(
        jnp.concatenate(spread, axis=0), came[:, :feats], ROWS_BY_ROWS, preferred_element_type=F32
    ).astype(BF16)
    routes = routes_ref[...]
    own = own_expert()
    result = jnp.zeros(routes.shape, F32)
    for index, expert in enumerate((own, 1 - own)):
        sums = lax.dot_general(
            came[index * half : (index + 1) * half, feats:],
            spread[index],
            ROWS_BY_ROWS,
            preferred_element_type=F32,
        )
        result = result + jnp.where(routes == expert, sums[0:1] + sums[1:2], 0.0)
    gate_out_ref[...] = result


def swap(array, axes, step):
    size = lax.axis_size(axes)
    if step == 0:
        return array
    return lax.ppermute(array, axes, [(index, index ^ step) for index in range(size)])


def body(tokens, grad_out, routes, gates, w_in, w_out):
    plane = ("node", "local")
    groups = lax.axis_size(plane)
    edatas = lax.axis_size("edata")
    half_groups = groups // WINDOW
    tok_rows, feats = tokens.shape
    hidden = w_in.shape[1]
    capacity = 2 * tok_rows // EXPERTS
    slots = WINDOW * capacity
    rows = groups * capacity
    wide = feats + GATE_LANES
    permutes = groups <= MOST_PERMUTES
    pieces = groups if permutes else 1
    shape = jax.ShapeDtypeStruct
    hbm = pl.BlockSpec(memory_space=pl.ANY)
    routes_t, gates_t = routes.T, gates.T

    own_rows, other_rows, place = call(
        gather_kernel,
        (
            shape((2 * capacity, wide), BF16),
            shape((2 * capacity, wide), BF16),
            shape((slots, tok_rows), BF16),
        ),
        4 * slots * tok_rows * feats,
        4 * tok_rows * feats + 4 * rows * feats,
        in_specs=[hbm] * 4,
        scratch_shapes=[
            pltpu.VMEM((2, tok_rows), jnp.int32),
            pltpu.VMEM((2, tok_rows), BF16),
            pltpu.VMEM((tok_rows, feats), BF16),
            pltpu.VMEM((tok_rows, feats), BF16),
            pltpu.SemaphoreType.DMA((4,)),
        ],
    )(routes_t, gates_t, tokens, grad_out)
    if permutes:
        got = [
            swap(own_rows if step < half_groups else other_rows, plane, step)
            for step in range(groups)
        ]
    else:
        expert_of = jnp.arange(groups) // half_groups
        mine = (expert_of == own_expert())[:, None, None]
        send = jnp.where(mine, own_rows[None], other_rows[None])
        got = lax.all_to_all(send, plane, split_axis=0, concat_axis=0, tiled=True)
        got = [got.reshape(2 * rows, wide)]
    chunk = rows // edatas
    *parts, gate_rows = call(
        functools.partial(part_kernel, capacity, pieces, edatas),
        (shape((chunk, 2 * hidden), F32),) * edatas + (shape((rows, GATE_LANES), F32),),
        8 * rows * feats * hidden,
        4 * rows * feats + 4 * feats * hidden,
        scratch_shapes=[pltpu.VMEM((rows, 2 * hidden), F32)],
    )(*got, w_in, w_out)
    parts = [swap(part, "edata", step) for step, part in enumerate(parts)]
    pack = call(
        functools.partial(hidden_kernel, edatas),
        shape((chunk, 2 * hidden + GATE_LANES), BF16),
        40 * chunk * hidden,
        8 * chunk * hidden * edatas,
    )(*parts, gate_rows)
    packs = [swap(pack, "edata", step) for step in range(edatas)]
    *slot_parts, dpre, act = call(
        functools.partial(slot_kernel, capacity, pieces, edatas),
        (shape((rows // pieces, wide), BF16),) * pieces
        + (shape((2 * rows, hidden), BF16), shape((2 * rows, hidden), BF16)),
        2 * rows * feats * hidden,
        2 * feats * hidden + 2 * rows * feats,
        scratch_shapes=[pltpu.VMEM((rows, 2 * hidden + GATE_LANES), BF16)],
    )(*packs, w_in)
    if permutes:
        came = [swap(part, plane, step) for step, part in enumerate(slot_parts)]
    else:
        came = lax.all_to_all(
            slot_parts[0].reshape(groups, capacity, wide),
            plane,
            split_axis=0,
            concat_axis=0,
            tiled=True,
        )
        came = jnp.roll(came.reshape(rows, wide), -own_expert() * (rows // WINDOW), axis=0)
        came = [came]
    grad_w_in, grad_w_out = call(
        functools.partial(weight_kernel, pieces),
        (shape((feats, hidden), F32), shape((hidden, feats), F32)),
        8 * rows * feats * hidden,
        8 * feats * hidden,
    )(*got, dpre, act)
    grad_tokens, grad_gates = call(
        functools.partial(combine_kernel, pieces),
        (shape((tok_rows, feats), BF16), shape((2, tok_rows), F32)),
        2 * rows * tok_rows * feats,
        2 * rows * feats + 2 * tok_rows * feats,
    )(*came, place, routes_t, gates_t)
    return (grad_tokens, grad_gates.T, grad_w_in, grad_w_out)


def solution(mesh):
    in_specs = (
        P(("node", "local"), "edata"),
        P(("node", "local"), "edata"),
        P(("node", "local"), None),
        P(("node", "local"), None),
        P("edata", ("node", "local")),
        P(("node", "local"), "edata"),
    )
    out_specs = (
        P(("node", "local"), "edata"),
        P(("node", "local"), None),
        P("edata", ("node", "local")),
        P(("node", "local"), "edata"),
    )
    return jax.shard_map(body, mesh=mesh, in_specs=in_specs, out_specs=out_specs, check_vma=False)
```

```python
import functools

import jax
import jax.numpy as jnp
from jax import lax
from jax.experimental import pallas as pl
from jax.experimental.pallas import tpu as pltpu
from jax.sharding import PartitionSpec as P

EXPERTS = 64
WINDOW = 2
LANES = 128
PLANE = ("node", "local")
VMEM_LIMIT = 40 * 1024 * 1024

BF16 = jnp.bfloat16
F32 = jnp.float32
I16 = jnp.int16
ROWS_BY_ROWS = (((0,), (0,)), ((), ()))
COLS_BY_COLS = (((1,), (1,)), ((), ()))


def gelu_pair(pre_act):
    coefficient = 0.7978845608028654
    square = pre_act * pre_act
    tanh_val = jnp.tanh(coefficient * (pre_act + 0.044715 * pre_act * square))
    half = 0.5 * (1.0 + tanh_val)
    activation = pre_act * half
    slopes = half + 0.5 * pre_act * (1.0 - tanh_val * tanh_val) * coefficient * (
        1.0 + 3.0 * 0.044715 * square
    )
    return (activation, slopes)


def call(kernel, out_shape, flops, moved, limit=VMEM_LIMIT, **more):
    return pl.pallas_call(
        kernel,
        out_shape=out_shape,
        compiler_params=pltpu.CompilerParams(vmem_limit_bytes=limit),
        cost_estimate=pl.CostEstimate(flops=flops, bytes_accessed=moved, transcendentals=0),
        **more,
    )


def own_expert():
    half_nodes = lax.axis_size("node") // WINDOW
    return lax.axis_index("node") // half_nodes


def split_value(value):
    high = value.astype(BF16).astype(F32)
    lane = lax.broadcasted_iota(jnp.int32, (value.shape[0], LANES), 1)
    return jnp.where(lane == 0, high, jnp.where(lane == 1, value - high, 0.0))


def encode(values):
    top = jnp.max(jnp.abs(values), axis=1, keepdims=True)
    power = jnp.ceil(jnp.log2(jnp.maximum(top, 1e-30)))
    codes = jnp.round(values * (1.999 * jnp.exp2(14.0 - power)))
    exponent = jnp.broadcast_to(power, (values.shape[0], LANES))
    return codes.astype(jnp.int32).astype(I16), exponent.astype(jnp.int32).astype(I16)


def decode(codes, exponent):
    power = exponent.astype(jnp.int32).astype(F32)[:, :1]
    return codes.astype(jnp.int32).astype(F32) * (jnp.exp2(power - 14.0) / 1.999)


def store_codes(out_ref, pair):
    hidden = pair[0].shape[1]
    for index, values in enumerate(pair):
        codes, exponent = encode(values)
        out_ref[:, index * hidden : (index + 1) * hidden] = codes
        start = 2 * hidden + index * LANES
        out_ref[:, start : start + LANES] = exponent


def load_codes(ref):
    hidden = (ref.shape[1] - 2 * LANES) // 2
    return [
        decode(
            ref[:, index * hidden : (index + 1) * hidden],
            ref[:, 2 * hidden + index * LANES : 2 * hidden + (index + 1) * LANES],
        )
        for index in range(2)
    ]


def gather_kernel(routes_hbm, gates_hbm, tokens_hbm, grads_hbm, own_ref, other_ref, place_ref,
                  routes_ref, gates_ref, tokens_ref, grads_ref, sems):
    tok_rows, feats = tokens_ref.shape
    slots = place_ref.shape[0]
    capacity = slots // WINDOW
    pairs = (
        (routes_hbm, routes_ref),
        (gates_hbm, gates_ref),
        (tokens_hbm, tokens_ref),
        (grads_hbm, grads_ref),
    )
    copies = [
        pltpu.make_async_copy(source, target, sems.at[index])
        for index, (source, target) in enumerate(pairs)
    ]
    for copy in copies:
        copy.start()
    earlier = lax.broadcasted_iota(jnp.int32, (tok_rows, tok_rows), 0) < lax.broadcasted_iota(
        jnp.int32, (tok_rows, tok_rows), 1
    )
    earlier = earlier.astype(F32).astype(BF16)
    slot_of = lax.broadcasted_iota(jnp.int32, (capacity, tok_rows), 0).astype(F32)
    row_of = lax.broadcasted_iota(jnp.int32, (8, tok_rows), 0)
    own = own_expert()
    copies[0].wait()
    copies[1].wait()
    routes = routes_ref[...]
    gates = gates_ref[...].astype(F32)
    named = []
    weight = []
    for expert in (own, 1 - own):
        hit = (routes == expert).astype(F32)
        named.append(hit[0:1] + hit[1:2])
        scaled = hit * gates
        weight.append(scaled[0:1] + scaled[1:2])
    names = jnp.where(row_of == 0, named[0], jnp.where(row_of == 1, named[1], 0.0)).astype(BF16)
    before = jnp.dot(names, earlier, preferred_element_type=F32)
    parts = [jnp.where(before[e : e + 1] == slot_of, named[e], 0.0) for e in range(WINDOW)]
    place = jnp.concatenate(parts, axis=0).astype(BF16)
    place_ref[...] = place
    copies[2].wait()
    rows_x = jnp.dot(place, tokens_ref[...], preferred_element_type=F32)
    copies[3].wait()
    rows_dy = jnp.dot(place, grads_ref[...], preferred_element_type=F32)
    for expert, out_ref in ((0, own_ref), (1, other_ref)):
        span = slice(expert * capacity, (expert + 1) * capacity)
        out_ref[:, :feats] = jnp.concatenate([rows_x[span], rows_dy[span]], axis=0).astype(BF16)
        gate = jnp.sum(parts[expert] * weight[expert], axis=1, keepdims=True)
        gate = jnp.concatenate([gate, gate], axis=0)
        out_ref[:, feats:] = jnp.broadcast_to(gate, (2 * capacity, LANES)).astype(BF16)


def join_kernel(first_ref, second_ref, out_ref):
    rows = first_ref.shape[0]
    out_ref[:rows] = first_ref[...]
    out_ref[rows:] = second_ref[...]


def part_kernel(capacity, first_ref, second_ref, w_in_ref, w_out_ref, part_ref, gate_ref):
    feats, hidden = w_in_ref.shape
    rows = jnp.concatenate([first_ref[...], second_ref[...]], axis=0)
    groups = rows.shape[0] // (2 * capacity)
    gate = rows[:, feats:].astype(F32).reshape(groups, 2 * capacity, LANES)
    gate_ref[...] = gate[:, :capacity].reshape(groups * capacity, LANES)
    rows = rows[:, :feats]
    pre = jnp.dot(rows, w_in_ref[...], preferred_element_type=F32)
    back = lax.dot_general(rows, w_out_ref[...], COLS_BY_COLS, preferred_element_type=F32)
    pre = pre.reshape(groups, 2 * capacity, hidden)[:, :capacity]
    back = back.reshape(groups, 2 * capacity, hidden)[:, capacity:]
    pair = [value.reshape(groups * capacity, hidden) for value in (pre, back)]
    store_codes(part_ref, pair)


def add_codes_kernel(first_ref, second_ref, out_ref):
    pairs = zip(load_codes(first_ref), load_codes(second_ref))
    store_codes(out_ref, [first + second for first, second in pairs])


def slot_kernel(capacity, first_ref, second_ref, gate_ref, w_in_ref, keep_ref, send_ref, dpre_ref,
                act_ref):
    feats, hidden = w_in_ref.shape
    pairs = zip(load_codes(first_ref), load_codes(second_ref))
    pre, back = [first + second for first, second in pairs]
    gate = gate_ref[:, :1]
    activation, slopes = gelu_pair(pre)
    dpre = (gate * back * slopes).astype(BF16)
    act = gate * activation
    rows = dpre.shape[0]
    slot = lax.dot_general(dpre, w_in_ref[...], COLS_BY_COLS, preferred_element_type=F32)
    slot_gate = split_value(jnp.sum(activation * back, axis=1, keepdims=True))
    half = rows // 2
    keep_ref[:, :feats] = slot[:half]
    keep_ref[:, feats:] = slot_gate[:half]
    send_ref[:, :feats] = slot[half:].astype(send_ref.dtype)
    send_ref[:, feats:] = slot_gate[half:].astype(send_ref.dtype)
    groups = rows // capacity
    dpre = dpre.astype(F32).reshape(groups, capacity, hidden)
    act = act.reshape(groups, capacity, hidden)
    blank = jnp.zeros_like(dpre)
    dpre_ref[...] = jnp.concatenate([dpre, blank], axis=1).reshape(2 * rows, hidden).astype(BF16)
    act_ref[...] = jnp.concatenate([blank, act], axis=1).reshape(2 * rows, hidden).astype(BF16)


def halve_kernel(kept_ref, came_ref, keep_ref, send_ref):
    half, wide = keep_ref.shape
    feats = wide - LANES
    total = kept_ref[...] + came_ref[...].astype(F32)
    keep_ref[...] = total[:half]
    send_ref[:, :feats] = total[half:, :feats].astype(send_ref.dtype)
    gate = jnp.sum(total[half:, feats:], axis=1, keepdims=True)
    send_ref[:, feats:] = split_value(gate).astype(send_ref.dtype)


def w_in_kernel(first_ref, second_ref, dpre_ref, out_ref):
    feats = out_ref.shape[0]
    rows = jnp.concatenate([first_ref[:, :feats], second_ref[:, :feats]], axis=0)
    out_ref[...] = lax.dot_general(rows, dpre_ref[...], ROWS_BY_ROWS, preferred_element_type=F32)


def w_out_kernel(first_ref, second_ref, act_ref, out_ref):
    feats = out_ref.shape[1]
    rows = jnp.concatenate([first_ref[:, :feats], second_ref[:, :feats]], axis=0)
    out_ref[...] = lax.dot_general(act_ref[...], rows, ROWS_BY_ROWS, preferred_element_type=F32)


def combine_kernel(kept_ref, came_ref, place_ref, routes_ref, gates_ref, tokens_ref, gate_out_ref):
    feats = tokens_ref.shape[1]
    slots = jnp.concatenate([kept_ref[...], came_ref[...].astype(F32)], axis=0)
    place = place_ref[...]
    grads = slots[:, :feats]
    high = grads.astype(BF16)
    low = (grads - high.astype(F32)).astype(BF16)
    tokens_ref[...] = lax.dot_general(
        jnp.concatenate([place, place], axis=0),
        jnp.concatenate([high, low], axis=0),
        ROWS_BY_ROWS,
        preferred_element_type=F32,
    ).astype(BF16)
    slot_gate = jnp.sum(slots[:, feats:], axis=1, keepdims=True)
    picked = place.astype(F32) * slot_gate
    capacity = picked.shape[0] // WINDOW
    routes = routes_ref[...]
    own = own_expert()
    result = jnp.zeros(routes.shape, F32)
    for index, expert in enumerate((own, 1 - own)):
        span = slice(index * capacity, (index + 1) * capacity)
        value = jnp.sum(picked[span], axis=0, keepdims=True)
        result = result + jnp.where(routes == expert, value, 0.0)
    gate_out_ref[...] = result


def swap(array, axes, bit):
    size = lax.axis_size(axes)
    return lax.ppermute(array, axes, [(index, index ^ bit) for index in range(size)])


def body(tokens, grad_out, routes, gates, w_in, w_out):
    groups = lax.axis_size(PLANE)
    edatas = lax.axis_size("edata")
    tok_rows, feats = tokens.shape
    hidden = w_in.shape[1]
    capacity = 2 * tok_rows // EXPERTS
    slots = WINDOW * capacity
    rows = groups * capacity
    wide = feats + LANES
    coded = 2 * hidden + 2 * LANES
    shape = jax.ShapeDtypeStruct
    hbm = pl.BlockSpec(memory_space=pl.ANY)
    routes_t, gates_t = routes.T, gates.T

    own_rows, other_rows, place = call(
        gather_kernel,
        (
            shape((2 * capacity, wide), BF16),
            shape((2 * capacity, wide), BF16),
            shape((slots, tok_rows), BF16),
        ),
        4 * slots * tok_rows * feats,
        4 * tok_rows * feats,
        limit=None,
        in_specs=[hbm] * 4,
        scratch_shapes=[
            pltpu.VMEM((2, tok_rows), jnp.int32),
            pltpu.VMEM((2, tok_rows), BF16),
            pltpu.VMEM((tok_rows, feats), BF16),
            pltpu.VMEM((tok_rows, feats), BF16),
            pltpu.SemaphoreType.DMA((4,)),
        ],
    )(routes_t, gates_t, tokens, grad_out)

    expert_bit = groups // WINDOW
    held, came = own_rows, swap(other_rows, PLANE, expert_bit)
    bit = expert_bit // 2
    while bit:
        count = held.shape[0]
        held = call(join_kernel, shape((2 * count, wide), BF16), 0, 8 * count * wide)(held, came)
        came = swap(held, PLANE, bit)
        bit //= 2

    part, gate_rows = call(
        functools.partial(part_kernel, capacity),
        (shape((rows, coded), I16), shape((rows, LANES), F32)),
        8 * rows * feats * hidden,
        4 * rows * feats + 4 * feats * hidden,
    )(held, came, w_in, w_out)
    bit = 1
    other = swap(part, "edata", bit)
    while 2 * bit < edatas:
        part = call(
            add_codes_kernel, shape((rows, coded), I16), 8 * rows * hidden, 6 * rows * coded
        )(part, other)
        bit *= 2
        other = swap(part, "edata", bit)

    half = rows // 2
    keep, send, dpre, act = call(
        functools.partial(slot_kernel, capacity),
        (
            shape((half, wide), F32),
            shape((half, wide), F32),
            shape((2 * rows, hidden), BF16),
            shape((2 * rows, hidden), BF16),
        ),
        2 * rows * feats * hidden,
        2 * feats * hidden + 2 * rows * feats,
    )(part, other, gate_rows, w_in)
    bit = 1
    while bit < expert_bit:
        back = swap(send, PLANE, bit)
        half //= 2
        keep, send = call(
            halve_kernel,
            (shape((half, wide), F32), shape((half, wide), BF16)),
            4 * half * wide,
            20 * half * wide,
        )(keep, back)
        bit *= 2
    back = swap(send, PLANE, expert_bit)
    grad_w_in = call(
        w_in_kernel,
        shape((feats, hidden), F32),
        4 * rows * feats * hidden,
        4 * feats * hidden,
    )(held, came, dpre)
    grad_w_out = call(
        w_out_kernel,
        shape((hidden, feats), F32),
        4 * rows * feats * hidden,
        4 * feats * hidden,
    )(held, came, act)
    grad_tokens, grad_gates = call(
        combine_kernel,
        (shape((tok_rows, feats), BF16), shape((2, tok_rows), F32)),
        4 * slots * tok_rows * feats,
        2 * tok_rows * feats,
    )(keep, back, place, routes_t, gates_t)
    return (grad_tokens, grad_gates.T, grad_w_in, grad_w_out)


def solution(mesh):
    in_specs = (
        P(("node", "local"), "edata"),
        P(("node", "local"), "edata"),
        P(("node", "local"), None),
        P(("node", "local"), None),
        P("edata", ("node", "local")),
        P(("node", "local"), "edata"),
    )
    out_specs = (
        P(("node", "local"), "edata"),
        P(("node", "local"), None),
        P("edata", ("node", "local")),
        P(("node", "local"), "edata"),
    )
    return jax.shard_map(body, mesh=mesh, in_specs=in_specs, out_specs=out_specs, check_vma=False)
```

```python
import functools

import jax
import jax.numpy as jnp
from jax import lax
from jax.experimental import pallas as pl
from jax.experimental.pallas import tpu as pltpu
from jax.sharding import PartitionSpec as P

EXPERTS = 64
WINDOW = 2
LANES = 128
PIECES = 4
VMEM_LIMIT = 40 * 1024 * 1024

BF16 = jnp.bfloat16
F32 = jnp.float32
I16 = jnp.int16
ROWS_BY_ROWS = (((0,), (0,)), ((), ()))
COLS_BY_COLS = (((1,), (1,)), ((), ()))


def gelu_pair(pre_act):
    coefficient = 0.7978845608028654
    square = pre_act * pre_act
    tanh_val = jnp.tanh(coefficient * (pre_act + 0.044715 * pre_act * square))
    half = 0.5 * (1.0 + tanh_val)
    activation = pre_act * half
    slopes = half + 0.5 * pre_act * (1.0 - tanh_val * tanh_val) * coefficient * (
        1.0 + 3.0 * 0.044715 * square
    )
    return (activation, slopes)


def call(kernel, out_shape, flops, moved, limit=VMEM_LIMIT, **more):
    return pl.pallas_call(
        kernel,
        out_shape=out_shape,
        compiler_params=pltpu.CompilerParams(vmem_limit_bytes=limit),
        cost_estimate=pl.CostEstimate(flops=flops, bytes_accessed=moved, transcendentals=0),
        **more,
    )


def own_expert():
    half_nodes = lax.axis_size("node") // WINDOW
    return lax.axis_index("node") // half_nodes


def split_value(value):
    high = value.astype(BF16).astype(F32)
    lane = lax.broadcasted_iota(jnp.int32, (value.shape[0], LANES), 1)
    return jnp.where(lane == 0, high, jnp.where(lane == 1, value - high, 0.0))


def encode(values):
    top = jnp.max(jnp.abs(values), axis=1, keepdims=True)
    power = jnp.ceil(jnp.log2(jnp.maximum(top, 1e-30)))
    codes = jnp.round(values * (1.999 * jnp.exp2(14.0 - power)))
    return codes.astype(jnp.int32).astype(I16), power


def decode(codes, power):
    return codes.astype(jnp.int32).astype(F32) * (jnp.exp2(power - 14.0) / 1.999)


def store_codes(out_ref, pair):
    hidden = pair[0].shape[1]
    lane = lax.broadcasted_iota(jnp.int32, (pair[0].shape[0], LANES), 1)
    powers = []
    for index, values in enumerate(pair):
        codes, power = encode(values)
        out_ref[:, index * hidden : (index + 1) * hidden] = codes
        powers.append(power)
    powers = jnp.where(lane == 0, powers[0], powers[1])
    out_ref[:, 2 * hidden :] = powers.astype(jnp.int32).astype(I16)


def load_codes(ref):
    hidden = (ref.shape[1] - LANES) // 2
    powers = ref[:, 2 * hidden :].astype(jnp.int32).astype(F32)
    return [
        decode(ref[:, index * hidden : (index + 1) * hidden], powers[:, index : index + 1])
        for index in range(2)
    ]


def gather_kernel(routes_hbm, gates_hbm, tokens_hbm, grads_hbm, own_ref, other_ref, place_ref,
                  routes_ref, gates_ref, tokens_ref, grads_ref, sems):
    tok_rows, feats = tokens_ref.shape
    capacity = own_ref.shape[0] // 2
    slots = WINDOW * capacity
    copies = [
        pltpu.make_async_copy(routes_hbm, routes_ref, sems.at[0]),
        pltpu.make_async_copy(gates_hbm, gates_ref, sems.at[1]),
    ]
    count = tok_rows // PIECES
    for source, target in ((tokens_hbm, tokens_ref), (grads_hbm, grads_ref)):
        for piece in range(PIECES):
            span = pl.ds(piece * count, count)
            copies.append(
                pltpu.make_async_copy(source.at[span], target.at[span], sems.at[len(copies)])
            )
    for copy in copies:
        copy.start()
    earlier = lax.broadcasted_iota(jnp.int32, (tok_rows, tok_rows), 0) < lax.broadcasted_iota(
        jnp.int32, (tok_rows, tok_rows), 1
    )
    earlier = earlier.astype(F32).astype(BF16)
    slot_of = lax.broadcasted_iota(jnp.int32, (capacity, tok_rows), 0).astype(F32)
    row_of = lax.broadcasted_iota(jnp.int32, (8, tok_rows), 0)
    own = own_expert()
    copies[0].wait()
    copies[1].wait()
    routes = routes_ref[...]
    gates = gates_ref[...].astype(F32)
    hits = [(routes == expert).astype(F32) for expert in (own, 1 - own)]
    named = [hit[0:1] + hit[1:2] for hit in hits]
    weight = [hit * gates for hit in hits]
    weight = [value[0:1] + value[1:2] for value in weight]
    names = jnp.where(row_of == 0, named[0], jnp.where(row_of == 1, named[1], 0.0)).astype(BF16)
    before = jnp.dot(names, earlier, preferred_element_type=F32)
    parts = [jnp.where(before[e : e + 1] == slot_of, named[e], 0.0) for e in range(WINDOW)]
    place = jnp.concatenate(parts, axis=0).astype(BF16)
    place_ref[:slots] = place
    masks = jnp.zeros((16, tok_rows), F32)
    row_of = lax.broadcasted_iota(jnp.int32, masks.shape, 0)
    for index, hit in enumerate(hits):
        for k in range(2):
            masks = jnp.where(row_of == 2 * index + k, hit[k : k + 1], masks)
    place_ref[slots:] = masks.astype(BF16)
    for copy in copies[2 : 2 + PIECES]:
        copy.wait()
    rows_x = jnp.dot(place, tokens_ref[...], preferred_element_type=F32)
    for copy in copies[2 + PIECES :]:
        copy.wait()
    rows_dy = jnp.dot(place, grads_ref[...], preferred_element_type=F32)
    for expert, out_ref in ((0, own_ref), (1, other_ref)):
        span = slice(expert * capacity, (expert + 1) * capacity)
        out_ref[:, :feats] = jnp.concatenate([rows_x[span], rows_dy[span]], axis=0).astype(BF16)
        gate = jnp.sum(parts[expert] * weight[expert], axis=1, keepdims=True)
        gate = jnp.concatenate([gate, gate], axis=0)
        out_ref[:, feats:] = jnp.broadcast_to(gate, (2 * capacity, LANES)).astype(BF16)


def join_kernel(*refs):
    *pieces, out_ref = refs
    rows = pieces[0].shape[0]
    for index, ref in enumerate(pieces):
        out_ref[index * rows : (index + 1) * rows] = ref[...]


def part_kernel(capacity, first_ref, second_ref, w_in_ref, w_out_ref, part_ref, gate_ref):
    feats, hidden = w_in_ref.shape
    rows = jnp.concatenate([first_ref[...], second_ref[...]], axis=0)
    groups = rows.shape[0] // (2 * capacity)
    gate = rows[:, feats:].astype(F32).reshape(groups, 2 * capacity, LANES)
    gate_ref[...] = gate[:, :capacity].reshape(groups * capacity, LANES)
    rows = rows[:, :feats]
    pre = jnp.dot(rows, w_in_ref[...], preferred_element_type=F32)
    back = lax.dot_general(rows, w_out_ref[...], COLS_BY_COLS, preferred_element_type=F32)
    pre = pre.reshape(groups, 2 * capacity, hidden)[:, :capacity]
    back = back.reshape(groups, 2 * capacity, hidden)[:, capacity:]
    pair = [value.reshape(groups * capacity, hidden) for value in (pre, back)]
    store_codes(part_ref, pair)


def add_codes_kernel(first_ref, second_ref, out_ref):
    pairs = zip(load_codes(first_ref), load_codes(second_ref))
    store_codes(out_ref, [first + second for first, second in pairs])


def slot_kernel(capacity, first_ref, second_ref, gate_ref, w_in_ref, keep_ref, send_ref, dpre_ref,
                act_ref):
    feats, hidden = w_in_ref.shape
    pairs = zip(load_codes(first_ref), load_codes(second_ref))
    pre, back = [first + second for first, second in pairs]
    gate = gate_ref[:, :1]
    activation, slopes = gelu_pair(pre)
    dpre = (gate * back * slopes).astype(BF16)
    act = gate * activation
    rows = dpre.shape[0]
    slot = lax.dot_general(dpre, w_in_ref[...], COLS_BY_COLS, preferred_element_type=F32)
    slot_gate = split_value(jnp.sum(activation * back, axis=1, keepdims=True))
    half = rows // 2
    keep_ref[:, :feats] = slot[:half]
    keep_ref[:, feats:] = slot_gate[:half]
    send_ref[:, :feats] = slot[half:].astype(send_ref.dtype)
    send_ref[:, feats:] = slot_gate[half:].astype(send_ref.dtype)
    groups = rows // capacity
    dpre = dpre.astype(F32).reshape(groups, capacity, hidden)
    act = act.reshape(groups, capacity, hidden)
    blank = jnp.zeros_like(dpre)
    dpre_ref[...] = jnp.concatenate([dpre, blank], axis=1).reshape(2 * rows, hidden).astype(BF16)
    act_ref[...] = jnp.concatenate([blank, act], axis=1).reshape(2 * rows, hidden).astype(BF16)


def halve_kernel(kept_ref, came_ref, keep_ref, send_ref):
    half = keep_ref.shape[0]
    total = kept_ref[...] + came_ref[...]
    keep_ref[...] = total[:half]
    send_ref[...] = total[half:]


def deal_kernel(kept_ref, came_ref, keep_ref, *send_refs):
    each, wide = keep_ref.shape
    feats = wide - LANES
    total = kept_ref[...] + came_ref[...]
    keep_ref[...] = total[:each]
    gate = split_value(jnp.sum(total[:, feats:], axis=1, keepdims=True))
    for index, send_ref in enumerate(send_refs):
        span = slice((index + 1) * each, (index + 2) * each)
        send_ref[:, :feats] = total[span, :feats].astype(BF16)
        send_ref[:, feats:] = gate[span].astype(BF16)


def w_in_kernel(first_ref, second_ref, dpre_ref, out_ref):
    feats = out_ref.shape[0]
    rows = jnp.concatenate([first_ref[:, :feats], second_ref[:, :feats]], axis=0)
    out_ref[...] = lax.dot_general(rows, dpre_ref[...], ROWS_BY_ROWS, preferred_element_type=F32)


def w_out_kernel(first_ref, second_ref, act_ref, out_ref):
    feats = out_ref.shape[1]
    rows = jnp.concatenate([first_ref[:, :feats], second_ref[:, :feats]], axis=0)
    out_ref[...] = lax.dot_general(act_ref[...], rows, ROWS_BY_ROWS, preferred_element_type=F32)


def combine_kernel(steps, *refs):
    kept_ref, came_refs = refs[0], refs[1:steps]
    place_ref, tokens_hbm, gate_out_ref, tokens_ref, sems = refs[steps:]
    tok_rows, feats = tokens_ref.shape
    capacity = kept_ref.shape[0]
    came = [ref[...].astype(F32) for ref in came_refs]
    half = steps // WINDOW
    own = sum(came[: half - 1], kept_ref[...])
    other = sum(came[half:], came[half - 1])
    slots = jnp.concatenate([own, other], axis=0)
    place = place_ref[: WINDOW * capacity]
    grads = slots[:, :feats]
    high = grads.astype(BF16)
    low = (grads - high.astype(F32)).astype(BF16)
    both = jnp.concatenate([high, low], axis=0)
    twice = jnp.concatenate([place, place], axis=0)
    count = tok_rows // PIECES
    copies = []
    for piece in range(PIECES):
        span = pl.ds(piece * count, count)
        tokens_ref[span] = lax.dot_general(
            twice[:, piece * count : (piece + 1) * count],
            both,
            ROWS_BY_ROWS,
            preferred_element_type=F32,
        ).astype(BF16)
        copy = pltpu.make_async_copy(tokens_ref.at[span], tokens_hbm.at[span], sems.at[piece])
        copy.start()
        copies.append(copy)
    slot_gate = jnp.sum(slots[:, feats:], axis=1, keepdims=True)
    picked = place.astype(F32) * slot_gate
    masks = place_ref[WINDOW * capacity :].astype(F32)
    result = jnp.zeros(gate_out_ref.shape, F32)
    for index in range(WINDOW):
        span = slice(index * capacity, (index + 1) * capacity)
        value = jnp.sum(picked[span], axis=0, keepdims=True)
        result = result + masks[2 * index : 2 * index + 2] * value
    gate_out_ref[...] = result
    for copy in copies:
        copy.wait()


def swap(array, axes, bit):
    size = lax.axis_size(axes)
    return lax.ppermute(array, axes, [(index, index ^ bit) for index in range(size)])


def body(tokens, grad_out, routes, gates, w_in, w_out):
    nodes = lax.axis_size("node")
    locals_ = lax.axis_size("local")
    edatas = lax.axis_size("edata")
    tok_rows, feats = tokens.shape
    hidden = w_in.shape[1]
    capacity = 2 * tok_rows // EXPERTS
    slots = WINDOW * capacity
    rows = nodes * locals_ * capacity
    wide = feats + LANES
    coded = 2 * hidden + LANES
    shape = jax.ShapeDtypeStruct
    hbm = pl.BlockSpec(memory_space=pltpu.HBM)
    vmem = pl.BlockSpec(memory_space=pltpu.VMEM)

    own_rows, other_rows, place = call(
        gather_kernel,
        (
            shape((2 * capacity, wide), BF16),
            shape((2 * capacity, wide), BF16),
            shape((slots + 16, tok_rows), BF16),
        ),
        4 * slots * tok_rows * feats,
        4 * tok_rows * feats,
        in_specs=[hbm] * 4,
        scratch_shapes=[
            pltpu.VMEM((2, tok_rows), jnp.int32),
            pltpu.VMEM((2, tok_rows), BF16),
            pltpu.VMEM((tok_rows, feats), BF16),
            pltpu.VMEM((tok_rows, feats), BF16),
            pltpu.SemaphoreType.DMA((2 + 2 * PIECES,)),
        ],
    )(routes.T, gates.T, tokens, grad_out)

    pieces = [own_rows]
    for step in range(1, nodes):
        pieces.append(swap(own_rows if step < nodes // WINDOW else other_rows, "node", step))
    count = nodes * 2 * capacity
    held = call(join_kernel, shape((count, wide), BF16), 0, 4 * count * wide)(*pieces)
    came = swap(held, "local", 1)
    bit = 2
    while bit < locals_:
        count = 2 * held.shape[0]
        held = call(join_kernel, shape((count, wide), BF16), 0, 4 * count * wide)(held, came)
        came = swap(held, "local", bit)
        bit *= 2

    part, gate_rows = call(
        functools.partial(part_kernel, capacity),
        (shape((rows, coded), I16), shape((rows, LANES), F32)),
        8 * rows * feats * hidden,
        4 * rows * feats + 4 * feats * hidden,
    )(held, came, w_in, w_out)
    bit = 1
    other = swap(part, "edata", bit)
    while 2 * bit < edatas:
        part = call(
            add_codes_kernel, shape((rows, coded), I16), 8 * rows * hidden, 6 * rows * coded
        )(part, other)
        bit *= 2
        other = swap(part, "edata", bit)

    half = rows // 2
    keep, send, dpre, act = call(
        functools.partial(slot_kernel, capacity),
        (
            shape((half, wide), F32),
            shape((half, wide), F32),
            shape((2 * rows, hidden), BF16),
            shape((2 * rows, hidden), BF16),
        ),
        2 * rows * feats * hidden,
        2 * feats * hidden + 2 * rows * feats,
    )(part, other, gate_rows, w_in)
    back = swap(send, "local", locals_ // 2)
    bit = locals_ // 4
    while bit:
        half //= 2
        keep, send = call(
            halve_kernel, (shape((half, wide), F32),) * 2, 4 * half * wide, 24 * half * wide
        )(keep, back)
        back = swap(send, "local", bit)
        bit //= 2
    keep, *sends = call(
        deal_kernel,
        (shape((capacity, wide), F32),) + (shape((capacity, wide), BF16),) * (nodes - 1),
        4 * half * wide,
        12 * half * wide,
    )(keep, back)
    backs = [swap(send, "node", step + 1) for step, send in enumerate(sends)]
    grad_w_in = call(
        w_in_kernel,
        shape((feats, hidden), F32),
        4 * rows * feats * hidden,
        4 * feats * hidden,
    )(held, came, dpre)
    grad_w_out = call(
        w_out_kernel,
        shape((hidden, feats), F32),
        4 * rows * feats * hidden,
        4 * feats * hidden,
    )(held, came, act)
    grad_tokens, grad_gates = call(
        functools.partial(combine_kernel, nodes),
        (shape((tok_rows, feats), BF16), shape((2, tok_rows), F32)),
        4 * slots * tok_rows * feats,
        2 * tok_rows * feats,
        in_specs=[vmem] * (nodes + 1),
        out_specs=[hbm, vmem],
        scratch_shapes=[
            pltpu.VMEM((tok_rows, feats), BF16),
            pltpu.SemaphoreType.DMA((PIECES,)),
        ],
    )(keep, *backs, place)
    return (grad_tokens, grad_gates.T, grad_w_in, grad_w_out)


def solution(mesh):
    in_specs = (
        P(("node", "local"), "edata"),
        P(("node", "local"), "edata"),
        P(("node", "local"), None),
        P(("node", "local"), None),
        P("edata", ("node", "local")),
        P(("node", "local"), "edata"),
    )
    out_specs = (
        P(("node", "local"), "edata"),
        P(("node", "local"), None),
        P("edata", ("node", "local")),
        P(("node", "local"), "edata"),
    )
    return jax.shard_map(body, mesh=mesh, in_specs=in_specs, out_specs=out_specs, check_vma=False)
```

```python
import functools

import jax
import jax.numpy as jnp
from jax import lax
from jax.experimental import pallas as pl
from jax.experimental.pallas import tpu as pltpu
from jax.sharding import PartitionSpec as P

EXPERTS = 64
WINDOW = 2
LANES = 128
PIECES = 4
VMEM_LIMIT = 40 * 1024 * 1024

BF16 = jnp.bfloat16
F32 = jnp.float32
I16 = jnp.int16
ROWS_BY_ROWS = (((0,), (0,)), ((), ()))
COLS_BY_COLS = (((1,), (1,)), ((), ()))


def gelu_pair(pre_act):
    coefficient = 0.7978845608028654
    square = pre_act * pre_act
    tanh_val = jnp.tanh(coefficient * (pre_act + 0.044715 * pre_act * square))
    half = 0.5 * (1.0 + tanh_val)
    activation = pre_act * half
    slopes = half + 0.5 * pre_act * (1.0 - tanh_val * tanh_val) * coefficient * (
        1.0 + 3.0 * 0.044715 * square
    )
    return (activation, slopes)


def call(kernel, out_shape, flops, moved, limit=VMEM_LIMIT, in_specs=None, after=(), **more):
    def run(*operands):
        given = in_specs or [pl.BlockSpec(memory_space=pltpu.VMEM)] * len(operands)
        return pl.pallas_call(
            lambda *refs: kernel(*refs[len(after) :]),
            out_shape=out_shape,
            in_specs=[pl.BlockSpec(memory_space=pl.ANY)] * len(after) + list(given),
            compiler_params=pltpu.CompilerParams(vmem_limit_bytes=limit),
            cost_estimate=pl.CostEstimate(flops=flops, bytes_accessed=moved, transcendentals=0),
            **more,
        )(*after, *operands)

    return run


def own_expert():
    half_nodes = lax.axis_size("node") // WINDOW
    return lax.axis_index("node") // half_nodes


def split_value(value):
    high = value.astype(BF16).astype(F32)
    lane = lax.broadcasted_iota(jnp.int32, (value.shape[0], LANES), 1)
    return jnp.where(lane == 0, high, jnp.where(lane == 1, value - high, 0.0))


def encode(values):
    top = jnp.max(jnp.abs(values), axis=1, keepdims=True)
    power = jnp.ceil(jnp.log2(jnp.maximum(top, 1e-30)))
    codes = jnp.round(values * (1.999 * jnp.exp2(14.0 - power)))
    return codes.astype(jnp.int32).astype(I16), power


def decode(codes, power):
    return codes.astype(jnp.int32).astype(F32) * (jnp.exp2(power - 14.0) / 1.999)


def store_codes(out_ref, pair):
    hidden = pair[0].shape[1]
    lane = lax.broadcasted_iota(jnp.int32, (pair[0].shape[0], LANES), 1)
    powers = []
    for index, values in enumerate(pair):
        codes, power = encode(values)
        out_ref[:, index * hidden : (index + 1) * hidden] = codes
        powers.append(power)
    powers = jnp.where(lane == 0, powers[0], powers[1])
    out_ref[:, 2 * hidden :] = powers.astype(jnp.int32).astype(I16)


def load_codes(ref):
    hidden = (ref.shape[1] - LANES) // 2
    powers = ref[:, 2 * hidden :].astype(jnp.int32).astype(F32)
    return [
        decode(ref[:, index * hidden : (index + 1) * hidden], powers[:, index : index + 1])
        for index in range(2)
    ]


def gather_kernel(routes_hbm, gates_hbm, tokens_hbm, grads_hbm, own_ref, other_ref, place_ref,
                  spread_ref, routes_ref, gates_ref, tokens_ref, grads_ref, sems):
    tok_rows, feats = tokens_ref.shape
    capacity = own_ref.shape[0] // 2
    slots = WINDOW * capacity
    copies = [
        pltpu.make_async_copy(routes_hbm, routes_ref, sems.at[0]),
        pltpu.make_async_copy(gates_hbm, gates_ref, sems.at[1]),
    ]
    count = tok_rows // PIECES
    for source, target in ((tokens_hbm, tokens_ref), (grads_hbm, grads_ref)):
        for piece in range(PIECES):
            span = pl.ds(piece * count, count)
            copies.append(
                pltpu.make_async_copy(source.at[span], target.at[span], sems.at[len(copies)])
            )
    for copy in copies:
        copy.start()
    earlier = lax.broadcasted_iota(jnp.int32, (tok_rows, tok_rows), 0) < lax.broadcasted_iota(
        jnp.int32, (tok_rows, tok_rows), 1
    )
    earlier = earlier.astype(F32).astype(BF16)
    slot_of = lax.broadcasted_iota(jnp.int32, (capacity, tok_rows), 0).astype(F32)
    row_of = lax.broadcasted_iota(jnp.int32, (8, tok_rows), 0)
    own = own_expert()
    copies[0].wait()
    copies[1].wait()
    routes = routes_ref[...]
    gates = gates_ref[...].astype(F32)
    hits = [(routes == expert).astype(F32) for expert in (own, 1 - own)]
    named = [hit[0:1] + hit[1:2] for hit in hits]
    weight = [hit * gates for hit in hits]
    weight = [value[0:1] + value[1:2] for value in weight]
    names = jnp.where(row_of == 0, named[0], jnp.where(row_of == 1, named[1], 0.0)).astype(BF16)
    before = jnp.dot(names, earlier, preferred_element_type=F32)
    parts = [jnp.where(before[e : e + 1] == slot_of, named[e], 0.0) for e in range(WINDOW)]
    place = jnp.concatenate(parts, axis=0).astype(BF16)
    place_ref[:slots] = place
    spread_ref[...] = jnp.concatenate(parts + parts, axis=0).T.astype(BF16)
    masks = jnp.zeros((16, tok_rows), F32)
    row_of = lax.broadcasted_iota(jnp.int32, masks.shape, 0)
    for index, hit in enumerate(hits):
        for k in range(2):
            masks = jnp.where(row_of == 2 * index + k, hit[k : k + 1], masks)
    place_ref[slots:] = masks.astype(BF16)
    for copy in copies[2 : 2 + PIECES]:
        copy.wait()
    rows_x = jnp.dot(place, tokens_ref[...], preferred_element_type=F32)
    for copy in copies[2 + PIECES :]:
        copy.wait()
    rows_dy = jnp.dot(place, grads_ref[...], preferred_element_type=F32)
    for expert, out_ref in ((0, own_ref), (1, other_ref)):
        span = slice(expert * capacity, (expert + 1) * capacity)
        out_ref[:, :feats] = jnp.concatenate([rows_x[span], rows_dy[span]], axis=0).astype(BF16)
        gate = jnp.sum(parts[expert] * weight[expert], axis=1, keepdims=True)
        gate = jnp.concatenate([gate, gate], axis=0)
        out_ref[:, feats:] = jnp.broadcast_to(gate, (2 * capacity, LANES)).astype(BF16)


def join_kernel(*refs):
    *pieces, out_ref = refs
    rows = pieces[0].shape[0]
    for index, ref in enumerate(pieces):
        out_ref[index * rows : (index + 1) * rows] = ref[...]


def part_kernel(capacity, rows_ref, w_in_ref, w_out_ref, part_ref, gate_ref):
    feats, hidden = w_in_ref.shape
    groups = rows_ref.shape[0] // (2 * capacity)
    gate = rows_ref[:, feats:].astype(F32).reshape(groups, 2 * capacity, LANES)
    gate_ref[...] = gate[:, :capacity].reshape(groups * capacity, LANES)
    rows = rows_ref[:, :feats]
    pre = jnp.dot(rows, w_in_ref[...], preferred_element_type=F32)
    back = lax.dot_general(rows, w_out_ref[...], COLS_BY_COLS, preferred_element_type=F32)
    pre = pre.reshape(groups, 2 * capacity, hidden)[:, :capacity]
    back = back.reshape(groups, 2 * capacity, hidden)[:, capacity:]
    store_codes(part_ref, [value.reshape(groups * capacity, hidden) for value in (pre, back)])


def add_codes_kernel(first_ref, second_ref, out_ref):
    pairs = zip(load_codes(first_ref), load_codes(second_ref))
    store_codes(out_ref, [first + second for first, second in pairs])


def slot_kernel(capacity, first_ref, second_ref, gate_ref, w_in_ref, slot_ref, dpre_ref, act_ref):
    feats, hidden = w_in_ref.shape
    pairs = zip(load_codes(first_ref), load_codes(second_ref))
    pre, back = [first + second for first, second in pairs]
    gate = gate_ref[:, :1]
    activation, slopes = gelu_pair(pre)
    dpre = (gate * back * slopes).astype(BF16)
    act = gate * activation
    rows = dpre.shape[0]
    slot_ref[:, :feats] = lax.dot_general(
        dpre, w_in_ref[...], COLS_BY_COLS, preferred_element_type=F32
    )
    slot_ref[:, feats:] = split_value(jnp.sum(activation * back, axis=1, keepdims=True))
    groups = rows // capacity
    dpre = dpre.astype(F32).reshape(groups, capacity, hidden)
    act = act.reshape(groups, capacity, hidden)
    blank = jnp.zeros_like(dpre)
    dpre_ref[...] = jnp.concatenate([dpre, blank], axis=1).reshape(2 * rows, hidden).astype(BF16)
    act_ref[...] = jnp.concatenate([blank, act], axis=1).reshape(2 * rows, hidden).astype(BF16)


def halve_kernel(kept_ref, came_ref, keep_ref, send_ref):
    half = keep_ref.shape[0]
    total = kept_ref[...] + came_ref[...]
    keep_ref[...] = total[:half]
    send_ref[...] = total[half:]


def deal_kernel(kept_ref, came_ref, keep_ref, *send_refs):
    each, wide = keep_ref.shape
    feats = wide - LANES
    total = kept_ref[...] + came_ref[...]
    keep_ref[...] = total[:each]
    gate = split_value(jnp.sum(total[:, feats:], axis=1, keepdims=True))
    for index, send_ref in enumerate(send_refs):
        span = slice((index + 1) * each, (index + 2) * each)
        send_ref[:, :feats] = total[span, :feats].astype(BF16)
        send_ref[:, feats:] = gate[span].astype(BF16)


def weight_kernel(held_ref, came_ref, dpre_held_ref, dpre_came_ref, act_held_ref, act_came_ref,
                  w_in_hbm, w_out_hbm, w_in_ref, w_out_ref, sems):
    feats, hidden = w_in_ref.shape
    rows = jnp.concatenate([held_ref[:, :feats], came_ref[:, :feats]], axis=0)
    dpre = jnp.concatenate([dpre_held_ref[...], dpre_came_ref[...]], axis=0)
    act = jnp.concatenate([act_held_ref[...], act_came_ref[...]], axis=0)
    count = feats // PIECES
    copies = []
    for piece in range(PIECES):
        span = slice(piece * count, (piece + 1) * count)
        part = rows[:, span]
        w_in_ref[span] = lax.dot_general(part, dpre, ROWS_BY_ROWS, preferred_element_type=F32)
        w_out_ref[:, span] = lax.dot_general(act, part, ROWS_BY_ROWS, preferred_element_type=F32)
        span = pl.ds(piece * count, count)
        for source, target in (
            (w_in_ref.at[span], w_in_hbm.at[span]),
            (w_out_ref.at[:, span], w_out_hbm.at[:, span]),
        ):
            copy = pltpu.make_async_copy(source, target, sems.at[len(copies)])
            copy.start()
            copies.append(copy)
    for copy in copies:
        copy.wait()


def combine_kernel(steps, *refs):
    kept_ref, came_refs = refs[0], refs[1:steps]
    place_ref, spread_ref, tokens_hbm, gate_out_ref, tokens_ref, sems = refs[steps:]
    feats = tokens_ref.shape[1]
    capacity = kept_ref.shape[0]
    came = [ref[...].astype(F32) for ref in came_refs]
    half = steps // WINDOW
    own = sum(came[: half - 1], kept_ref[...])
    other = sum(came[half:], came[half - 1])
    slots = jnp.concatenate([own, other], axis=0)
    grads = slots[:, :feats]
    high = grads.astype(BF16)
    low = (grads - high.astype(F32)).astype(BF16)
    both = jnp.concatenate([high, low], axis=0)
    spread = spread_ref[...]
    count = feats // PIECES
    copies = []
    for piece in range(PIECES):
        span = slice(piece * count, (piece + 1) * count)
        tokens_ref[:, span] = jnp.dot(
            spread, both[:, span], preferred_element_type=F32
        ).astype(BF16)
        span = pl.ds(piece * count, count)
        copy = pltpu.make_async_copy(tokens_ref.at[:, span], tokens_hbm.at[:, span], sems.at[piece])
        copy.start()
        copies.append(copy)
    slot_gate = jnp.sum(slots[:, feats:], axis=1, keepdims=True)
    picked = place_ref[: WINDOW * capacity].astype(F32) * slot_gate
    masks = place_ref[WINDOW * capacity :].astype(F32)
    result = jnp.zeros(gate_out_ref.shape, F32)
    for index in range(WINDOW):
        span = slice(index * capacity, (index + 1) * capacity)
        value = jnp.sum(picked[span], axis=0, keepdims=True)
        result = result + masks[2 * index : 2 * index + 2] * value
    gate_out_ref[...] = result
    for copy in copies:
        copy.wait()


def swap(array, axes, bit):
    size = lax.axis_size(axes)
    return lax.ppermute(array, axes, [(index, index ^ bit) for index in range(size)])


def join(pieces):
    rows, wide = pieces[0].shape
    rows *= len(pieces)
    return call(join_kernel, jax.ShapeDtypeStruct((rows, wide), BF16), 0, 4 * rows * wide)(*pieces)


def body(tokens, grad_out, routes, gates, w_in, w_out):
    nodes = lax.axis_size("node")
    locals_ = lax.axis_size("local")
    edatas = lax.axis_size("edata")
    tok_rows, feats = tokens.shape
    hidden = w_in.shape[1]
    capacity = 2 * tok_rows // EXPERTS
    slots = WINDOW * capacity
    rows = nodes * locals_ * capacity
    wide = feats + LANES
    coded = 2 * hidden + LANES
    shape = jax.ShapeDtypeStruct
    hbm = pl.BlockSpec(memory_space=pltpu.HBM)
    vmem = pl.BlockSpec(memory_space=pltpu.VMEM)

    routes_t, gates_t, tokens, grad_out = [
        pltpu.with_memory_space_constraint(value, pltpu.HBM)
        for value in (routes.T, gates.T, tokens, grad_out)
    ]
    own_rows, other_rows, place, spread = call(
        gather_kernel,
        (
            pltpu.VMEM((2 * capacity, wide), BF16),
            pltpu.VMEM((2 * capacity, wide), BF16),
            pltpu.VMEM((slots + 16, tok_rows), BF16),
            pltpu.VMEM((tok_rows, 2 * slots), BF16),
        ),
        4 * slots * tok_rows * feats,
        4 * tok_rows * feats,
        in_specs=[hbm] * 4,
        scratch_shapes=[
            pltpu.VMEM((2, tok_rows), jnp.int32),
            pltpu.VMEM((2, tok_rows), BF16),
            pltpu.VMEM((tok_rows, feats), BF16),
            pltpu.VMEM((tok_rows, feats), BF16),
            pltpu.SemaphoreType.DMA((2 + 2 * PIECES,)),
        ],
    )(routes_t, gates_t, tokens, grad_out)

    pieces = [own_rows] * nodes
    for step in reversed(range(1, nodes)):
        pieces[step] = swap(own_rows if step < nodes // WINDOW else other_rows, "node", step)
    held = join(pieces)
    came = swap(held, "local", 1)
    bit = 2
    while bit < locals_:
        held = join([held, came])
        came = swap(held, "local", bit)
        bit *= 2

    half = rows // 2
    last = ()
    sums = []
    for chunk in (held, came):
        part, gate_rows = call(
            functools.partial(part_kernel, capacity),
            (shape((half, coded), I16), shape((half, LANES), F32)),
            8 * half * feats * hidden,
            4 * half * feats + 4 * feats * hidden,
            after=last,
        )(chunk, w_in, w_out)
        last = (part,)
        sums.append([part, swap(part, "edata", 1), gate_rows])
    bit = 2
    while bit < edatas:
        for index, (part, other, gate_rows) in enumerate(sums):
            part = call(
                add_codes_kernel,
                shape((half, coded), I16),
                8 * half * hidden,
                6 * half * coded,
                after=last,
            )(part, other)
            last = (part,)
            sums[index] = [part, swap(part, "edata", bit), gate_rows]
        bit *= 2
    slot_parts = []
    operands = []
    for part, other, gate_rows in sums:
        slot, dpre, act = call(
            functools.partial(slot_kernel, capacity),
            (
                shape((half, wide), F32),
                shape((2 * half, hidden), BF16),
                shape((2 * half, hidden), BF16),
            ),
            2 * half * feats * hidden,
            2 * feats * hidden + 4 * half * feats,
            after=last,
        )(part, other, gate_rows, w_in)
        last = (dpre,)
        slot_parts.append(slot)
        operands.append((dpre, act))

    keep, send = slot_parts
    back = swap(send, "local", locals_ // 2)
    bit = locals_ // 4
    while bit:
        half //= 2
        keep, send = call(
            halve_kernel, (shape((half, wide), F32),) * 2, 4 * half * wide, 24 * half * wide
        )(keep, back)
        back = swap(send, "local", bit)
        bit //= 2
    keep, *sends = call(
        deal_kernel,
        (shape((capacity, wide), F32),) + (shape((capacity, wide), BF16),) * (nodes - 1),
        4 * half * wide,
        12 * half * wide,
    )(keep, back)
    backs = [swap(send, "node", step + 1) for step, send in reversed(list(enumerate(sends)))]
    (dpre_held, act_held), (dpre_came, act_came) = operands
    grad_w_in, grad_w_out = call(
        weight_kernel,
        (shape((feats, hidden), F32), shape((hidden, feats), F32)),
        8 * rows * feats * hidden,
        8 * feats * hidden,
        in_specs=[vmem] * 6,
        out_specs=[hbm] * 2,
        scratch_shapes=[
            pltpu.VMEM((feats, hidden), F32),
            pltpu.VMEM((hidden, feats), F32),
            pltpu.SemaphoreType.DMA((2 * PIECES,)),
        ],
    )(held, came, dpre_held, dpre_came, act_held, act_came)
    grad_tokens, grad_gates = call(
        functools.partial(combine_kernel, nodes),
        (shape((tok_rows, feats), BF16), shape((2, tok_rows), F32)),
        4 * slots * tok_rows * feats,
        2 * tok_rows * feats,
        in_specs=[vmem] * (nodes + 2),
        out_specs=[hbm, vmem],
        scratch_shapes=[
            pltpu.VMEM((tok_rows, feats), BF16),
            pltpu.SemaphoreType.DMA((PIECES,)),
        ],
    )(keep, *reversed(backs), place, spread)
    return (grad_tokens, grad_gates.T, grad_w_in, grad_w_out)


def solution(mesh):
    in_specs = (
        P(("node", "local"), "edata"),
        P(("node", "local"), "edata"),
        P(("node", "local"), None),
        P(("node", "local"), None),
        P("edata", ("node", "local")),
        P(("node", "local"), "edata"),
    )
    out_specs = (
        P(("node", "local"), "edata"),
        P(("node", "local"), None),
        P("edata", ("node", "local")),
        P(("node", "local"), "edata"),
    )
    return jax.shard_map(body, mesh=mesh, in_specs=in_specs, out_specs=out_specs, check_vma=False)
```

```python
import functools

import jax
import jax.numpy as jnp
from jax import lax
from jax.experimental import pallas as pl
from jax.experimental.pallas import tpu as pltpu
from jax.sharding import PartitionSpec as P

EXPERTS = 64
WINDOW = 2
LANES = 128
PIECES = 4
VMEM_LIMIT = 40 * 1024 * 1024

BF16 = jnp.bfloat16
F32 = jnp.float32
I16 = jnp.int16
ROWS_BY_ROWS = (((0,), (0,)), ((), ()))
COLS_BY_COLS = (((1,), (1,)), ((), ()))


def gelu_pair(pre_act):
    coefficient = 0.7978845608028654
    square = pre_act * pre_act
    tanh_val = jnp.tanh(coefficient * (pre_act + 0.044715 * pre_act * square))
    half = 0.5 * (1.0 + tanh_val)
    activation = pre_act * half
    slopes = half + 0.5 * pre_act * (1.0 - tanh_val * tanh_val) * coefficient * (
        1.0 + 3.0 * 0.044715 * square
    )
    return (activation, slopes)


def call(kernel, out_shape, flops, moved, limit=VMEM_LIMIT, in_specs=None, after=(), **more):
    def run(*operands):
        given = in_specs or [pl.BlockSpec(memory_space=pltpu.VMEM)] * len(operands)
        return pl.pallas_call(
            lambda *refs: kernel(*refs[len(after) :]),
            out_shape=out_shape,
            in_specs=[pl.BlockSpec(memory_space=pl.ANY)] * len(after) + list(given),
            compiler_params=pltpu.CompilerParams(vmem_limit_bytes=limit),
            cost_estimate=pl.CostEstimate(flops=flops, bytes_accessed=moved, transcendentals=0),
            **more,
        )(*after, *operands)

    return run


def own_expert():
    half_nodes = lax.axis_size("node") // WINDOW
    return lax.axis_index("node") // half_nodes


def split_value(value):
    high = value.astype(BF16).astype(F32)
    lane = lax.broadcasted_iota(jnp.int32, (value.shape[0], LANES), 1)
    return jnp.where(lane == 0, high, jnp.where(lane == 1, value - high, 0.0))


def encode(values):
    top = jnp.max(jnp.abs(values), axis=1, keepdims=True)
    power = jnp.ceil(jnp.log2(jnp.maximum(top, 1e-30)))
    codes = jnp.round(values * (1.999 * jnp.exp2(14.0 - power)))
    return codes.astype(jnp.int32).astype(I16), power


def decode(codes, power):
    return codes.astype(jnp.int32).astype(F32) * (jnp.exp2(power - 14.0) / 1.999)


def store_codes(out_ref, pair):
    hidden = pair[0].shape[1]
    lane = lax.broadcasted_iota(jnp.int32, (pair[0].shape[0], LANES), 1)
    powers = []
    for index, values in enumerate(pair):
        codes, power = encode(values)
        out_ref[:, index * hidden : (index + 1) * hidden] = codes
        powers.append(power)
    powers = jnp.where(lane == 0, powers[0], powers[1])
    out_ref[:, 2 * hidden :] = powers.astype(jnp.int32).astype(I16)


def load_codes(ref):
    hidden = (ref.shape[1] - LANES) // 2
    powers = ref[:, 2 * hidden :].astype(jnp.int32).astype(F32)
    return [
        decode(ref[:, index * hidden : (index + 1) * hidden], powers[:, index : index + 1])
        for index in range(2)
    ]


def gather_kernel(routes_hbm, gates_hbm, tokens_hbm, grads_hbm, own_ref, other_ref, place_ref,
                  spread_ref, routes_ref, gates_ref, tokens_ref, grads_ref, sems):
    tok_rows, feats = tokens_ref.shape
    capacity = own_ref.shape[0] // 2
    slots = WINDOW * capacity
    copies = [
        pltpu.make_async_copy(routes_hbm, routes_ref, sems.at[0]),
        pltpu.make_async_copy(gates_hbm, gates_ref, sems.at[1]),
    ]
    count = tok_rows // PIECES
    for source, target in ((tokens_hbm, tokens_ref), (grads_hbm, grads_ref)):
        for piece in range(PIECES):
            span = pl.ds(piece * count, count)
            copies.append(
                pltpu.make_async_copy(source.at[span], target.at[span], sems.at[len(copies)])
            )
    for copy in copies:
        copy.start()
    earlier = lax.broadcasted_iota(jnp.int32, (tok_rows, tok_rows), 0) < lax.broadcasted_iota(
        jnp.int32, (tok_rows, tok_rows), 1
    )
    earlier = earlier.astype(F32).astype(BF16)
    slot_of = lax.broadcasted_iota(jnp.int32, (capacity, tok_rows), 0).astype(F32)
    row_of = lax.broadcasted_iota(jnp.int32, (8, tok_rows), 0)
    own = own_expert()
    copies[0].wait()
    copies[1].wait()
    routes = routes_ref[...]
    gates = gates_ref[...].astype(F32)
    hits = [(routes == expert).astype(F32) for expert in (own, 1 - own)]
    named = [hit[0:1] + hit[1:2] for hit in hits]
    weight = [hit * gates for hit in hits]
    weight = [value[0:1] + value[1:2] for value in weight]
    names = jnp.where(row_of == 0, named[0], jnp.where(row_of == 1, named[1], 0.0)).astype(BF16)
    before = jnp.dot(names, earlier, preferred_element_type=F32)
    parts = [jnp.where(before[e : e + 1] == slot_of, named[e], 0.0) for e in range(WINDOW)]
    place = jnp.concatenate(parts, axis=0).astype(BF16)
    place_ref[:slots] = place
    spread_ref[...] = jnp.concatenate(parts + parts, axis=0).T.astype(BF16)
    masks = jnp.zeros((16, tok_rows), F32)
    row_of = lax.broadcasted_iota(jnp.int32, masks.shape, 0)
    for index, hit in enumerate(hits):
        for k in range(2):
            masks = jnp.where(row_of == 2 * index + k, hit[k : k + 1], masks)
    place_ref[slots:] = masks.astype(BF16)
    for copy in copies[2 : 2 + PIECES]:
        copy.wait()
    rows_x = jnp.dot(place, tokens_ref[...], preferred_element_type=F32)
    for copy in copies[2 + PIECES :]:
        copy.wait()
    rows_dy = jnp.dot(place, grads_ref[...], preferred_element_type=F32)
    for expert, out_ref in ((0, own_ref), (1, other_ref)):
        span = slice(expert * capacity, (expert + 1) * capacity)
        out_ref[:, :feats] = jnp.concatenate([rows_x[span], rows_dy[span]], axis=0).astype(BF16)
        gate = jnp.sum(parts[expert] * weight[expert], axis=1, keepdims=True)
        gate = jnp.concatenate([gate, gate], axis=0)
        out_ref[:, feats:] = jnp.broadcast_to(gate, (2 * capacity, LANES)).astype(BF16)


def join_kernel(*refs):
    *pieces, out_ref = refs
    rows = pieces[0].shape[0]
    for index, ref in enumerate(pieces):
        out_ref[index * rows : (index + 1) * rows] = ref[...]


def part_kernel(capacity, rows_ref, w_in_ref, w_in_other_ref, w_out_ref, w_out_other_ref, part_ref,
                gate_ref):
    feats, hidden = w_in_ref.shape
    groups = rows_ref.shape[0] // (2 * capacity)
    gate = rows_ref[:, feats:].astype(F32).reshape(groups, 2 * capacity, LANES)
    gate_ref[...] = gate[:, :capacity].reshape(groups * capacity, LANES)
    rows = rows_ref[:, :feats]
    pre = [
        jnp.dot(rows, ref[...], preferred_element_type=F32) for ref in (w_in_ref, w_in_other_ref)
    ]
    back = [
        lax.dot_general(rows, ref[...], COLS_BY_COLS, preferred_element_type=F32)
        for ref in (w_out_ref, w_out_other_ref)
    ]
    pair = []
    for values, span in ((pre, slice(0, capacity)), (back, slice(capacity, 2 * capacity))):
        values = jnp.concatenate(values, axis=1).reshape(groups, 2 * capacity, 2 * hidden)
        pair.append(values[:, span].reshape(groups * capacity, 2 * hidden))
    store_codes(part_ref, pair)


def add_codes_kernel(first_ref, second_ref, out_ref):
    pairs = zip(load_codes(first_ref), load_codes(second_ref))
    store_codes(out_ref, [first + second for first, second in pairs])


def deal(total, keep_ref, send_refs):
    each, wide = keep_ref.shape
    feats = wide - LANES
    keep_ref[...] = total[:each]
    gate = split_value(jnp.sum(total[:, feats:], axis=1, keepdims=True))
    for index, send_ref in enumerate(send_refs):
        span = slice((index + 1) * each, (index + 2) * each)
        send_ref[:, :feats] = total[span, :feats].astype(BF16)
        send_ref[:, feats:] = gate[span].astype(BF16)


def slot_kernel(capacity, first_ref, second_ref, gate_ref, w_in_ref, w_in_other_ref, mine_ref,
                theirs_ref, *slot_refs):
    hidden = w_in_ref.shape[1]
    pairs = zip(load_codes(first_ref), load_codes(second_ref))
    pre, back = [first + second for first, second in pairs]
    gate = gate_ref[:, :1]
    activation, slopes = gelu_pair(pre)
    dpre = (gate * back * slopes).astype(BF16)
    act = gate * activation
    slot = lax.dot_general(
        dpre[:, :hidden], w_in_ref[...], COLS_BY_COLS, preferred_element_type=F32
    ) + lax.dot_general(
        dpre[:, hidden:], w_in_other_ref[...], COLS_BY_COLS, preferred_element_type=F32
    )
    slot_gate = split_value(jnp.sum(activation * back, axis=1, keepdims=True))
    total = jnp.concatenate([slot, slot_gate], axis=1)
    if len(slot_refs) == 1:
        slot_refs[0][...] = total
    else:
        deal(total, slot_refs[0], slot_refs[1:])
    rows = dpre.shape[0]
    both = [
        value.reshape(rows // capacity, capacity, 2 * hidden) for value in (dpre.astype(F32), act)
    ]
    both = jnp.concatenate(both, axis=1).reshape(2 * rows, 2 * hidden).astype(BF16)
    mine_ref[...] = both[:, :hidden]
    theirs_ref[...] = both[:, hidden:]


def halve_kernel(kept_ref, came_ref, keep_ref, send_ref):
    half = keep_ref.shape[0]
    total = kept_ref[...] + came_ref[...]
    keep_ref[...] = total[:half]
    send_ref[...] = total[half:]


def deal_kernel(kept_ref, came_ref, keep_ref, *send_refs):
    deal(kept_ref[...] + came_ref[...], keep_ref, send_refs)


def weight_kernel(capacity, held_ref, came_ref, mine_ref, back_ref, w_in_hbm, w_out_hbm,
                  written_ref, w_in_ref, w_out_ref, sems):
    feats, hidden = w_in_ref.shape
    rows = jnp.concatenate([held_ref[:, :feats], came_ref[:, :feats]], axis=0)
    both = jnp.concatenate([mine_ref[...], back_ref[...]], axis=0).astype(F32)
    of_x = lax.broadcasted_iota(jnp.int32, both.shape, 0) % (2 * capacity) < capacity
    dpre = jnp.where(of_x, both, 0.0).astype(BF16)
    act = jnp.where(of_x, 0.0, both).astype(BF16)
    count = feats // PIECES
    copies = []
    for piece in range(PIECES):
        span = slice(piece * count, (piece + 1) * count)
        part = rows[:, span]
        w_in_ref[span] = lax.dot_general(part, dpre, ROWS_BY_ROWS, preferred_element_type=F32)
        w_out_ref[:, span] = lax.dot_general(act, part, ROWS_BY_ROWS, preferred_element_type=F32)
        span = pl.ds(piece * count, count)
        for source, target in (
            (w_in_ref.at[span], w_in_hbm.at[span]),
            (w_out_ref.at[:, span], w_out_hbm.at[:, span]),
        ):
            copy = pltpu.make_async_copy(source, target, sems.at[len(copies)])
            copy.start()
            copies.append(copy)
    for copy in copies:
        copy.wait()
    written_ref[...] = jnp.zeros(written_ref.shape, F32)


def combine_kernel(steps, *refs):
    kept_ref, came_refs = refs[0], refs[1:steps]
    place_ref, spread_ref, tokens_ref, gate_out_ref = refs[steps:]
    feats = tokens_ref.shape[1]
    capacity = kept_ref.shape[0]
    came = [ref[...].astype(F32) for ref in came_refs]
    half = steps // WINDOW
    own = sum(came[: half - 1], kept_ref[...])
    other = sum(came[half:], came[half - 1])
    slots = jnp.concatenate([own, other], axis=0)
    grads = slots[:, :feats]
    high = grads.astype(BF16)
    low = (grads - high.astype(F32)).astype(BF16)
    both = jnp.concatenate([high, low], axis=0)
    tokens_ref[...] = jnp.dot(spread_ref[...], both, preferred_element_type=F32).astype(BF16)
    slot_gate = jnp.sum(slots[:, feats:], axis=1, keepdims=True)
    picked = place_ref[: WINDOW * capacity].astype(F32) * slot_gate
    masks = place_ref[WINDOW * capacity :].astype(F32)
    result = jnp.zeros(gate_out_ref.shape, F32)
    for index in range(WINDOW):
        span = slice(index * capacity, (index + 1) * capacity)
        value = jnp.sum(picked[span], axis=0, keepdims=True)
        result = result + masks[2 * index : 2 * index + 2] * value
    gate_out_ref[...] = result


def swap(array, axes, bit):
    size = lax.axis_size(axes)
    return lax.ppermute(array, axes, [(index, index ^ bit) for index in range(size)])


def join(pieces):
    rows, wide = pieces[0].shape
    rows *= len(pieces)
    return call(join_kernel, jax.ShapeDtypeStruct((rows, wide), BF16), 0, 4 * rows * wide)(*pieces)


def body(tokens, grad_out, routes, gates, w_in, w_out):
    nodes = lax.axis_size("node")
    locals_ = lax.axis_size("local")
    edatas = lax.axis_size("edata")
    tok_rows, feats = tokens.shape
    hidden = w_in.shape[1]
    capacity = 2 * tok_rows // EXPERTS
    slots = WINDOW * capacity
    rows = nodes * (locals_ // 2) * capacity
    wide = feats + LANES
    coded = 4 * hidden + LANES
    shape = jax.ShapeDtypeStruct
    hbm = pl.BlockSpec(memory_space=pltpu.HBM)
    vmem = pl.BlockSpec(memory_space=pltpu.VMEM)

    routes_t, gates_t, tokens, grad_out = [
        pltpu.with_memory_space_constraint(value, pltpu.HBM)
        for value in (routes.T, gates.T, tokens, grad_out)
    ]
    own_rows, other_rows, place, spread = call(
        gather_kernel,
        (
            pltpu.VMEM((2 * capacity, wide), BF16),
            pltpu.VMEM((2 * capacity, wide), BF16),
            pltpu.VMEM((slots + 16, tok_rows), BF16),
            pltpu.VMEM((tok_rows, 2 * slots), BF16),
        ),
        4 * slots * tok_rows * feats,
        4 * tok_rows * feats,
        in_specs=[hbm] * 4,
        scratch_shapes=[
            pltpu.VMEM((2, tok_rows), jnp.int32),
            pltpu.VMEM((2, tok_rows), BF16),
            pltpu.VMEM((tok_rows, feats), BF16),
            pltpu.VMEM((tok_rows, feats), BF16),
            pltpu.SemaphoreType.DMA((2 + 2 * PIECES,)),
        ],
    )(routes_t, gates_t, tokens, grad_out)

    w_in_other, w_out_other = swap(w_in, "local", 1), swap(w_out, "local", 1)

    pieces = [own_rows] * nodes
    for step in reversed(range(1, nodes)):
        pieces[step] = swap(own_rows if step < nodes // WINDOW else other_rows, "node", step)
    held = join(pieces)
    bit = 2
    while bit < locals_:
        held = join([held, swap(held, "local", bit)])
        bit *= 2
    came = swap(held, "local", 1)

    part, gate_rows = call(
        functools.partial(part_kernel, capacity),
        (shape((rows, coded), I16), shape((rows, LANES), F32)),
        16 * rows * feats * hidden,
        4 * rows * feats + 8 * feats * hidden,
    )(held, w_in, w_in_other, w_out, w_out_other)
    bit = 1
    other = swap(part, "edata", bit)
    while 2 * bit < edatas:
        part = call(
            add_codes_kernel, shape((rows, coded), I16), 16 * rows * hidden, 6 * rows * coded
        )(part, other)
        bit *= 2
        other = swap(part, "edata", bit)

    dealt = (shape((capacity, wide), F32),) + (shape((capacity, wide), BF16),) * (nodes - 1)
    mine, theirs, *slot_parts = call(
        functools.partial(slot_kernel, capacity),
        (shape((2 * rows, hidden), BF16),) * 2
        + (dealt if locals_ == 2 else (shape((rows, wide), F32),)),
        4 * rows * feats * hidden,
        4 * feats * hidden + 4 * rows * feats,
    )(part, other, gate_rows, w_in, w_in_other)
    back = swap(theirs, "local", 1)
    if locals_ > 2:
        half = rows // 2
        keep, send = slot_parts[0][:half], slot_parts[0][half:]
        bit = locals_ // 2
        while bit > 2:
            half //= 2
            keep, send = call(
                halve_kernel, (shape((half, wide), F32),) * 2, 4 * half * wide, 24 * half * wide
            )(keep, swap(send, "local", bit))
            bit //= 2
        slot_parts = call(deal_kernel, dealt, 4 * half * wide, 12 * half * wide)(
            keep, swap(send, "local", bit)
        )
    keep, *sends = slot_parts
    backs = [swap(send, "node", step + 1) for step, send in enumerate(sends)]
    grad_w_in, grad_w_out, written = call(
        functools.partial(weight_kernel, capacity),
        (shape((feats, hidden), F32), shape((hidden, feats), F32), shape((8, LANES), F32)),
        16 * rows * feats * hidden,
        8 * feats * hidden,
        in_specs=[vmem] * 4,
        out_specs=[hbm, hbm, vmem],
        scratch_shapes=[
            pltpu.VMEM((feats, hidden), F32),
            pltpu.VMEM((hidden, feats), F32),
            pltpu.SemaphoreType.DMA((2 * PIECES,)),
        ],
    )(held, came, mine, back)
    grad_tokens, grad_gates = call(
        functools.partial(combine_kernel, nodes),
        (shape((tok_rows, feats), BF16), shape((2, tok_rows), F32)),
        4 * slots * tok_rows * feats,
        2 * tok_rows * feats,
        after=(written,),
    )(keep, *backs, place, spread)
    return (grad_tokens, grad_gates.T, grad_w_in, grad_w_out)


def solution(mesh):
    in_specs = (
        P(("node", "local"), "edata"),
        P(("node", "local"), "edata"),
        P(("node", "local"), None),
        P(("node", "local"), None),
        P("edata", ("node", "local")),
        P(("node", "local"), "edata"),
    )
    out_specs = (
        P(("node", "local"), "edata"),
        P(("node", "local"), None),
        P("edata", ("node", "local")),
        P(("node", "local"), "edata"),
    )
    return jax.shard_map(body, mesh=mesh, in_specs=in_specs, out_specs=out_specs, check_vma=False)
```

```python
import functools

import jax
import jax.numpy as jnp
from jax import lax
from jax.experimental import pallas as pl
from jax.experimental.pallas import tpu as pltpu
from jax.sharding import PartitionSpec as P

EXPERTS = 64
WINDOW = 2
LANES = 128
PIECES = 4
VMEM_LIMIT = 40 * 1024 * 1024

BF16 = jnp.bfloat16
F32 = jnp.float32
I16 = jnp.int16
ROWS_BY_ROWS = (((0,), (0,)), ((), ()))
COLS_BY_COLS = (((1,), (1,)), ((), ()))


def gelu_pair(pre_act):
    coefficient = 0.7978845608028654
    square = pre_act * pre_act
    tanh_val = jnp.tanh(coefficient * (pre_act + 0.044715 * pre_act * square))
    half = 0.5 * (1.0 + tanh_val)
    activation = pre_act * half
    slopes = half + 0.5 * pre_act * (1.0 - tanh_val * tanh_val) * coefficient * (
        1.0 + 3.0 * 0.044715 * square
    )
    return (activation, slopes)


def call(kernel, out_shape, flops, moved, limit=VMEM_LIMIT, in_specs=None, after=(), **more):
    def run(*operands):
        given = in_specs or [pl.BlockSpec(memory_space=pltpu.VMEM)] * len(operands)
        return pl.pallas_call(
            lambda *refs: kernel(*refs[len(after) :]),
            out_shape=out_shape,
            in_specs=[pl.BlockSpec(memory_space=pl.ANY)] * len(after) + list(given),
            compiler_params=pltpu.CompilerParams(vmem_limit_bytes=limit),
            cost_estimate=pl.CostEstimate(flops=flops, bytes_accessed=moved, transcendentals=0),
            **more,
        )(*after, *operands)

    return run


def own_expert():
    half_nodes = lax.axis_size("node") // WINDOW
    return lax.axis_index("node") // half_nodes


def split_value(value):
    high = value.astype(BF16).astype(F32)
    lane = lax.broadcasted_iota(jnp.int32, (value.shape[0], LANES), 1)
    return jnp.where(lane == 0, high, jnp.where(lane == 1, value - high, 0.0))


def encode(values):
    top = jnp.max(jnp.abs(values), axis=1, keepdims=True)
    power = jnp.ceil(jnp.log2(jnp.maximum(top, 1e-30)))
    codes = jnp.round(values * (1.999 * jnp.exp2(14.0 - power)))
    return codes.astype(jnp.int32).astype(I16), power


def decode(codes, power):
    return codes.astype(jnp.int32).astype(F32) * (jnp.exp2(power - 14.0) / 1.999)


def store_codes(out_ref, pair):
    hidden = pair[0].shape[1]
    lane = lax.broadcasted_iota(jnp.int32, (pair[0].shape[0], LANES), 1)
    powers = []
    for index, values in enumerate(pair):
        codes, power = encode(values)
        out_ref[:, index * hidden : (index + 1) * hidden] = codes
        powers.append(power)
    powers = jnp.where(lane == 0, powers[0], powers[1])
    out_ref[:, 2 * hidden :] = powers.astype(jnp.int32).astype(I16)


def load_codes(ref):
    hidden = (ref.shape[1] - LANES) // 2
    powers = ref[:, 2 * hidden :].astype(jnp.int32).astype(F32)
    return [
        decode(ref[:, index * hidden : (index + 1) * hidden], powers[:, index : index + 1])
        for index in range(2)
    ]


def gather_kernel(routes_hbm, gates_hbm, tokens_hbm, grads_hbm, own_ref, other_ref, place_ref,
                  spread_ref, routes_ref, gates_ref, tokens_ref, grads_ref, sems):
    tok_rows, feats = tokens_ref.shape
    capacity = own_ref.shape[0] // 2
    slots = WINDOW * capacity
    copies = [
        pltpu.make_async_copy(routes_hbm, routes_ref, sems.at[0]),
        pltpu.make_async_copy(gates_hbm, gates_ref, sems.at[1]),
    ]
    count = tok_rows // PIECES
    for source, target in ((tokens_hbm, tokens_ref), (grads_hbm, grads_ref)):
        for piece in range(PIECES):
            span = pl.ds(piece * count, count)
            copies.append(
                pltpu.make_async_copy(source.at[span], target.at[span], sems.at[len(copies)])
            )
    for copy in copies:
        copy.start()
    earlier = lax.broadcasted_iota(jnp.int32, (tok_rows, tok_rows), 0) < lax.broadcasted_iota(
        jnp.int32, (tok_rows, tok_rows), 1
    )
    earlier = earlier.astype(F32).astype(BF16)
    slot_of = lax.broadcasted_iota(jnp.int32, (capacity, tok_rows), 0).astype(F32)
    row_of = lax.broadcasted_iota(jnp.int32, (8, tok_rows), 0)
    own = own_expert()
    copies[0].wait()
    copies[1].wait()
    routes = routes_ref[...]
    gates = gates_ref[...].astype(F32)
    hits = [(routes == expert).astype(F32) for expert in (own, 1 - own)]
    named = [hit[0:1] + hit[1:2] for hit in hits]
    weight = [hit * gates for hit in hits]
    weight = [value[0:1] + value[1:2] for value in weight]
    names = jnp.where(row_of == 0, named[0], jnp.where(row_of == 1, named[1], 0.0)).astype(BF16)
    before = jnp.dot(names, earlier, preferred_element_type=F32)
    parts = [jnp.where(before[e : e + 1] == slot_of, named[e], 0.0) for e in range(WINDOW)]
    place = jnp.concatenate(parts, axis=0).astype(BF16)
    place_ref[:slots] = place
    spread_ref[...] = jnp.concatenate(parts + parts, axis=0).T.astype(BF16)
    masks = jnp.zeros((16, tok_rows), F32)
    row_of = lax.broadcasted_iota(jnp.int32, masks.shape, 0)
    for index, hit in enumerate(hits):
        for k in range(2):
            masks = jnp.where(row_of == 2 * index + k, hit[k : k + 1], masks)
    place_ref[slots:] = masks.astype(BF16)
    for copy in copies[2 : 2 + PIECES]:
        copy.wait()
    rows_x = jnp.dot(place, tokens_ref[...], preferred_element_type=F32)
    for copy in copies[2 + PIECES :]:
        copy.wait()
    rows_dy = jnp.dot(place, grads_ref[...], preferred_element_type=F32)
    for expert, out_ref in ((0, own_ref), (1, other_ref)):
        span = slice(expert * capacity, (expert + 1) * capacity)
        out_ref[:, :feats] = jnp.concatenate([rows_x[span], rows_dy[span]], axis=0).astype(BF16)
        gate = jnp.sum(parts[expert] * weight[expert], axis=1, keepdims=True)
        gate = jnp.concatenate([gate, gate], axis=0)
        out_ref[:, feats:] = jnp.broadcast_to(gate, (2 * capacity, LANES)).astype(BF16)


def join_kernel(*refs):
    *pieces, out_ref = refs
    rows = pieces[0].shape[0]
    for index, ref in enumerate(pieces):
        out_ref[index * rows : (index + 1) * rows] = ref[...]


def part_kernel(capacity, rows_ref, w_in_ref, w_in_other_ref, w_out_ref, w_out_other_ref, part_ref,
                gate_ref):
    feats, hidden = w_in_ref.shape
    groups = rows_ref.shape[0] // (2 * capacity)
    gate = rows_ref[:, feats:].astype(F32).reshape(groups, 2 * capacity, LANES)
    gate_ref[...] = gate[:, :capacity].reshape(groups * capacity, LANES)
    rows = rows_ref[:, :feats]
    pre = [
        jnp.dot(rows, ref[...], preferred_element_type=F32) for ref in (w_in_ref, w_in_other_ref)
    ]
    back = [
        lax.dot_general(rows, ref[...], COLS_BY_COLS, preferred_element_type=F32)
        for ref in (w_out_ref, w_out_other_ref)
    ]
    pair = []
    for values, span in ((pre, slice(0, capacity)), (back, slice(capacity, 2 * capacity))):
        values = jnp.concatenate(values, axis=1).reshape(groups, 2 * capacity, 2 * hidden)
        pair.append(values[:, span].reshape(groups * capacity, 2 * hidden))
    store_codes(part_ref, pair)


def add_codes_kernel(first_ref, second_ref, out_ref):
    pairs = zip(load_codes(first_ref), load_codes(second_ref))
    store_codes(out_ref, [first + second for first, second in pairs])


def deal(total, refs):
    each, wide = refs[0].shape
    feats = wide - LANES
    gate = split_value(jnp.sum(total[:, feats:], axis=1, keepdims=True))
    for index, ref in enumerate(refs):
        span = slice(index * each, (index + 1) * each)
        ref[:, :feats] = total[span, :feats].astype(ref.dtype)
        ref[:, feats:] = gate[span].astype(ref.dtype)


def slot_kernel(capacity, first_ref, second_ref, gate_ref, w_in_ref, w_in_other_ref, mine_ref,
                theirs_ref, *slot_refs):
    hidden = w_in_ref.shape[1]
    pairs = zip(load_codes(first_ref), load_codes(second_ref))
    pre, back = [first + second for first, second in pairs]
    gate = gate_ref[:, :1]
    activation, slopes = gelu_pair(pre)
    dpre = (gate * back * slopes).astype(BF16)
    act = gate * activation
    slot = lax.dot_general(
        dpre[:, :hidden], w_in_ref[...], COLS_BY_COLS, preferred_element_type=F32
    ) + lax.dot_general(
        dpre[:, hidden:], w_in_other_ref[...], COLS_BY_COLS, preferred_element_type=F32
    )
    slot_gate = split_value(jnp.sum(activation * back, axis=1, keepdims=True))
    total = jnp.concatenate([slot, slot_gate], axis=1)
    if len(slot_refs) == 1:
        slot_refs[0][...] = total
    else:
        deal(total, slot_refs)
    rows = dpre.shape[0]
    both = [
        value.reshape(rows // capacity, capacity, 2 * hidden) for value in (dpre.astype(F32), act)
    ]
    both = jnp.concatenate(both, axis=1).reshape(2 * rows, 2 * hidden).astype(BF16)
    mine_ref[...] = both[:, :hidden]
    theirs_ref[...] = both[:, hidden:]


def halve_kernel(kept_ref, came_ref, keep_ref, send_ref):
    half = keep_ref.shape[0]
    total = kept_ref[...] + came_ref[...]
    keep_ref[...] = total[:half]
    send_ref[...] = total[half:]


def deal_kernel(kept_ref, came_ref, *refs):
    deal(kept_ref[...] + came_ref[...], refs)


def weight_kernel(capacity, *refs):
    rows_refs, both_refs = refs[:4], refs[4:8]
    w_in_hbm, w_out_hbm, written_ref, w_in_ref, w_out_ref, sems = refs[8:]
    feats, hidden = w_in_ref.shape
    rows = jnp.concatenate([ref[:, :feats] for ref in rows_refs], axis=0)
    both = jnp.concatenate([ref[...] for ref in both_refs], axis=0).astype(F32)
    of_x = lax.broadcasted_iota(jnp.int32, both.shape, 0) % (2 * capacity) < capacity
    dpre = jnp.where(of_x, both, 0.0).astype(BF16)
    act = jnp.where(of_x, 0.0, both).astype(BF16)
    count = feats // PIECES
    copies = []
    for piece in range(PIECES):
        span = slice(piece * count, (piece + 1) * count)
        part = rows[:, span]
        w_in_ref[span] = lax.dot_general(part, dpre, ROWS_BY_ROWS, preferred_element_type=F32)
        w_out_ref[:, span] = lax.dot_general(act, part, ROWS_BY_ROWS, preferred_element_type=F32)
        span = pl.ds(piece * count, count)
        for source, target in (
            (w_in_ref.at[span], w_in_hbm.at[span]),
            (w_out_ref.at[:, span], w_out_hbm.at[:, span]),
        ):
            copy = pltpu.make_async_copy(source, target, sems.at[len(copies)])
            copy.start()
            copies.append(copy)
    for copy in copies:
        copy.wait()
    written_ref[...] = jnp.zeros(written_ref.shape, F32)


def combine_kernel(steps, *refs):
    kept_ref, came_refs = refs[0], refs[1:steps]
    place_ref, spread_ref, tokens_ref, gate_out_ref = refs[steps:]
    feats = tokens_ref.shape[1]
    capacity = kept_ref.shape[0]
    came = [ref[...].astype(F32) for ref in came_refs]
    half = steps // WINDOW
    own = sum(came[: half - 1], kept_ref[...])
    other = sum(came[half:], came[half - 1])
    slots = jnp.concatenate([own, other], axis=0)
    grads = slots[:, :feats]
    high = grads.astype(BF16)
    low = (grads - high.astype(F32)).astype(BF16)
    both = jnp.concatenate([high, low], axis=0)
    tokens_ref[...] = jnp.dot(spread_ref[...], both, preferred_element_type=F32).astype(BF16)
    slot_gate = jnp.sum(slots[:, feats:], axis=1, keepdims=True)
    picked = place_ref[: WINDOW * capacity].astype(F32) * slot_gate
    masks = place_ref[WINDOW * capacity :].astype(F32)
    result = jnp.zeros(gate_out_ref.shape, F32)
    for index in range(WINDOW):
        span = slice(index * capacity, (index + 1) * capacity)
        value = jnp.sum(picked[span], axis=0, keepdims=True)
        result = result + masks[2 * index : 2 * index + 2] * value
    gate_out_ref[...] = result


def swap(array, axes, bit):
    size = lax.axis_size(axes)
    return lax.ppermute(array, axes, [(index, index ^ bit) for index in range(size)])


def join(pieces, after=()):
    rows, wide = pieces[0].shape
    rows *= len(pieces)
    shape = jax.ShapeDtypeStruct((rows, wide), BF16)
    return call(join_kernel, shape, 0, 4 * rows * wide, after=after)(*pieces)


def body(tokens, grad_out, routes, gates, w_in, w_out):
    nodes = lax.axis_size("node")
    locals_ = lax.axis_size("local")
    edatas = lax.axis_size("edata")
    tok_rows, feats = tokens.shape
    hidden = w_in.shape[1]
    capacity = 2 * tok_rows // EXPERTS
    slots = WINDOW * capacity
    wide = feats + LANES
    coded = 4 * hidden + LANES
    shape = jax.ShapeDtypeStruct
    hbm = pl.BlockSpec(memory_space=pltpu.HBM)
    vmem = pl.BlockSpec(memory_space=pltpu.VMEM)

    routes_t, gates_t, tokens, grad_out = [
        pltpu.with_memory_space_constraint(value, pltpu.HBM)
        for value in (routes.T, gates.T, tokens, grad_out)
    ]
    own_rows, other_rows, place, spread = call(
        gather_kernel,
        (
            pltpu.VMEM((2 * capacity, wide), BF16),
            pltpu.VMEM((2 * capacity, wide), BF16),
            pltpu.VMEM((slots + 16, tok_rows), BF16),
            pltpu.VMEM((tok_rows, 2 * slots), BF16),
        ),
        4 * slots * tok_rows * feats,
        4 * tok_rows * feats,
        in_specs=[hbm] * 4,
        scratch_shapes=[
            pltpu.VMEM((2, tok_rows), jnp.int32),
            pltpu.VMEM((2, tok_rows), BF16),
            pltpu.VMEM((tok_rows, feats), BF16),
            pltpu.VMEM((tok_rows, feats), BF16),
            pltpu.SemaphoreType.DMA((2 + 2 * PIECES,)),
        ],
    )(routes_t, gates_t, tokens, grad_out)

    w_in_other, w_out_other = swap(w_in, "local", 1), swap(w_out, "local", 1)

    half_nodes = nodes // WINDOW
    pieces = [own_rows]
    for step in range(1, nodes):
        pieces.append(swap(own_rows if step < half_nodes else other_rows, "node", step))
    rows = half_nodes * (locals_ // 2) * capacity
    last = ()
    chains = []
    held = []
    for chunk in (pieces[:half_nodes], pieces[half_nodes:]):
        chunk = join(chunk, last)
        bit = 2
        while bit < locals_:
            chunk = join([chunk, swap(chunk, "local", bit)])
            bit *= 2
        held.append(chunk)
        part, gate_rows = call(
            functools.partial(part_kernel, capacity),
            (shape((rows, coded), I16), shape((rows, LANES), F32)),
            16 * rows * feats * hidden,
            4 * rows * feats + 8 * feats * hidden,
            after=last,
        )(chunk, w_in, w_in_other, w_out, w_out_other)
        last = (part,)
        chains.append((part, swap(part, "edata", 1), gate_rows))
    bit = 2
    while bit < edatas:
        for index, (part, other, gate_rows) in enumerate(chains):
            part = call(
                add_codes_kernel,
                shape((rows, coded), I16),
                16 * rows * hidden,
                6 * rows * coded,
                after=last,
            )(part, other)
            last = (part,)
            chains[index] = (part, swap(part, "edata", bit), gate_rows)
        bit *= 2

    mine = []
    back = []
    slots_back = []
    for index, (part, other, gate_rows) in enumerate(chains):
        dealt = [shape((capacity, wide), BF16)] * half_nodes
        if index == 0:
            dealt[0] = shape((capacity, wide), F32)
        own, theirs, *slot_parts = call(
            functools.partial(slot_kernel, capacity),
            [shape((2 * rows, hidden), BF16)] * 2
            + (dealt if locals_ == 2 else [shape((rows, wide), F32)]),
            4 * rows * feats * hidden,
            4 * feats * hidden + 4 * rows * feats,
            after=last,
        )(part, other, gate_rows, w_in, w_in_other)
        last = (own,)
        mine.append(own)
        back.append(swap(theirs, "local", 1))
        if locals_ > 2:
            half = rows // 2
            keep, send = slot_parts[0][:half], slot_parts[0][half:]
            bit = locals_ // 2
            while bit > 2:
                half //= 2
                keep, send = call(
                    halve_kernel,
                    (shape((half, wide), F32),) * 2,
                    4 * half * wide,
                    24 * half * wide,
                )(keep, swap(send, "local", bit))
                bit //= 2
            slot_parts = call(deal_kernel, dealt, 4 * half * wide, 12 * half * wide)(
                keep, swap(send, "local", bit)
            )
        for step, send in enumerate(slot_parts, index * half_nodes):
            slots_back.append(swap(send, "node", step) if step else send)
    came = [swap(chunk, "local", 1) for chunk in held]
    grad_w_in, grad_w_out, written = call(
        functools.partial(weight_kernel, capacity),
        (shape((feats, hidden), F32), shape((hidden, feats), F32), shape((8, LANES), F32)),
        32 * rows * feats * hidden,
        8 * feats * hidden,
        in_specs=[vmem] * 8,
        after=slots_back[1:half_nodes],
        out_specs=[hbm, hbm, vmem],
        scratch_shapes=[
            pltpu.VMEM((feats, hidden), F32),
            pltpu.VMEM((hidden, feats), F32),
            pltpu.SemaphoreType.DMA((2 * PIECES,)),
        ],
    )(*held, *came, *mine, *back)
    grad_tokens, grad_gates = call(
        functools.partial(combine_kernel, nodes),
        (shape((tok_rows, feats), BF16), shape((2, tok_rows), F32)),
        4 * slots * tok_rows * feats,
        2 * tok_rows * feats,
        after=(written,),
    )(*slots_back, place, spread)
    return (grad_tokens, grad_gates.T, grad_w_in, grad_w_out)


def solution(mesh):
    in_specs = (
        P(("node", "local"), "edata"),
        P(("node", "local"), "edata"),
        P(("node", "local"), None),
        P(("node", "local"), None),
        P("edata", ("node", "local")),
        P(("node", "local"), "edata"),
    )
    out_specs = (
        P(("node", "local"), "edata"),
        P(("node", "local"), None),
        P("edata", ("node", "local")),
        P(("node", "local"), "edata"),
    )
    return jax.shard_map(body, mesh=mesh, in_specs=in_specs, out_specs=out_specs, check_vma=False)
```

```python
import functools

import jax
import jax.numpy as jnp
from jax import lax
from jax.experimental import pallas as pl
from jax.experimental.pallas import tpu as pltpu
from jax.sharding import PartitionSpec as P

EXPERTS = 64
WINDOW = 2
LANES = 128
PIECES = 4
VMEM_LIMIT = 40 * 1024 * 1024

BF16 = jnp.bfloat16
F32 = jnp.float32
I16 = jnp.int16
ROWS_BY_ROWS = (((0,), (0,)), ((), ()))
COLS_BY_COLS = (((1,), (1,)), ((), ()))


def gelu_pair(pre_act):
    coefficient = 0.7978845608028654
    square = pre_act * pre_act
    tanh_val = jnp.tanh(coefficient * (pre_act + 0.044715 * pre_act * square))
    half = 0.5 * (1.0 + tanh_val)
    activation = pre_act * half
    slopes = half + 0.5 * pre_act * (1.0 - tanh_val * tanh_val) * coefficient * (
        1.0 + 3.0 * 0.044715 * square
    )
    return (activation, slopes)


def call(kernel, out_shape, flops, moved, limit=VMEM_LIMIT, in_specs=None, after=(), **more):
    def run(*operands):
        given = in_specs or [pl.BlockSpec(memory_space=pltpu.VMEM)] * len(operands)
        return pl.pallas_call(
            lambda *refs: kernel(*refs[len(after) :]),
            out_shape=out_shape,
            in_specs=[pl.BlockSpec(memory_space=pl.ANY)] * len(after) + list(given),
            compiler_params=pltpu.CompilerParams(vmem_limit_bytes=limit),
            cost_estimate=pl.CostEstimate(flops=flops, bytes_accessed=moved, transcendentals=0),
            **more,
        )(*after, *operands)

    return run


def own_expert():
    half_nodes = lax.axis_size("node") // WINDOW
    return lax.axis_index("node") // half_nodes


def split_value(value):
    high = value.astype(BF16).astype(F32)
    lane = lax.broadcasted_iota(jnp.int32, (value.shape[0], LANES), 1)
    return jnp.where(lane == 0, high, jnp.where(lane == 1, value - high, 0.0))


def encode(values):
    top = jnp.max(jnp.abs(values), axis=1, keepdims=True)
    power = jnp.ceil(jnp.log2(jnp.maximum(top, 1e-30)))
    codes = jnp.round(values * (1.999 * jnp.exp2(14.0 - power)))
    return codes.astype(jnp.int32).astype(I16), power


def decode(codes, power):
    return codes.astype(jnp.int32).astype(F32) * (jnp.exp2(power - 14.0) / 1.999)


def store_codes(out_ref, pair):
    hidden = pair[0].shape[1]
    lane = lax.broadcasted_iota(jnp.int32, (pair[0].shape[0], LANES), 1)
    powers = []
    for index, values in enumerate(pair):
        codes, power = encode(values)
        out_ref[:, index * hidden : (index + 1) * hidden] = codes
        powers.append(power)
    powers = jnp.where(lane == 0, powers[0], powers[1])
    out_ref[:, 2 * hidden :] = powers.astype(jnp.int32).astype(I16)


def load_codes(ref):
    hidden = (ref.shape[1] - LANES) // 2
    powers = ref[:, 2 * hidden :].astype(jnp.int32).astype(F32)
    return [
        decode(ref[:, index * hidden : (index + 1) * hidden], powers[:, index : index + 1])
        for index in range(2)
    ]


def gather_kernel(routes_hbm, gates_hbm, tokens_hbm, grads_hbm, w_in_hbm, w_out_hbm, own_ref,
                  other_ref, place_ref, spread_ref, w_ref, routes_ref, gates_ref, tokens_ref,
                  grads_ref, sems):
    tok_rows, feats = tokens_ref.shape
    capacity = own_ref.shape[0] // 2
    slots = WINDOW * capacity
    copies = [
        pltpu.make_async_copy(routes_hbm, routes_ref, sems.at[0]),
        pltpu.make_async_copy(gates_hbm, gates_ref, sems.at[1]),
    ]
    count = tok_rows // PIECES
    for source, target in ((tokens_hbm, tokens_ref), (grads_hbm, grads_ref)):
        for piece in range(PIECES):
            span = pl.ds(piece * count, count)
            copies.append(
                pltpu.make_async_copy(source.at[span], target.at[span], sems.at[len(copies)])
            )
    hidden = w_out_hbm.shape[0]
    upper, lower = pl.ds(0, hidden), pl.ds(hidden, hidden)
    moves = [(w_out_hbm, w_ref.at[upper])]
    for block in range(0, feats, hidden):
        span = pl.ds(block, hidden)
        moves.append((w_in_hbm.at[span], w_ref.at[lower, span]))
    for source, target in moves:
        copies.append(pltpu.make_async_copy(source, target, sems.at[len(copies)]))
    for copy in copies:
        copy.start()
    earlier = lax.broadcasted_iota(jnp.int32, (tok_rows, tok_rows), 0) < lax.broadcasted_iota(
        jnp.int32, (tok_rows, tok_rows), 1
    )
    earlier = earlier.astype(F32).astype(BF16)
    slot_of = lax.broadcasted_iota(jnp.int32, (capacity, tok_rows), 0).astype(F32)
    row_of = lax.broadcasted_iota(jnp.int32, (8, tok_rows), 0)
    own = own_expert()
    copies[0].wait()
    copies[1].wait()
    routes = routes_ref[...]
    gates = gates_ref[...].astype(F32)
    hits = [(routes == expert).astype(F32) for expert in (own, 1 - own)]
    named = [hit[0:1] + hit[1:2] for hit in hits]
    weight = [hit * gates for hit in hits]
    weight = [value[0:1] + value[1:2] for value in weight]
    names = jnp.where(row_of == 0, named[0], jnp.where(row_of == 1, named[1], 0.0)).astype(BF16)
    before = jnp.dot(names, earlier, preferred_element_type=F32)
    parts = [jnp.where(before[e : e + 1] == slot_of, named[e], 0.0) for e in range(WINDOW)]
    place = jnp.concatenate(parts, axis=0).astype(BF16)
    place_ref[:slots] = place
    spread_ref[...] = jnp.concatenate(parts + parts, axis=0).T.astype(BF16)
    masks = jnp.zeros((16, tok_rows), F32)
    row_of = lax.broadcasted_iota(jnp.int32, masks.shape, 0)
    for index, hit in enumerate(hits):
        for k in range(2):
            masks = jnp.where(row_of == 2 * index + k, hit[k : k + 1], masks)
    place_ref[slots:] = masks.astype(BF16)
    for copy in copies[2 : 2 + PIECES]:
        copy.wait()
    rows_x = jnp.dot(place, tokens_ref[...], preferred_element_type=F32)
    for copy in copies[2 + PIECES : 2 + 2 * PIECES]:
        copy.wait()
    rows_dy = jnp.dot(place, grads_ref[...], preferred_element_type=F32)
    for expert, out_ref in ((0, own_ref), (1, other_ref)):
        span = slice(expert * capacity, (expert + 1) * capacity)
        out_ref[:, :feats] = jnp.concatenate([rows_x[span], rows_dy[span]], axis=0).astype(BF16)
        gate = jnp.sum(parts[expert] * weight[expert], axis=1, keepdims=True)
        gate = jnp.concatenate([gate, gate], axis=0)
        out_ref[:, feats:] = jnp.broadcast_to(gate, (2 * capacity, LANES)).astype(BF16)
    for copy in copies[2 + 2 * PIECES :]:
        copy.wait()


def join_kernel(*refs):
    *pieces, out_ref = refs
    rows = pieces[0].shape[0]
    for index, ref in enumerate(pieces):
        out_ref[index * rows : (index + 1) * rows] = ref[...]


def part_kernel(capacity, rows_ref, w_ref, w_other_ref, part_ref, gate_ref):
    feats = w_ref.shape[1]
    hidden = w_ref.shape[0] // 2
    groups = rows_ref.shape[0] // (2 * capacity)
    gate = rows_ref[:, feats:].astype(F32).reshape(groups, 2 * capacity, LANES)
    gate_ref[...] = gate[:, :capacity].reshape(groups * capacity, LANES)
    rows = rows_ref[:, :feats]
    pre = []
    back = []
    for ref in (w_ref, w_other_ref):
        pre.append(
            sum(
                jnp.dot(
                    rows[:, block : block + hidden],
                    ref[hidden:, block : block + hidden],
                    preferred_element_type=F32,
                )
                for block in range(0, feats, hidden)
            )
        )
        back.append(
            lax.dot_general(rows, ref[:hidden], COLS_BY_COLS, preferred_element_type=F32)
        )
    pair = []
    for values, span in ((pre, slice(0, capacity)), (back, slice(capacity, 2 * capacity))):
        values = jnp.concatenate(values, axis=1).reshape(groups, 2 * capacity, 2 * hidden)
        pair.append(values[:, span].reshape(groups * capacity, 2 * hidden))
    store_codes(part_ref, pair)


def add_codes_kernel(first_ref, second_ref, out_ref):
    pairs = zip(load_codes(first_ref), load_codes(second_ref))
    store_codes(out_ref, [first + second for first, second in pairs])


def deal(total, refs):
    each, wide = refs[0].shape
    feats = wide - LANES
    gate = split_value(jnp.sum(total[:, feats:], axis=1, keepdims=True))
    for index, ref in enumerate(refs):
        span = slice(index * each, (index + 1) * each)
        ref[:, :feats] = total[span, :feats].astype(ref.dtype)
        ref[:, feats:] = gate[span].astype(ref.dtype)


def slot_kernel(capacity, first_ref, second_ref, gate_ref, w_ref, w_other_ref, mine_ref,
                theirs_ref, *slot_refs):
    hidden = w_ref.shape[0] // 2
    pairs = zip(load_codes(first_ref), load_codes(second_ref))
    pre, back = [first + second for first, second in pairs]
    gate = gate_ref[:, :1]
    activation, slopes = gelu_pair(pre)
    dpre = (gate * back * slopes).astype(BF16)
    act = gate * activation
    slot = []
    for block in range(0, w_ref.shape[1], hidden):
        span = slice(block, block + hidden)
        slot.append(
            sum(
                lax.dot_general(
                    part, ref[hidden:, span], COLS_BY_COLS, preferred_element_type=F32
                )
                for part, ref in ((dpre[:, :hidden], w_ref), (dpre[:, hidden:], w_other_ref))
            )
        )
    slot_gate = split_value(jnp.sum(activation * back, axis=1, keepdims=True))
    total = jnp.concatenate(slot + [slot_gate], axis=1)
    if len(slot_refs) == 1:
        slot_refs[0][...] = total
    else:
        deal(total, slot_refs)
    rows = dpre.shape[0]
    both = [
        value.reshape(rows // capacity, capacity, 2 * hidden) for value in (dpre.astype(F32), act)
    ]
    both = jnp.concatenate(both, axis=1).reshape(2 * rows, 2 * hidden).astype(BF16)
    mine_ref[...] = both[:, :hidden]
    theirs_ref[...] = both[:, hidden:]


def halve_kernel(kept_ref, came_ref, keep_ref, send_ref):
    half = keep_ref.shape[0]
    total = kept_ref[...] + came_ref[...]
    keep_ref[...] = total[:half]
    send_ref[...] = total[half:]


def deal_kernel(kept_ref, came_ref, *refs):
    deal(kept_ref[...] + came_ref[...], refs)


def weight_kernel(capacity, *refs):
    rows_refs, both_refs = refs[:4], refs[4:8]
    w_in_hbm, w_out_hbm, written_ref, w_in_ref, w_out_ref, sems = refs[8:]
    feats, hidden = w_in_ref.shape
    rows = jnp.concatenate([ref[:, :feats] for ref in rows_refs], axis=0)
    both = jnp.concatenate([ref[...] for ref in both_refs], axis=0).astype(F32)
    of_x = lax.broadcasted_iota(jnp.int32, both.shape, 0) % (2 * capacity) < capacity
    dpre = jnp.where(of_x, both, 0.0).astype(BF16)
    act = jnp.where(of_x, 0.0, both).astype(BF16)
    count = feats // PIECES
    copies = []
    for piece in range(PIECES):
        span = slice(piece * count, (piece + 1) * count)
        part = rows[:, span]
        w_in_ref[span] = lax.dot_general(part, dpre, ROWS_BY_ROWS, preferred_element_type=F32)
        w_out_ref[:, span] = lax.dot_general(act, part, ROWS_BY_ROWS, preferred_element_type=F32)
        span = pl.ds(piece * count, count)
        for source, target in (
            (w_in_ref.at[span], w_in_hbm.at[span]),
            (w_out_ref.at[:, span], w_out_hbm.at[:, span]),
        ):
            copy = pltpu.make_async_copy(source, target, sems.at[len(copies)])
            copy.start()
            copies.append(copy)
    for copy in copies:
        copy.wait()
    written_ref[...] = jnp.zeros(written_ref.shape, F32)


def combine_kernel(steps, *refs):
    kept_ref, came_refs = refs[0], refs[1:steps]
    place_ref, spread_ref, tokens_ref, gate_out_ref = refs[steps:]
    feats = tokens_ref.shape[1]
    capacity = kept_ref.shape[0]
    came = [ref[...].astype(F32) for ref in came_refs]
    half = steps // WINDOW
    own = sum(came[: half - 1], kept_ref[...])
    other = sum(came[half:], came[half - 1])
    slots = jnp.concatenate([own, other], axis=0)
    grads = slots[:, :feats]
    high = grads.astype(BF16)
    low = (grads - high.astype(F32)).astype(BF16)
    both = jnp.concatenate([high, low], axis=0)
    tokens_ref[...] = jnp.dot(spread_ref[...], both, preferred_element_type=F32).astype(BF16)
    slot_gate = jnp.sum(slots[:, feats:], axis=1, keepdims=True)
    picked = place_ref[: WINDOW * capacity].astype(F32) * slot_gate
    masks = place_ref[WINDOW * capacity :].astype(F32)
    result = jnp.zeros(gate_out_ref.shape, F32)
    for index in range(WINDOW):
        span = slice(index * capacity, (index + 1) * capacity)
        value = jnp.sum(picked[span], axis=0, keepdims=True)
        result = result + masks[2 * index : 2 * index + 2] * value
    gate_out_ref[...] = result


def swap(array, axes, bit):
    size = lax.axis_size(axes)
    return lax.ppermute(array, axes, [(index, index ^ bit) for index in range(size)])


def join(pieces, after=()):
    rows, wide = pieces[0].shape
    rows *= len(pieces)
    shape = jax.ShapeDtypeStruct((rows, wide), BF16)
    return call(join_kernel, shape, 0, 4 * rows * wide, after=after)(*pieces)


def body(tokens, grad_out, routes, gates, w_in, w_out):
    nodes = lax.axis_size("node")
    locals_ = lax.axis_size("local")
    edatas = lax.axis_size("edata")
    tok_rows, feats = tokens.shape
    hidden = w_in.shape[1]
    capacity = 2 * tok_rows // EXPERTS
    slots = WINDOW * capacity
    wide = feats + LANES
    coded = 4 * hidden + LANES
    shape = jax.ShapeDtypeStruct
    hbm = pl.BlockSpec(memory_space=pltpu.HBM)
    vmem = pl.BlockSpec(memory_space=pltpu.VMEM)

    inputs = [
        pltpu.with_memory_space_constraint(value, pltpu.HBM)
        for value in (routes.T, gates.T, tokens, grad_out, w_in, w_out)
    ]
    own_rows, other_rows, place, spread, weights = call(
        gather_kernel,
        (
            pltpu.VMEM((2 * capacity, wide), BF16),
            pltpu.VMEM((2 * capacity, wide), BF16),
            pltpu.VMEM((slots + 16, tok_rows), BF16),
            pltpu.VMEM((tok_rows, 2 * slots), BF16),
            pltpu.VMEM((2 * hidden, feats), BF16),
        ),
        4 * slots * tok_rows * feats,
        4 * tok_rows * feats + 4 * hidden * feats,
        in_specs=[hbm] * 6,
        scratch_shapes=[
            pltpu.VMEM((2, tok_rows), jnp.int32),
            pltpu.VMEM((2, tok_rows), BF16),
            pltpu.VMEM((tok_rows, feats), BF16),
            pltpu.VMEM((tok_rows, feats), BF16),
            pltpu.SemaphoreType.DMA((3 + 2 * PIECES + feats // hidden,)),
        ],
    )(*inputs)

    other_weights = swap(weights, "local", 1)

    half_nodes = nodes // WINDOW
    pieces = [own_rows]
    for step in range(1, nodes):
        pieces.append(swap(own_rows if step < half_nodes else other_rows, "node", step))
    rows = half_nodes * (locals_ // 2) * capacity
    last = ()
    chains = []
    held = []
    for chunk in (pieces[:half_nodes], pieces[half_nodes:]):
        chunk = join(chunk, last)
        bit = 2
        while bit < locals_:
            chunk = join([chunk, swap(chunk, "local", bit)])
            bit *= 2
        held.append(chunk)
        part, gate_rows = call(
            functools.partial(part_kernel, capacity),
            (shape((rows, coded), I16), shape((rows, LANES), F32)),
            16 * rows * feats * hidden,
            4 * rows * feats + 8 * feats * hidden,
            after=last,
        )(chunk, weights, other_weights)
        last = (part,)
        chains.append((part, swap(part, "edata", 1), gate_rows))
    bit = 2
    while bit < edatas:
        for index, (part, other, gate_rows) in enumerate(chains):
            part = call(
                add_codes_kernel,
                shape((rows, coded), I16),
                16 * rows * hidden,
                6 * rows * coded,
                after=last,
            )(part, other)
            last = (part,)
            chains[index] = (part, swap(part, "edata", bit), gate_rows)
        bit *= 2

    mine = []
    back = []
    slots_back = []
    for index, (part, other, gate_rows) in enumerate(chains):
        dealt = [shape((capacity, wide), BF16)] * half_nodes
        if index == 0:
            dealt[0] = shape((capacity, wide), F32)
        own, theirs, *slot_parts = call(
            functools.partial(slot_kernel, capacity),
            [shape((2 * rows, hidden), BF16)] * 2
            + (dealt if locals_ == 2 else [shape((rows, wide), F32)]),
            4 * rows * feats * hidden,
            4 * feats * hidden + 4 * rows * feats,
            after=last,
        )(part, other, gate_rows, weights, other_weights)
        last = (own,)
        mine.append(own)
        back.append(swap(theirs, "local", 1))
        if locals_ > 2:
            half = rows // 2
            keep, send = slot_parts[0][:half], slot_parts[0][half:]
            bit = locals_ // 2
            while bit > 2:
                half //= 2
                keep, send = call(
                    halve_kernel,
                    (shape((half, wide), F32),) * 2,
                    4 * half * wide,
                    24 * half * wide,
                )(keep, swap(send, "local", bit))
                bit //= 2
            slot_parts = call(deal_kernel, dealt, 4 * half * wide, 12 * half * wide)(
                keep, swap(send, "local", bit)
            )
        for step, send in enumerate(slot_parts, index * half_nodes):
            slots_back.append(swap(send, "node", step) if step else send)
    came = [swap(chunk, "local", 1) for chunk in held]
    grad_w_in, grad_w_out, written = call(
        functools.partial(weight_kernel, capacity),
        (shape((feats, hidden), F32), shape((hidden, feats), F32), shape((8, LANES), F32)),
        32 * rows * feats * hidden,
        8 * feats * hidden,
        in_specs=[vmem] * 8,
        after=slots_back[1:half_nodes],
        out_specs=[hbm, hbm, vmem],
        scratch_shapes=[
            pltpu.VMEM((feats, hidden), F32),
            pltpu.VMEM((hidden, feats), F32),
            pltpu.SemaphoreType.DMA((2 * PIECES,)),
        ],
    )(*held, *came, *mine, *back)
    grad_tokens, grad_gates = call(
        functools.partial(combine_kernel, nodes),
        (shape((tok_rows, feats), BF16), shape((2, tok_rows), F32)),
        4 * slots * tok_rows * feats,
        2 * tok_rows * feats,
        after=(written,),
    )(*slots_back[:half_nodes], *reversed(slots_back[half_nodes:]), place, spread)
    return (grad_tokens, grad_gates.T, grad_w_in, grad_w_out)


def solution(mesh):
    in_specs = (
        P(("node", "local"), "edata"),
        P(("node", "local"), "edata"),
        P(("node", "local"), None),
        P(("node", "local"), None),
        P("edata", ("node", "local")),
        P(("node", "local"), "edata"),
    )
    out_specs = (
        P(("node", "local"), "edata"),
        P(("node", "local"), None),
        P("edata", ("node", "local")),
        P(("node", "local"), "edata"),
    )
    return jax.shard_map(body, mesh=mesh, in_specs=in_specs, out_specs=out_specs, check_vma=False)
```

```python
import functools

import jax
import jax.numpy as jnp
from jax import lax
from jax.experimental import pallas as pl
from jax.experimental.pallas import tpu as pltpu
from jax.sharding import PartitionSpec as P

EXPERTS = 64
WINDOW = 2
LANES = 128
PIECES = 4
PLANE = ("node", "local")
VMEM_LIMIT = 40 * 1024 * 1024

BF16 = jnp.bfloat16
F32 = jnp.float32
I16 = jnp.int16
ROWS_BY_ROWS = (((0,), (0,)), ((), ()))
COLS_BY_COLS = (((1,), (1,)), ((), ()))


def gelu_pair(pre_act):
    coefficient = 0.7978845608028654
    square = pre_act * pre_act
    tanh_val = jnp.tanh(coefficient * (pre_act + 0.044715 * pre_act * square))
    half = 0.5 * (1.0 + tanh_val)
    activation = pre_act * half
    slopes = half + 0.5 * pre_act * (1.0 - tanh_val * tanh_val) * coefficient * (
        1.0 + 3.0 * 0.044715 * square
    )
    return (activation, slopes)


def call(kernel, out_shape, flops, moved, limit=VMEM_LIMIT, in_specs=None, after=(), **more):
    def run(*operands):
        given = in_specs or [pl.BlockSpec(memory_space=pltpu.VMEM)] * len(operands)
        return pl.pallas_call(
            lambda *refs: kernel(*refs[len(after) :]),
            out_shape=out_shape,
            in_specs=[pl.BlockSpec(memory_space=pl.ANY)] * len(after) + list(given),
            compiler_params=pltpu.CompilerParams(vmem_limit_bytes=limit),
            cost_estimate=pl.CostEstimate(flops=flops, bytes_accessed=moved, transcendentals=0),
            **more,
        )(*after, *operands)

    return run


def own_expert():
    half_nodes = lax.axis_size("node") // WINDOW
    return lax.axis_index("node") // half_nodes


def on_worker():
    return lax.axis_index("local") % 2 == 1


def split_value(value):
    high = value.astype(BF16).astype(F32)
    lane = lax.broadcasted_iota(jnp.int32, (value.shape[0], LANES), 1)
    return jnp.where(lane == 0, high, jnp.where(lane == 1, value - high, 0.0))


def encode(values):
    top = jnp.max(jnp.abs(values), axis=1, keepdims=True)
    power = jnp.ceil(jnp.log2(jnp.maximum(top, 1e-30)))
    codes = jnp.round(values * (1.999 * jnp.exp2(14.0 - power)))
    return codes.astype(jnp.int32).astype(I16), power


def decode(codes, power):
    return codes.astype(jnp.int32).astype(F32) * (jnp.exp2(power - 14.0) / 1.999)


def store_codes(out_ref, pair):
    hidden = pair[0].shape[1]
    lane = lax.broadcasted_iota(jnp.int32, (pair[0].shape[0], LANES), 1)
    powers = []
    for index, values in enumerate(pair):
        codes, power = encode(values)
        out_ref[:, index * hidden : (index + 1) * hidden] = codes
        powers.append(power)
    powers = jnp.where(lane == 0, powers[0], powers[1])
    out_ref[:, 2 * hidden :] = powers.astype(jnp.int32).astype(I16)


def load_codes(ref):
    hidden = (ref.shape[1] - LANES) // 2
    powers = ref[:, 2 * hidden :].astype(jnp.int32).astype(F32)
    return [
        decode(ref[:, index * hidden : (index + 1) * hidden], powers[:, index : index + 1])
        for index in range(2)
    ]


def gather_kernel(routes_hbm, gates_hbm, tokens_hbm, grads_hbm, w_in_hbm, w_out_hbm, rows_ref,
                  place_ref, spread_ref, w_ref, routes_ref, gates_ref, tokens_ref,
                  grads_ref, sems):
    tok_rows, feats = tokens_ref.shape
    slots = rows_ref.shape[0] // 2
    capacity = slots // WINDOW
    copies = [
        pltpu.make_async_copy(routes_hbm, routes_ref, sems.at[0]),
        pltpu.make_async_copy(gates_hbm, gates_ref, sems.at[1]),
    ]
    count = tok_rows // PIECES
    for source, target in ((tokens_hbm, tokens_ref), (grads_hbm, grads_ref)):
        for piece in range(PIECES):
            span = pl.ds(piece * count, count)
            copies.append(
                pltpu.make_async_copy(source.at[span], target.at[span], sems.at[len(copies)])
            )
    hidden = w_out_hbm.shape[0]
    upper, lower = pl.ds(0, hidden), pl.ds(hidden, hidden)
    moves = [(w_out_hbm, w_ref.at[upper])]
    for block in range(0, feats, hidden):
        span = pl.ds(block, hidden)
        moves.append((w_in_hbm.at[span], w_ref.at[lower, span]))
    for source, target in moves:
        copies.append(pltpu.make_async_copy(source, target, sems.at[len(copies)]))
    for copy in copies:
        copy.start()
    earlier = lax.broadcasted_iota(jnp.int32, (tok_rows, tok_rows), 0) < lax.broadcasted_iota(
        jnp.int32, (tok_rows, tok_rows), 1
    )
    earlier = earlier.astype(F32).astype(BF16)
    slot_of = lax.broadcasted_iota(jnp.int32, (capacity, tok_rows), 0).astype(F32)
    row_of = lax.broadcasted_iota(jnp.int32, (8, tok_rows), 0)
    own = own_expert()
    copies[0].wait()
    copies[1].wait()
    routes = routes_ref[...]
    gates = gates_ref[...].astype(F32)
    hits = [(routes == expert).astype(F32) for expert in (own, 1 - own)]
    named = [hit[0:1] + hit[1:2] for hit in hits]
    weight = [hit * gates for hit in hits]
    weight = [value[0:1] + value[1:2] for value in weight]
    names = jnp.where(row_of == 0, named[0], jnp.where(row_of == 1, named[1], 0.0)).astype(BF16)
    before = jnp.dot(names, earlier, preferred_element_type=F32)
    parts = [jnp.where(before[e : e + 1] == slot_of, named[e], 0.0) for e in range(WINDOW)]
    place = jnp.concatenate(parts, axis=0).astype(BF16)
    place_ref[:slots] = place
    spread_ref[...] = jnp.concatenate(parts + parts, axis=0).T.astype(BF16)
    masks = jnp.zeros((16, tok_rows), F32)
    row_of = lax.broadcasted_iota(jnp.int32, masks.shape, 0)
    for index, hit in enumerate(hits):
        for k in range(2):
            masks = jnp.where(row_of == 2 * index + k, hit[k : k + 1], masks)
    place_ref[slots:] = masks.astype(BF16)
    for copy in copies[2 : 2 + PIECES]:
        copy.wait()
    rows_x = jnp.dot(place, tokens_ref[...], preferred_element_type=F32)
    for copy in copies[2 + PIECES : 2 + 2 * PIECES]:
        copy.wait()
    rows_dy = jnp.dot(place, grads_ref[...], preferred_element_type=F32)
    chunks = []
    gates = []
    for expert in range(WINDOW):
        span = slice(expert * capacity, (expert + 1) * capacity)
        chunks += [rows_x[span], rows_dy[span]]
        gates += [jnp.sum(parts[expert] * weight[expert], axis=1, keepdims=True)] * 2
    rows_ref[:, :feats] = jnp.concatenate(chunks, axis=0).astype(BF16)
    gates = jnp.broadcast_to(jnp.concatenate(gates, axis=0), (2 * slots, LANES))
    rows_ref[:, feats:] = gates.astype(BF16)
    for copy in copies[2 + 2 * PIECES :]:
        copy.wait()


def sort_kernel(first_ref, second_ref, own_ref, other_ref):
    half = first_ref.shape[0] // WINDOW
    for index, ref in enumerate((first_ref, second_ref)):
        span = slice(index * half, (index + 1) * half)
        own_ref[span] = ref[:half]
        other_ref[span] = ref[half:]


def join_kernel(*refs):
    *pieces, out_ref = refs
    rows = pieces[0].shape[0]
    for index, ref in enumerate(pieces):
        out_ref[index * rows : (index + 1) * rows] = ref[...]


def part_kernel(capacity, rows_ref, w_ref, w_other_ref, part_ref, gate_ref):
    feats = w_ref.shape[1]
    hidden = w_ref.shape[0] // 2
    groups = rows_ref.shape[0] // (2 * capacity)
    gate = rows_ref[:, feats:].astype(F32).reshape(groups, 2 * capacity, LANES)
    gate_ref[...] = gate[:, :capacity].reshape(groups * capacity, LANES)
    rows = rows_ref[:, :feats]
    pre = []
    back = []
    for ref in (w_ref, w_other_ref):
        pre.append(
            sum(
                jnp.dot(
                    rows[:, block : block + hidden],
                    ref[hidden:, block : block + hidden],
                    preferred_element_type=F32,
                )
                for block in range(0, feats, hidden)
            )
        )
        back.append(
            lax.dot_general(rows, ref[:hidden], COLS_BY_COLS, preferred_element_type=F32)
        )
    pair = []
    for values, span in ((pre, slice(0, capacity)), (back, slice(capacity, 2 * capacity))):
        values = jnp.concatenate(values, axis=1).reshape(groups, 2 * capacity, 2 * hidden)
        pair.append(values[:, span].reshape(groups * capacity, 2 * hidden))
    store_codes(part_ref, pair)


def add_codes_kernel(first_ref, second_ref, out_ref):
    pairs = zip(load_codes(first_ref), load_codes(second_ref))
    store_codes(out_ref, [first + second for first, second in pairs])


def deal(total, refs):
    each, wide = refs[0].shape
    feats = wide - LANES
    gate = split_value(jnp.sum(total[:, feats:], axis=1, keepdims=True))
    for index, ref in enumerate(refs):
        span = slice(index * each, (index + 1) * each)
        ref[:, :feats] = total[span, :feats].astype(ref.dtype)
        ref[:, feats:] = gate[span].astype(ref.dtype)


def slot_kernel(capacity, before, first_ref, second_ref, gate_ref, w_ref, w_other_ref, *refs):
    before_refs, (mine_ref, theirs_ref, *slot_refs) = refs[:before], refs[before:]
    hidden = w_ref.shape[0] // 2
    pairs = zip(load_codes(first_ref), load_codes(second_ref))
    pre, back = [first + second for first, second in pairs]
    gate = gate_ref[:, :1]
    activation, slopes = gelu_pair(pre)
    dpre = (gate * back * slopes).astype(BF16)
    act = gate * activation
    slot = []
    for block in range(0, w_ref.shape[1], hidden):
        span = slice(block, block + hidden)
        slot.append(
            sum(
                lax.dot_general(
                    part, ref[hidden:, span], COLS_BY_COLS, preferred_element_type=F32
                )
                for part, ref in ((dpre[:, :hidden], w_ref), (dpre[:, hidden:], w_other_ref))
            )
        )
    slot_gate = split_value(jnp.sum(activation * back, axis=1, keepdims=True))
    total = jnp.concatenate(slot + [slot_gate], axis=1)
    if len(slot_refs) == 1:
        slot_refs[0][...] = total
    else:
        deal(total, slot_refs)
    rows = dpre.shape[0]
    both = [
        value.reshape(rows // capacity, capacity, 2 * hidden) for value in (dpre.astype(F32), act)
    ]
    both = jnp.concatenate(both, axis=1).reshape(2 * rows, 2 * hidden).astype(BF16)
    mine_ref[...] = both[:, :hidden]
    count = 2 * rows
    for index, ref in enumerate(before_refs):
        theirs_ref[index * count : (index + 1) * count] = ref[...]
    theirs_ref[before * count :] = both[:, hidden:]


def halve_kernel(kept_ref, came_ref, keep_ref, send_ref):
    half = keep_ref.shape[0]
    total = kept_ref[...] + came_ref[...]
    keep_ref[...] = total[:half]
    send_ref[...] = total[half:]


def deal_kernel(kept_ref, came_ref, *refs):
    deal(kept_ref[...] + came_ref[...], refs)


def touch_kernel(out_ref):
    out_ref[...] = jnp.zeros(out_ref.shape, F32)


def sum_kernel(half_nodes, *refs):
    pieces, out_refs = refs[:half_nodes], refs[half_nodes:]
    total = sum([ref[...].astype(F32) for ref in pieces[1:]], pieces[0][...])
    deal(total, out_refs)


def weight_kernel(capacity, *refs):
    held_refs, came_refs, mine_refs, theirs_ref = refs[:2], refs[2:4], refs[4:6], refs[6]
    w_in_hbm, w_out_hbm, written_ref, w_in_ref, w_out_ref, sems = refs[7:]
    feats, hidden = w_in_ref.shape
    worker = on_worker()
    rows = [
        jnp.where(worker, held[:, :feats], came[:, :feats])
        for held, came in zip(held_refs, came_refs)
    ]
    rows = jnp.concatenate(rows, axis=0)
    mine = jnp.concatenate([ref[...] for ref in mine_refs], axis=0)
    both = jnp.where(worker, mine, theirs_ref[...]).astype(F32)
    of_x = lax.broadcasted_iota(jnp.int32, both.shape, 0) % (2 * capacity) < capacity
    dpre = jnp.where(of_x, both, 0.0).astype(BF16)
    act = jnp.where(of_x, 0.0, both).astype(BF16)
    count = feats // PIECES
    copies = []
    for piece in range(PIECES):
        span = slice(piece * count, (piece + 1) * count)
        part = rows[:, span]
        w_in_ref[span] = lax.dot_general(part, dpre, ROWS_BY_ROWS, preferred_element_type=F32)
        w_out_ref[:, span] = lax.dot_general(act, part, ROWS_BY_ROWS, preferred_element_type=F32)
        span = pl.ds(piece * count, count)
        for source, target in (
            (w_in_ref.at[span], w_in_hbm.at[span]),
            (w_out_ref.at[:, span], w_out_hbm.at[:, span]),
        ):
            copy = pltpu.make_async_copy(source, target, sems.at[len(copies)])
            copy.start()
            copies.append(copy)
    for copy in copies:
        copy.wait()
    written_ref[...] = jnp.zeros(written_ref.shape, F32)


def combine_kernel(steps, *refs):
    slot_refs = refs[: 2 * steps]
    place_ref, spread_ref, tokens_ref, gate_out_ref = refs[2 * steps :]
    feats = tokens_ref.shape[1]
    worker = on_worker()
    came = [
        jnp.where(worker, for_worker[...].astype(F32), for_other[...].astype(F32))
        for for_worker, for_other in zip(slot_refs[::2], slot_refs[1::2])
    ]
    own = came[0]
    other = sum(came[2:], came[1])
    capacity = own.shape[0]
    slots = jnp.concatenate([own, other], axis=0)
    grads = slots[:, :feats]
    high = grads.astype(BF16)
    low = (grads - high.astype(F32)).astype(BF16)
    both = jnp.concatenate([high, low], axis=0)
    tokens_ref[...] = jnp.dot(spread_ref[...], both, preferred_element_type=F32).astype(BF16)
    slot_gate = jnp.sum(slots[:, feats:], axis=1, keepdims=True)
    picked = place_ref[: WINDOW * capacity].astype(F32) * slot_gate
    masks = place_ref[WINDOW * capacity :].astype(F32)
    result = jnp.zeros(gate_out_ref.shape, F32)
    for index in range(WINDOW):
        span = slice(index * capacity, (index + 1) * capacity)
        value = jnp.sum(picked[span], axis=0, keepdims=True)
        result = result + masks[2 * index : 2 * index + 2] * value
    gate_out_ref[...] = result


def among_workers(array, step, bit):
    nodes, locals_ = lax.axis_size("node"), lax.axis_size("local")
    pairs = [
        (node * locals_ + local, (node ^ step) * locals_ + (local ^ bit))
        for node in range(nodes)
        for local in range(1, locals_, 2)
    ]
    return lax.ppermute(array, PLANE, pairs)


def to_workers(array):
    size = lax.axis_size(PLANE)
    return lax.ppermute(array, PLANE, [(core, core + 1) for core in range(0, size, 2)])


def from_workers(array, step):
    nodes, locals_ = lax.axis_size("node"), lax.axis_size("local")
    pairs = [
        (node * locals_ + local, (node ^ step) * locals_ + local - 1)
        for node in range(nodes)
        for local in range(1, locals_, 2)
    ]
    return lax.ppermute(array, PLANE, pairs)


def along_edata(array, bit):
    sizes = [lax.axis_size(axis) for axis in PLANE]
    edatas = lax.axis_size("edata")
    pairs = []
    for core in range(1, sizes[0] * sizes[1], 2):
        for place in range(edatas):
            pairs.append((core * edatas + place, core * edatas + (place ^ bit)))
    return lax.ppermute(array, (*PLANE, "edata"), pairs)


def join(pieces, after=()):
    rows, wide = pieces[0].shape
    rows *= len(pieces)
    shape = jax.ShapeDtypeStruct((rows, wide), BF16)
    return call(join_kernel, shape, 0, 4 * rows * wide, after=after)(*pieces)


def body(tokens, grad_out, routes, gates, w_in, w_out):
    nodes = lax.axis_size("node")
    locals_ = lax.axis_size("local")
    edatas = lax.axis_size("edata")
    tok_rows, feats = tokens.shape
    hidden = w_in.shape[1]
    capacity = 2 * tok_rows // EXPERTS
    slots = WINDOW * capacity
    wide = feats + LANES
    coded = 4 * hidden + LANES
    shape = jax.ShapeDtypeStruct
    hbm = pl.BlockSpec(memory_space=pltpu.HBM)
    vmem = pl.BlockSpec(memory_space=pltpu.VMEM)

    inputs = [
        pltpu.with_memory_space_constraint(value, pltpu.HBM)
        for value in (routes.T, gates.T, tokens, grad_out, w_in, w_out)
    ]
    core_rows, place, spread, weights = call(
        gather_kernel,
        (
            pltpu.VMEM((2 * slots, wide), BF16),
            pltpu.VMEM((slots + 16, tok_rows), BF16),
            pltpu.VMEM((tok_rows, 2 * slots), BF16),
            pltpu.VMEM((2 * hidden, feats), BF16),
        ),
        4 * slots * tok_rows * feats,
        4 * tok_rows * feats + 4 * hidden * feats,
        in_specs=[hbm] * 6,
        scratch_shapes=[
            pltpu.VMEM((2, tok_rows), jnp.int32),
            pltpu.VMEM((2, tok_rows), BF16),
            pltpu.VMEM((tok_rows, feats), BF16),
            pltpu.VMEM((tok_rows, feats), BF16),
            pltpu.SemaphoreType.DMA((3 + 2 * PIECES + feats // hidden,)),
        ],
    )(*inputs)

    other_weights = to_workers(weights)
    own_rows, other_rows = call(
        sort_kernel, (shape((2 * slots, wide), BF16),) * 2, 0, 16 * slots * wide
    )(core_rows, to_workers(core_rows))

    half_nodes = nodes // WINDOW
    steps = (list(range(half_nodes)), list(reversed(range(half_nodes, nodes))))
    pieces = [
        [among_workers(source, step, 0) if step else source for step in group]
        for source, group in zip((own_rows, other_rows), steps)
    ]
    rows = half_nodes * locals_ * capacity
    last = ()
    chains = []
    held = []
    for chunk in pieces:
        chunk = join(chunk, last)
        bit = 2
        while bit < locals_:
            chunk = join([chunk, among_workers(chunk, 0, bit)])
            bit *= 2
        held.append(chunk)
        part, gate_rows = call(
            functools.partial(part_kernel, capacity),
            (shape((rows, coded), I16), shape((rows, LANES), F32)),
            16 * rows * feats * hidden,
            4 * rows * feats + 8 * feats * hidden,
            after=last,
        )(chunk, weights, other_weights)
        last = (part,)
        chains.append((part, along_edata(part, 1), gate_rows))
    bit = 2
    while bit < edatas:
        for index, (part, other, gate_rows) in enumerate(chains):
            part = call(
                add_codes_kernel,
                shape((rows, coded), I16),
                16 * rows * hidden,
                6 * rows * coded,
                after=last,
            )(part, other)
            last = (part,)
            chains[index] = (part, along_edata(part, bit), gate_rows)
        bit *= 2

    came = [from_workers(chunk, 0) for chunk in held]
    last += (call(touch_kernel, shape((8, LANES), F32), 0, 0, after=came)(),)
    dealt = (
        [shape((2 * capacity, wide), F32)] * half_nodes,
        [shape((capacity, wide), BF16)] * nodes,
    )
    mine = []
    theirs = ()
    returned = []
    for index, (part, other, gate_rows) in enumerate(chains):
        own, packed, *slot_parts = call(
            functools.partial(slot_kernel, capacity, len(theirs)),
            [
                shape((2 * rows, hidden), BF16),
                shape(((1 + len(theirs)) * 2 * rows, hidden), BF16),
                *(dealt[index] if locals_ == 2 else [shape((rows, wide), F32)]),
            ],
            4 * rows * feats * hidden,
            4 * feats * hidden + 4 * rows * feats,
            after=last,
        )(part, other, gate_rows, weights, other_weights, *theirs)
        last = (own,)
        mine.append(own)
        theirs = (packed,)
        if locals_ > 2:
            half = rows // 2
            keep, send = slot_parts[0][:half], slot_parts[0][half:]
            bit = locals_ // 2
            while bit > 2:
                half //= 2
                keep, send = call(
                    halve_kernel,
                    (shape((half, wide), F32),) * 2,
                    4 * half * wide,
                    24 * half * wide,
                )(keep, among_workers(send, 0, bit))
                bit //= 2
            slot_parts = call(deal_kernel, dealt[index], 4 * half * wide, 12 * half * wide)(
                keep, among_workers(send, 0, bit)
            )
        if index == 0:
            returned.append(
                [
                    among_workers(part, step, 0) if step else part
                    for step, part in zip(steps[index], slot_parts)
                ]
            )
        else:
            pairs = zip(steps[index], slot_parts[::2], slot_parts[1::2])
            returned.append([])
            for step, for_worker, for_other in pairs:
                returned[-1] += [among_workers(for_worker, step, 0), from_workers(for_other, step)]
    theirs = from_workers(theirs[0], 0)
    own_sum, other_sum = call(
        functools.partial(sum_kernel, half_nodes),
        [shape((capacity, wide), BF16)] * 2,
        2 * nodes * capacity * wide,
        8 * nodes * capacity * wide,
        after=(theirs,),
    )(*returned[0])
    other_sum = from_workers(other_sum, 0)
    grad_w_in, grad_w_out, written = call(
        functools.partial(weight_kernel, capacity),
        (shape((feats, hidden), F32), shape((hidden, feats), F32), shape((8, LANES), F32)),
        32 * rows * feats * hidden,
        8 * feats * hidden,
        in_specs=[vmem] * 7,
        out_specs=[hbm, hbm, vmem],
        scratch_shapes=[
            pltpu.VMEM((feats, hidden), F32),
            pltpu.VMEM((hidden, feats), F32),
            pltpu.SemaphoreType.DMA((2 * PIECES,)),
        ],
    )(*held, *came, *mine, theirs)
    grad_tokens, grad_gates = call(
        functools.partial(combine_kernel, half_nodes + 1),
        (shape((tok_rows, feats), BF16), shape((2, tok_rows), F32)),
        4 * slots * tok_rows * feats,
        2 * tok_rows * feats,
        after=(written,),
    )(own_sum, other_sum, *returned[1], place, spread)
    return (grad_tokens, grad_gates.T, grad_w_in, grad_w_out)


def solution(mesh):
    in_specs = (
        P(("node", "local"), "edata"),
        P(("node", "local"), "edata"),
        P(("node", "local"), None),
        P(("node", "local"), None),
        P("edata", ("node", "local")),
        P(("node", "local"), "edata"),
    )
    out_specs = (
        P(("node", "local"), "edata"),
        P(("node", "local"), None),
        P("edata", ("node", "local")),
        P(("node", "local"), "edata"),
    )
    return jax.shard_map(body, mesh=mesh, in_specs=in_specs, out_specs=out_specs, check_vma=False)
```

```python
import functools

import jax
import jax.numpy as jnp
from jax import lax
from jax.experimental import pallas as pl
from jax.experimental.pallas import tpu as pltpu
from jax.sharding import PartitionSpec as P

EXPERTS = 64
WINDOW = 2
LANES = 128
PIECES = 4
PLANE = ("node", "local")
VMEM_LIMIT = 40 * 1024 * 1024

BF16 = jnp.bfloat16
F32 = jnp.float32
I16 = jnp.int16
ROWS_BY_ROWS = (((0,), (0,)), ((), ()))
COLS_BY_COLS = (((1,), (1,)), ((), ()))


def gelu_pair(pre_act):
    coefficient = 0.7978845608028654
    square = pre_act * pre_act
    tanh_val = jnp.tanh(coefficient * (pre_act + 0.044715 * pre_act * square))
    half = 0.5 * (1.0 + tanh_val)
    activation = pre_act * half
    slopes = half + 0.5 * pre_act * (1.0 - tanh_val * tanh_val) * coefficient * (
        1.0 + 3.0 * 0.044715 * square
    )
    return (activation, slopes)


def call(kernel, out_shape, flops, moved, limit=VMEM_LIMIT, in_specs=None, after=(), **more):
    def run(*operands):
        given = in_specs or [pl.BlockSpec(memory_space=pltpu.VMEM)] * len(operands)
        return pl.pallas_call(
            lambda *refs: kernel(*refs[len(after) :]),
            out_shape=out_shape,
            in_specs=[pl.BlockSpec(memory_space=pl.ANY)] * len(after) + list(given),
            compiler_params=pltpu.CompilerParams(vmem_limit_bytes=limit),
            cost_estimate=pl.CostEstimate(flops=flops, bytes_accessed=moved, transcendentals=0),
            **more,
        )(*after, *operands)

    return run


def own_expert():
    half_nodes = lax.axis_size("node") // WINDOW
    return lax.axis_index("node") // half_nodes


def on_worker():
    return lax.axis_index("local") % 2 == 1


def split_value(value):
    high = value.astype(BF16).astype(F32)
    lane = lax.broadcasted_iota(jnp.int32, (value.shape[0], LANES), 1)
    return jnp.where(lane == 0, high, jnp.where(lane == 1, value - high, 0.0))


def encode(values):
    top = jnp.max(jnp.abs(values), axis=1, keepdims=True)
    power = jnp.ceil(jnp.log2(jnp.maximum(top, 1e-30)))
    codes = jnp.round(values * (1.999 * jnp.exp2(14.0 - power)))
    return codes.astype(jnp.int32).astype(I16), power


def decode(codes, power):
    return codes.astype(jnp.int32).astype(F32) * (jnp.exp2(power - 14.0) / 1.999)


def store_codes(out_ref, pair):
    hidden = pair[0].shape[1]
    lane = lax.broadcasted_iota(jnp.int32, (pair[0].shape[0], LANES), 1)
    powers = []
    for index, values in enumerate(pair):
        codes, power = encode(values)
        out_ref[:, index * hidden : (index + 1) * hidden] = codes
        powers.append(power)
    powers = jnp.where(lane == 0, powers[0], powers[1])
    out_ref[:, 2 * hidden :] = powers.astype(jnp.int32).astype(I16)


def load_codes(ref):
    hidden = (ref.shape[1] - LANES) // 2
    powers = ref[:, 2 * hidden :].astype(jnp.int32).astype(F32)
    return [
        decode(ref[:, index * hidden : (index + 1) * hidden], powers[:, index : index + 1])
        for index in range(2)
    ]


def gather_kernel(routes_hbm, gates_hbm, tokens_hbm, grads_hbm, w_in_hbm, w_out_hbm, rows_ref,
                  place_ref, spread_ref, w_ref, routes_ref, gates_ref, tokens_ref,
                  grads_ref, sems):
    tok_rows, feats = tokens_ref.shape
    slots = rows_ref.shape[0] // 2
    capacity = slots // WINDOW
    copies = [
        pltpu.make_async_copy(routes_hbm, routes_ref, sems.at[0]),
        pltpu.make_async_copy(gates_hbm, gates_ref, sems.at[1]),
    ]
    count = tok_rows // PIECES
    for source, target in ((tokens_hbm, tokens_ref), (grads_hbm, grads_ref)):
        for piece in range(PIECES):
            span = pl.ds(piece * count, count)
            copies.append(
                pltpu.make_async_copy(source.at[span], target.at[span], sems.at[len(copies)])
            )
    hidden = w_out_hbm.shape[0]
    upper, lower = pl.ds(0, hidden), pl.ds(hidden, hidden)
    moves = [(w_out_hbm, w_ref.at[upper])]
    for block in range(0, feats, hidden):
        span = pl.ds(block, hidden)
        moves.append((w_in_hbm.at[span], w_ref.at[lower, span]))
    for source, target in moves:
        copies.append(pltpu.make_async_copy(source, target, sems.at[len(copies)]))
    for copy in copies:
        copy.start()
    earlier = lax.broadcasted_iota(jnp.int32, (tok_rows, tok_rows), 0) < lax.broadcasted_iota(
        jnp.int32, (tok_rows, tok_rows), 1
    )
    earlier = earlier.astype(F32).astype(BF16)
    slot_of = lax.broadcasted_iota(jnp.int32, (capacity, tok_rows), 0).astype(F32)
    row_of = lax.broadcasted_iota(jnp.int32, (8, tok_rows), 0)
    own = own_expert()
    copies[0].wait()
    copies[1].wait()
    routes = routes_ref[...]
    gates = gates_ref[...].astype(F32)
    hits = [(routes == expert).astype(F32) for expert in (own, 1 - own)]
    named = [hit[0:1] + hit[1:2] for hit in hits]
    weight = [hit * gates for hit in hits]
    weight = [value[0:1] + value[1:2] for value in weight]
    names = jnp.where(row_of == 0, named[0], jnp.where(row_of == 1, named[1], 0.0)).astype(BF16)
    before = jnp.dot(names, earlier, preferred_element_type=F32)
    parts = [jnp.where(before[e : e + 1] == slot_of, named[e], 0.0) for e in range(WINDOW)]
    place = jnp.concatenate(parts, axis=0).astype(BF16)
    place_ref[:slots] = place
    spread_ref[...] = jnp.concatenate(parts + parts, axis=0).T.astype(BF16)
    masks = jnp.zeros((16, tok_rows), F32)
    row_of = lax.broadcasted_iota(jnp.int32, masks.shape, 0)
    for index, hit in enumerate(hits):
        for k in range(2):
            masks = jnp.where(row_of == 2 * index + k, hit[k : k + 1], masks)
    place_ref[slots:] = masks.astype(BF16)
    for copy in copies[2 : 2 + PIECES]:
        copy.wait()
    rows_x = jnp.dot(place, tokens_ref[...], preferred_element_type=F32)
    for copy in copies[2 + PIECES : 2 + 2 * PIECES]:
        copy.wait()
    rows_dy = jnp.dot(place, grads_ref[...], preferred_element_type=F32)
    chunks = []
    gates = []
    for expert in range(WINDOW):
        span = slice(expert * capacity, (expert + 1) * capacity)
        chunks += [rows_x[span], rows_dy[span]]
        gates += [jnp.sum(parts[expert] * weight[expert], axis=1, keepdims=True)] * 2
    rows_ref[:, :feats] = jnp.concatenate(chunks, axis=0).astype(BF16)
    gates = jnp.broadcast_to(jnp.concatenate(gates, axis=0), (2 * slots, LANES))
    rows_ref[:, feats:] = gates.astype(BF16)
    for copy in copies[2 + 2 * PIECES :]:
        copy.wait()


def sort_kernel(first_ref, second_ref, own_ref, other_ref):
    half = first_ref.shape[0] // WINDOW
    for index, ref in enumerate((first_ref, second_ref)):
        span = slice(index * half, (index + 1) * half)
        own_ref[span] = ref[:half]
        other_ref[span] = ref[half:]


def join_kernel(*refs):
    *pieces, out_ref = refs
    rows = pieces[0].shape[0]
    for index, ref in enumerate(pieces):
        out_ref[index * rows : (index + 1) * rows] = ref[...]


def part_kernel(capacity, rows_ref, w_ref, w_other_ref, part_ref, gate_ref):
    feats = w_ref.shape[1]
    hidden = w_ref.shape[0] // 2
    groups = rows_ref.shape[0] // (2 * capacity)
    gate = rows_ref[:, feats:].astype(F32).reshape(groups, 2 * capacity, LANES)
    gate_ref[...] = gate[:, :capacity].reshape(groups * capacity, LANES)
    rows = rows_ref[:, :feats]
    pre = []
    back = []
    for ref in (w_ref, w_other_ref):
        pre.append(
            sum(
                jnp.dot(
                    rows[:, block : block + hidden],
                    ref[hidden:, block : block + hidden],
                    preferred_element_type=F32,
                )
                for block in range(0, feats, hidden)
            )
        )
        back.append(
            lax.dot_general(rows, ref[:hidden], COLS_BY_COLS, preferred_element_type=F32)
        )
    pair = []
    for values, span in ((pre, slice(0, capacity)), (back, slice(capacity, 2 * capacity))):
        values = jnp.concatenate(values, axis=1).reshape(groups, 2 * capacity, 2 * hidden)
        pair.append(values[:, span].reshape(groups * capacity, 2 * hidden))
    store_codes(part_ref, pair)


def add_codes_kernel(first_ref, second_ref, out_ref):
    pairs = zip(load_codes(first_ref), load_codes(second_ref))
    store_codes(out_ref, [first + second for first, second in pairs])


def deal(total, refs):
    each, wide = refs[0].shape
    feats = wide - LANES
    gate = split_value(jnp.sum(total[:, feats:], axis=1, keepdims=True))
    for index, ref in enumerate(refs):
        span = slice(index * each, (index + 1) * each)
        ref[:, :feats] = total[span, :feats].astype(ref.dtype)
        ref[:, feats:] = gate[span].astype(ref.dtype)


def slot_kernel(capacity, before, first_ref, second_ref, gate_ref, w_ref, w_other_ref, *refs):
    before_refs, (mine_ref, theirs_ref, *slot_refs) = refs[:before], refs[before:]
    hidden = w_ref.shape[0] // 2
    pairs = zip(load_codes(first_ref), load_codes(second_ref))
    pre, back = [first + second for first, second in pairs]
    gate = gate_ref[:, :1]
    activation, slopes = gelu_pair(pre)
    dpre = (gate * back * slopes).astype(BF16)
    act = gate * activation
    slot = []
    for block in range(0, w_ref.shape[1], hidden):
        span = slice(block, block + hidden)
        slot.append(
            sum(
                lax.dot_general(
                    part, ref[hidden:, span], COLS_BY_COLS, preferred_element_type=F32
                )
                for part, ref in ((dpre[:, :hidden], w_ref), (dpre[:, hidden:], w_other_ref))
            )
        )
    slot_gate = split_value(jnp.sum(activation * back, axis=1, keepdims=True))
    total = jnp.concatenate(slot + [slot_gate], axis=1)
    if len(slot_refs) == 1:
        slot_refs[0][...] = total
    else:
        deal(total, slot_refs)
    rows = dpre.shape[0]
    both = [
        value.reshape(rows // capacity, capacity, 2 * hidden) for value in (dpre.astype(F32), act)
    ]
    both = jnp.concatenate(both, axis=1).reshape(2 * rows, 2 * hidden).astype(BF16)
    mine_ref[...] = both[:, :hidden]
    count = 2 * rows
    for index, ref in enumerate(before_refs):
        theirs_ref[index * count : (index + 1) * count] = ref[...]
    theirs_ref[before * count :] = both[:, hidden:]


def halve_kernel(kept_ref, came_ref, keep_ref, send_ref):
    half = keep_ref.shape[0]
    total = kept_ref[...] + came_ref[...]
    keep_ref[...] = total[:half]
    send_ref[...] = total[half:]


def deal_kernel(kept_ref, came_ref, *refs):
    deal(kept_ref[...] + came_ref[...], refs)


def touch_kernel(out_ref):
    out_ref[...] = jnp.zeros(out_ref.shape, F32)


def sum_kernel(half_nodes, *refs):
    pieces, out_refs = refs[:half_nodes], refs[half_nodes:]
    total = sum([ref[...].astype(F32) for ref in pieces[1:]], pieces[0][...])
    deal(total, out_refs)


def weight_kernel(capacity, *refs):
    held_refs, came_refs, mine_refs, theirs_ref = refs[:2], refs[2:4], refs[4:6], refs[6]
    w_in_hbm, w_out_hbm, written_ref, w_in_ref, w_out_ref, sems = refs[7:]
    feats, hidden = w_in_ref.shape
    worker = on_worker()
    rows = [
        jnp.where(worker, held[:, :feats], came[:, :feats])
        for held, came in zip(held_refs, came_refs)
    ]
    rows = jnp.concatenate(rows, axis=0)
    mine = jnp.concatenate([ref[...] for ref in mine_refs], axis=0)
    both = jnp.where(worker, mine, theirs_ref[...]).astype(F32)
    of_x = lax.broadcasted_iota(jnp.int32, both.shape, 0) % (2 * capacity) < capacity
    dpre = jnp.where(of_x, both, 0.0).astype(BF16)
    act = jnp.where(of_x, 0.0, both).astype(BF16)
    count = feats // PIECES
    copies = []
    for piece in range(PIECES):
        span = slice(piece * count, (piece + 1) * count)
        part = rows[:, span]
        w_in_ref[span] = lax.dot_general(part, dpre, ROWS_BY_ROWS, preferred_element_type=F32)
        w_out_ref[:, span] = lax.dot_general(act, part, ROWS_BY_ROWS, preferred_element_type=F32)
        span = pl.ds(piece * count, count)
        for source, target in (
            (w_in_ref.at[span], w_in_hbm.at[span]),
            (w_out_ref.at[:, span], w_out_hbm.at[:, span]),
        ):
            copy = pltpu.make_async_copy(source, target, sems.at[len(copies)])
            copy.start()
            copies.append(copy)
    for copy in copies:
        copy.wait()
    written_ref[...] = jnp.zeros(written_ref.shape, F32)


def combine_kernel(steps, *refs):
    slot_refs = refs[: 2 * steps]
    place_ref, spread_ref, tokens_ref, gate_out_ref = refs[2 * steps :]
    feats = tokens_ref.shape[1]
    worker = on_worker()
    came = [
        jnp.where(worker, for_worker[...].astype(F32), for_other[...].astype(F32))
        for for_worker, for_other in zip(slot_refs[::2], slot_refs[1::2])
    ]
    own = came[0]
    other = sum(came[2:], came[1])
    capacity = own.shape[0]
    slots = jnp.concatenate([own, other], axis=0)
    grads = slots[:, :feats]
    high = grads.astype(BF16)
    low = (grads - high.astype(F32)).astype(BF16)
    both = jnp.concatenate([high, low], axis=0)
    tokens_ref[...] = jnp.dot(spread_ref[...], both, preferred_element_type=F32).astype(BF16)
    slot_gate = jnp.sum(slots[:, feats:], axis=1, keepdims=True)
    picked = place_ref[: WINDOW * capacity].astype(F32) * slot_gate
    masks = place_ref[WINDOW * capacity :].astype(F32)
    result = jnp.zeros(gate_out_ref.shape, F32)
    for index in range(WINDOW):
        span = slice(index * capacity, (index + 1) * capacity)
        value = jnp.sum(picked[span], axis=0, keepdims=True)
        result = result + masks[2 * index : 2 * index + 2] * value
    gate_out_ref[...] = result


def among_workers(array, step, bit):
    locals_ = lax.axis_size("local")
    pairs = []
    for core in range(lax.axis_size(PLANE)):
        pairs.append((core, core ^ (step * locals_ + bit) if core % 2 else core))
    return lax.ppermute(array, PLANE, pairs)


def to_workers(array):
    size = lax.axis_size(PLANE)
    return lax.ppermute(array, PLANE, [(core, core ^ 1) for core in range(size)])


def from_workers(array, step):
    other = step * lax.axis_size("local") + 1
    size = lax.axis_size(PLANE)
    return lax.ppermute(array, PLANE, [(core, core ^ other) for core in range(size)])


def along_edata(array, bit):
    edatas = lax.axis_size("edata")
    pairs = []
    for device in range(lax.axis_size((*PLANE, "edata"))):
        pairs.append((device, device ^ bit if device // edatas % 2 else device))
    return lax.ppermute(array, (*PLANE, "edata"), pairs)


def join(pieces, after=()):
    rows, wide = pieces[0].shape
    rows *= len(pieces)
    shape = jax.ShapeDtypeStruct((rows, wide), BF16)
    return call(join_kernel, shape, 0, 4 * rows * wide, after=after)(*pieces)


def body(tokens, grad_out, routes, gates, w_in, w_out):
    nodes = lax.axis_size("node")
    locals_ = lax.axis_size("local")
    edatas = lax.axis_size("edata")
    tok_rows, feats = tokens.shape
    hidden = w_in.shape[1]
    capacity = 2 * tok_rows // EXPERTS
    slots = WINDOW * capacity
    wide = feats + LANES
    coded = 4 * hidden + LANES
    shape = jax.ShapeDtypeStruct
    hbm = pl.BlockSpec(memory_space=pltpu.HBM)
    vmem = pl.BlockSpec(memory_space=pltpu.VMEM)

    inputs = [
        pltpu.with_memory_space_constraint(value, pltpu.HBM)
        for value in (routes.T, gates.T, tokens, grad_out, w_in, w_out)
    ]
    core_rows, place, spread, weights = call(
        gather_kernel,
        (
            pltpu.VMEM((2 * slots, wide), BF16),
            pltpu.VMEM((slots + 16, tok_rows), BF16),
            pltpu.VMEM((tok_rows, 2 * slots), BF16),
            pltpu.VMEM((2 * hidden, feats), BF16),
        ),
        4 * slots * tok_rows * feats,
        4 * tok_rows * feats + 4 * hidden * feats,
        in_specs=[hbm] * 6,
        scratch_shapes=[
            pltpu.VMEM((2, tok_rows), jnp.int32),
            pltpu.VMEM((2, tok_rows), BF16),
            pltpu.VMEM((tok_rows, feats), BF16),
            pltpu.VMEM((tok_rows, feats), BF16),
            pltpu.SemaphoreType.DMA((3 + 2 * PIECES + feats // hidden,)),
        ],
    )(*inputs)

    other_weights = to_workers(weights)
    own_rows, other_rows = call(
        sort_kernel, (shape((2 * slots, wide), BF16),) * 2, 0, 16 * slots * wide
    )(core_rows, to_workers(core_rows))

    half_nodes = nodes // WINDOW
    steps = (list(range(half_nodes)), list(reversed(range(half_nodes, nodes))))
    pieces = [
        [among_workers(source, step, 0) if step else source for step in group]
        for source, group in zip((own_rows, other_rows), steps)
    ]
    rows = half_nodes * locals_ * capacity
    last = ()
    chains = []
    held = []
    for chunk in pieces:
        chunk = join(chunk, last)
        bit = 2
        while bit < locals_:
            chunk = join([chunk, among_workers(chunk, 0, bit)])
            bit *= 2
        held.append(chunk)
        part, gate_rows = call(
            functools.partial(part_kernel, capacity),
            (shape((rows, coded), I16), shape((rows, LANES), F32)),
            16 * rows * feats * hidden,
            4 * rows * feats + 8 * feats * hidden,
            after=last,
        )(chunk, weights, other_weights)
        last = (part,)
        chains.append((part, along_edata(part, 1), gate_rows))
    bit = 2
    while bit < edatas:
        for index, (part, other, gate_rows) in enumerate(chains):
            part = call(
                add_codes_kernel,
                shape((rows, coded), I16),
                16 * rows * hidden,
                6 * rows * coded,
                after=last,
            )(part, other)
            last = (part,)
            chains[index] = (part, along_edata(part, bit), gate_rows)
        bit *= 2

    came = [from_workers(chunk, 0) for chunk in held]
    last += (call(touch_kernel, shape((8, LANES), F32), 0, 0, after=came)(),)
    dealt = (
        [shape((2 * capacity, wide), F32)] * half_nodes,
        [shape((capacity, wide), BF16)] * nodes,
    )
    mine = []
    theirs = ()
    returned = []
    for index, (part, other, gate_rows) in enumerate(chains):
        own, packed, *slot_parts = call(
            functools.partial(slot_kernel, capacity, len(theirs)),
            [
                shape((2 * rows, hidden), BF16),
                shape(((1 + len(theirs)) * 2 * rows, hidden), BF16),
                *(dealt[index] if locals_ == 2 else [shape((rows, wide), F32)]),
            ],
            4 * rows * feats * hidden,
            4 * feats * hidden + 4 * rows * feats,
            after=last,
        )(part, other, gate_rows, weights, other_weights, *theirs)
        last = (own,)
        mine.append(own)
        theirs = (packed,)
        if locals_ > 2:
            half = rows // 2
            keep, send = slot_parts[0][:half], slot_parts[0][half:]
            bit = locals_ // 2
            while bit > 2:
                half //= 2
                keep, send = call(
                    halve_kernel,
                    (shape((half, wide), F32),) * 2,
                    4 * half * wide,
                    24 * half * wide,
                )(keep, among_workers(send, 0, bit))
                bit //= 2
            slot_parts = call(deal_kernel, dealt[index], 4 * half * wide, 12 * half * wide)(
                keep, among_workers(send, 0, bit)
            )
        if index == 0:
            returned.append(
                [
                    among_workers(part, step, 0) if step else part
                    for step, part in zip(steps[index], slot_parts)
                ]
            )
        else:
            pairs = zip(steps[index], slot_parts[::2], slot_parts[1::2])
            returned.append([])
            for step, for_worker, for_other in pairs:
                returned[-1] += [among_workers(for_worker, step, 0), from_workers(for_other, step)]
    theirs = from_workers(theirs[0], 0)
    own_sum, other_sum = call(
        functools.partial(sum_kernel, half_nodes),
        [shape((capacity, wide), BF16)] * 2,
        2 * nodes * capacity * wide,
        8 * nodes * capacity * wide,
        after=(theirs,),
    )(*returned[0])
    other_sum = from_workers(other_sum, 0)
    grad_w_in, grad_w_out, written = call(
        functools.partial(weight_kernel, capacity),
        (shape((feats, hidden), F32), shape((hidden, feats), F32), shape((8, LANES), F32)),
        32 * rows * feats * hidden,
        8 * feats * hidden,
        in_specs=[vmem] * 7,
        out_specs=[hbm, hbm, vmem],
        scratch_shapes=[
            pltpu.VMEM((feats, hidden), F32),
            pltpu.VMEM((hidden, feats), F32),
            pltpu.SemaphoreType.DMA((2 * PIECES,)),
        ],
    )(*held, *came, *mine, theirs)
    grad_tokens, grad_gates = call(
        functools.partial(combine_kernel, half_nodes + 1),
        (shape((tok_rows, feats), BF16), shape((2, tok_rows), F32)),
        4 * slots * tok_rows * feats,
        2 * tok_rows * feats,
        after=(written,),
    )(own_sum, other_sum, *returned[1], place, spread)
    return (grad_tokens, grad_gates.T, grad_w_in, grad_w_out)


def solution(mesh):
    in_specs = (
        P(("node", "local"), "edata"),
        P(("node", "local"), "edata"),
        P(("node", "local"), None),
        P(("node", "local"), None),
        P("edata", ("node", "local")),
        P(("node", "local"), "edata"),
    )
    out_specs = (
        P(("node", "local"), "edata"),
        P(("node", "local"), None),
        P("edata", ("node", "local")),
        P(("node", "local"), "edata"),
    )
    return jax.shard_map(body, mesh=mesh, in_specs=in_specs, out_specs=out_specs, check_vma=False)
```

```python
import functools

import jax
import jax.numpy as jnp
from jax import lax
from jax.experimental import pallas as pl
from jax.experimental.pallas import tpu as pltpu
from jax.sharding import PartitionSpec as P

EXPERTS = 64
WINDOW = 2
LANES = 128
PIECES = 4
VMEM_LIMIT = 40 * 1024 * 1024

BF16 = jnp.bfloat16
F32 = jnp.float32
I16 = jnp.int16
ROWS_BY_ROWS = (((0,), (0,)), ((), ()))
COLS_BY_COLS = (((1,), (1,)), ((), ()))


def gelu_pair(pre_act):
    coefficient = 0.7978845608028654
    square = pre_act * pre_act
    tanh_val = jnp.tanh(coefficient * (pre_act + 0.044715 * pre_act * square))
    half = 0.5 * (1.0 + tanh_val)
    activation = pre_act * half
    slopes = half + 0.5 * pre_act * (1.0 - tanh_val * tanh_val) * coefficient * (
        1.0 + 3.0 * 0.044715 * square
    )
    return (activation, slopes)


def call(kernel, out_shape, flops, moved, limit=VMEM_LIMIT, in_specs=None, after=(), **more):
    def run(*operands):
        given = in_specs or [pl.BlockSpec(memory_space=pltpu.VMEM)] * len(operands)
        return pl.pallas_call(
            lambda *refs: kernel(*refs[len(after) :]),
            out_shape=out_shape,
            in_specs=[pl.BlockSpec(memory_space=pl.ANY)] * len(after) + list(given),
            compiler_params=pltpu.CompilerParams(vmem_limit_bytes=limit),
            cost_estimate=pl.CostEstimate(flops=flops, bytes_accessed=moved, transcendentals=0),
            **more,
        )(*after, *operands)

    return run


def own_expert():
    half_nodes = lax.axis_size("node") // WINDOW
    return lax.axis_index("node") // half_nodes


def split_value(value):
    high = value.astype(BF16).astype(F32)
    lane = lax.broadcasted_iota(jnp.int32, (value.shape[0], LANES), 1)
    return jnp.where(lane == 0, high, jnp.where(lane == 1, value - high, 0.0))


def encode(values):
    top = jnp.max(jnp.abs(values), axis=1, keepdims=True)
    power = jnp.ceil(jnp.log2(jnp.maximum(top, 1e-30)))
    codes = jnp.round(values * (1.999 * jnp.exp2(14.0 - power)))
    return codes.astype(jnp.int32).astype(I16), power


def decode(codes, power):
    return codes.astype(jnp.int32).astype(F32) * (jnp.exp2(power - 14.0) / 1.999)


def store_codes(out_ref, pair):
    hidden = pair[0].shape[1]
    lane = lax.broadcasted_iota(jnp.int32, (pair[0].shape[0], LANES), 1)
    powers = []
    for index, values in enumerate(pair):
        codes, power = encode(values)
        out_ref[:, index * hidden : (index + 1) * hidden] = codes
        powers.append(power)
    powers = jnp.where(lane == 0, powers[0], powers[1])
    out_ref[:, 2 * hidden :] = powers.astype(jnp.int32).astype(I16)


def load_codes(ref):
    hidden = (ref.shape[1] - LANES) // 2
    powers = ref[:, 2 * hidden :].astype(jnp.int32).astype(F32)
    return [
        decode(ref[:, index * hidden : (index + 1) * hidden], powers[:, index : index + 1])
        for index in range(2)
    ]


def gather_kernel(routes_hbm, gates_hbm, tokens_hbm, grads_hbm, w_in_hbm, w_out_hbm, own_ref,
                  other_ref, place_ref, spread_ref, w_ref, routes_ref, gates_ref, tokens_ref,
                  grads_ref, sems):
    tok_rows, feats = tokens_ref.shape
    capacity = own_ref.shape[0] // 2
    slots = WINDOW * capacity
    copies = [
        pltpu.make_async_copy(routes_hbm, routes_ref, sems.at[0]),
        pltpu.make_async_copy(gates_hbm, gates_ref, sems.at[1]),
    ]
    count = tok_rows // PIECES
    for source, target in ((tokens_hbm, tokens_ref), (grads_hbm, grads_ref)):
        for piece in range(PIECES):
            span = pl.ds(piece * count, count)
            copies.append(
                pltpu.make_async_copy(source.at[span], target.at[span], sems.at[len(copies)])
            )
    hidden = w_out_hbm.shape[0]
    upper, lower = pl.ds(0, hidden), pl.ds(hidden, hidden)
    moves = [(w_out_hbm, w_ref.at[upper])]
    for block in range(0, feats, hidden):
        span = pl.ds(block, hidden)
        moves.append((w_in_hbm.at[span], w_ref.at[lower, span]))
    for source, target in moves:
        copies.append(pltpu.make_async_copy(source, target, sems.at[len(copies)]))
    for copy in copies:
        copy.start()
    earlier = lax.broadcasted_iota(jnp.int32, (tok_rows, tok_rows), 0) < lax.broadcasted_iota(
        jnp.int32, (tok_rows, tok_rows), 1
    )
    earlier = earlier.astype(F32).astype(BF16)
    slot_of = lax.broadcasted_iota(jnp.int32, (capacity, tok_rows), 0).astype(F32)
    row_of = lax.broadcasted_iota(jnp.int32, (8, tok_rows), 0)
    own = own_expert()
    copies[0].wait()
    copies[1].wait()
    routes = routes_ref[...]
    gates = gates_ref[...].astype(F32)
    hits = [(routes == expert).astype(F32) for expert in (own, 1 - own)]
    named = [hit[0:1] + hit[1:2] for hit in hits]
    weight = [hit * gates for hit in hits]
    weight = [value[0:1] + value[1:2] for value in weight]
    names = jnp.where(row_of == 0, named[0], jnp.where(row_of == 1, named[1], 0.0)).astype(BF16)
    before = jnp.dot(names, earlier, preferred_element_type=F32)
    parts = [jnp.where(before[e : e + 1] == slot_of, named[e], 0.0) for e in range(WINDOW)]
    place = jnp.concatenate(parts, axis=0).astype(BF16)
    place_ref[:slots] = place
    spread_ref[...] = jnp.concatenate(parts + parts, axis=0).T.astype(BF16)
    masks = jnp.zeros((16, tok_rows), F32)
    row_of = lax.broadcasted_iota(jnp.int32, masks.shape, 0)
    for index, hit in enumerate(hits):
        for k in range(2):
            masks = jnp.where(row_of == 2 * index + k, hit[k : k + 1], masks)
    place_ref[slots:] = masks.astype(BF16)
    for copy in copies[2 : 2 + PIECES]:
        copy.wait()
    rows_x = jnp.dot(place, tokens_ref[...], preferred_element_type=F32)
    for copy in copies[2 + PIECES : 2 + 2 * PIECES]:
        copy.wait()
    rows_dy = jnp.dot(place, grads_ref[...], preferred_element_type=F32)
    for expert, out_ref in ((0, own_ref), (1, other_ref)):
        span = slice(expert * capacity, (expert + 1) * capacity)
        out_ref[:, :feats] = jnp.concatenate([rows_x[span], rows_dy[span]], axis=0).astype(BF16)
        gate = jnp.sum(parts[expert] * weight[expert], axis=1, keepdims=True)
        gate = jnp.concatenate([gate, gate], axis=0)
        out_ref[:, feats:] = jnp.broadcast_to(gate, (2 * capacity, LANES)).astype(BF16)
    for copy in copies[2 + 2 * PIECES :]:
        copy.wait()


def join_kernel(*refs):
    *pieces, out_ref = refs
    rows = pieces[0].shape[0]
    for index, ref in enumerate(pieces):
        out_ref[index * rows : (index + 1) * rows] = ref[...]


def part_kernel(capacity, rows_ref, w_ref, w_other_ref, part_ref, gate_ref):
    feats = w_ref.shape[1]
    hidden = w_ref.shape[0] // 2
    groups = rows_ref.shape[0] // (2 * capacity)
    gate = rows_ref[:, feats:].astype(F32).reshape(groups, 2 * capacity, LANES)
    gate_ref[...] = gate[:, :capacity].reshape(groups * capacity, LANES)
    rows = rows_ref[:, :feats]
    pre = []
    back = []
    for ref in (w_ref, w_other_ref):
        pre.append(
            sum(
                jnp.dot(
                    rows[:, block : block + hidden],
                    ref[hidden:, block : block + hidden],
                    preferred_element_type=F32,
                )
                for block in range(0, feats, hidden)
            )
        )
        back.append(
            lax.dot_general(rows, ref[:hidden], COLS_BY_COLS, preferred_element_type=F32)
        )
    pair = []
    for values, span in ((pre, slice(0, capacity)), (back, slice(capacity, 2 * capacity))):
        values = jnp.concatenate(values, axis=1).reshape(groups, 2 * capacity, 2 * hidden)
        pair.append(values[:, span].reshape(groups * capacity, 2 * hidden))
    store_codes(part_ref, pair)


def add_codes_kernel(first_ref, second_ref, out_ref):
    pairs = zip(load_codes(first_ref), load_codes(second_ref))
    store_codes(out_ref, [first + second for first, second in pairs])


def deal(total, refs):
    each, wide = refs[0].shape
    feats = wide - LANES
    gate = split_value(jnp.sum(total[:, feats:], axis=1, keepdims=True))
    for index, ref in enumerate(refs):
        span = slice(index * each, (index + 1) * each)
        ref[:, :feats] = total[span, :feats].astype(ref.dtype)
        ref[:, feats:] = gate[span].astype(ref.dtype)


def slot_kernel(capacity, before, first_ref, second_ref, gate_ref, w_ref, w_other_ref, *refs):
    before_refs, (mine_ref, theirs_ref, *slot_refs) = refs[:before], refs[before:]
    hidden = w_ref.shape[0] // 2
    pairs = zip(load_codes(first_ref), load_codes(second_ref))
    pre, back = [first + second for first, second in pairs]
    gate = gate_ref[:, :1]
    activation, slopes = gelu_pair(pre)
    dpre = (gate * back * slopes).astype(BF16)
    act = gate * activation
    slot = []
    for block in range(0, w_ref.shape[1], hidden):
        span = slice(block, block + hidden)
        slot.append(
            sum(
                lax.dot_general(
                    part, ref[hidden:, span], COLS_BY_COLS, preferred_element_type=F32
                )
                for part, ref in ((dpre[:, :hidden], w_ref), (dpre[:, hidden:], w_other_ref))
            )
        )
    slot_gate = split_value(jnp.sum(activation * back, axis=1, keepdims=True))
    total = jnp.concatenate(slot + [slot_gate], axis=1)
    if len(slot_refs) == 1:
        slot_refs[0][...] = total
    else:
        deal(total, slot_refs)
    rows = dpre.shape[0]
    both = [
        value.reshape(rows // capacity, capacity, 2 * hidden) for value in (dpre.astype(F32), act)
    ]
    both = jnp.concatenate(both, axis=1).reshape(2 * rows, 2 * hidden).astype(BF16)
    mine_ref[...] = both[:, :hidden]
    count = 2 * rows
    for index, ref in enumerate(before_refs):
        theirs_ref[index * count : (index + 1) * count] = ref[...]
    theirs_ref[before * count :] = both[:, hidden:]


def halve_kernel(kept_ref, came_ref, keep_ref, send_ref):
    half = keep_ref.shape[0]
    total = kept_ref[...] + came_ref[...]
    keep_ref[...] = total[:half]
    send_ref[...] = total[half:]


def deal_kernel(kept_ref, came_ref, *refs):
    deal(kept_ref[...] + came_ref[...], refs)


def weight_kernel(capacity, *refs):
    rows_refs, both_refs = refs[:4], refs[4:7]
    w_in_hbm, w_out_hbm, written_ref, w_in_ref, w_out_ref, sems = refs[7:]
    feats, hidden = w_in_ref.shape
    rows = jnp.concatenate([ref[:, :feats] for ref in rows_refs], axis=0)
    both = jnp.concatenate([ref[...] for ref in both_refs], axis=0).astype(F32)
    of_x = lax.broadcasted_iota(jnp.int32, both.shape, 0) % (2 * capacity) < capacity
    dpre = jnp.where(of_x, both, 0.0).astype(BF16)
    act = jnp.where(of_x, 0.0, both).astype(BF16)
    count = feats // PIECES
    copies = []
    for piece in range(PIECES):
        span = slice(piece * count, (piece + 1) * count)
        part = rows[:, span]
        w_in_ref[span] = lax.dot_general(part, dpre, ROWS_BY_ROWS, preferred_element_type=F32)
        w_out_ref[:, span] = lax.dot_general(act, part, ROWS_BY_ROWS, preferred_element_type=F32)
        span = pl.ds(piece * count, count)
        for source, target in (
            (w_in_ref.at[span], w_in_hbm.at[span]),
            (w_out_ref.at[:, span], w_out_hbm.at[:, span]),
        ):
            copy = pltpu.make_async_copy(source, target, sems.at[len(copies)])
            copy.start()
            copies.append(copy)
    for copy in copies:
        copy.wait()
    written_ref[...] = jnp.zeros(written_ref.shape, F32)


def combine_kernel(steps, *refs):
    kept_ref, came_refs = refs[0], refs[1:steps]
    place_ref, spread_ref, tokens_ref, gate_out_ref = refs[steps:]
    feats = tokens_ref.shape[1]
    capacity = kept_ref.shape[0]
    came = [ref[...].astype(F32) for ref in came_refs]
    half = steps // WINDOW
    own = sum(came[: half - 1], kept_ref[...])
    other = sum(came[half:], came[half - 1])
    slots = jnp.concatenate([own, other], axis=0)
    grads = slots[:, :feats]
    high = grads.astype(BF16)
    low = (grads - high.astype(F32)).astype(BF16)
    both = jnp.concatenate([high, low], axis=0)
    tokens_ref[...] = jnp.dot(spread_ref[...], both, preferred_element_type=F32).astype(BF16)
    slot_gate = jnp.sum(slots[:, feats:], axis=1, keepdims=True)
    picked = place_ref[: WINDOW * capacity].astype(F32) * slot_gate
    masks = place_ref[WINDOW * capacity :].astype(F32)
    result = jnp.zeros(gate_out_ref.shape, F32)
    for index in range(WINDOW):
        span = slice(index * capacity, (index + 1) * capacity)
        value = jnp.sum(picked[span], axis=0, keepdims=True)
        result = result + masks[2 * index : 2 * index + 2] * value
    gate_out_ref[...] = result


def swap(array, axes, bit):
    size = lax.axis_size(axes)
    return lax.ppermute(array, axes, [(index, index ^ bit) for index in range(size)])


def swap_nodes(array, step):
    return swap(array, ("node", "local"), step * lax.axis_size("local") + 1)


def join(pieces, after=()):
    rows, wide = pieces[0].shape
    rows *= len(pieces)
    shape = jax.ShapeDtypeStruct((rows, wide), BF16)
    return call(join_kernel, shape, 0, 4 * rows * wide, after=after)(*pieces)


def body(tokens, grad_out, routes, gates, w_in, w_out):
    nodes = lax.axis_size("node")
    locals_ = lax.axis_size("local")
    edatas = lax.axis_size("edata")
    tok_rows, feats = tokens.shape
    hidden = w_in.shape[1]
    capacity = 2 * tok_rows // EXPERTS
    slots = WINDOW * capacity
    wide = feats + LANES
    coded = 4 * hidden + LANES
    shape = jax.ShapeDtypeStruct
    hbm = pl.BlockSpec(memory_space=pltpu.HBM)
    vmem = pl.BlockSpec(memory_space=pltpu.VMEM)

    inputs = [
        pltpu.with_memory_space_constraint(value, pltpu.HBM)
        for value in (routes.T, gates.T, tokens, grad_out, w_in, w_out)
    ]
    own_rows, other_rows, place, spread, weights = call(
        gather_kernel,
        (
            pltpu.VMEM((2 * capacity, wide), BF16),
            pltpu.VMEM((2 * capacity, wide), BF16),
            pltpu.VMEM((slots + 16, tok_rows), BF16),
            pltpu.VMEM((tok_rows, 2 * slots), BF16),
            pltpu.VMEM((2 * hidden, feats), BF16),
        ),
        4 * slots * tok_rows * feats,
        4 * tok_rows * feats + 4 * hidden * feats,
        in_specs=[hbm] * 6,
        scratch_shapes=[
            pltpu.VMEM((2, tok_rows), jnp.int32),
            pltpu.VMEM((2, tok_rows), BF16),
            pltpu.VMEM((tok_rows, feats), BF16),
            pltpu.VMEM((tok_rows, feats), BF16),
            pltpu.SemaphoreType.DMA((3 + 2 * PIECES + feats // hidden,)),
        ],
    )(*inputs)

    other_weights = swap(weights, "local", 1)

    half_nodes = nodes // WINDOW
    pieces = [own_rows]
    for step in range(1, nodes):
        pieces.append(swap_nodes(own_rows if step < half_nodes else other_rows, step))
    rows = half_nodes * (locals_ // 2) * capacity
    last = ()
    chains = []
    held = []
    for chunk in (pieces[:half_nodes], pieces[half_nodes:]):
        chunk = join(chunk, last)
        bit = 2
        while bit < locals_:
            chunk = join([chunk, swap(chunk, "local", bit)])
            bit *= 2
        held.append(chunk)
        part, gate_rows = call(
            functools.partial(part_kernel, capacity),
            (shape((rows, coded), I16), shape((rows, LANES), F32)),
            16 * rows * feats * hidden,
            4 * rows * feats + 8 * feats * hidden,
            after=last,
        )(chunk, weights, other_weights)
        last = (part,)
        chains.append((part, swap(part, "edata", 1), gate_rows))
    bit = 2
    while bit < edatas:
        for index, (part, other, gate_rows) in enumerate(chains):
            part = call(
                add_codes_kernel,
                shape((rows, coded), I16),
                16 * rows * hidden,
                6 * rows * coded,
                after=last,
            )(part, other)
            last = (part,)
            chains[index] = (part, swap(part, "edata", bit), gate_rows)
        bit *= 2

    mine = []
    theirs = ()
    slots_back = []
    for index, (part, other, gate_rows) in enumerate(chains):
        dealt = [shape((capacity, wide), BF16 if index else F32)] * half_nodes
        own, packed, *slot_parts = call(
            functools.partial(slot_kernel, capacity, len(theirs)),
            [
                shape((2 * rows, hidden), BF16),
                shape(((1 + len(theirs)) * 2 * rows, hidden), BF16),
                *(dealt if locals_ == 2 else [shape((rows, wide), F32)]),
            ],
            4 * rows * feats * hidden,
            4 * feats * hidden + 4 * rows * feats,
            after=last,
        )(part, other, gate_rows, weights, other_weights, *theirs)
        last = (own,)
        mine.append(own)
        theirs = (packed,)
        if locals_ > 2:
            half = rows // 2
            keep, send = slot_parts[0][:half], slot_parts[0][half:]
            bit = locals_ // 2
            while bit > 2:
                half //= 2
                keep, send = call(
                    halve_kernel,
                    (shape((half, wide), F32),) * 2,
                    4 * half * wide,
                    24 * half * wide,
                )(keep, swap(send, "local", bit))
                bit //= 2
            slot_parts = call(deal_kernel, dealt, 4 * half * wide, 12 * half * wide)(
                keep, swap(send, "local", bit)
            )
        for step, send in enumerate(slot_parts, index * half_nodes):
            slots_back.append(swap_nodes(send, step) if step else send)
    came = [swap(chunk, "local", 1) for chunk in held]
    back = swap(theirs[0], "local", 1)
    grad_w_in, grad_w_out, written = call(
        functools.partial(weight_kernel, capacity),
        (shape((feats, hidden), F32), shape((hidden, feats), F32), shape((8, LANES), F32)),
        32 * rows * feats * hidden,
        8 * feats * hidden,
        in_specs=[vmem] * 7,
        after=slots_back[1:half_nodes],
        out_specs=[hbm, hbm, vmem],
        scratch_shapes=[
            pltpu.VMEM((feats, hidden), F32),
            pltpu.VMEM((hidden, feats), F32),
            pltpu.SemaphoreType.DMA((2 * PIECES,)),
        ],
    )(*held, *came, *mine, back)
    grad_tokens, grad_gates = call(
        functools.partial(combine_kernel, nodes),
        (shape((tok_rows, feats), BF16), shape((2, tok_rows), F32)),
        4 * slots * tok_rows * feats,
        2 * tok_rows * feats,
        after=(written,),
    )(*slots_back[:half_nodes], *reversed(slots_back[half_nodes:]), place, spread)
    return (grad_tokens, grad_gates.T, grad_w_in, grad_w_out)


def solution(mesh):
    in_specs = (
        P(("node", "local"), "edata"),
        P(("node", "local"), "edata"),
        P(("node", "local"), None),
        P(("node", "local"), None),
        P("edata", ("node", "local")),
        P(("node", "local"), "edata"),
    )
    out_specs = (
        P(("node", "local"), "edata"),
        P(("node", "local"), None),
        P("edata", ("node", "local")),
        P(("node", "local"), "edata"),
    )
    return jax.shard_map(body, mesh=mesh, in_specs=in_specs, out_specs=out_specs, check_vma=False)
```

```python
import functools

import jax
import jax.numpy as jnp
from jax import lax
from jax.experimental import pallas as pl
from jax.experimental.pallas import tpu as pltpu
from jax.sharding import PartitionSpec as P

EXPERTS = 64
WINDOW = 2
LANES = 128
PIECES = 4
VMEM_LIMIT = 40 * 1024 * 1024

BF16 = jnp.bfloat16
F32 = jnp.float32
I16 = jnp.int16
ROWS_BY_ROWS = (((0,), (0,)), ((), ()))
COLS_BY_COLS = (((1,), (1,)), ((), ()))


def gelu_pair(pre_act):
    coefficient = 0.7978845608028654
    square = pre_act * pre_act
    tanh_val = jnp.tanh(coefficient * (pre_act + 0.044715 * pre_act * square))
    half = 0.5 * (1.0 + tanh_val)
    activation = pre_act * half
    slopes = half + 0.5 * pre_act * (1.0 - tanh_val * tanh_val) * coefficient * (
        1.0 + 3.0 * 0.044715 * square
    )
    return (activation, slopes)


def call(kernel, out_shape, flops, moved, limit=VMEM_LIMIT, in_specs=None, after=(), **more):
    def run(*operands):
        given = in_specs or [pl.BlockSpec(memory_space=pltpu.VMEM)] * len(operands)
        return pl.pallas_call(
            lambda *refs: kernel(*refs[len(after) :]),
            out_shape=out_shape,
            in_specs=[pl.BlockSpec(memory_space=pl.ANY)] * len(after) + list(given),
            compiler_params=pltpu.CompilerParams(vmem_limit_bytes=limit),
            cost_estimate=pl.CostEstimate(flops=flops, bytes_accessed=moved, transcendentals=0),
            **more,
        )(*after, *operands)

    return run


def own_expert():
    half_nodes = lax.axis_size("node") // WINDOW
    return lax.axis_index("node") // half_nodes


def split_value(value):
    high = value.astype(BF16).astype(F32)
    lane = lax.broadcasted_iota(jnp.int32, (value.shape[0], LANES), 1)
    return jnp.where(lane == 0, high, jnp.where(lane == 1, value - high, 0.0))


def encode(values):
    top = jnp.max(jnp.abs(values), axis=1, keepdims=True)
    power = jnp.ceil(jnp.log2(jnp.maximum(top, 1e-30)))
    codes = jnp.round(values * (1.999 * jnp.exp2(14.0 - power)))
    return codes.astype(jnp.int32).astype(I16), power


def decode(codes, power):
    return codes.astype(jnp.int32).astype(F32) * (jnp.exp2(power - 14.0) / 1.999)


def store_codes(out_ref, pair):
    hidden = pair[0].shape[1]
    lane = lax.broadcasted_iota(jnp.int32, (pair[0].shape[0], LANES), 1)
    powers = []
    for index, values in enumerate(pair):
        codes, power = encode(values)
        out_ref[:, index * hidden : (index + 1) * hidden] = codes
        powers.append(power)
    powers = jnp.where(lane == 0, powers[0], powers[1])
    out_ref[:, 2 * hidden :] = powers.astype(jnp.int32).astype(I16)


def load_codes(ref):
    hidden = (ref.shape[1] - LANES) // 2
    powers = ref[:, 2 * hidden :].astype(jnp.int32).astype(F32)
    return [
        decode(ref[:, index * hidden : (index + 1) * hidden], powers[:, index : index + 1])
        for index in range(2)
    ]


def gather_kernel(routes_hbm, gates_hbm, tokens_hbm, grads_hbm, w_in_hbm, w_out_hbm, own_ref,
                  other_ref, place_ref, spread_ref, w_ref, routes_ref, gates_ref, tokens_ref,
                  grads_ref, sems):
    tok_rows, feats = tokens_ref.shape
    capacity = own_ref.shape[0] // 2
    slots = WINDOW * capacity
    copies = [
        pltpu.make_async_copy(routes_hbm, routes_ref, sems.at[0]),
        pltpu.make_async_copy(gates_hbm, gates_ref, sems.at[1]),
    ]
    count = tok_rows // PIECES
    for source, target in ((tokens_hbm, tokens_ref), (grads_hbm, grads_ref)):
        for piece in range(PIECES):
            span = pl.ds(piece * count, count)
            copies.append(
                pltpu.make_async_copy(source.at[span], target.at[span], sems.at[len(copies)])
            )
    hidden = w_out_hbm.shape[0]
    upper, lower = pl.ds(0, hidden), pl.ds(hidden, hidden)
    moves = [(w_out_hbm, w_ref.at[upper])]
    for block in range(0, feats, hidden):
        span = pl.ds(block, hidden)
        moves.append((w_in_hbm.at[span], w_ref.at[lower, span]))
    for source, target in moves:
        copies.append(pltpu.make_async_copy(source, target, sems.at[len(copies)]))
    for copy in copies:
        copy.start()
    earlier = lax.broadcasted_iota(jnp.int32, (tok_rows, tok_rows), 0) < lax.broadcasted_iota(
        jnp.int32, (tok_rows, tok_rows), 1
    )
    earlier = earlier.astype(F32).astype(BF16)
    slot_of = lax.broadcasted_iota(jnp.int32, (capacity, tok_rows), 0).astype(F32)
    row_of = lax.broadcasted_iota(jnp.int32, (8, tok_rows), 0)
    own = own_expert()
    copies[0].wait()
    copies[1].wait()
    routes = routes_ref[...]
    gates = gates_ref[...].astype(F32)
    hits = [(routes == expert).astype(F32) for expert in (own, 1 - own)]
    named = [hit[0:1] + hit[1:2] for hit in hits]
    weight = [hit * gates for hit in hits]
    weight = [value[0:1] + value[1:2] for value in weight]
    names = jnp.where(row_of == 0, named[0], jnp.where(row_of == 1, named[1], 0.0)).astype(BF16)
    before = jnp.dot(names, earlier, preferred_element_type=F32)
    parts = [jnp.where(before[e : e + 1] == slot_of, named[e], 0.0) for e in range(WINDOW)]
    place = jnp.concatenate(parts, axis=0).astype(BF16)
    place_ref[:slots] = place
    spread_ref[...] = jnp.concatenate(parts + parts, axis=0).T.astype(BF16)
    masks = jnp.zeros((16, tok_rows), F32)
    row_of = lax.broadcasted_iota(jnp.int32, masks.shape, 0)
    for index, hit in enumerate(hits):
        for k in range(2):
            masks = jnp.where(row_of == 2 * index + k, hit[k : k + 1], masks)
    place_ref[slots:] = masks.astype(BF16)
    for copy in copies[2 : 2 + PIECES]:
        copy.wait()
    rows_x = jnp.dot(place, tokens_ref[...], preferred_element_type=F32)
    for copy in copies[2 + PIECES : 2 + 2 * PIECES]:
        copy.wait()
    rows_dy = jnp.dot(place, grads_ref[...], preferred_element_type=F32)
    for expert, out_ref in ((0, own_ref), (1, other_ref)):
        span = slice(expert * capacity, (expert + 1) * capacity)
        out_ref[:, :feats] = jnp.concatenate([rows_x[span], rows_dy[span]], axis=0).astype(BF16)
        gate = jnp.sum(parts[expert] * weight[expert], axis=1, keepdims=True)
        gate = jnp.concatenate([gate, gate], axis=0)
        out_ref[:, feats:] = jnp.broadcast_to(gate, (2 * capacity, LANES)).astype(BF16)
    for copy in copies[2 + 2 * PIECES :]:
        copy.wait()


def join_kernel(*refs):
    *pieces, out_ref = refs
    rows = pieces[0].shape[0]
    for index, ref in enumerate(pieces):
        out_ref[index * rows : (index + 1) * rows] = ref[...]


def part_kernel(capacity, rows_ref, w_ref, w_other_ref, part_ref, gate_ref):
    feats = w_ref.shape[1]
    hidden = w_ref.shape[0] // 2
    groups = rows_ref.shape[0] // (2 * capacity)
    gate = rows_ref[:, feats:].astype(F32).reshape(groups, 2 * capacity, LANES)
    gate_ref[...] = gate[:, :capacity].reshape(groups * capacity, LANES)
    rows = rows_ref[:, :feats]
    pre = []
    back = []
    for ref in (w_ref, w_other_ref):
        pre.append(
            sum(
                jnp.dot(
                    rows[:, block : block + hidden],
                    ref[hidden:, block : block + hidden],
                    preferred_element_type=F32,
                )
                for block in range(0, feats, hidden)
            )
        )
        back.append(
            lax.dot_general(rows, ref[:hidden], COLS_BY_COLS, preferred_element_type=F32)
        )
    pair = []
    for values, span in ((pre, slice(0, capacity)), (back, slice(capacity, 2 * capacity))):
        values = jnp.concatenate(values, axis=1).reshape(groups, 2 * capacity, 2 * hidden)
        pair.append(values[:, span].reshape(groups * capacity, 2 * hidden))
    store_codes(part_ref, pair)


def add_codes_kernel(first_ref, second_ref, out_ref):
    pairs = zip(load_codes(first_ref), load_codes(second_ref))
    store_codes(out_ref, [first + second for first, second in pairs])


def deal(total, refs):
    each, wide = refs[0].shape
    feats = wide - LANES
    gate = split_value(jnp.sum(total[:, feats:], axis=1, keepdims=True))
    for index, ref in enumerate(refs):
        span = slice(index * each, (index + 1) * each)
        ref[:, :feats] = total[span, :feats].astype(ref.dtype)
        ref[:, feats:] = gate[span].astype(ref.dtype)


def slot_kernel(capacity, before, first_ref, second_ref, gate_ref, w_ref, w_other_ref, *refs):
    before_refs, (mine_ref, theirs_ref, *slot_refs) = refs[:before], refs[before:]
    hidden = w_ref.shape[0] // 2
    pairs = zip(load_codes(first_ref), load_codes(second_ref))
    pre, back = [first + second for first, second in pairs]
    gate = gate_ref[:, :1]
    activation, slopes = gelu_pair(pre)
    dpre = (gate * back * slopes).astype(BF16)
    act = gate * activation
    slot = []
    for block in range(0, w_ref.shape[1], hidden):
        span = slice(block, block + hidden)
        slot.append(
            sum(
                lax.dot_general(
                    part, ref[hidden:, span], COLS_BY_COLS, preferred_element_type=F32
                )
                for part, ref in ((dpre[:, :hidden], w_ref), (dpre[:, hidden:], w_other_ref))
            )
        )
    slot_gate = split_value(jnp.sum(activation * back, axis=1, keepdims=True))
    total = jnp.concatenate(slot + [slot_gate], axis=1)
    if len(slot_refs) == 1:
        slot_refs[0][...] = total
    else:
        deal(total, slot_refs)
    rows = dpre.shape[0]
    both = [
        value.reshape(rows // capacity, capacity, 2 * hidden) for value in (dpre.astype(F32), act)
    ]
    both = jnp.concatenate(both, axis=1).reshape(2 * rows, 2 * hidden).astype(BF16)
    mine_ref[...] = both[:, :hidden]
    count = 2 * rows
    for index, ref in enumerate(before_refs):
        theirs_ref[index * count : (index + 1) * count] = ref[...]
    theirs_ref[before * count :] = both[:, hidden:]


def halve_kernel(kept_ref, came_ref, keep_ref, send_ref):
    half = keep_ref.shape[0]
    total = kept_ref[...] + came_ref[...]
    keep_ref[...] = total[:half]
    send_ref[...] = total[half:]


def deal_kernel(kept_ref, came_ref, *refs):
    deal(kept_ref[...] + came_ref[...], refs)


def weight_kernel(capacity, *refs):
    rows_refs, both_refs = refs[:4], refs[4:7]
    w_in_hbm, w_out_hbm, written_ref, w_in_ref, w_out_ref, sems = refs[7:]
    feats, hidden = w_in_ref.shape
    rows = jnp.concatenate([ref[:, :feats] for ref in rows_refs], axis=0)
    both = jnp.concatenate([ref[...] for ref in both_refs], axis=0).astype(F32)
    of_x = lax.broadcasted_iota(jnp.int32, both.shape, 0) % (2 * capacity) < capacity
    dpre = jnp.where(of_x, both, 0.0).astype(BF16)
    act = jnp.where(of_x, 0.0, both).astype(BF16)
    count = feats // PIECES
    copies = []
    for piece in range(PIECES):
        span = slice(piece * count, (piece + 1) * count)
        part = rows[:, span]
        w_in_ref[span] = lax.dot_general(part, dpre, ROWS_BY_ROWS, preferred_element_type=F32)
        w_out_ref[:, span] = lax.dot_general(act, part, ROWS_BY_ROWS, preferred_element_type=F32)
        span = pl.ds(piece * count, count)
        for source, target in (
            (w_in_ref.at[span], w_in_hbm.at[span]),
            (w_out_ref.at[:, span], w_out_hbm.at[:, span]),
        ):
            copy = pltpu.make_async_copy(source, target, sems.at[len(copies)])
            copy.start()
            copies.append(copy)
    for copy in copies:
        copy.wait()
    written_ref[...] = jnp.zeros(written_ref.shape, F32)


def combine_kernel(steps, *refs):
    kept_ref, came_refs = refs[0], refs[1:steps]
    place_ref, spread_ref, tokens_ref, gate_out_ref = refs[steps:]
    feats = tokens_ref.shape[1]
    capacity = kept_ref.shape[0]
    came = [ref[...].astype(F32) for ref in came_refs]
    half = steps // WINDOW
    own = sum(came[: half - 1], kept_ref[...])
    other = sum(came[half:], came[half - 1])
    slots = jnp.concatenate([own, other], axis=0)
    grads = slots[:, :feats]
    high = grads.astype(BF16)
    low = (grads - high.astype(F32)).astype(BF16)
    both = jnp.concatenate([high, low], axis=0)
    tokens_ref[...] = jnp.dot(spread_ref[...], both, preferred_element_type=F32).astype(BF16)
    slot_gate = jnp.sum(slots[:, feats:], axis=1, keepdims=True)
    picked = place_ref[: WINDOW * capacity].astype(F32) * slot_gate
    masks = place_ref[WINDOW * capacity :].astype(F32)
    result = jnp.zeros(gate_out_ref.shape, F32)
    for index in range(WINDOW):
        span = slice(index * capacity, (index + 1) * capacity)
        value = jnp.sum(picked[span], axis=0, keepdims=True)
        result = result + masks[2 * index : 2 * index + 2] * value
    gate_out_ref[...] = result


def swap(array, axes, bit):
    size = lax.axis_size(axes)
    return lax.ppermute(array, axes, [(index, index ^ bit) for index in range(size)])


def swap_nodes(array, step):
    return swap(array, ("node", "local"), step * lax.axis_size("local") + 1)


def join(pieces, after=()):
    rows, wide = pieces[0].shape
    rows *= len(pieces)
    shape = jax.ShapeDtypeStruct((rows, wide), BF16)
    return call(join_kernel, shape, 0, 4 * rows * wide, after=after)(*pieces)


def body(tokens, grad_out, routes, gates, w_in, w_out):
    nodes = lax.axis_size("node")
    locals_ = lax.axis_size("local")
    edatas = lax.axis_size("edata")
    tok_rows, feats = tokens.shape
    hidden = w_in.shape[1]
    capacity = 2 * tok_rows // EXPERTS
    slots = WINDOW * capacity
    wide = feats + LANES
    coded = 4 * hidden + LANES
    shape = jax.ShapeDtypeStruct
    hbm = pl.BlockSpec(memory_space=pltpu.HBM)
    vmem = pl.BlockSpec(memory_space=pltpu.VMEM)

    inputs = [
        pltpu.with_memory_space_constraint(value, pltpu.HBM)
        for value in (routes.T, gates.T, tokens, grad_out, w_in, w_out)
    ]
    own_rows, other_rows, place, spread, weights = call(
        gather_kernel,
        (
            pltpu.VMEM((2 * capacity, wide), BF16),
            pltpu.VMEM((2 * capacity, wide), BF16),
            pltpu.VMEM((slots + 16, tok_rows), BF16),
            pltpu.VMEM((tok_rows, 2 * slots), BF16),
            pltpu.VMEM((2 * hidden, feats), BF16),
        ),
        4 * slots * tok_rows * feats,
        4 * tok_rows * feats + 4 * hidden * feats,
        in_specs=[hbm] * 6,
        scratch_shapes=[
            pltpu.VMEM((2, tok_rows), jnp.int32),
            pltpu.VMEM((2, tok_rows), BF16),
            pltpu.VMEM((tok_rows, feats), BF16),
            pltpu.VMEM((tok_rows, feats), BF16),
            pltpu.SemaphoreType.DMA((3 + 2 * PIECES + feats // hidden,)),
        ],
    )(*inputs)

    other_weights = swap(weights, "local", 1)

    half_nodes = nodes // WINDOW
    pieces = [own_rows]
    for step in range(1, nodes):
        pieces.append(swap_nodes(own_rows if step < half_nodes else other_rows, step))
    rows = half_nodes * (locals_ // 2) * capacity
    last = ()
    chains = []
    held = []
    for chunk in (pieces[half_nodes:], pieces[:half_nodes]):
        chunk = join(chunk, last)
        bit = 2
        while bit < locals_:
            chunk = join([chunk, swap(chunk, "local", bit)])
            bit *= 2
        held.append(chunk)
        part, gate_rows = call(
            functools.partial(part_kernel, capacity),
            (shape((rows, coded), I16), shape((rows, LANES), F32)),
            16 * rows * feats * hidden,
            4 * rows * feats + 8 * feats * hidden,
            after=last,
        )(chunk, weights, other_weights)
        last = (part,)
        chains.append((part, swap(part, "edata", 1), gate_rows))
    bit = 2
    while bit < edatas:
        for index, (part, other, gate_rows) in enumerate(chains):
            part = call(
                add_codes_kernel,
                shape((rows, coded), I16),
                16 * rows * hidden,
                6 * rows * coded,
                after=last,
            )(part, other)
            last = (part,)
            chains[index] = (part, swap(part, "edata", bit), gate_rows)
        bit *= 2

    mine = []
    theirs = ()
    slots_back = []
    for index, (part, other, gate_rows) in enumerate(chains):
        dealt = [shape((capacity, wide), BF16 if index else F32)] * half_nodes
        if index:
            dealt[0] = shape((capacity, wide), F32)
        own, packed, *slot_parts = call(
            functools.partial(slot_kernel, capacity, len(theirs)),
            [
                shape((2 * rows, hidden), BF16),
                shape(((1 + len(theirs)) * 2 * rows, hidden), BF16),
                *(dealt if locals_ == 2 else [shape((rows, wide), F32)]),
            ],
            4 * rows * feats * hidden,
            4 * feats * hidden + 4 * rows * feats,
            after=last,
        )(part, other, gate_rows, weights, other_weights, *theirs)
        last = (own,)
        mine.append(own)
        theirs = (packed,)
        if locals_ > 2:
            half = rows // 2
            keep, send = slot_parts[0][:half], slot_parts[0][half:]
            bit = locals_ // 2
            while bit > 2:
                half //= 2
                keep, send = call(
                    halve_kernel,
                    (shape((half, wide), F32),) * 2,
                    4 * half * wide,
                    24 * half * wide,
                )(keep, swap(send, "local", bit))
                bit //= 2
            slot_parts = call(deal_kernel, dealt, 4 * half * wide, 12 * half * wide)(
                keep, swap(send, "local", bit)
            )
        came = []
        for step, send in enumerate(slot_parts, (1 - index) * half_nodes):
            came.append(swap_nodes(send, step) if step else send)
        slots_back = came + slots_back
    came = [swap(chunk, "local", 1) for chunk in held]
    back = swap(theirs[0], "local", 1)
    grad_w_in, grad_w_out, written = call(
        functools.partial(weight_kernel, capacity),
        (shape((feats, hidden), F32), shape((hidden, feats), F32), shape((8, LANES), F32)),
        32 * rows * feats * hidden,
        8 * feats * hidden,
        in_specs=[vmem] * 7,
        after=slots_back[half_nodes + 1 :],
        out_specs=[hbm, hbm, vmem],
        scratch_shapes=[
            pltpu.VMEM((feats, hidden), F32),
            pltpu.VMEM((hidden, feats), F32),
            pltpu.SemaphoreType.DMA((2 * PIECES,)),
        ],
    )(*held, *came, *mine, back)
    grad_tokens, grad_gates = call(
        functools.partial(combine_kernel, nodes),
        (shape((tok_rows, feats), BF16), shape((2, tok_rows), F32)),
        4 * slots * tok_rows * feats,
        2 * tok_rows * feats,
        after=(written,),
    )(*slots_back[:half_nodes], *reversed(slots_back[half_nodes:]), place, spread)
    return (grad_tokens, grad_gates.T, grad_w_in, grad_w_out)


def solution(mesh):
    in_specs = (
        P(("node", "local"), "edata"),
        P(("node", "local"), "edata"),
        P(("node", "local"), None),
        P(("node", "local"), None),
        P("edata", ("node", "local")),
        P(("node", "local"), "edata"),
    )
    out_specs = (
        P(("node", "local"), "edata"),
        P(("node", "local"), None),
        P("edata", ("node", "local")),
        P(("node", "local"), "edata"),
    )
    return jax.shard_map(body, mesh=mesh, in_specs=in_specs, out_specs=out_specs, check_vma=False)
```

```python
import functools

import jax
import jax.numpy as jnp
from jax import lax
from jax.experimental import pallas as pl
from jax.experimental.pallas import tpu as pltpu
from jax.sharding import PartitionSpec as P

EXPERTS = 64
WINDOW = 2
LANES = 128
PIECES = 4
VMEM_LIMIT = 40 * 1024 * 1024

BF16 = jnp.bfloat16
F32 = jnp.float32
I16 = jnp.int16
ROWS_BY_ROWS = (((0,), (0,)), ((), ()))
COLS_BY_COLS = (((1,), (1,)), ((), ()))


def gelu_pair(pre_act):
    coefficient = 0.7978845608028654
    square = pre_act * pre_act
    tanh_val = jnp.tanh(coefficient * (pre_act + 0.044715 * pre_act * square))
    half = 0.5 * (1.0 + tanh_val)
    activation = pre_act * half
    slopes = half + 0.5 * pre_act * (1.0 - tanh_val * tanh_val) * coefficient * (
        1.0 + 3.0 * 0.044715 * square
    )
    return (activation, slopes)


def call(kernel, out_shape, flops, moved, limit=VMEM_LIMIT, in_specs=None, after=(), **more):
    def run(*operands):
        given = in_specs or [pl.BlockSpec(memory_space=pltpu.VMEM)] * len(operands)
        return pl.pallas_call(
            lambda *refs: kernel(*refs[len(after) :]),
            out_shape=out_shape,
            in_specs=[pl.BlockSpec(memory_space=pl.ANY)] * len(after) + list(given),
            compiler_params=pltpu.CompilerParams(vmem_limit_bytes=limit),
            cost_estimate=pl.CostEstimate(flops=flops, bytes_accessed=moved, transcendentals=0),
            **more,
        )(*after, *operands)

    return run


def own_expert():
    half_nodes = lax.axis_size("node") // WINDOW
    return lax.axis_index("node") // half_nodes


def split_value(value):
    high = value.astype(BF16).astype(F32)
    lane = lax.broadcasted_iota(jnp.int32, (value.shape[0], LANES), 1)
    return jnp.where(lane == 0, high, jnp.where(lane == 1, value - high, 0.0))


def encode(values):
    top = jnp.max(jnp.abs(values), axis=1, keepdims=True)
    power = jnp.ceil(jnp.log2(jnp.maximum(top, 1e-30)))
    codes = jnp.round(values * (1.999 * jnp.exp2(14.0 - power)))
    return codes.astype(jnp.int32).astype(I16), power


def decode(codes, power):
    return codes.astype(jnp.int32).astype(F32) * (jnp.exp2(power - 14.0) / 1.999)


def store_codes(out_ref, pair):
    hidden = pair[0].shape[1]
    lane = lax.broadcasted_iota(jnp.int32, (pair[0].shape[0], LANES), 1)
    powers = []
    for index, values in enumerate(pair):
        codes, power = encode(values)
        out_ref[:, index * hidden : (index + 1) * hidden] = codes
        powers.append(power)
    powers = jnp.where(lane == 0, powers[0], powers[1])
    out_ref[:, 2 * hidden :] = powers.astype(jnp.int32).astype(I16)


def load_codes(ref):
    hidden = (ref.shape[1] - LANES) // 2
    powers = ref[:, 2 * hidden :].astype(jnp.int32).astype(F32)
    return [
        decode(ref[:, index * hidden : (index + 1) * hidden], powers[:, index : index + 1])
        for index in range(2)
    ]


def gather_kernel(routes_hbm, gates_hbm, tokens_hbm, grads_hbm, w_in_hbm, w_out_hbm, own_ref,
                  other_ref, place_ref, spread_ref, w_ref, routes_ref, gates_ref, tokens_ref,
                  grads_ref, sems):
    tok_rows, feats = tokens_ref.shape
    capacity = own_ref.shape[0] // 2
    slots = WINDOW * capacity
    copies = [
        pltpu.make_async_copy(routes_hbm, routes_ref, sems.at[0]),
        pltpu.make_async_copy(gates_hbm, gates_ref, sems.at[1]),
    ]
    count = tok_rows // PIECES
    for source, target in ((tokens_hbm, tokens_ref), (grads_hbm, grads_ref)):
        for piece in range(PIECES):
            span = pl.ds(piece * count, count)
            copies.append(
                pltpu.make_async_copy(source.at[span], target.at[span], sems.at[len(copies)])
            )
    hidden = w_out_hbm.shape[0]
    upper, lower = pl.ds(0, hidden), pl.ds(hidden, hidden)
    moves = [(w_out_hbm, w_ref.at[upper])]
    for block in range(0, feats, hidden):
        span = pl.ds(block, hidden)
        moves.append((w_in_hbm.at[span], w_ref.at[lower, span]))
    for source, target in moves:
        copies.append(pltpu.make_async_copy(source, target, sems.at[len(copies)]))
    for copy in copies:
        copy.start()
    earlier = lax.broadcasted_iota(jnp.int32, (tok_rows, tok_rows), 0) < lax.broadcasted_iota(
        jnp.int32, (tok_rows, tok_rows), 1
    )
    earlier = earlier.astype(F32).astype(BF16)
    slot_of = lax.broadcasted_iota(jnp.int32, (capacity, tok_rows), 0).astype(F32)
    row_of = lax.broadcasted_iota(jnp.int32, (8, tok_rows), 0)
    own = own_expert()
    copies[0].wait()
    copies[1].wait()
    routes = routes_ref[...]
    gates = gates_ref[...].astype(F32)
    hits = [(routes == expert).astype(F32) for expert in (own, 1 - own)]
    named = [hit[0:1] + hit[1:2] for hit in hits]
    weight = [hit * gates for hit in hits]
    weight = [value[0:1] + value[1:2] for value in weight]
    names = jnp.where(row_of == 0, named[0], jnp.where(row_of == 1, named[1], 0.0)).astype(BF16)
    before = jnp.dot(names, earlier, preferred_element_type=F32)
    parts = [jnp.where(before[e : e + 1] == slot_of, named[e], 0.0) for e in range(WINDOW)]
    place = jnp.concatenate(parts, axis=0).astype(BF16)
    place_ref[:slots] = place
    spread_ref[...] = jnp.concatenate(parts + parts, axis=0).T.astype(BF16)
    masks = jnp.zeros((16, tok_rows), F32)
    row_of = lax.broadcasted_iota(jnp.int32, masks.shape, 0)
    for index, hit in enumerate(hits):
        for k in range(2):
            masks = jnp.where(row_of == 2 * index + k, hit[k : k + 1], masks)
    place_ref[slots:] = masks.astype(BF16)
    for copy in copies[2 : 2 + PIECES]:
        copy.wait()
    rows_x = jnp.dot(place, tokens_ref[...], preferred_element_type=F32)
    for copy in copies[2 + PIECES : 2 + 2 * PIECES]:
        copy.wait()
    rows_dy = jnp.dot(place, grads_ref[...], preferred_element_type=F32)
    for expert, out_ref in ((0, own_ref), (1, other_ref)):
        span = slice(expert * capacity, (expert + 1) * capacity)
        out_ref[:, :feats] = jnp.concatenate([rows_x[span], rows_dy[span]], axis=0).astype(BF16)
        gate = jnp.sum(parts[expert] * weight[expert], axis=1, keepdims=True)
        gate = jnp.concatenate([gate, gate], axis=0)
        out_ref[:, feats:] = jnp.broadcast_to(gate, (2 * capacity, LANES)).astype(BF16)
    for copy in copies[2 + 2 * PIECES :]:
        copy.wait()


def join_kernel(*refs):
    *pieces, out_ref = refs
    rows = pieces[0].shape[0]
    for index, ref in enumerate(pieces):
        out_ref[index * rows : (index + 1) * rows] = ref[...]


def part_kernel(capacity, rows_ref, w_ref, w_other_ref, part_ref, gate_ref):
    feats = w_ref.shape[1]
    hidden = w_ref.shape[0] // 2
    groups = rows_ref.shape[0] // (2 * capacity)
    gate = rows_ref[:, feats:].astype(F32).reshape(groups, 2 * capacity, LANES)
    gate_ref[...] = gate[:, :capacity].reshape(groups * capacity, LANES)
    rows = rows_ref[:, :feats]
    pre = []
    back = []
    for ref in (w_ref, w_other_ref):
        pre.append(
            sum(
                jnp.dot(
                    rows[:, block : block + hidden],
                    ref[hidden:, block : block + hidden],
                    preferred_element_type=F32,
                )
                for block in range(0, feats, hidden)
            )
        )
        back.append(
            lax.dot_general(rows, ref[:hidden], COLS_BY_COLS, preferred_element_type=F32)
        )
    pair = []
    for values, span in ((pre, slice(0, capacity)), (back, slice(capacity, 2 * capacity))):
        values = jnp.concatenate(values, axis=1).reshape(groups, 2 * capacity, 2 * hidden)
        pair.append(values[:, span].reshape(groups * capacity, 2 * hidden))
    store_codes(part_ref, pair)


def add_codes_kernel(first_ref, second_ref, out_ref):
    pairs = zip(load_codes(first_ref), load_codes(second_ref))
    store_codes(out_ref, [first + second for first, second in pairs])


def deal(total, refs):
    each, wide = refs[0].shape
    feats = wide - LANES
    gate = split_value(jnp.sum(total[:, feats:], axis=1, keepdims=True))
    for index, ref in enumerate(refs):
        span = slice(index * each, (index + 1) * each)
        ref[:, :feats] = total[span, :feats].astype(ref.dtype)
        ref[:, feats:] = gate[span].astype(ref.dtype)


def slot_kernel(capacity, before, first_ref, second_ref, gate_ref, w_ref, w_other_ref, *refs):
    before_refs, (mine_ref, theirs_ref, *slot_refs) = refs[:before], refs[before:]
    hidden = w_ref.shape[0] // 2
    pairs = zip(load_codes(first_ref), load_codes(second_ref))
    pre, back = [first + second for first, second in pairs]
    gate = gate_ref[:, :1]
    activation, slopes = gelu_pair(pre)
    dpre = (gate * back * slopes).astype(BF16)
    act = gate * activation
    slot = []
    for block in range(0, w_ref.shape[1], hidden):
        span = slice(block, block + hidden)
        slot.append(
            sum(
                lax.dot_general(
                    part, ref[hidden:, span], COLS_BY_COLS, preferred_element_type=F32
                )
                for part, ref in ((dpre[:, :hidden], w_ref), (dpre[:, hidden:], w_other_ref))
            )
        )
    slot_gate = split_value(jnp.sum(activation * back, axis=1, keepdims=True))
    total = jnp.concatenate(slot + [slot_gate], axis=1)
    if len(slot_refs) == 1:
        slot_refs[0][...] = total
    else:
        deal(total, slot_refs)
    rows = dpre.shape[0]
    both = [
        value.reshape(rows // capacity, capacity, 2 * hidden) for value in (dpre.astype(F32), act)
    ]
    both = jnp.concatenate(both, axis=1).reshape(2 * rows, 2 * hidden).astype(BF16)
    mine_ref[...] = both[:, :hidden]
    count = 2 * rows
    for index, ref in enumerate(before_refs):
        theirs_ref[index * count : (index + 1) * count] = ref[...]
    theirs_ref[before * count :] = both[:, hidden:]


def halve_kernel(kept_ref, came_ref, keep_ref, send_ref):
    half = keep_ref.shape[0]
    total = kept_ref[...] + came_ref[...]
    keep_ref[...] = total[:half]
    send_ref[...] = total[half:]


def deal_kernel(kept_ref, came_ref, *refs):
    deal(kept_ref[...] + came_ref[...], refs)


def weight_kernel(capacity, *refs):
    rows_refs, both_refs = refs[:4], refs[4:7]
    w_in_hbm, w_out_hbm, written_ref, w_in_ref, w_out_ref, sems = refs[7:]
    feats, hidden = w_in_ref.shape
    rows = jnp.concatenate([ref[:, :feats] for ref in rows_refs], axis=0)
    both = jnp.concatenate([ref[...] for ref in both_refs], axis=0).astype(F32)
    of_x = lax.broadcasted_iota(jnp.int32, both.shape, 0) % (2 * capacity) < capacity
    dpre = jnp.where(of_x, both, 0.0).astype(BF16)
    act = jnp.where(of_x, 0.0, both).astype(BF16)
    count = feats // PIECES
    copies = []
    for piece in range(PIECES):
        span = slice(piece * count, (piece + 1) * count)
        part = rows[:, span]
        w_in_ref[span] = lax.dot_general(part, dpre, ROWS_BY_ROWS, preferred_element_type=F32)
        w_out_ref[:, span] = lax.dot_general(act, part, ROWS_BY_ROWS, preferred_element_type=F32)
        span = pl.ds(piece * count, count)
        for source, target in (
            (w_in_ref.at[span], w_in_hbm.at[span]),
            (w_out_ref.at[:, span], w_out_hbm.at[:, span]),
        ):
            copy = pltpu.make_async_copy(source, target, sems.at[len(copies)])
            copy.start()
            copies.append(copy)
    for copy in copies:
        copy.wait()
    written_ref[...] = jnp.zeros(written_ref.shape, F32)


def combine_kernel(steps, *refs):
    kept_ref, came_refs = refs[0], refs[1:steps]
    place_ref, spread_ref, tokens_ref, gate_out_ref = refs[steps:]
    feats = tokens_ref.shape[1]
    capacity = kept_ref.shape[0]
    came = [ref[...].astype(F32) for ref in came_refs]
    half = steps // WINDOW
    own = sum(came[: half - 1], kept_ref[...])
    other = sum(came[half:], came[half - 1])
    slots = jnp.concatenate([own, other], axis=0)
    grads = slots[:, :feats]
    high = grads.astype(BF16)
    low = (grads - high.astype(F32)).astype(BF16)
    both = jnp.concatenate([high, low], axis=0)
    tokens_ref[...] = jnp.dot(spread_ref[...], both, preferred_element_type=F32).astype(BF16)
    slot_gate = jnp.sum(slots[:, feats:], axis=1, keepdims=True)
    picked = place_ref[: WINDOW * capacity].astype(F32) * slot_gate
    masks = place_ref[WINDOW * capacity :].astype(F32)
    result = jnp.zeros(gate_out_ref.shape, F32)
    for index in range(WINDOW):
        span = slice(index * capacity, (index + 1) * capacity)
        value = jnp.sum(picked[span], axis=0, keepdims=True)
        result = result + masks[2 * index : 2 * index + 2] * value
    gate_out_ref[...] = result


def swap(array, axes, bit):
    size = lax.axis_size(axes)
    return lax.ppermute(array, axes, [(index, index ^ bit) for index in range(size)])


def swap_nodes(array, step):
    return swap(array, ("node", "local"), step * lax.axis_size("local") + 1)


def join(pieces, after=()):
    rows, wide = pieces[0].shape
    rows *= len(pieces)
    shape = jax.ShapeDtypeStruct((rows, wide), BF16)
    return call(join_kernel, shape, 0, 4 * rows * wide, after=after)(*pieces)


def body(tokens, grad_out, routes, gates, w_in, w_out):
    nodes = lax.axis_size("node")
    locals_ = lax.axis_size("local")
    edatas = lax.axis_size("edata")
    tok_rows, feats = tokens.shape
    hidden = w_in.shape[1]
    capacity = 2 * tok_rows // EXPERTS
    slots = WINDOW * capacity
    wide = feats + LANES
    coded = 4 * hidden + LANES
    shape = jax.ShapeDtypeStruct
    hbm = pl.BlockSpec(memory_space=pltpu.HBM)
    vmem = pl.BlockSpec(memory_space=pltpu.VMEM)

    inputs = [
        pltpu.with_memory_space_constraint(value, pltpu.HBM)
        for value in (routes.T, gates.T, tokens, grad_out, w_in, w_out)
    ]
    own_rows, other_rows, place, spread, weights = call(
        gather_kernel,
        (
            pltpu.VMEM((2 * capacity, wide), BF16),
            pltpu.VMEM((2 * capacity, wide), BF16),
            pltpu.VMEM((slots + 16, tok_rows), BF16),
            pltpu.VMEM((tok_rows, 2 * slots), BF16),
            pltpu.VMEM((2 * hidden, feats), BF16),
        ),
        4 * slots * tok_rows * feats,
        4 * tok_rows * feats + 4 * hidden * feats,
        in_specs=[hbm] * 6,
        scratch_shapes=[
            pltpu.VMEM((2, tok_rows), jnp.int32),
            pltpu.VMEM((2, tok_rows), BF16),
            pltpu.VMEM((tok_rows, feats), BF16),
            pltpu.VMEM((tok_rows, feats), BF16),
            pltpu.SemaphoreType.DMA((3 + 2 * PIECES + feats // hidden,)),
        ],
    )(*inputs)

    other_weights = swap(weights, "local", 1)

    half_nodes = nodes // WINDOW
    pieces = [own_rows]
    for step in range(1, nodes):
        pieces.append(swap_nodes(own_rows if step < half_nodes else other_rows, step))
    rows = half_nodes * (locals_ // 2) * capacity
    last = ()
    chains = []
    held = []
    for chunk in (pieces[:half_nodes], pieces[half_nodes:]):
        chunk = join(chunk, last)
        bit = 2
        while bit < locals_:
            chunk = join([chunk, swap(chunk, "local", bit)])
            bit *= 2
        held.append(chunk)
        part, gate_rows = call(
            functools.partial(part_kernel, capacity),
            (shape((rows, coded), I16), shape((rows, LANES), F32)),
            16 * rows * feats * hidden,
            4 * rows * feats + 8 * feats * hidden,
            after=last,
        )(chunk, weights, other_weights)
        last = (part,)
        chains.append((part, swap(part, "edata", edatas // 2), gate_rows))
    bit = edatas // 4
    while bit:
        for index, (part, other, gate_rows) in enumerate(chains):
            part = call(
                add_codes_kernel,
                shape((rows, coded), I16),
                16 * rows * hidden,
                6 * rows * coded,
                after=last,
            )(part, other)
            last = (part,)
            chains[index] = (part, swap(part, "edata", bit), gate_rows)
        bit //= 2

    mine = []
    theirs = ()
    slots_back = []
    for index, (part, other, gate_rows) in enumerate(chains):
        dealt = [shape((capacity, wide), BF16 if index else F32)] * half_nodes
        own, packed, *slot_parts = call(
            functools.partial(slot_kernel, capacity, len(theirs)),
            [
                shape((2 * rows, hidden), BF16),
                shape(((1 + len(theirs)) * 2 * rows, hidden), BF16),
                *(dealt if locals_ == 2 else [shape((rows, wide), F32)]),
            ],
            4 * rows * feats * hidden,
            4 * feats * hidden + 4 * rows * feats,
            after=last,
        )(part, other, gate_rows, weights, other_weights, *theirs)
        last = (own,)
        mine.append(own)
        theirs = (packed,)
        if locals_ > 2:
            half = rows // 2
            keep, send = slot_parts[0][:half], slot_parts[0][half:]
            bit = locals_ // 2
            while bit > 2:
                half //= 2
                keep, send = call(
                    halve_kernel,
                    (shape((half, wide), F32),) * 2,
                    4 * half * wide,
                    24 * half * wide,
                )(keep, swap(send, "local", bit))
                bit //= 2
            slot_parts = call(deal_kernel, dealt, 4 * half * wide, 12 * half * wide)(
                keep, swap(send, "local", bit)
            )
        for step, send in enumerate(slot_parts, index * half_nodes):
            slots_back.append(swap_nodes(send, step) if step else send)
    came = [swap(chunk, "local", 1) for chunk in held]
    back = swap(theirs[0], "local", 1)
    grad_w_in, grad_w_out, written = call(
        functools.partial(weight_kernel, capacity),
        (shape((feats, hidden), F32), shape((hidden, feats), F32), shape((8, LANES), F32)),
        32 * rows * feats * hidden,
        8 * feats * hidden,
        in_specs=[vmem] * 7,
        after=slots_back[1:half_nodes],
        out_specs=[hbm, hbm, vmem],
        scratch_shapes=[
            pltpu.VMEM((feats, hidden), F32),
            pltpu.VMEM((hidden, feats), F32),
            pltpu.SemaphoreType.DMA((2 * PIECES,)),
        ],
    )(*held, *came, *mine, back)
    grad_tokens, grad_gates = call(
        functools.partial(combine_kernel, nodes),
        (shape((tok_rows, feats), BF16), shape((2, tok_rows), F32)),
        4 * slots * tok_rows * feats,
        2 * tok_rows * feats,
        after=(written,),
    )(*slots_back[:half_nodes], *reversed(slots_back[half_nodes:]), place, spread)
    return (grad_tokens, grad_gates.T, grad_w_in, grad_w_out)


def solution(mesh):
    in_specs = (
        P(("node", "local"), "edata"),
        P(("node", "local"), "edata"),
        P(("node", "local"), None),
        P(("node", "local"), None),
        P("edata", ("node", "local")),
        P(("node", "local"), "edata"),
    )
    out_specs = (
        P(("node", "local"), "edata"),
        P(("node", "local"), None),
        P("edata", ("node", "local")),
        P(("node", "local"), "edata"),
    )
    return jax.shard_map(body, mesh=mesh, in_specs=in_specs, out_specs=out_specs, check_vma=False)
```

```python
import functools

import jax
import jax.numpy as jnp
from jax import lax
from jax.experimental import pallas as pl
from jax.experimental.pallas import tpu as pltpu
from jax.sharding import PartitionSpec as P

EXPERTS = 64
WINDOW = 2
LANES = 128
PIECES = 4
VMEM_LIMIT = 40 * 1024 * 1024

BF16 = jnp.bfloat16
F32 = jnp.float32
I16 = jnp.int16
ROWS_BY_ROWS = (((0,), (0,)), ((), ()))
COLS_BY_COLS = (((1,), (1,)), ((), ()))


def gelu_pair(pre_act):
    coefficient = 0.7978845608028654
    square = pre_act * pre_act
    tanh_val = jnp.tanh(coefficient * (pre_act + 0.044715 * pre_act * square))
    half = 0.5 * (1.0 + tanh_val)
    activation = pre_act * half
    slopes = half + 0.5 * pre_act * (1.0 - tanh_val * tanh_val) * coefficient * (
        1.0 + 3.0 * 0.044715 * square
    )
    return (activation, slopes)


def call(kernel, out_shape, flops, moved, limit=VMEM_LIMIT, in_specs=None, after=(), **more):
    def run(*operands):
        given = in_specs or [pl.BlockSpec(memory_space=pltpu.VMEM)] * len(operands)
        return pl.pallas_call(
            lambda *refs: kernel(*refs[len(after) :]),
            out_shape=out_shape,
            in_specs=[pl.BlockSpec(memory_space=pl.ANY)] * len(after) + list(given),
            compiler_params=pltpu.CompilerParams(vmem_limit_bytes=limit),
            cost_estimate=pl.CostEstimate(flops=flops, bytes_accessed=moved, transcendentals=0),
            **more,
        )(*after, *operands)

    return run


def own_expert():
    half_nodes = lax.axis_size("node") // WINDOW
    return lax.axis_index("node") // half_nodes


def split_value(value):
    high = value.astype(BF16).astype(F32)
    lane = lax.broadcasted_iota(jnp.int32, (value.shape[0], LANES), 1)
    return jnp.where(lane == 0, high, jnp.where(lane == 1, value - high, 0.0))


def encode(values):
    top = jnp.max(jnp.abs(values), axis=1, keepdims=True)
    power = jnp.ceil(jnp.log2(jnp.maximum(top, 1e-30)))
    codes = jnp.round(values * (1.999 * jnp.exp2(14.0 - power)))
    return codes.astype(jnp.int32).astype(I16), power


def decode(codes, power):
    return codes.astype(jnp.int32).astype(F32) * (jnp.exp2(power - 14.0) / 1.999)


def store_codes(out_ref, pair):
    hidden = pair[0].shape[1]
    lane = lax.broadcasted_iota(jnp.int32, (pair[0].shape[0], LANES), 1)
    powers = []
    for index, values in enumerate(pair):
        codes, power = encode(values)
        out_ref[:, index * hidden : (index + 1) * hidden] = codes
        powers.append(power)
    powers = jnp.where(lane == 0, powers[0], powers[1])
    out_ref[:, 2 * hidden :] = powers.astype(jnp.int32).astype(I16)


def load_codes(ref):
    hidden = (ref.shape[1] - LANES) // 2
    powers = ref[:, 2 * hidden :].astype(jnp.int32).astype(F32)
    return [
        decode(ref[:, index * hidden : (index + 1) * hidden], powers[:, index : index + 1])
        for index in range(2)
    ]


def gather_kernel(routes_hbm, gates_hbm, tokens_hbm, grads_hbm, w_in_hbm, w_out_hbm, own_ref,
                  other_ref, place_ref, spread_ref, w_ref, routes_ref, gates_ref, tokens_ref,
                  grads_ref, sems):
    tok_rows, feats = tokens_ref.shape
    capacity = own_ref.shape[0] // 2
    slots = WINDOW * capacity
    copies = [
        pltpu.make_async_copy(routes_hbm, routes_ref, sems.at[0]),
        pltpu.make_async_copy(gates_hbm, gates_ref, sems.at[1]),
    ]
    count = tok_rows // PIECES
    for source, target in ((tokens_hbm, tokens_ref), (grads_hbm, grads_ref)):
        for piece in range(PIECES):
            span = pl.ds(piece * count, count)
            copies.append(
                pltpu.make_async_copy(source.at[span], target.at[span], sems.at[len(copies)])
            )
    hidden = w_out_hbm.shape[0]
    upper, lower = pl.ds(0, hidden), pl.ds(hidden, hidden)
    moves = [(w_out_hbm, w_ref.at[upper])]
    for block in range(0, feats, hidden):
        span = pl.ds(block, hidden)
        moves.append((w_in_hbm.at[span], w_ref.at[lower, span]))
    for source, target in moves:
        copies.append(pltpu.make_async_copy(source, target, sems.at[len(copies)]))
    for copy in copies:
        copy.start()
    earlier = lax.broadcasted_iota(jnp.int32, (tok_rows, tok_rows), 0) < lax.broadcasted_iota(
        jnp.int32, (tok_rows, tok_rows), 1
    )
    earlier = earlier.astype(F32).astype(BF16)
    slot_of = lax.broadcasted_iota(jnp.int32, (capacity, tok_rows), 0).astype(F32)
    row_of = lax.broadcasted_iota(jnp.int32, (8, tok_rows), 0)
    own = own_expert()
    copies[0].wait()
    copies[1].wait()
    routes = routes_ref[...]
    gates = gates_ref[...].astype(F32)
    hits = [(routes == expert).astype(F32) for expert in (own, 1 - own)]
    named = [hit[0:1] + hit[1:2] for hit in hits]
    weight = [hit * gates for hit in hits]
    weight = [value[0:1] + value[1:2] for value in weight]
    names = jnp.where(row_of == 0, named[0], jnp.where(row_of == 1, named[1], 0.0)).astype(BF16)
    before = jnp.dot(names, earlier, preferred_element_type=F32)
    parts = [jnp.where(before[e : e + 1] == slot_of, named[e], 0.0) for e in range(WINDOW)]
    place = jnp.concatenate(parts, axis=0).astype(BF16)
    place_ref[:slots] = place
    spread_ref[...] = jnp.concatenate(parts + parts, axis=0).T.astype(BF16)
    masks = jnp.zeros((16, tok_rows), F32)
    row_of = lax.broadcasted_iota(jnp.int32, masks.shape, 0)
    for index, hit in enumerate(hits):
        for k in range(2):
            masks = jnp.where(row_of == 2 * index + k, hit[k : k + 1], masks)
    place_ref[slots:] = masks.astype(BF16)
    for copy in copies[2 : 2 + PIECES]:
        copy.wait()
    rows_x = jnp.dot(place, tokens_ref[...], preferred_element_type=F32)
    for copy in copies[2 + PIECES : 2 + 2 * PIECES]:
        copy.wait()
    rows_dy = jnp.dot(place, grads_ref[...], preferred_element_type=F32)
    for expert, out_ref in ((0, own_ref), (1, other_ref)):
        span = slice(expert * capacity, (expert + 1) * capacity)
        out_ref[:, :feats] = jnp.concatenate([rows_x[span], rows_dy[span]], axis=0).astype(BF16)
        gate = jnp.sum(parts[expert] * weight[expert], axis=1, keepdims=True)
        gate = jnp.concatenate([gate, gate], axis=0)
        out_ref[:, feats:] = jnp.broadcast_to(gate, (2 * capacity, LANES)).astype(BF16)
    for copy in copies[2 + 2 * PIECES :]:
        copy.wait()


def join_kernel(*refs):
    *pieces, out_ref = refs
    rows = pieces[0].shape[0]
    for index, ref in enumerate(pieces):
        out_ref[index * rows : (index + 1) * rows] = ref[...]


def part_kernel(capacity, rows_ref, w_ref, w_other_ref, part_ref, gate_ref):
    feats = w_ref.shape[1]
    hidden = w_ref.shape[0] // 2
    groups = rows_ref.shape[0] // (2 * capacity)
    gate = rows_ref[:, feats:].astype(F32).reshape(groups, 2 * capacity, LANES)
    gate_ref[...] = gate[:, :capacity].reshape(groups * capacity, LANES)
    rows = rows_ref[:, :feats]
    pre = []
    back = []
    for ref in (w_ref, w_other_ref):
        pre.append(
            sum(
                jnp.dot(
                    rows[:, block : block + hidden],
                    ref[hidden:, block : block + hidden],
                    preferred_element_type=F32,
                )
                for block in range(0, feats, hidden)
            )
        )
        back.append(
            lax.dot_general(rows, ref[:hidden], COLS_BY_COLS, preferred_element_type=F32)
        )
    pair = []
    for values, span in ((pre, slice(0, capacity)), (back, slice(capacity, 2 * capacity))):
        values = jnp.concatenate(values, axis=1).reshape(groups, 2 * capacity, 2 * hidden)
        pair.append(values[:, span].reshape(groups * capacity, 2 * hidden))
    store_codes(part_ref, pair)


def add_codes_kernel(first_ref, second_ref, out_ref):
    pairs = zip(load_codes(first_ref), load_codes(second_ref))
    store_codes(out_ref, [first + second for first, second in pairs])


def deal(total, refs):
    each, wide = refs[0].shape
    feats = wide - LANES
    gate = split_value(jnp.sum(total[:, feats:], axis=1, keepdims=True))
    for index, ref in enumerate(refs):
        span = slice(index * each, (index + 1) * each)
        ref[:, :feats] = total[span, :feats].astype(ref.dtype)
        ref[:, feats:] = gate[span].astype(ref.dtype)


def slot_kernel(capacity, before, first_ref, second_ref, gate_ref, w_ref, w_other_ref, *refs):
    before_refs, (mine_ref, theirs_ref, *slot_refs) = refs[:before], refs[before:]
    hidden = w_ref.shape[0] // 2
    pairs = zip(load_codes(first_ref), load_codes(second_ref))
    pre, back = [first + second for first, second in pairs]
    gate = gate_ref[:, :1]
    activation, slopes = gelu_pair(pre)
    dpre = (gate * back * slopes).astype(BF16)
    act = gate * activation
    slot = []
    for block in range(0, w_ref.shape[1], hidden):
        span = slice(block, block + hidden)
        slot.append(
            sum(
                lax.dot_general(
                    part, ref[hidden:, span], COLS_BY_COLS, preferred_element_type=F32
                )
                for part, ref in ((dpre[:, :hidden], w_ref), (dpre[:, hidden:], w_other_ref))
            )
        )
    slot_gate = split_value(jnp.sum(activation * back, axis=1, keepdims=True))
    total = jnp.concatenate(slot + [slot_gate], axis=1)
    if len(slot_refs) == 1:
        slot_refs[0][...] = total
    else:
        deal(total, slot_refs)
    rows = dpre.shape[0]
    both = [
        value.reshape(rows // capacity, capacity, 2 * hidden) for value in (dpre.astype(F32), act)
    ]
    both = jnp.concatenate(both, axis=1).reshape(2 * rows, 2 * hidden).astype(BF16)
    mine_ref[...] = both[:, :hidden]
    count = 2 * rows
    for index, ref in enumerate(before_refs):
        theirs_ref[index * count : (index + 1) * count] = ref[...]
    theirs_ref[before * count :] = both[:, hidden:]


def halve_kernel(kept_ref, came_ref, keep_ref, send_ref):
    half = keep_ref.shape[0]
    total = kept_ref[...] + came_ref[...]
    keep_ref[...] = total[:half]
    send_ref[...] = total[half:]


def deal_kernel(kept_ref, came_ref, *refs):
    deal(kept_ref[...] + came_ref[...], refs)


def weight_kernel(capacity, *refs):
    rows_refs, both_refs = refs[:4], refs[4:7]
    w_in_hbm, w_out_hbm, written_ref, w_in_ref, w_out_ref, sems = refs[7:]
    feats, hidden = w_in_ref.shape
    rows = jnp.concatenate([ref[:, :feats] for ref in rows_refs], axis=0)
    both = jnp.concatenate([ref[...] for ref in both_refs], axis=0).astype(F32)
    of_x = lax.broadcasted_iota(jnp.int32, both.shape, 0) % (2 * capacity) < capacity
    dpre = jnp.where(of_x, both, 0.0).astype(BF16)
    act = jnp.where(of_x, 0.0, both).astype(BF16)
    count = feats // PIECES
    copies = []
    for piece in range(PIECES):
        span = slice(piece * count, (piece + 1) * count)
        part = rows[:, span]
        w_in_ref[span] = lax.dot_general(part, dpre, ROWS_BY_ROWS, preferred_element_type=F32)
        w_out_ref[:, span] = lax.dot_general(act, part, ROWS_BY_ROWS, preferred_element_type=F32)
        span = pl.ds(piece * count, count)
        for source, target in (
            (w_in_ref.at[span], w_in_hbm.at[span]),
            (w_out_ref.at[:, span], w_out_hbm.at[:, span]),
        ):
            copy = pltpu.make_async_copy(source, target, sems.at[len(copies)])
            copy.start()
            copies.append(copy)
    for copy in copies:
        copy.wait()
    written_ref[...] = jnp.zeros(written_ref.shape, F32)


def combine_kernel(steps, *refs):
    kept_ref, came_refs = refs[0], refs[1:steps]
    place_ref, spread_ref, tokens_ref, gate_out_ref = refs[steps:]
    feats = tokens_ref.shape[1]
    capacity = kept_ref.shape[0]
    came = [ref[...].astype(F32) for ref in came_refs]
    half = steps // WINDOW
    own = sum(came[: half - 1], kept_ref[...])
    other = sum(came[half:], came[half - 1])
    slots = jnp.concatenate([own, other], axis=0)
    grads = slots[:, :feats]
    high = grads.astype(BF16)
    low = (grads - high.astype(F32)).astype(BF16)
    both = jnp.concatenate([high, low], axis=0)
    tokens_ref[...] = jnp.dot(spread_ref[...], both, preferred_element_type=F32).astype(BF16)
    slot_gate = jnp.sum(slots[:, feats:], axis=1, keepdims=True)
    picked = place_ref[: WINDOW * capacity].astype(F32) * slot_gate
    masks = place_ref[WINDOW * capacity :].astype(F32)
    result = jnp.zeros(gate_out_ref.shape, F32)
    for index in range(WINDOW):
        span = slice(index * capacity, (index + 1) * capacity)
        value = jnp.sum(picked[span], axis=0, keepdims=True)
        result = result + masks[2 * index : 2 * index + 2] * value
    gate_out_ref[...] = result


def swap(array, axes, bit):
    size = lax.axis_size(axes)
    return lax.ppermute(array, axes, [(index, index ^ bit) for index in range(size)])


def swap_nodes(array, step):
    return swap(array, ("node", "local"), step * lax.axis_size("local") + 1)


def join(pieces, after=()):
    rows, wide = pieces[0].shape
    rows *= len(pieces)
    shape = jax.ShapeDtypeStruct((rows, wide), BF16)
    return call(join_kernel, shape, 0, 4 * rows * wide, after=after)(*pieces)


def body(tokens, grad_out, routes, gates, w_in, w_out):
    nodes = lax.axis_size("node")
    locals_ = lax.axis_size("local")
    edatas = lax.axis_size("edata")
    tok_rows, feats = tokens.shape
    hidden = w_in.shape[1]
    capacity = 2 * tok_rows // EXPERTS
    slots = WINDOW * capacity
    wide = feats + LANES
    coded = 4 * hidden + LANES
    shape = jax.ShapeDtypeStruct
    hbm = pl.BlockSpec(memory_space=pltpu.HBM)
    vmem = pl.BlockSpec(memory_space=pltpu.VMEM)

    inputs = [
        pltpu.with_memory_space_constraint(value, pltpu.HBM)
        for value in (routes.T, gates.T, tokens, grad_out, w_in, w_out)
    ]
    own_rows, other_rows, place, spread, weights = call(
        gather_kernel,
        (
            pltpu.VMEM((2 * capacity, wide), BF16),
            pltpu.VMEM((2 * capacity, wide), BF16),
            pltpu.VMEM((slots + 16, tok_rows), BF16),
            pltpu.VMEM((tok_rows, 2 * slots), BF16),
            pltpu.VMEM((2 * hidden, feats), BF16),
        ),
        4 * slots * tok_rows * feats,
        4 * tok_rows * feats + 4 * hidden * feats,
        in_specs=[hbm] * 6,
        scratch_shapes=[
            pltpu.VMEM((2, tok_rows), jnp.int32),
            pltpu.VMEM((2, tok_rows), BF16),
            pltpu.VMEM((tok_rows, feats), BF16),
            pltpu.VMEM((tok_rows, feats), BF16),
            pltpu.SemaphoreType.DMA((3 + 2 * PIECES + feats // hidden,)),
        ],
    )(*inputs)

    other_weights = swap(weights, "local", 1)

    quarter = nodes // 4
    far = [*range(quarter), *range(nodes - quarter, nodes)]
    near = list(range(quarter, nodes - quarter))
    half_nodes = nodes // WINDOW
    pieces = [own_rows]
    for step in range(1, nodes):
        pieces.append(swap_nodes(own_rows if step < half_nodes else other_rows, step))
    rows = half_nodes * (locals_ // 2) * capacity
    last = ()
    chains = []
    held = []
    for steps in (far, near):
        chunk = join([pieces[step] for step in steps], last)
        bit = 2
        while bit < locals_:
            chunk = join([chunk, swap(chunk, "local", bit)])
            bit *= 2
        held.append(chunk)
        part, gate_rows = call(
            functools.partial(part_kernel, capacity),
            (shape((rows, coded), I16), shape((rows, LANES), F32)),
            16 * rows * feats * hidden,
            4 * rows * feats + 8 * feats * hidden,
            after=last,
        )(chunk, weights, other_weights)
        last = (part,)
        chains.append((part, swap(part, "edata", edatas // 2), gate_rows))
    bit = edatas // 4
    while bit:
        for index, (part, other, gate_rows) in enumerate(chains):
            part = call(
                add_codes_kernel,
                shape((rows, coded), I16),
                16 * rows * hidden,
                6 * rows * coded,
                after=last,
            )(part, other)
            last = (part,)
            chains[index] = (part, swap(part, "edata", bit), gate_rows)
        bit //= 2

    mine = []
    theirs = ()
    slots_back = {}
    for index, (part, other, gate_rows) in enumerate(chains):
        dealt = [shape((capacity, wide), BF16 if index else F32)] * half_nodes
        own, packed, *slot_parts = call(
            functools.partial(slot_kernel, capacity, len(theirs)),
            [
                shape((2 * rows, hidden), BF16),
                shape(((1 + len(theirs)) * 2 * rows, hidden), BF16),
                *(dealt if locals_ == 2 else [shape((rows, wide), F32)]),
            ],
            4 * rows * feats * hidden,
            4 * feats * hidden + 4 * rows * feats,
            after=last,
        )(part, other, gate_rows, weights, other_weights, *theirs)
        last = (own,)
        mine.append(own)
        theirs = (packed,)
        if locals_ > 2:
            half = rows // 2
            keep, send = slot_parts[0][:half], slot_parts[0][half:]
            bit = locals_ // 2
            while bit > 2:
                half //= 2
                keep, send = call(
                    halve_kernel,
                    (shape((half, wide), F32),) * 2,
                    4 * half * wide,
                    24 * half * wide,
                )(keep, swap(send, "local", bit))
                bit //= 2
            slot_parts = call(deal_kernel, dealt, 4 * half * wide, 12 * half * wide)(
                keep, swap(send, "local", bit)
            )
        for step, send in zip(near if index else far, slot_parts):
            slots_back[step] = swap_nodes(send, step) if step else send
    came = [swap(chunk, "local", 1) for chunk in held]
    back = swap(theirs[0], "local", 1)
    grad_w_in, grad_w_out, written = call(
        functools.partial(weight_kernel, capacity),
        (shape((feats, hidden), F32), shape((hidden, feats), F32), shape((8, LANES), F32)),
        32 * rows * feats * hidden,
        8 * feats * hidden,
        in_specs=[vmem] * 7,
        after=[slots_back[step] for step in far[1:]],
        out_specs=[hbm, hbm, vmem],
        scratch_shapes=[
            pltpu.VMEM((feats, hidden), F32),
            pltpu.VMEM((hidden, feats), F32),
            pltpu.SemaphoreType.DMA((2 * PIECES,)),
        ],
    )(*held, *came, *mine, back)
    grad_tokens, grad_gates = call(
        functools.partial(combine_kernel, nodes),
        (shape((tok_rows, feats), BF16), shape((2, tok_rows), F32)),
        4 * slots * tok_rows * feats,
        2 * tok_rows * feats,
        after=(written,),
    )(*[slots_back[step] for step in range(nodes)], place, spread)
    return (grad_tokens, grad_gates.T, grad_w_in, grad_w_out)


def solution(mesh):
    in_specs = (
        P(("node", "local"), "edata"),
        P(("node", "local"), "edata"),
        P(("node", "local"), None),
        P(("node", "local"), None),
        P("edata", ("node", "local")),
        P(("node", "local"), "edata"),
    )
    out_specs = (
        P(("node", "local"), "edata"),
        P(("node", "local"), None),
        P("edata", ("node", "local")),
        P(("node", "local"), "edata"),
    )
    return jax.shard_map(body, mesh=mesh, in_specs=in_specs, out_specs=out_specs, check_vma=False)
```

```python
import functools

import jax
import jax.numpy as jnp
from jax import lax
from jax.experimental import pallas as pl
from jax.experimental.pallas import tpu as pltpu
from jax.sharding import PartitionSpec as P

EXPERTS = 64
WINDOW = 2
LANES = 128
PIECES = 4
VMEM_LIMIT = 40 * 1024 * 1024

BF16 = jnp.bfloat16
F32 = jnp.float32
I16 = jnp.int16
ROWS_BY_ROWS = (((0,), (0,)), ((), ()))
COLS_BY_COLS = (((1,), (1,)), ((), ()))


def gelu_pair(pre_act):
    coefficient = 0.7978845608028654
    square = pre_act * pre_act
    tanh_val = jnp.tanh(coefficient * (pre_act + 0.044715 * pre_act * square))
    half = 0.5 * (1.0 + tanh_val)
    activation = pre_act * half
    slopes = half + 0.5 * pre_act * (1.0 - tanh_val * tanh_val) * coefficient * (
        1.0 + 3.0 * 0.044715 * square
    )
    return (activation, slopes)


def call(kernel, out_shape, flops, moved, limit=VMEM_LIMIT, in_specs=None, after=(), **more):
    def run(*operands):
        given = in_specs or [pl.BlockSpec(memory_space=pltpu.VMEM)] * len(operands)
        return pl.pallas_call(
            lambda *refs: kernel(*refs[len(after) :]),
            out_shape=out_shape,
            in_specs=[pl.BlockSpec(memory_space=pl.ANY)] * len(after) + list(given),
            compiler_params=pltpu.CompilerParams(vmem_limit_bytes=limit),
            cost_estimate=pl.CostEstimate(flops=flops, bytes_accessed=moved, transcendentals=0),
            **more,
        )(*after, *operands)

    return run


def own_expert():
    half_nodes = lax.axis_size("node") // WINDOW
    return lax.axis_index("node") // half_nodes


def split_value(value):
    high = value.astype(BF16).astype(F32)
    lane = lax.broadcasted_iota(jnp.int32, (value.shape[0], LANES), 1)
    return jnp.where(lane == 0, high, jnp.where(lane == 1, value - high, 0.0))


def encode(values):
    top = jnp.max(jnp.abs(values), axis=1, keepdims=True)
    power = jnp.ceil(jnp.log2(jnp.maximum(top, 1e-30)))
    codes = jnp.round(values * (1.999 * jnp.exp2(14.0 - power)))
    return codes.astype(jnp.int32).astype(I16), power


def decode(codes, power):
    return codes.astype(jnp.int32).astype(F32) * (jnp.exp2(power - 14.0) / 1.999)


def store_codes(out_ref, pair):
    hidden = pair[0].shape[1]
    lane = lax.broadcasted_iota(jnp.int32, (pair[0].shape[0], LANES), 1)
    powers = []
    for index, values in enumerate(pair):
        codes, power = encode(values)
        out_ref[:, index * hidden : (index + 1) * hidden] = codes
        powers.append(power)
    powers = jnp.where(lane == 0, powers[0], powers[1])
    out_ref[:, 2 * hidden :] = powers.astype(jnp.int32).astype(I16)


def load_codes(ref):
    hidden = (ref.shape[1] - LANES) // 2
    powers = ref[:, 2 * hidden :].astype(jnp.int32).astype(F32)
    return [
        decode(ref[:, index * hidden : (index + 1) * hidden], powers[:, index : index + 1])
        for index in range(2)
    ]


def gather_kernel(routes_hbm, gates_hbm, tokens_hbm, grads_hbm, w_in_hbm, w_out_hbm, own_ref,
                  other_ref, place_ref, spread_ref, w_ref, routes_ref, gates_ref, tokens_ref,
                  grads_ref, sems):
    tok_rows, feats = tokens_ref.shape
    capacity = own_ref.shape[0] // 2
    slots = WINDOW * capacity
    copies = [
        pltpu.make_async_copy(routes_hbm, routes_ref, sems.at[0]),
        pltpu.make_async_copy(gates_hbm, gates_ref, sems.at[1]),
    ]
    count = tok_rows // PIECES
    for source, target in ((tokens_hbm, tokens_ref), (grads_hbm, grads_ref)):
        for piece in range(PIECES):
            span = pl.ds(piece * count, count)
            copies.append(
                pltpu.make_async_copy(source.at[span], target.at[span], sems.at[len(copies)])
            )
    hidden = w_out_hbm.shape[0]
    upper, lower = pl.ds(0, hidden), pl.ds(hidden, hidden)
    moves = [(w_out_hbm, w_ref.at[upper])]
    for block in range(0, feats, hidden):
        span = pl.ds(block, hidden)
        moves.append((w_in_hbm.at[span], w_ref.at[lower, span]))
    for source, target in moves:
        copies.append(pltpu.make_async_copy(source, target, sems.at[len(copies)]))
    for copy in copies:
        copy.start()
    earlier = lax.broadcasted_iota(jnp.int32, (tok_rows, tok_rows), 0) < lax.broadcasted_iota(
        jnp.int32, (tok_rows, tok_rows), 1
    )
    earlier = earlier.astype(F32).astype(BF16)
    slot_of = lax.broadcasted_iota(jnp.int32, (capacity, tok_rows), 0).astype(F32)
    row_of = lax.broadcasted_iota(jnp.int32, (8, tok_rows), 0)
    own = own_expert()
    copies[0].wait()
    copies[1].wait()
    routes = routes_ref[...]
    gates = gates_ref[...].astype(F32)
    hits = [(routes == expert).astype(F32) for expert in (own, 1 - own)]
    named = [hit[0:1] + hit[1:2] for hit in hits]
    weight = [hit * gates for hit in hits]
    weight = [value[0:1] + value[1:2] for value in weight]
    names = jnp.where(row_of == 0, named[0], jnp.where(row_of == 1, named[1], 0.0)).astype(BF16)
    before = jnp.dot(names, earlier, preferred_element_type=F32)
    parts = [jnp.where(before[e : e + 1] == slot_of, named[e], 0.0) for e in range(WINDOW)]
    place = jnp.concatenate(parts, axis=0).astype(BF16)
    place_ref[:slots] = place
    spread_ref[...] = jnp.concatenate(parts + parts, axis=0).T.astype(BF16)
    masks = jnp.zeros((16, tok_rows), F32)
    row_of = lax.broadcasted_iota(jnp.int32, masks.shape, 0)
    for index, hit in enumerate(hits):
        for k in range(2):
            masks = jnp.where(row_of == 2 * index + k, hit[k : k + 1], masks)
    place_ref[slots:] = masks.astype(BF16)
    for copy in copies[2 : 2 + PIECES]:
        copy.wait()
    rows_x = jnp.dot(place, tokens_ref[...], preferred_element_type=F32)
    for copy in copies[2 + PIECES : 2 + 2 * PIECES]:
        copy.wait()
    rows_dy = jnp.dot(place, grads_ref[...], preferred_element_type=F32)
    for expert, out_ref in ((0, own_ref), (1, other_ref)):
        span = slice(expert * capacity, (expert + 1) * capacity)
        out_ref[:, :feats] = jnp.concatenate([rows_x[span], rows_dy[span]], axis=0).astype(BF16)
        gate = jnp.sum(parts[expert] * weight[expert], axis=1, keepdims=True)
        gate = jnp.concatenate([gate, gate], axis=0)
        out_ref[:, feats:] = jnp.broadcast_to(gate, (2 * capacity, LANES)).astype(BF16)
    for copy in copies[2 + 2 * PIECES :]:
        copy.wait()


def join_kernel(*refs):
    *pieces, out_ref = refs
    rows = pieces[0].shape[0]
    for index, ref in enumerate(pieces):
        out_ref[index * rows : (index + 1) * rows] = ref[...]


def part_kernel(capacity, rows_ref, w_ref, w_other_ref, part_ref, gate_ref):
    feats = w_ref.shape[1]
    hidden = w_ref.shape[0] // 2
    groups = rows_ref.shape[0] // (2 * capacity)
    gate = rows_ref[:, feats:].astype(F32).reshape(groups, 2 * capacity, LANES)
    gate_ref[...] = gate[:, :capacity].reshape(groups * capacity, LANES)
    rows = rows_ref[:, :feats]
    pre = []
    back = []
    for ref in (w_ref, w_other_ref):
        pre.append(
            sum(
                jnp.dot(
                    rows[:, block : block + hidden],
                    ref[hidden:, block : block + hidden],
                    preferred_element_type=F32,
                )
                for block in range(0, feats, hidden)
            )
        )
        back.append(
            lax.dot_general(rows, ref[:hidden], COLS_BY_COLS, preferred_element_type=F32)
        )
    pair = []
    for values, span in ((pre, slice(0, capacity)), (back, slice(capacity, 2 * capacity))):
        values = jnp.concatenate(values, axis=1).reshape(groups, 2 * capacity, 2 * hidden)
        pair.append(values[:, span].reshape(groups * capacity, 2 * hidden))
    store_codes(part_ref, pair)


def add_codes_kernel(first_ref, second_ref, out_ref):
    pairs = zip(load_codes(first_ref), load_codes(second_ref))
    store_codes(out_ref, [first + second for first, second in pairs])


def deal(total, refs):
    each, wide = refs[0].shape
    feats = wide - LANES
    gate = split_value(jnp.sum(total[:, feats:], axis=1, keepdims=True))
    for index, ref in enumerate(refs):
        span = slice(index * each, (index + 1) * each)
        ref[:, :feats] = total[span, :feats].astype(ref.dtype)
        ref[:, feats:] = gate[span].astype(ref.dtype)


def slot_kernel(capacity, before, first_ref, second_ref, gate_ref, w_ref, w_other_ref, *refs):
    before_refs, (mine_ref, theirs_ref, *slot_refs) = refs[:before], refs[before:]
    hidden = w_ref.shape[0] // 2
    pairs = zip(load_codes(first_ref), load_codes(second_ref))
    pre, back = [first + second for first, second in pairs]
    gate = gate_ref[:, :1]
    activation, slopes = gelu_pair(pre)
    dpre = (gate * back * slopes).astype(BF16)
    act = gate * activation
    slot = []
    for block in range(0, w_ref.shape[1], hidden):
        span = slice(block, block + hidden)
        slot.append(
            sum(
                lax.dot_general(
                    part, ref[hidden:, span], COLS_BY_COLS, preferred_element_type=F32
                )
                for part, ref in ((dpre[:, :hidden], w_ref), (dpre[:, hidden:], w_other_ref))
            )
        )
    slot_gate = split_value(jnp.sum(activation * back, axis=1, keepdims=True))
    total = jnp.concatenate(slot + [slot_gate], axis=1)
    if len(slot_refs) == 1:
        slot_refs[0][...] = total
    else:
        deal(total, slot_refs)
    rows = dpre.shape[0]
    both = [
        value.reshape(rows // capacity, capacity, 2 * hidden) for value in (dpre.astype(F32), act)
    ]
    both = jnp.concatenate(both, axis=1).reshape(2 * rows, 2 * hidden).astype(BF16)
    mine_ref[...] = both[:, :hidden]
    count = 2 * rows
    for index, ref in enumerate(before_refs):
        theirs_ref[index * count : (index + 1) * count] = ref[...]
    theirs_ref[before * count :] = both[:, hidden:]


def halve_kernel(kept_ref, came_ref, keep_ref, send_ref):
    half = keep_ref.shape[0]
    total = kept_ref[...] + came_ref[...]
    keep_ref[...] = total[:half]
    send_ref[...] = total[half:]


def deal_kernel(kept_ref, came_ref, *refs):
    deal(kept_ref[...] + came_ref[...], refs)


def weight_kernel(capacity, *refs):
    rows_refs, both_refs = refs[:4], refs[4:7]
    w_in_hbm, w_out_hbm, written_ref, w_in_ref, w_out_ref, sems = refs[7:]
    feats, hidden = w_in_ref.shape
    rows = jnp.concatenate([ref[:, :feats] for ref in rows_refs], axis=0)
    both = jnp.concatenate([ref[...] for ref in both_refs], axis=0).astype(F32)
    of_x = lax.broadcasted_iota(jnp.int32, both.shape, 0) % (2 * capacity) < capacity
    dpre = jnp.where(of_x, both, 0.0).astype(BF16)
    act = jnp.where(of_x, 0.0, both).astype(BF16)
    count = feats // PIECES
    copies = []
    for piece in range(PIECES):
        span = slice(piece * count, (piece + 1) * count)
        part = rows[:, span]
        w_in_ref[span] = lax.dot_general(part, dpre, ROWS_BY_ROWS, preferred_element_type=F32)
        w_out_ref[:, span] = lax.dot_general(act, part, ROWS_BY_ROWS, preferred_element_type=F32)
        span = pl.ds(piece * count, count)
        for source, target in (
            (w_in_ref.at[span], w_in_hbm.at[span]),
            (w_out_ref.at[:, span], w_out_hbm.at[:, span]),
        ):
            copy = pltpu.make_async_copy(source, target, sems.at[len(copies)])
            copy.start()
            copies.append(copy)
    for copy in copies:
        copy.wait()
    written_ref[...] = jnp.zeros(written_ref.shape, F32)


def combine_kernel(steps, *refs):
    kept_ref, came_refs = refs[0], refs[1:steps]
    place_ref, spread_ref, tokens_ref, gate_out_ref = refs[steps:]
    feats = tokens_ref.shape[1]
    capacity = kept_ref.shape[0]
    came = [ref[...].astype(F32) for ref in came_refs]
    half = steps // WINDOW
    own = sum(came[: half - 1], kept_ref[...])
    other = sum(came[half:], came[half - 1])
    slots = jnp.concatenate([own, other], axis=0)
    grads = slots[:, :feats]
    high = grads.astype(BF16)
    low = (grads - high.astype(F32)).astype(BF16)
    both = jnp.concatenate([high, low], axis=0)
    tokens_ref[...] = jnp.dot(spread_ref[...], both, preferred_element_type=F32).astype(BF16)
    slot_gate = jnp.sum(slots[:, feats:], axis=1, keepdims=True)
    picked = place_ref[: WINDOW * capacity].astype(F32) * slot_gate
    masks = place_ref[WINDOW * capacity :].astype(F32)
    result = jnp.zeros(gate_out_ref.shape, F32)
    for index in range(WINDOW):
        span = slice(index * capacity, (index + 1) * capacity)
        value = jnp.sum(picked[span], axis=0, keepdims=True)
        result = result + masks[2 * index : 2 * index + 2] * value
    gate_out_ref[...] = result


def swap(array, axes, bit):
    size = lax.axis_size(axes)
    return lax.ppermute(array, axes, [(index, index ^ bit) for index in range(size)])


def swap_nodes(array, step):
    return swap(array, ("node", "local"), step * lax.axis_size("local") + 1)


def join(pieces, after=()):
    rows, wide = pieces[0].shape
    rows *= len(pieces)
    shape = jax.ShapeDtypeStruct((rows, wide), BF16)
    return call(join_kernel, shape, 0, 4 * rows * wide, after=after)(*pieces)


def body(tokens, grad_out, routes, gates, w_in, w_out):
    nodes = lax.axis_size("node")
    locals_ = lax.axis_size("local")
    edatas = lax.axis_size("edata")
    tok_rows, feats = tokens.shape
    hidden = w_in.shape[1]
    capacity = 2 * tok_rows // EXPERTS
    slots = WINDOW * capacity
    wide = feats + LANES
    coded = 4 * hidden + LANES
    shape = jax.ShapeDtypeStruct
    hbm = pl.BlockSpec(memory_space=pltpu.HBM)
    vmem = pl.BlockSpec(memory_space=pltpu.VMEM)

    inputs = [
        pltpu.with_memory_space_constraint(value, pltpu.HBM)
        for value in (routes.T, gates.T, tokens, grad_out, w_in, w_out)
    ]
    own_rows, other_rows, place, spread, weights = call(
        gather_kernel,
        (
            pltpu.VMEM((2 * capacity, wide), BF16),
            pltpu.VMEM((2 * capacity, wide), BF16),
            pltpu.VMEM((slots + 16, tok_rows), BF16),
            pltpu.VMEM((tok_rows, 2 * slots), BF16),
            pltpu.VMEM((2 * hidden, feats), BF16),
        ),
        4 * slots * tok_rows * feats,
        4 * tok_rows * feats + 4 * hidden * feats,
        in_specs=[hbm] * 6,
        scratch_shapes=[
            pltpu.VMEM((2, tok_rows), jnp.int32),
            pltpu.VMEM((2, tok_rows), BF16),
            pltpu.VMEM((tok_rows, feats), BF16),
            pltpu.VMEM((tok_rows, feats), BF16),
            pltpu.SemaphoreType.DMA((3 + 2 * PIECES + feats // hidden,)),
        ],
    )(*inputs)

    other_weights = swap(weights, "local", 1)

    quarter = nodes // 4
    far = [*range(quarter), *range(nodes - quarter, nodes)]
    near = list(range(quarter, nodes - quarter))
    half_nodes = nodes // WINDOW
    pieces = [own_rows]
    for step in range(1, nodes):
        pieces.append(swap_nodes(own_rows if step < half_nodes else other_rows, step))
    rows = half_nodes * (locals_ // 2) * capacity
    bits = [1 << place for place in range(edatas.bit_length() - 1)]
    orders = (bits[::-1], bits)
    last = ()
    chains = []
    held = []
    for steps, order in zip((far, near), orders):
        chunk = join([pieces[step] for step in steps], last)
        bit = 2
        while bit < locals_:
            chunk = join([chunk, swap(chunk, "local", bit)])
            bit *= 2
        held.append(chunk)
        part, gate_rows = call(
            functools.partial(part_kernel, capacity),
            (shape((rows, coded), I16), shape((rows, LANES), F32)),
            16 * rows * feats * hidden,
            4 * rows * feats + 8 * feats * hidden,
            after=last,
        )(chunk, weights, other_weights)
        last = (part,)
        chains.append((part, swap(part, "edata", order[0]), gate_rows))
    for stage in range(1, len(bits)):
        for index, (part, other, gate_rows) in enumerate(chains):
            part = call(
                add_codes_kernel,
                shape((rows, coded), I16),
                16 * rows * hidden,
                6 * rows * coded,
                after=last,
            )(part, other)
            last = (part,)
            chains[index] = (part, swap(part, "edata", orders[index][stage]), gate_rows)

    mine = []
    theirs = ()
    slots_back = {}
    for index, (part, other, gate_rows) in enumerate(chains):
        dealt = [shape((capacity, wide), BF16 if index else F32)] * half_nodes
        own, packed, *slot_parts = call(
            functools.partial(slot_kernel, capacity, len(theirs)),
            [
                shape((2 * rows, hidden), BF16),
                shape(((1 + len(theirs)) * 2 * rows, hidden), BF16),
                *(dealt if locals_ == 2 else [shape((rows, wide), F32)]),
            ],
            4 * rows * feats * hidden,
            4 * feats * hidden + 4 * rows * feats,
            after=last,
        )(part, other, gate_rows, weights, other_weights, *theirs)
        last = (own,)
        mine.append(own)
        theirs = (packed,)
        if locals_ > 2:
            half = rows // 2
            keep, send = slot_parts[0][:half], slot_parts[0][half:]
            bit = locals_ // 2
            while bit > 2:
                half //= 2
                keep, send = call(
                    halve_kernel,
                    (shape((half, wide), F32),) * 2,
                    4 * half * wide,
                    24 * half * wide,
                )(keep, swap(send, "local", bit))
                bit //= 2
            slot_parts = call(deal_kernel, dealt, 4 * half * wide, 12 * half * wide)(
                keep, swap(send, "local", bit)
            )
        for step, send in zip(near if index else far, slot_parts):
            slots_back[step] = swap_nodes(send, step) if step else send
    came = [swap(chunk, "local", 1) for chunk in held]
    back = swap(theirs[0], "local", 1)
    grad_w_in, grad_w_out, written = call(
        functools.partial(weight_kernel, capacity),
        (shape((feats, hidden), F32), shape((hidden, feats), F32), shape((8, LANES), F32)),
        32 * rows * feats * hidden,
        8 * feats * hidden,
        in_specs=[vmem] * 7,
        after=[slots_back[step] for step in far[1:]],
        out_specs=[hbm, hbm, vmem],
        scratch_shapes=[
            pltpu.VMEM((feats, hidden), F32),
            pltpu.VMEM((hidden, feats), F32),
            pltpu.SemaphoreType.DMA((2 * PIECES,)),
        ],
    )(*held, *came, *mine, back)
    grad_tokens, grad_gates = call(
        functools.partial(combine_kernel, nodes),
        (shape((tok_rows, feats), BF16), shape((2, tok_rows), F32)),
        4 * slots * tok_rows * feats,
        2 * tok_rows * feats,
        after=(written,),
    )(*[slots_back[step] for step in range(nodes)], place, spread)
    return (grad_tokens, grad_gates.T, grad_w_in, grad_w_out)


def solution(mesh):
    in_specs = (
        P(("node", "local"), "edata"),
        P(("node", "local"), "edata"),
        P(("node", "local"), None),
        P(("node", "local"), None),
        P("edata", ("node", "local")),
        P(("node", "local"), "edata"),
    )
    out_specs = (
        P(("node", "local"), "edata"),
        P(("node", "local"), None),
        P("edata", ("node", "local")),
        P(("node", "local"), "edata"),
    )
    return jax.shard_map(body, mesh=mesh, in_specs=in_specs, out_specs=out_specs, check_vma=False)
```

```python
import functools

import jax
import jax.numpy as jnp
from jax import lax
from jax.experimental import pallas as pl
from jax.experimental.pallas import tpu as pltpu
from jax.sharding import PartitionSpec as P

EXPERTS = 64
WINDOW = 2
LANES = 128
PIECES = 4
VMEM_LIMIT = 40 * 1024 * 1024

BF16 = jnp.bfloat16
F32 = jnp.float32
I16 = jnp.int16
ROWS_BY_ROWS = (((0,), (0,)), ((), ()))
COLS_BY_COLS = (((1,), (1,)), ((), ()))


def gelu_pair(pre_act):
    coefficient = 0.7978845608028654
    square = pre_act * pre_act
    tanh_val = jnp.tanh(coefficient * (pre_act + 0.044715 * pre_act * square))
    half = 0.5 * (1.0 + tanh_val)
    activation = pre_act * half
    slopes = half + 0.5 * pre_act * (1.0 - tanh_val * tanh_val) * coefficient * (
        1.0 + 3.0 * 0.044715 * square
    )
    return (activation, slopes)


def call(kernel, out_shape, flops, moved, limit=VMEM_LIMIT, in_specs=None, after=(), **more):
    def run(*operands):
        given = in_specs or [pl.BlockSpec(memory_space=pltpu.VMEM)] * len(operands)
        return pl.pallas_call(
            lambda *refs: kernel(*refs[len(after) :]),
            out_shape=out_shape,
            in_specs=[pl.BlockSpec(memory_space=pl.ANY)] * len(after) + list(given),
            compiler_params=pltpu.CompilerParams(vmem_limit_bytes=limit),
            cost_estimate=pl.CostEstimate(flops=flops, bytes_accessed=moved, transcendentals=0),
            **more,
        )(*after, *operands)

    return run


def own_expert():
    half_nodes = lax.axis_size("node") // WINDOW
    return lax.axis_index("node") // half_nodes


def split_value(value):
    high = value.astype(BF16).astype(F32)
    lane = lax.broadcasted_iota(jnp.int32, (value.shape[0], LANES), 1)
    return jnp.where(lane == 0, high, jnp.where(lane == 1, value - high, 0.0))


def encode(values):
    top = jnp.max(jnp.abs(values), axis=1, keepdims=True)
    power = jnp.ceil(jnp.log2(jnp.maximum(top, 1e-30)))
    codes = jnp.round(values * (1.999 * jnp.exp2(14.0 - power)))
    return codes.astype(jnp.int32).astype(I16), power


def decode(codes, power):
    return codes.astype(jnp.int32).astype(F32) * (jnp.exp2(power - 14.0) / 1.999)


def store_codes(out_ref, pair):
    hidden = pair[0].shape[1]
    lane = lax.broadcasted_iota(jnp.int32, (pair[0].shape[0], LANES), 1)
    powers = []
    for index, values in enumerate(pair):
        codes, power = encode(values)
        out_ref[:, index * hidden : (index + 1) * hidden] = codes
        powers.append(power)
    powers = jnp.where(lane == 0, powers[0], powers[1])
    out_ref[:, 2 * hidden :] = powers.astype(jnp.int32).astype(I16)


def load_codes(ref):
    hidden = (ref.shape[1] - LANES) // 2
    powers = ref[:, 2 * hidden :].astype(jnp.int32).astype(F32)
    return [
        decode(ref[:, index * hidden : (index + 1) * hidden], powers[:, index : index + 1])
        for index in range(2)
    ]


def gather_kernel(routes_hbm, gates_hbm, tokens_hbm, grads_hbm, w_in_hbm, w_out_hbm, own_ref,
                  other_ref, place_ref, spread_ref, w_ref, routes_ref, gates_ref, tokens_ref,
                  grads_ref, sems):
    tok_rows, feats = tokens_ref.shape
    capacity = own_ref.shape[0] // 2
    slots = WINDOW * capacity
    copies = [
        pltpu.make_async_copy(routes_hbm, routes_ref, sems.at[0]),
        pltpu.make_async_copy(gates_hbm, gates_ref, sems.at[1]),
    ]
    count = tok_rows // PIECES
    for source, target in ((tokens_hbm, tokens_ref), (grads_hbm, grads_ref)):
        for piece in range(PIECES):
            span = pl.ds(piece * count, count)
            copies.append(
                pltpu.make_async_copy(source.at[span], target.at[span], sems.at[len(copies)])
            )
    hidden = w_out_hbm.shape[0]
    upper, lower = pl.ds(0, hidden), pl.ds(hidden, hidden)
    moves = [(w_out_hbm, w_ref.at[upper])]
    for block in range(0, feats, hidden):
        span = pl.ds(block, hidden)
        moves.append((w_in_hbm.at[span], w_ref.at[lower, span]))
    for source, target in moves:
        copies.append(pltpu.make_async_copy(source, target, sems.at[len(copies)]))
    for copy in copies:
        copy.start()
    earlier = lax.broadcasted_iota(jnp.int32, (tok_rows, tok_rows), 0) < lax.broadcasted_iota(
        jnp.int32, (tok_rows, tok_rows), 1
    )
    earlier = earlier.astype(F32).astype(BF16)
    slot_of = lax.broadcasted_iota(jnp.int32, (capacity, tok_rows), 0).astype(F32)
    row_of = lax.broadcasted_iota(jnp.int32, (8, tok_rows), 0)
    own = own_expert()
    copies[0].wait()
    copies[1].wait()
    routes = routes_ref[...]
    gates = gates_ref[...].astype(F32)
    hits = [(routes == expert).astype(F32) for expert in (own, 1 - own)]
    named = [hit[0:1] + hit[1:2] for hit in hits]
    weight = [hit * gates for hit in hits]
    weight = [value[0:1] + value[1:2] for value in weight]
    names = jnp.where(row_of == 0, named[0], jnp.where(row_of == 1, named[1], 0.0)).astype(BF16)
    before = jnp.dot(names, earlier, preferred_element_type=F32)
    parts = [jnp.where(before[e : e + 1] == slot_of, named[e], 0.0) for e in range(WINDOW)]
    place = jnp.concatenate(parts, axis=0).astype(BF16)
    place_ref[:slots] = place
    spread_ref[...] = jnp.concatenate(parts + parts, axis=0).T.astype(BF16)
    masks = jnp.zeros((16, tok_rows), F32)
    row_of = lax.broadcasted_iota(jnp.int32, masks.shape, 0)
    for index, hit in enumerate(hits):
        for k in range(2):
            masks = jnp.where(row_of == 2 * index + k, hit[k : k + 1], masks)
    place_ref[slots:] = masks.astype(BF16)
    for copy in copies[2 : 2 + PIECES]:
        copy.wait()
    rows_x = jnp.dot(place, tokens_ref[...], preferred_element_type=F32)
    for copy in copies[2 + PIECES : 2 + 2 * PIECES]:
        copy.wait()
    rows_dy = jnp.dot(place, grads_ref[...], preferred_element_type=F32)
    for expert, out_ref in ((0, own_ref), (1, other_ref)):
        span = slice(expert * capacity, (expert + 1) * capacity)
        out_ref[:, :feats] = jnp.concatenate([rows_x[span], rows_dy[span]], axis=0).astype(BF16)
        gate = jnp.sum(parts[expert] * weight[expert], axis=1, keepdims=True)
        gate = jnp.concatenate([gate, gate], axis=0)
        out_ref[:, feats:] = jnp.broadcast_to(gate, (2 * capacity, LANES)).astype(BF16)
    for copy in copies[2 + 2 * PIECES :]:
        copy.wait()


def join_kernel(*refs):
    *pieces, out_ref = refs
    start = 0
    for ref in pieces:
        out_ref[start : start + ref.shape[0]] = ref[...]
        start += ref.shape[0]


def part_kernel(capacity, rows_ref, w_ref, w_other_ref, part_ref, gate_ref):
    feats = w_ref.shape[1]
    hidden = w_ref.shape[0] // 2
    groups = rows_ref.shape[0] // (2 * capacity)
    gate = rows_ref[:, feats:].astype(F32).reshape(groups, 2 * capacity, LANES)
    gate_ref[...] = gate[:, :capacity].reshape(groups * capacity, LANES)
    rows = rows_ref[:, :feats]
    pre = []
    back = []
    for ref in (w_ref, w_other_ref):
        pre.append(
            sum(
                jnp.dot(
                    rows[:, block : block + hidden],
                    ref[hidden:, block : block + hidden],
                    preferred_element_type=F32,
                )
                for block in range(0, feats, hidden)
            )
        )
        back.append(
            lax.dot_general(rows, ref[:hidden], COLS_BY_COLS, preferred_element_type=F32)
        )
    pair = []
    for values, span in ((pre, slice(0, capacity)), (back, slice(capacity, 2 * capacity))):
        values = jnp.concatenate(values, axis=1).reshape(groups, 2 * capacity, 2 * hidden)
        pair.append(values[:, span].reshape(groups * capacity, 2 * hidden))
    store_codes(part_ref, pair)


def add_codes_kernel(first_ref, second_ref, out_ref):
    pairs = zip(load_codes(first_ref), load_codes(second_ref))
    store_codes(out_ref, [first + second for first, second in pairs])


def deal(total, refs):
    each, wide = refs[0].shape
    feats = wide - LANES
    gate = split_value(jnp.sum(total[:, feats:], axis=1, keepdims=True))
    for index, ref in enumerate(refs):
        span = slice(index * each, (index + 1) * each)
        ref[:, :feats] = total[span, :feats].astype(ref.dtype)
        ref[:, feats:] = gate[span].astype(ref.dtype)


def slot_kernel(capacity, before, first_ref, second_ref, gate_ref, w_ref, w_other_ref, *refs):
    before_refs, (mine_ref, theirs_ref, *slot_refs) = refs[:before], refs[before:]
    hidden = w_ref.shape[0] // 2
    pairs = zip(load_codes(first_ref), load_codes(second_ref))
    pre, back = [first + second for first, second in pairs]
    gate = gate_ref[:, :1]
    activation, slopes = gelu_pair(pre)
    dpre = (gate * back * slopes).astype(BF16)
    act = gate * activation
    slot = []
    for block in range(0, w_ref.shape[1], hidden):
        span = slice(block, block + hidden)
        slot.append(
            sum(
                lax.dot_general(
                    part, ref[hidden:, span], COLS_BY_COLS, preferred_element_type=F32
                )
                for part, ref in ((dpre[:, :hidden], w_ref), (dpre[:, hidden:], w_other_ref))
            )
        )
    slot_gate = split_value(jnp.sum(activation * back, axis=1, keepdims=True))
    total = jnp.concatenate(slot + [slot_gate], axis=1)
    if len(slot_refs) == 1:
        slot_refs[0][...] = total
    else:
        deal(total, slot_refs)
    rows = dpre.shape[0]
    both = [
        value.reshape(rows // capacity, capacity, 2 * hidden) for value in (dpre.astype(F32), act)
    ]
    both = jnp.concatenate(both, axis=1).reshape(2 * rows, 2 * hidden).astype(BF16)
    mine_ref[...] = both[:, :hidden]
    count = 2 * rows
    for index, ref in enumerate(before_refs):
        theirs_ref[index * count : (index + 1) * count] = ref[...]
    theirs_ref[before * count :] = both[:, hidden:]


def halve_kernel(kept_ref, came_ref, keep_ref, send_ref):
    half = keep_ref.shape[0]
    total = kept_ref[...] + came_ref[...]
    keep_ref[...] = total[:half]
    send_ref[...] = total[half:]


def deal_kernel(kept_ref, came_ref, *refs):
    deal(kept_ref[...] + came_ref[...], refs)


def weight_kernel(capacity, *refs):
    rows_refs, both_refs = refs[:2], refs[2:4]
    w_in_hbm, w_out_hbm, written_ref, w_in_ref, w_out_ref, sems = refs[4:]
    feats, hidden = w_in_ref.shape
    rows = jnp.concatenate([ref[:, :feats] for ref in rows_refs], axis=0)
    both = jnp.concatenate([ref[...] for ref in both_refs], axis=0).astype(F32)
    of_x = lax.broadcasted_iota(jnp.int32, both.shape, 0) % (2 * capacity) < capacity
    dpre = jnp.where(of_x, both, 0.0).astype(BF16)
    act = jnp.where(of_x, 0.0, both).astype(BF16)
    count = feats // PIECES
    copies = []
    for piece in range(PIECES):
        span = slice(piece * count, (piece + 1) * count)
        part = rows[:, span]
        w_in_ref[span] = lax.dot_general(part, dpre, ROWS_BY_ROWS, preferred_element_type=F32)
        w_out_ref[:, span] = lax.dot_general(act, part, ROWS_BY_ROWS, preferred_element_type=F32)
        span = pl.ds(piece * count, count)
        for source, target in (
            (w_in_ref.at[span], w_in_hbm.at[span]),
            (w_out_ref.at[:, span], w_out_hbm.at[:, span]),
        ):
            copy = pltpu.make_async_copy(source, target, sems.at[len(copies)])
            copy.start()
            copies.append(copy)
    for copy in copies:
        copy.wait()
    written_ref[...] = jnp.zeros(written_ref.shape, F32)


def combine_kernel(steps, *refs):
    slot_refs = dict(zip(steps, refs))
    place_ref, spread_ref, tokens_ref, gate_out_ref = refs[len(steps) :]
    feats = tokens_ref.shape[1]
    capacity = slot_refs[0].shape[0]
    half = len(steps) // WINDOW
    came = [slot_refs[step][...].astype(F32) for step in range(len(steps))]
    own = sum(came[1:half], came[0])
    other = sum(came[half + 1 :], came[half])
    slots = jnp.concatenate([own, other], axis=0)
    grads = slots[:, :feats]
    high = grads.astype(BF16)
    low = (grads - high.astype(F32)).astype(BF16)
    both = jnp.concatenate([high, low], axis=0)
    tokens_ref[...] = jnp.dot(spread_ref[...], both, preferred_element_type=F32).astype(BF16)
    slot_gate = jnp.sum(slots[:, feats:], axis=1, keepdims=True)
    picked = place_ref[: WINDOW * capacity].astype(F32) * slot_gate
    masks = place_ref[WINDOW * capacity :].astype(F32)
    result = jnp.zeros(gate_out_ref.shape, F32)
    for index in range(WINDOW):
        span = slice(index * capacity, (index + 1) * capacity)
        value = jnp.sum(picked[span], axis=0, keepdims=True)
        result = result + masks[2 * index : 2 * index + 2] * value
    gate_out_ref[...] = result


def swap(array, axes, bit):
    size = lax.axis_size(axes)
    return lax.ppermute(array, axes, [(index, index ^ bit) for index in range(size)])


def swap_nodes(array, step):
    return swap(array, ("node", "local"), step * lax.axis_size("local") + 1)


def join(pieces):
    wide = pieces[0].shape[1]
    rows = sum(piece.shape[0] for piece in pieces)
    return call(join_kernel, jax.ShapeDtypeStruct((rows, wide), BF16), 0, 4 * rows * wide)(*pieces)


def body(tokens, grad_out, routes, gates, w_in, w_out):
    nodes = lax.axis_size("node")
    locals_ = lax.axis_size("local")
    edatas = lax.axis_size("edata")
    tok_rows, feats = tokens.shape
    hidden = w_in.shape[1]
    capacity = 2 * tok_rows // EXPERTS
    slots = WINDOW * capacity
    wide = feats + LANES
    coded = 4 * hidden + LANES
    shape = jax.ShapeDtypeStruct
    hbm = pl.BlockSpec(memory_space=pltpu.HBM)
    vmem = pl.BlockSpec(memory_space=pltpu.VMEM)

    inputs = [
        pltpu.with_memory_space_constraint(value, pltpu.HBM)
        for value in (routes.T, gates.T, tokens, grad_out, w_in, w_out)
    ]
    own_rows, other_rows, place, spread, weights = call(
        gather_kernel,
        (
            pltpu.VMEM((2 * capacity, wide), BF16),
            pltpu.VMEM((2 * capacity, wide), BF16),
            pltpu.VMEM((slots + 16, tok_rows), BF16),
            pltpu.VMEM((tok_rows, 2 * slots), BF16),
            pltpu.VMEM((2 * hidden, feats), BF16),
        ),
        4 * slots * tok_rows * feats,
        4 * tok_rows * feats + 4 * hidden * feats,
        in_specs=[hbm] * 6,
        scratch_shapes=[
            pltpu.VMEM((2, tok_rows), jnp.int32),
            pltpu.VMEM((2, tok_rows), BF16),
            pltpu.VMEM((tok_rows, feats), BF16),
            pltpu.VMEM((tok_rows, feats), BF16),
            pltpu.SemaphoreType.DMA((3 + 2 * PIECES + feats // hidden,)),
        ],
    )(*inputs)

    other_weights = swap(weights, "local", 1)

    quarter = nodes // 4
    far = [*range(quarter), *range(nodes - quarter, nodes)]
    steps = [*far, *range(quarter, nodes - quarter)]
    pieces = [
        swap_nodes(own_rows if step < nodes // WINDOW else other_rows, step) if step else own_rows
        for step in steps
    ]
    held = join([join(pieces[: len(far)]), *pieces[len(far) :]])
    bit = 2
    while bit < locals_:
        held = join([held, swap(held, "local", bit)])
        bit *= 2
    rows = nodes * (locals_ // 2) * capacity
    part, gate_rows = call(
        functools.partial(part_kernel, capacity),
        (shape((rows, coded), I16), shape((rows, LANES), F32)),
        16 * rows * feats * hidden,
        4 * rows * feats + 8 * feats * hidden,
    )(held, weights, other_weights)
    bit = edatas // 2
    other = swap(part, "edata", bit)
    came = swap(held, "local", 1)
    while bit > 1:
        part = call(
            add_codes_kernel, shape((rows, coded), I16), 16 * rows * hidden, 6 * rows * coded
        )(part, other)
        bit //= 2
        other = swap(part, "edata", bit)

    dealt = [shape((capacity, wide), BF16 if step else F32) for step in steps]
    mine, theirs, *slot_parts = call(
        functools.partial(slot_kernel, capacity, 0),
        [
            *[shape((2 * rows, hidden), BF16)] * 2,
            *(dealt if locals_ == 2 else [shape((rows, wide), F32)]),
        ],
        4 * rows * feats * hidden,
        4 * feats * hidden + 4 * rows * feats,
    )(part, other, gate_rows, weights, other_weights)
    if locals_ > 2:
        half = rows // 2
        keep, send = slot_parts[0][:half], slot_parts[0][half:]
        bit = locals_ // 2
        while bit > 2:
            half //= 2
            keep, send = call(
                halve_kernel, (shape((half, wide), F32),) * 2, 4 * half * wide, 24 * half * wide
            )(keep, swap(send, "local", bit))
            bit //= 2
        slot_parts = call(deal_kernel, dealt, 4 * half * wide, 12 * half * wide)(
            keep, swap(send, "local", bit)
        )
    returned = [
        swap_nodes(send, step) if step else send for step, send in zip(steps, slot_parts)
    ]
    back = swap(theirs, "local", 1)
    grad_w_in, grad_w_out, written = call(
        functools.partial(weight_kernel, capacity),
        (shape((feats, hidden), F32), shape((hidden, feats), F32), shape((8, LANES), F32)),
        16 * rows * feats * hidden,
        8 * feats * hidden,
        in_specs=[vmem] * 4,
        out_specs=[hbm, hbm, vmem],
        scratch_shapes=[
            pltpu.VMEM((feats, hidden), F32),
            pltpu.VMEM((hidden, feats), F32),
            pltpu.SemaphoreType.DMA((2 * PIECES,)),
        ],
    )(held, came, mine, back)
    grad_tokens, grad_gates = call(
        functools.partial(combine_kernel, steps),
        (shape((tok_rows, feats), BF16), shape((2, tok_rows), F32)),
        4 * slots * tok_rows * feats,
        2 * tok_rows * feats,
        after=(written,),
    )(*returned, place, spread)
    return (grad_tokens, grad_gates.T, grad_w_in, grad_w_out)


def solution(mesh):
    in_specs = (
        P(("node", "local"), "edata"),
        P(("node", "local"), "edata"),
        P(("node", "local"), None),
        P(("node", "local"), None),
        P("edata", ("node", "local")),
        P(("node", "local"), "edata"),
    )
    out_specs = (
        P(("node", "local"), "edata"),
        P(("node", "local"), None),
        P("edata", ("node", "local")),
        P(("node", "local"), "edata"),
    )
    return jax.shard_map(body, mesh=mesh, in_specs=in_specs, out_specs=out_specs, check_vma=False)
```

```python
import functools

import jax
import jax.numpy as jnp
from jax import lax
from jax.experimental import pallas as pl
from jax.experimental.pallas import tpu as pltpu
from jax.sharding import PartitionSpec as P

EXPERTS = 64
WINDOW = 2
LANES = 128
PIECES = 4
VMEM_LIMIT = 40 * 1024 * 1024

BF16 = jnp.bfloat16
F32 = jnp.float32
I16 = jnp.int16
ROWS_BY_ROWS = (((0,), (0,)), ((), ()))
COLS_BY_COLS = (((1,), (1,)), ((), ()))


def gelu_pair(pre_act):
    coefficient = 0.7978845608028654
    square = pre_act * pre_act
    tanh_val = jnp.tanh(coefficient * (pre_act + 0.044715 * pre_act * square))
    half = 0.5 * (1.0 + tanh_val)
    activation = pre_act * half
    slopes = half + 0.5 * pre_act * (1.0 - tanh_val * tanh_val) * coefficient * (
        1.0 + 3.0 * 0.044715 * square
    )
    return (activation, slopes)


def call(kernel, out_shape, flops, moved, limit=VMEM_LIMIT, in_specs=None, after=(), **more):
    def run(*operands):
        given = in_specs or [pl.BlockSpec(memory_space=pltpu.VMEM)] * len(operands)
        return pl.pallas_call(
            lambda *refs: kernel(*refs[len(after) :]),
            out_shape=out_shape,
            in_specs=[pl.BlockSpec(memory_space=pl.ANY)] * len(after) + list(given),
            compiler_params=pltpu.CompilerParams(vmem_limit_bytes=limit),
            cost_estimate=pl.CostEstimate(flops=flops, bytes_accessed=moved, transcendentals=0),
            **more,
        )(*after, *operands)

    return run


def own_expert():
    half_nodes = lax.axis_size("node") // WINDOW
    return lax.axis_index("node") // half_nodes


def split_value(value):
    high = value.astype(BF16).astype(F32)
    lane = lax.broadcasted_iota(jnp.int32, (value.shape[0], LANES), 1)
    return jnp.where(lane == 0, high, jnp.where(lane == 1, value - high, 0.0))


def encode(values):
    top = jnp.max(jnp.abs(values), axis=1, keepdims=True)
    power = jnp.ceil(jnp.log2(jnp.maximum(top, 1e-30)))
    codes = jnp.round(values * (1.999 * jnp.exp2(14.0 - power)))
    return codes.astype(jnp.int32).astype(I16), power


def decode(codes, power):
    return codes.astype(jnp.int32).astype(F32) * (jnp.exp2(power - 14.0) / 1.999)


def store_codes(out_ref, pair):
    hidden = pair[0].shape[1]
    lane = lax.broadcasted_iota(jnp.int32, (pair[0].shape[0], LANES), 1)
    powers = []
    for index, values in enumerate(pair):
        codes, power = encode(values)
        out_ref[:, index * hidden : (index + 1) * hidden] = codes
        powers.append(power)
    powers = jnp.where(lane == 0, powers[0], powers[1])
    out_ref[:, 2 * hidden :] = powers.astype(jnp.int32).astype(I16)


def load_codes(ref):
    hidden = (ref.shape[1] - LANES) // 2
    powers = ref[:, 2 * hidden :].astype(jnp.int32).astype(F32)
    return [
        decode(ref[:, index * hidden : (index + 1) * hidden], powers[:, index : index + 1])
        for index in range(2)
    ]


def gather_kernel(routes_hbm, gates_hbm, tokens_hbm, grads_hbm, w_in_hbm, w_out_hbm, own_ref,
                  other_ref, place_ref, routes_ref, w_ref, gates_ref, tokens_ref, grads_ref, sems):
    tok_rows, feats = tokens_ref.shape
    capacity = own_ref.shape[0] // 2
    slots = WINDOW * capacity
    copies = [
        pltpu.make_async_copy(routes_hbm, routes_ref, sems.at[0]),
        pltpu.make_async_copy(gates_hbm, gates_ref, sems.at[1]),
    ]
    count = tok_rows // PIECES
    for source, target in ((tokens_hbm, tokens_ref), (grads_hbm, grads_ref)):
        for piece in range(PIECES):
            span = pl.ds(piece * count, count)
            copies.append(
                pltpu.make_async_copy(source.at[span], target.at[span], sems.at[len(copies)])
            )
    hidden = w_out_hbm.shape[0]
    upper, lower = pl.ds(0, hidden), pl.ds(hidden, hidden)
    moves = [(w_out_hbm, w_ref.at[upper])]
    for block in range(0, feats, hidden):
        span = pl.ds(block, hidden)
        moves.append((w_in_hbm.at[span], w_ref.at[lower, span]))
    for source, target in moves:
        copies.append(pltpu.make_async_copy(source, target, sems.at[len(copies)]))
    for copy in copies:
        copy.start()
    earlier = lax.broadcasted_iota(jnp.int32, (tok_rows, tok_rows), 0) < lax.broadcasted_iota(
        jnp.int32, (tok_rows, tok_rows), 1
    )
    earlier = earlier.astype(F32).astype(BF16)
    slot_of = lax.broadcasted_iota(jnp.int32, (capacity, tok_rows), 0).astype(F32)
    row_of = lax.broadcasted_iota(jnp.int32, (8, tok_rows), 0)
    own = own_expert()
    copies[0].wait()
    copies[1].wait()
    routes = routes_ref[...]
    gates = gates_ref[...].astype(F32)
    hits = [(routes == expert).astype(F32) for expert in (own, 1 - own)]
    named = [hit[0:1] + hit[1:2] for hit in hits]
    weight = [hit * gates for hit in hits]
    weight = [value[0:1] + value[1:2] for value in weight]
    names = jnp.where(row_of == 0, named[0], jnp.where(row_of == 1, named[1], 0.0)).astype(BF16)
    before = jnp.dot(names, earlier, preferred_element_type=F32)
    parts = [jnp.where(before[e : e + 1] == slot_of, named[e], 0.0) for e in range(WINDOW)]
    place = jnp.concatenate(parts, axis=0).astype(BF16)
    place_ref[...] = place
    for copy in copies[2 : 2 + PIECES]:
        copy.wait()
    rows_x = jnp.dot(place, tokens_ref[...], preferred_element_type=F32)
    for copy in copies[2 + PIECES : 2 + 2 * PIECES]:
        copy.wait()
    rows_dy = jnp.dot(place, grads_ref[...], preferred_element_type=F32)
    for expert, out_ref in ((0, own_ref), (1, other_ref)):
        span = slice(expert * capacity, (expert + 1) * capacity)
        out_ref[:, :feats] = jnp.concatenate([rows_x[span], rows_dy[span]], axis=0).astype(BF16)
        gate = jnp.sum(parts[expert] * weight[expert], axis=1, keepdims=True)
        gate = jnp.concatenate([gate, gate], axis=0)
        out_ref[:, feats:] = jnp.broadcast_to(gate, (2 * capacity, LANES)).astype(BF16)
    for copy in copies[2 + 2 * PIECES :]:
        copy.wait()


def plan_kernel(place_ref, routes_ref, spread_ref, masks_ref):
    place = place_ref[...].astype(F32)
    spread_ref[...] = jnp.concatenate([place, place], axis=0).T.astype(BF16)
    routes = routes_ref[...]
    own = own_expert()
    for index, expert in enumerate((own, 1 - own)):
        masks_ref[2 * index : 2 * index + 2] = (routes == expert).astype(F32)


def join_kernel(*refs):
    *pieces, out_ref = refs
    rows = pieces[0].shape[0]
    for index, ref in enumerate(pieces):
        out_ref[index * rows : (index + 1) * rows] = ref[...]


def part_kernel(capacity, rows_ref, w_ref, w_other_ref, part_ref, gate_ref):
    feats = w_ref.shape[1]
    hidden = w_ref.shape[0] // 2
    groups = rows_ref.shape[0] // (2 * capacity)
    gate = rows_ref[:, feats:].astype(F32).reshape(groups, 2 * capacity, LANES)
    gate_ref[...] = gate[:, :capacity].reshape(groups * capacity, LANES)
    rows = rows_ref[:, :feats]
    pre = []
    back = []
    for ref in (w_ref, w_other_ref):
        pre.append(
            sum(
                jnp.dot(
                    rows[:, block : block + hidden],
                    ref[hidden:, block : block + hidden],
                    preferred_element_type=F32,
                )
                for block in range(0, feats, hidden)
            )
        )
        back.append(
            lax.dot_general(rows, ref[:hidden], COLS_BY_COLS, preferred_element_type=F32)
        )
    pair = []
    for values, span in ((pre, slice(0, capacity)), (back, slice(capacity, 2 * capacity))):
        values = jnp.concatenate(values, axis=1).reshape(groups, 2 * capacity, 2 * hidden)
        pair.append(values[:, span].reshape(groups * capacity, 2 * hidden))
    store_codes(part_ref, pair)


def add_codes_kernel(first_ref, second_ref, out_ref):
    pairs = zip(load_codes(first_ref), load_codes(second_ref))
    store_codes(out_ref, [first + second for first, second in pairs])


def deal(total, refs):
    each, wide = refs[0].shape
    feats = wide - LANES
    gate = split_value(jnp.sum(total[:, feats:], axis=1, keepdims=True))
    for index, ref in enumerate(refs):
        span = slice(index * each, (index + 1) * each)
        ref[:, :feats] = total[span, :feats].astype(ref.dtype)
        ref[:, feats:] = gate[span].astype(ref.dtype)


def slot_kernel(capacity, before, first_ref, second_ref, gate_ref, w_ref, w_other_ref, *refs):
    before_refs, (mine_ref, theirs_ref, *slot_refs) = refs[:before], refs[before:]
    hidden = w_ref.shape[0] // 2
    pairs = zip(load_codes(first_ref), load_codes(second_ref))
    pre, back = [first + second for first, second in pairs]
    gate = gate_ref[:, :1]
    activation, slopes = gelu_pair(pre)
    dpre = (gate * back * slopes).astype(BF16)
    act = gate * activation
    slot = []
    for block in range(0, w_ref.shape[1], hidden):
        span = slice(block, block + hidden)
        slot.append(
            sum(
                lax.dot_general(
                    part, ref[hidden:, span], COLS_BY_COLS, preferred_element_type=F32
                )
                for part, ref in ((dpre[:, :hidden], w_ref), (dpre[:, hidden:], w_other_ref))
            )
        )
    slot_gate = split_value(jnp.sum(activation * back, axis=1, keepdims=True))
    total = jnp.concatenate(slot + [slot_gate], axis=1)
    if len(slot_refs) == 1:
        slot_refs[0][...] = total
    else:
        deal(total, slot_refs)
    rows = dpre.shape[0]
    both = [
        value.reshape(rows // capacity, capacity, 2 * hidden) for value in (dpre.astype(F32), act)
    ]
    both = jnp.concatenate(both, axis=1).reshape(2 * rows, 2 * hidden).astype(BF16)
    mine_ref[...] = both[:, :hidden]
    count = 2 * rows
    for index, ref in enumerate(before_refs):
        theirs_ref[index * count : (index + 1) * count] = ref[...]
    theirs_ref[before * count :] = both[:, hidden:]


def halve_kernel(kept_ref, came_ref, keep_ref, send_ref):
    half = keep_ref.shape[0]
    total = kept_ref[...] + came_ref[...]
    keep_ref[...] = total[:half]
    send_ref[...] = total[half:]


def deal_kernel(kept_ref, came_ref, *refs):
    deal(kept_ref[...] + came_ref[...], refs)


def weight_kernel(capacity, *refs):
    rows_refs, both_refs = refs[:4], refs[4:7]
    w_in_hbm, w_out_hbm, written_ref, w_in_ref, w_out_ref, sems = refs[7:]
    feats, hidden = w_in_ref.shape
    rows = jnp.concatenate([ref[:, :feats] for ref in rows_refs], axis=0)
    both = jnp.concatenate([ref[...] for ref in both_refs], axis=0).astype(F32)
    of_x = lax.broadcasted_iota(jnp.int32, both.shape, 0) % (2 * capacity) < capacity
    dpre = jnp.where(of_x, both, 0.0).astype(BF16)
    act = jnp.where(of_x, 0.0, both).astype(BF16)
    count = feats // PIECES
    copies = []
    for piece in range(PIECES):
        span = slice(piece * count, (piece + 1) * count)
        part = rows[:, span]
        w_in_ref[span] = lax.dot_general(part, dpre, ROWS_BY_ROWS, preferred_element_type=F32)
        w_out_ref[:, span] = lax.dot_general(act, part, ROWS_BY_ROWS, preferred_element_type=F32)
        span = pl.ds(piece * count, count)
        for source, target in (
            (w_in_ref.at[span], w_in_hbm.at[span]),
            (w_out_ref.at[:, span], w_out_hbm.at[:, span]),
        ):
            copy = pltpu.make_async_copy(source, target, sems.at[len(copies)])
            copy.start()
            copies.append(copy)
    for copy in copies:
        copy.wait()
    written_ref[...] = jnp.zeros(written_ref.shape, F32)


def combine_kernel(steps, *refs):
    kept_ref, came_refs = refs[0], refs[1:steps]
    place_ref, spread_ref, masks_ref, tokens_ref, gate_out_ref = refs[steps:]
    feats = tokens_ref.shape[1]
    capacity = kept_ref.shape[0]
    came = [ref[...].astype(F32) for ref in came_refs]
    half = steps // WINDOW
    own = sum(came[: half - 1], kept_ref[...])
    other = sum(came[half:], came[half - 1])
    slots = jnp.concatenate([own, other], axis=0)
    grads = slots[:, :feats]
    high = grads.astype(BF16)
    low = (grads - high.astype(F32)).astype(BF16)
    both = jnp.concatenate([high, low], axis=0)
    tokens_ref[...] = jnp.dot(spread_ref[...], both, preferred_element_type=F32).astype(BF16)
    slot_gate = jnp.sum(slots[:, feats:], axis=1, keepdims=True)
    picked = place_ref[...].astype(F32) * slot_gate
    masks = masks_ref[...]
    result = jnp.zeros(gate_out_ref.shape, F32)
    for index in range(WINDOW):
        span = slice(index * capacity, (index + 1) * capacity)
        value = jnp.sum(picked[span], axis=0, keepdims=True)
        result = result + masks[2 * index : 2 * index + 2] * value
    gate_out_ref[...] = result


def swap(array, axes, bit):
    size = lax.axis_size(axes)
    return lax.ppermute(array, axes, [(index, index ^ bit) for index in range(size)])


def swap_nodes(array, step):
    return swap(array, ("node", "local"), step * lax.axis_size("local") + 1)


def join(pieces, after=()):
    rows, wide = pieces[0].shape
    rows *= len(pieces)
    shape = jax.ShapeDtypeStruct((rows, wide), BF16)
    return call(join_kernel, shape, 0, 4 * rows * wide, after=after)(*pieces)


def body(tokens, grad_out, routes, gates, w_in, w_out):
    nodes = lax.axis_size("node")
    locals_ = lax.axis_size("local")
    edatas = lax.axis_size("edata")
    tok_rows, feats = tokens.shape
    hidden = w_in.shape[1]
    capacity = 2 * tok_rows // EXPERTS
    slots = WINDOW * capacity
    wide = feats + LANES
    coded = 4 * hidden + LANES
    shape = jax.ShapeDtypeStruct
    hbm = pl.BlockSpec(memory_space=pltpu.HBM)
    vmem = pl.BlockSpec(memory_space=pltpu.VMEM)

    inputs = [
        pltpu.with_memory_space_constraint(value, pltpu.HBM)
        for value in (routes.T, gates.T, tokens, grad_out, w_in, w_out)
    ]
    own_rows, other_rows, place, routes, weights = call(
        gather_kernel,
        (
            pltpu.VMEM((2 * capacity, wide), BF16),
            pltpu.VMEM((2 * capacity, wide), BF16),
            pltpu.VMEM((slots, tok_rows), BF16),
            pltpu.VMEM((2, tok_rows), jnp.int32),
            pltpu.VMEM((2 * hidden, feats), BF16),
        ),
        4 * slots * tok_rows * feats,
        4 * tok_rows * feats + 4 * hidden * feats,
        in_specs=[hbm] * 6,
        scratch_shapes=[
            pltpu.VMEM((2, tok_rows), BF16),
            pltpu.VMEM((tok_rows, feats), BF16),
            pltpu.VMEM((tok_rows, feats), BF16),
            pltpu.SemaphoreType.DMA((3 + 2 * PIECES + feats // hidden,)),
        ],
    )(*inputs)

    other_weights = swap(weights, "local", 1)

    half_nodes = nodes // WINDOW
    pieces = [own_rows]
    for step in range(1, nodes):
        pieces.append(swap_nodes(own_rows if step < half_nodes else other_rows, step))
    rows = half_nodes * (locals_ // 2) * capacity
    last = ()
    chains = []
    held = []
    for chunk in (pieces[:half_nodes], pieces[half_nodes:]):
        chunk = join(chunk, last)
        bit = 2
        while bit < locals_:
            chunk = join([chunk, swap(chunk, "local", bit)])
            bit *= 2
        held.append(chunk)
        part, gate_rows = call(
            functools.partial(part_kernel, capacity),
            (shape((rows, coded), I16), shape((rows, LANES), F32)),
            16 * rows * feats * hidden,
            4 * rows * feats + 8 * feats * hidden,
            after=last,
        )(chunk, weights, other_weights)
        last = (part,)
        chains.append((part, swap(part, "edata", edatas // 2), gate_rows))
    bit = edatas // 4
    while bit:
        for index, (part, other, gate_rows) in enumerate(chains):
            part = call(
                add_codes_kernel,
                shape((rows, coded), I16),
                16 * rows * hidden,
                6 * rows * coded,
                after=last,
            )(part, other)
            last = (part,)
            chains[index] = (part, swap(part, "edata", bit), gate_rows)
        bit //= 2

    mine = []
    theirs = ()
    slots_back = []
    for index, (part, other, gate_rows) in enumerate(chains):
        dealt = [shape((capacity, wide), BF16 if index else F32)] * half_nodes
        own, packed, *slot_parts = call(
            functools.partial(slot_kernel, capacity, len(theirs)),
            [
                shape((2 * rows, hidden), BF16),
                shape(((1 + len(theirs)) * 2 * rows, hidden), BF16),
                *(dealt if locals_ == 2 else [shape((rows, wide), F32)]),
            ],
            4 * rows * feats * hidden,
            4 * feats * hidden + 4 * rows * feats,
            after=last,
        )(part, other, gate_rows, weights, other_weights, *theirs)
        last = (own,)
        if index == 0:
            spread, masks = call(
                plan_kernel,
                (shape((tok_rows, 2 * slots), BF16), shape((2 * WINDOW, tok_rows), F32)),
                0,
                8 * slots * tok_rows,
                after=last,
            )(place, routes)
            last = (spread,)
        mine.append(own)
        theirs = (packed,)
        if locals_ > 2:
            half = rows // 2
            keep, send = slot_parts[0][:half], slot_parts[0][half:]
            bit = locals_ // 2
            while bit > 2:
                half //= 2
                keep, send = call(
                    halve_kernel,
                    (shape((half, wide), F32),) * 2,
                    4 * half * wide,
                    24 * half * wide,
                )(keep, swap(send, "local", bit))
                bit //= 2
            slot_parts = call(deal_kernel, dealt, 4 * half * wide, 12 * half * wide)(
                keep, swap(send, "local", bit)
            )
        for step, send in enumerate(slot_parts, index * half_nodes):
            slots_back.append(swap_nodes(send, step) if step else send)
    came = [swap(chunk, "local", 1) for chunk in held]
    back = swap(theirs[0], "local", 1)
    grad_w_in, grad_w_out, written = call(
        functools.partial(weight_kernel, capacity),
        (shape((feats, hidden), F32), shape((hidden, feats), F32), shape((8, LANES), F32)),
        32 * rows * feats * hidden,
        8 * feats * hidden,
        in_specs=[vmem] * 7,
        after=slots_back[1:half_nodes],
        out_specs=[hbm, hbm, vmem],
        scratch_shapes=[
            pltpu.VMEM((feats, hidden), F32),
            pltpu.VMEM((hidden, feats), F32),
            pltpu.SemaphoreType.DMA((2 * PIECES,)),
        ],
    )(*held, *came, *mine, back)
    grad_tokens, grad_gates = call(
        functools.partial(combine_kernel, nodes),
        (shape((tok_rows, feats), BF16), shape((2, tok_rows), F32)),
        4 * slots * tok_rows * feats,
        2 * tok_rows * feats,
        after=(written,),
    )(*slots_back[:half_nodes], *reversed(slots_back[half_nodes:]), place, spread, masks)
    return (grad_tokens, grad_gates.T, grad_w_in, grad_w_out)


def solution(mesh):
    in_specs = (
        P(("node", "local"), "edata"),
        P(("node", "local"), "edata"),
        P(("node", "local"), None),
        P(("node", "local"), None),
        P("edata", ("node", "local")),
        P(("node", "local"), "edata"),
    )
    out_specs = (
        P(("node", "local"), "edata"),
        P(("node", "local"), None),
        P("edata", ("node", "local")),
        P(("node", "local"), "edata"),
    )
    return jax.shard_map(body, mesh=mesh, in_specs=in_specs, out_specs=out_specs, check_vma=False)
```

```python
import functools

import jax
import jax.numpy as jnp
from jax import lax
from jax.experimental import pallas as pl
from jax.experimental.pallas import tpu as pltpu
from jax.sharding import PartitionSpec as P

EXPERTS = 64
WINDOW = 2
LANES = 128
PIECES = 4
LOADS = 8
VMEM_LIMIT = 40 * 1024 * 1024

BF16 = jnp.bfloat16
F32 = jnp.float32
I16 = jnp.int16
ROWS_BY_ROWS = (((0,), (0,)), ((), ()))
COLS_BY_COLS = (((1,), (1,)), ((), ()))


def gelu_pair(pre_act):
    coefficient = 0.7978845608028654
    square = pre_act * pre_act
    tanh_val = jnp.tanh(coefficient * (pre_act + 0.044715 * pre_act * square))
    half = 0.5 * (1.0 + tanh_val)
    activation = pre_act * half
    slopes = half + 0.5 * pre_act * (1.0 - tanh_val * tanh_val) * coefficient * (
        1.0 + 3.0 * 0.044715 * square
    )
    return (activation, slopes)


def call(kernel, out_shape, flops, moved, limit=VMEM_LIMIT, in_specs=None, after=(), **more):
    def run(*operands):
        given = in_specs or [pl.BlockSpec(memory_space=pltpu.VMEM)] * len(operands)
        return pl.pallas_call(
            lambda *refs: kernel(*refs[len(after) :]),
            out_shape=out_shape,
            in_specs=[pl.BlockSpec(memory_space=pl.ANY)] * len(after) + list(given),
            compiler_params=pltpu.CompilerParams(vmem_limit_bytes=limit),
            cost_estimate=pl.CostEstimate(flops=flops, bytes_accessed=moved, transcendentals=0),
            **more,
        )(*after, *operands)

    return run


def own_expert():
    half_nodes = lax.axis_size("node") // WINDOW
    return lax.axis_index("node") // half_nodes


def split_value(value):
    high = value.astype(BF16).astype(F32)
    lane = lax.broadcasted_iota(jnp.int32, (value.shape[0], LANES), 1)
    return jnp.where(lane == 0, high, jnp.where(lane == 1, value - high, 0.0))


def encode(values):
    top = jnp.max(jnp.abs(values), axis=1, keepdims=True)
    power = jnp.ceil(jnp.log2(jnp.maximum(top, 1e-30)))
    codes = jnp.round(values * (1.999 * jnp.exp2(14.0 - power)))
    return codes.astype(jnp.int32).astype(I16), power


def decode(codes, power):
    return codes.astype(jnp.int32).astype(F32) * (jnp.exp2(power - 14.0) / 1.999)


def store_codes(out_ref, pair):
    hidden = pair[0].shape[1]
    lane = lax.broadcasted_iota(jnp.int32, (pair[0].shape[0], LANES), 1)
    powers = []
    for index, values in enumerate(pair):
        codes, power = encode(values)
        out_ref[:, index * hidden : (index + 1) * hidden] = codes
        powers.append(power)
    powers = jnp.where(lane == 0, powers[0], powers[1])
    out_ref[:, 2 * hidden :] = powers.astype(jnp.int32).astype(I16)


def load_codes(ref):
    hidden = (ref.shape[1] - LANES) // 2
    powers = ref[:, 2 * hidden :].astype(jnp.int32).astype(F32)
    return [
        decode(ref[:, index * hidden : (index + 1) * hidden], powers[:, index : index + 1])
        for index in range(2)
    ]


def gather_kernel(routes_hbm, gates_hbm, tokens_hbm, grads_hbm, w_in_hbm, w_out_hbm, own_ref,
                  other_ref, place_ref, routes_ref, w_ref, gates_ref, tokens_ref, grads_ref, sems):
    tok_rows, feats = tokens_ref.shape
    capacity = own_ref.shape[0] // 2
    slots = WINDOW * capacity
    copies = [
        pltpu.make_async_copy(routes_hbm, routes_ref, sems.at[0]),
        pltpu.make_async_copy(gates_hbm, gates_ref, sems.at[1]),
    ]
    count = tok_rows // LOADS
    for source, target in ((tokens_hbm, tokens_ref), (grads_hbm, grads_ref)):
        for piece in range(LOADS):
            span = pl.ds(piece * count, count)
            copies.append(
                pltpu.make_async_copy(source.at[span], target.at[span], sems.at[len(copies)])
            )
    hidden = w_out_hbm.shape[0]
    lower = pl.ds(hidden, hidden)
    moves = []
    for block in range(0, hidden, hidden // PIECES):
        span = pl.ds(block, hidden // PIECES)
        moves.append((w_out_hbm.at[span], w_ref.at[span]))
    for block in range(0, feats, hidden):
        span = pl.ds(block, hidden)
        moves.append((w_in_hbm.at[span], w_ref.at[lower, span]))
    for source, target in moves:
        copies.append(pltpu.make_async_copy(source, target, sems.at[len(copies)]))
    for copy in copies:
        copy.start()
    earlier = lax.broadcasted_iota(jnp.int32, (tok_rows, tok_rows), 0) < lax.broadcasted_iota(
        jnp.int32, (tok_rows, tok_rows), 1
    )
    earlier = earlier.astype(F32).astype(BF16)
    slot_of = lax.broadcasted_iota(jnp.int32, (capacity, tok_rows), 0).astype(F32)
    row_of = lax.broadcasted_iota(jnp.int32, (8, tok_rows), 0)
    own = own_expert()
    copies[0].wait()
    copies[1].wait()
    routes = routes_ref[...]
    gates = gates_ref[...].astype(F32)
    hits = [(routes == expert).astype(F32) for expert in (own, 1 - own)]
    named = [hit[0:1] + hit[1:2] for hit in hits]
    weight = [hit * gates for hit in hits]
    weight = [value[0:1] + value[1:2] for value in weight]
    names = jnp.where(row_of == 0, named[0], jnp.where(row_of == 1, named[1], 0.0)).astype(BF16)
    before = jnp.dot(names, earlier, preferred_element_type=F32)
    parts = [jnp.where(before[e : e + 1] == slot_of, named[e], 0.0) for e in range(WINDOW)]
    place = jnp.concatenate(parts, axis=0).astype(BF16)
    place_ref[...] = place
    for copy in copies[2 : 2 + LOADS]:
        copy.wait()
    rows_x = jnp.dot(place, tokens_ref[...], preferred_element_type=F32)
    for copy in copies[2 + LOADS : 2 + 2 * LOADS]:
        copy.wait()
    rows_dy = jnp.dot(place, grads_ref[...], preferred_element_type=F32)
    for expert, out_ref in ((0, own_ref), (1, other_ref)):
        span = slice(expert * capacity, (expert + 1) * capacity)
        out_ref[:, :feats] = jnp.concatenate([rows_x[span], rows_dy[span]], axis=0).astype(BF16)
        gate = jnp.sum(parts[expert] * weight[expert], axis=1, keepdims=True)
        gate = jnp.concatenate([gate, gate], axis=0)
        out_ref[:, feats:] = jnp.broadcast_to(gate, (2 * capacity, LANES)).astype(BF16)
    for copy in copies[2 + 2 * LOADS :]:
        copy.wait()


def plan_kernel(place_ref, routes_ref, spread_ref, masks_ref):
    place = place_ref[...].astype(F32)
    spread_ref[...] = jnp.concatenate([place, place], axis=0).T.astype(BF16)
    routes = routes_ref[...]
    own = own_expert()
    for index, expert in enumerate((own, 1 - own)):
        masks_ref[2 * index : 2 * index + 2] = (routes == expert).astype(F32)


def join_kernel(*refs):
    *pieces, out_ref = refs
    rows = pieces[0].shape[0]
    for index, ref in enumerate(pieces):
        out_ref[index * rows : (index + 1) * rows] = ref[...]


def part_kernel(capacity, rows_ref, w_ref, w_other_ref, part_ref, gate_ref):
    feats = w_ref.shape[1]
    hidden = w_ref.shape[0] // 2
    groups = rows_ref.shape[0] // (2 * capacity)
    gate = rows_ref[:, feats:].astype(F32).reshape(groups, 2 * capacity, LANES)
    gate_ref[...] = gate[:, :capacity].reshape(groups * capacity, LANES)
    rows = rows_ref[:, :feats]
    pre = []
    back = []
    for ref in (w_ref, w_other_ref):
        pre.append(
            sum(
                jnp.dot(
                    rows[:, block : block + hidden],
                    ref[hidden:, block : block + hidden],
                    preferred_element_type=F32,
                )
                for block in range(0, feats, hidden)
            )
        )
        back.append(
            lax.dot_general(rows, ref[:hidden], COLS_BY_COLS, preferred_element_type=F32)
        )
    pair = []
    for values, span in ((pre, slice(0, capacity)), (back, slice(capacity, 2 * capacity))):
        values = jnp.concatenate(values, axis=1).reshape(groups, 2 * capacity, 2 * hidden)
        pair.append(values[:, span].reshape(groups * capacity, 2 * hidden))
    store_codes(part_ref, pair)


def add_codes_kernel(first_ref, second_ref, out_ref):
    pairs = zip(load_codes(first_ref), load_codes(second_ref))
    store_codes(out_ref, [first + second for first, second in pairs])


def deal(total, refs):
    each, wide = refs[0].shape
    feats = wide - LANES
    gate = split_value(jnp.sum(total[:, feats:], axis=1, keepdims=True))
    for index, ref in enumerate(refs):
        span = slice(index * each, (index + 1) * each)
        ref[:, :feats] = total[span, :feats].astype(ref.dtype)
        ref[:, feats:] = gate[span].astype(ref.dtype)


def slot_kernel(capacity, before, first_ref, second_ref, gate_ref, w_ref, w_other_ref, *refs):
    before_refs, (mine_ref, theirs_ref, *slot_refs) = refs[:before], refs[before:]
    hidden = w_ref.shape[0] // 2
    pairs = zip(load_codes(first_ref), load_codes(second_ref))
    pre, back = [first + second for first, second in pairs]
    gate = gate_ref[:, :1]
    activation, slopes = gelu_pair(pre)
    dpre = (gate * back * slopes).astype(BF16)
    act = gate * activation
    slot = []
    for block in range(0, w_ref.shape[1], hidden):
        span = slice(block, block + hidden)
        slot.append(
            sum(
                lax.dot_general(
                    part, ref[hidden:, span], COLS_BY_COLS, preferred_element_type=F32
                )
                for part, ref in ((dpre[:, :hidden], w_ref), (dpre[:, hidden:], w_other_ref))
            )
        )
    slot_gate = split_value(jnp.sum(activation * back, axis=1, keepdims=True))
    total = jnp.concatenate(slot + [slot_gate], axis=1)
    if len(slot_refs) == 1:
        slot_refs[0][...] = total
    else:
        deal(total, slot_refs)
    rows = dpre.shape[0]
    both = [
        value.reshape(rows // capacity, capacity, 2 * hidden) for value in (dpre.astype(F32), act)
    ]
    both = jnp.concatenate(both, axis=1).reshape(2 * rows, 2 * hidden).astype(BF16)
    mine_ref[...] = both[:, :hidden]
    count = 2 * rows
    for index, ref in enumerate(before_refs):
        theirs_ref[index * count : (index + 1) * count] = ref[...]
    theirs_ref[before * count :] = both[:, hidden:]


def halve_kernel(kept_ref, came_ref, keep_ref, send_ref):
    half = keep_ref.shape[0]
    total = kept_ref[...] + came_ref[...]
    keep_ref[...] = total[:half]
    send_ref[...] = total[half:]


def deal_kernel(kept_ref, came_ref, *refs):
    deal(kept_ref[...] + came_ref[...], refs)


def weight_kernel(capacity, *refs):
    rows_refs, both_refs = refs[:4], refs[4:7]
    w_in_hbm, w_out_hbm, written_ref, w_in_ref, w_out_ref, sems = refs[7:]
    feats, hidden = w_in_ref.shape
    rows = jnp.concatenate([ref[:, :feats] for ref in rows_refs], axis=0)
    both = jnp.concatenate([ref[...] for ref in both_refs], axis=0).astype(F32)
    of_x = lax.broadcasted_iota(jnp.int32, both.shape, 0) % (2 * capacity) < capacity
    dpre = jnp.where(of_x, both, 0.0).astype(BF16)
    act = jnp.where(of_x, 0.0, both).astype(BF16)
    count = feats // PIECES
    copies = []
    for piece in range(PIECES):
        span = slice(piece * count, (piece + 1) * count)
        part = rows[:, span]
        w_in_ref[span] = lax.dot_general(part, dpre, ROWS_BY_ROWS, preferred_element_type=F32)
        w_out_ref[:, span] = lax.dot_general(act, part, ROWS_BY_ROWS, preferred_element_type=F32)
        span = pl.ds(piece * count, count)
        for source, target in (
            (w_in_ref.at[span], w_in_hbm.at[span]),
            (w_out_ref.at[:, span], w_out_hbm.at[:, span]),
        ):
            copy = pltpu.make_async_copy(source, target, sems.at[len(copies)])
            copy.start()
            copies.append(copy)
    for copy in copies:
        copy.wait()
    written_ref[...] = jnp.zeros(written_ref.shape, F32)


def combine_kernel(steps, *refs):
    kept_ref, came_refs = refs[0], refs[1:steps]
    place_ref, spread_ref, masks_ref, tokens_ref, gate_out_ref = refs[steps:]
    feats = tokens_ref.shape[1]
    capacity = kept_ref.shape[0]
    came = [ref[...].astype(F32) for ref in came_refs]
    half = steps // WINDOW
    own = sum(came[: half - 1], kept_ref[...])
    other = sum(came[half:], came[half - 1])
    slots = jnp.concatenate([own, other], axis=0)
    grads = slots[:, :feats]
    high = grads.astype(BF16)
    low = (grads - high.astype(F32)).astype(BF16)
    both = jnp.concatenate([high, low], axis=0)
    tokens_ref[...] = jnp.dot(spread_ref[...], both, preferred_element_type=F32).astype(BF16)
    slot_gate = jnp.sum(slots[:, feats:], axis=1, keepdims=True)
    picked = place_ref[...].astype(F32) * slot_gate
    masks = masks_ref[...]
    result = jnp.zeros(gate_out_ref.shape, F32)
    for index in range(WINDOW):
        span = slice(index * capacity, (index + 1) * capacity)
        value = jnp.sum(picked[span], axis=0, keepdims=True)
        result = result + masks[2 * index : 2 * index + 2] * value
    gate_out_ref[...] = result


def swap(array, axes, bit):
    size = lax.axis_size(axes)
    return lax.ppermute(array, axes, [(index, index ^ bit) for index in range(size)])


def swap_nodes(array, step):
    return swap(array, ("node", "local"), step * lax.axis_size("local") + 1)


def join(pieces, after=()):
    rows, wide = pieces[0].shape
    rows *= len(pieces)
    shape = jax.ShapeDtypeStruct((rows, wide), BF16)
    return call(join_kernel, shape, 0, 4 * rows * wide, after=after)(*pieces)


def body(tokens, grad_out, routes, gates, w_in, w_out):
    nodes = lax.axis_size("node")
    locals_ = lax.axis_size("local")
    edatas = lax.axis_size("edata")
    tok_rows, feats = tokens.shape
    hidden = w_in.shape[1]
    capacity = 2 * tok_rows // EXPERTS
    slots = WINDOW * capacity
    wide = feats + LANES
    coded = 4 * hidden + LANES
    shape = jax.ShapeDtypeStruct
    hbm = pl.BlockSpec(memory_space=pltpu.HBM)
    vmem = pl.BlockSpec(memory_space=pltpu.VMEM)

    inputs = [
        pltpu.with_memory_space_constraint(value, pltpu.HBM)
        for value in (routes.T, gates.T, tokens, grad_out, w_in, w_out)
    ]
    own_rows, other_rows, place, routes, weights = call(
        gather_kernel,
        (
            pltpu.VMEM((2 * capacity, wide), BF16),
            pltpu.VMEM((2 * capacity, wide), BF16),
            pltpu.VMEM((slots, tok_rows), BF16),
            pltpu.VMEM((2, tok_rows), jnp.int32),
            pltpu.VMEM((2 * hidden, feats), BF16),
        ),
        4 * slots * tok_rows * feats,
        4 * tok_rows * feats + 4 * hidden * feats,
        in_specs=[hbm] * 6,
        scratch_shapes=[
            pltpu.VMEM((2, tok_rows), BF16),
            pltpu.VMEM((tok_rows, feats), BF16),
            pltpu.VMEM((tok_rows, feats), BF16),
            pltpu.SemaphoreType.DMA((2 + 2 * LOADS + PIECES + feats // hidden,)),
        ],
    )(*inputs)

    other_weights = swap(weights, "local", 1)

    half_nodes = nodes // WINDOW
    pieces = [own_rows]
    for step in range(1, nodes):
        pieces.append(swap_nodes(own_rows if step < half_nodes else other_rows, step))
    rows = half_nodes * (locals_ // 2) * capacity
    last = ()
    chains = []
    held = []
    for chunk in (pieces[:half_nodes], pieces[half_nodes:]):
        chunk = join(chunk, last)
        bit = 2
        while bit < locals_:
            chunk = join([chunk, swap(chunk, "local", bit)])
            bit *= 2
        held.append(chunk)
        part, gate_rows = call(
            functools.partial(part_kernel, capacity),
            (shape((rows, coded), I16), shape((rows, LANES), F32)),
            16 * rows * feats * hidden,
            4 * rows * feats + 8 * feats * hidden,
            after=last,
        )(chunk, weights, other_weights)
        last = (part,)
        chains.append((part, swap(part, "edata", edatas // 2), gate_rows))
    bit = edatas // 4
    while bit:
        for index, (part, other, gate_rows) in enumerate(chains):
            part = call(
                add_codes_kernel,
                shape((rows, coded), I16),
                16 * rows * hidden,
                6 * rows * coded,
                after=last,
            )(part, other)
            last = (part,)
            chains[index] = (part, swap(part, "edata", bit), gate_rows)
        bit //= 2

    mine = []
    theirs = ()
    slots_back = []
    for index, (part, other, gate_rows) in enumerate(chains):
        dealt = [shape((capacity, wide), BF16 if index else F32)] * half_nodes
        own, packed, *slot_parts = call(
            functools.partial(slot_kernel, capacity, len(theirs)),
            [
                shape((2 * rows, hidden), BF16),
                shape(((1 + len(theirs)) * 2 * rows, hidden), BF16),
                *(dealt if locals_ == 2 else [shape((rows, wide), F32)]),
            ],
            4 * rows * feats * hidden,
            4 * feats * hidden + 4 * rows * feats,
            after=last,
        )(part, other, gate_rows, weights, other_weights, *theirs)
        last = (own,)
        if index == 0:
            spread, masks = call(
                plan_kernel,
                (shape((tok_rows, 2 * slots), BF16), shape((2 * WINDOW, tok_rows), F32)),
                0,
                8 * slots * tok_rows,
                after=last,
            )(place, routes)
            last = (spread,)
        mine.append(own)
        theirs = (packed,)
        if locals_ > 2:
            half = rows // 2
            keep, send = slot_parts[0][:half], slot_parts[0][half:]
            bit = locals_ // 2
            while bit > 2:
                half //= 2
                keep, send = call(
                    halve_kernel,
                    (shape((half, wide), F32),) * 2,
                    4 * half * wide,
                    24 * half * wide,
                )(keep, swap(send, "local", bit))
                bit //= 2
            slot_parts = call(deal_kernel, dealt, 4 * half * wide, 12 * half * wide)(
                keep, swap(send, "local", bit)
            )
        for step, send in enumerate(slot_parts, index * half_nodes):
            slots_back.append(swap_nodes(send, step) if step else send)
    came = [swap(chunk, "local", 1) for chunk in held]
    back = swap(theirs[0], "local", 1)
    grad_w_in, grad_w_out, written = call(
        functools.partial(weight_kernel, capacity),
        (shape((feats, hidden), F32), shape((hidden, feats), F32), shape((8, LANES), F32)),
        32 * rows * feats * hidden,
        8 * feats * hidden,
        in_specs=[vmem] * 7,
        after=slots_back[1:half_nodes],
        out_specs=[hbm, hbm, vmem],
        scratch_shapes=[
            pltpu.VMEM((feats, hidden), F32),
            pltpu.VMEM((hidden, feats), F32),
            pltpu.SemaphoreType.DMA((2 * PIECES,)),
        ],
    )(*held, *came, *mine, back)
    grad_tokens, grad_gates = call(
        functools.partial(combine_kernel, nodes),
        (shape((tok_rows, feats), BF16), shape((2, tok_rows), F32)),
        4 * slots * tok_rows * feats,
        2 * tok_rows * feats,
        after=(written,),
    )(*slots_back[:half_nodes], *reversed(slots_back[half_nodes:]), place, spread, masks)
    return (grad_tokens, grad_gates.T, grad_w_in, grad_w_out)


def solution(mesh):
    in_specs = (
        P(("node", "local"), "edata"),
        P(("node", "local"), "edata"),
        P(("node", "local"), None),
        P(("node", "local"), None),
        P("edata", ("node", "local")),
        P(("node", "local"), "edata"),
    )
    out_specs = (
        P(("node", "local"), "edata"),
        P(("node", "local"), None),
        P("edata", ("node", "local")),
        P(("node", "local"), "edata"),
    )
    return jax.shard_map(body, mesh=mesh, in_specs=in_specs, out_specs=out_specs, check_vma=False)
```

```python
import functools

import jax
import jax.numpy as jnp
from jax import lax
from jax.experimental import pallas as pl
from jax.experimental.pallas import tpu as pltpu
from jax.sharding import PartitionSpec as P

EXPERTS = 64
WINDOW = 2
LANES = 128
PIECES = 4
VMEM_LIMIT = 40 * 1024 * 1024

BF16 = jnp.bfloat16
F32 = jnp.float32
I16 = jnp.int16
ROWS_BY_ROWS = (((0,), (0,)), ((), ()))
COLS_BY_COLS = (((1,), (1,)), ((), ()))


def gelu_pair(pre_act):
    coefficient = 0.7978845608028654
    square = pre_act * pre_act
    tanh_val = jnp.tanh(coefficient * (pre_act + 0.044715 * pre_act * square))
    half = 0.5 * (1.0 + tanh_val)
    activation = pre_act * half
    slopes = half + 0.5 * pre_act * (1.0 - tanh_val * tanh_val) * coefficient * (
        1.0 + 3.0 * 0.044715 * square
    )
    return (activation, slopes)


def call(kernel, out_shape, flops, moved, limit=VMEM_LIMIT, in_specs=None, after=(), **more):
    def run(*operands):
        given = in_specs or [pl.BlockSpec(memory_space=pltpu.VMEM)] * len(operands)
        return pl.pallas_call(
            lambda *refs: kernel(*refs[len(after) :]),
            out_shape=out_shape,
            in_specs=[pl.BlockSpec(memory_space=pl.ANY)] * len(after) + list(given),
            compiler_params=pltpu.CompilerParams(vmem_limit_bytes=limit),
            cost_estimate=pl.CostEstimate(flops=flops, bytes_accessed=moved, transcendentals=0),
            **more,
        )(*after, *operands)

    return run


def own_expert():
    half_nodes = lax.axis_size("node") // WINDOW
    return lax.axis_index("node") // half_nodes


def split_value(value):
    high = value.astype(BF16).astype(F32)
    lane = lax.broadcasted_iota(jnp.int32, (value.shape[0], LANES), 1)
    return jnp.where(lane == 0, high, jnp.where(lane == 1, value - high, 0.0))


def encode(values):
    top = jnp.max(jnp.abs(values), axis=1, keepdims=True)
    power = jnp.ceil(jnp.log2(jnp.maximum(top, 1e-30)))
    codes = jnp.round(values * (1.999 * jnp.exp2(14.0 - power)))
    return codes.astype(jnp.int32).astype(I16), power


def decode(codes, power):
    return codes.astype(jnp.int32).astype(F32) * (jnp.exp2(power - 14.0) / 1.999)


def store_codes(out_ref, pair):
    hidden = pair[0].shape[1]
    lane = lax.broadcasted_iota(jnp.int32, (pair[0].shape[0], LANES), 1)
    powers = []
    for index, values in enumerate(pair):
        codes, power = encode(values)
        out_ref[:, index * hidden : (index + 1) * hidden] = codes
        powers.append(power)
    powers = jnp.where(lane == 0, powers[0], powers[1])
    out_ref[:, 2 * hidden :] = powers.astype(jnp.int32).astype(I16)


def load_codes(ref):
    hidden = (ref.shape[1] - LANES) // 2
    powers = ref[:, 2 * hidden :].astype(jnp.int32).astype(F32)
    return [
        decode(ref[:, index * hidden : (index + 1) * hidden], powers[:, index : index + 1])
        for index in range(2)
    ]


def gather_kernel(routes_hbm, gates_hbm, tokens_hbm, grads_hbm, w_in_hbm, w_out_hbm, own_ref,
                  other_ref, place_ref, routes_ref, w_ref, gates_ref, tokens_ref, grads_ref, sems):
    tok_rows, feats = tokens_ref.shape
    capacity = own_ref.shape[0] // 2
    slots = WINDOW * capacity
    copies = [
        pltpu.make_async_copy(routes_hbm, routes_ref, sems.at[0]),
        pltpu.make_async_copy(gates_hbm, gates_ref, sems.at[1]),
    ]
    count = tok_rows // PIECES
    for source, target in ((tokens_hbm, tokens_ref), (grads_hbm, grads_ref)):
        for piece in range(PIECES):
            span = pl.ds(piece * count, count)
            copies.append(
                pltpu.make_async_copy(source.at[span], target.at[span], sems.at[len(copies)])
            )
    hidden = w_out_hbm.shape[0]
    upper, lower = pl.ds(0, hidden), pl.ds(hidden, hidden)
    moves = [(w_out_hbm, w_ref.at[upper])]
    for block in range(0, feats, hidden):
        span = pl.ds(block, hidden)
        moves.append((w_in_hbm.at[span], w_ref.at[lower, span]))
    for source, target in moves:
        copies.append(pltpu.make_async_copy(source, target, sems.at[len(copies)]))
    for copy in copies:
        copy.start()
    earlier = lax.broadcasted_iota(jnp.int32, (tok_rows, tok_rows), 0) < lax.broadcasted_iota(
        jnp.int32, (tok_rows, tok_rows), 1
    )
    earlier = earlier.astype(F32).astype(BF16)
    slot_of = lax.broadcasted_iota(jnp.int32, (capacity, tok_rows), 0).astype(F32)
    row_of = lax.broadcasted_iota(jnp.int32, (8, tok_rows), 0)
    own = own_expert()
    copies[0].wait()
    copies[1].wait()
    routes = routes_ref[...]
    gates = gates_ref[...].astype(F32)
    hits = [(routes == expert).astype(F32) for expert in (own, 1 - own)]
    named = [hit[0:1] + hit[1:2] for hit in hits]
    weight = [hit * gates for hit in hits]
    weight = [value[0:1] + value[1:2] for value in weight]
    names = jnp.where(row_of == 0, named[0], jnp.where(row_of == 1, named[1], 0.0)).astype(BF16)
    before = jnp.dot(names, earlier, preferred_element_type=F32)
    parts = [jnp.where(before[e : e + 1] == slot_of, named[e], 0.0) for e in range(WINDOW)]
    place = jnp.concatenate(parts, axis=0).astype(BF16)
    place_ref[...] = place
    for copy in copies[2 : 2 + PIECES]:
        copy.wait()
    rows_x = jnp.dot(place, tokens_ref[...], preferred_element_type=F32)
    for copy in copies[2 + PIECES : 2 + 2 * PIECES]:
        copy.wait()
    rows_dy = jnp.dot(place, grads_ref[...], preferred_element_type=F32)
    for expert, out_ref in ((0, own_ref), (1, other_ref)):
        span = slice(expert * capacity, (expert + 1) * capacity)
        out_ref[:, :feats] = jnp.concatenate([rows_x[span], rows_dy[span]], axis=0).astype(BF16)
        gate = jnp.sum(parts[expert] * weight[expert], axis=1, keepdims=True)
        gate = jnp.concatenate([gate, gate], axis=0)
        out_ref[:, feats:] = jnp.broadcast_to(gate, (2 * capacity, LANES)).astype(BF16)
    for copy in copies[2 + 2 * PIECES :]:
        copy.wait()


def plan_kernel(place_ref, routes_ref, spread_ref, masks_ref):
    place = place_ref[...].astype(F32)
    spread_ref[...] = jnp.concatenate([place, place], axis=0).T.astype(BF16)
    routes = routes_ref[...]
    own = own_expert()
    for index, expert in enumerate((own, 1 - own)):
        masks_ref[2 * index : 2 * index + 2] = (routes == expert).astype(F32)


def join_kernel(*refs):
    *pieces, out_ref = refs
    rows = pieces[0].shape[0]
    for index, ref in enumerate(pieces):
        out_ref[index * rows : (index + 1) * rows] = ref[...]


def part_kernel(capacity, rows_ref, w_ref, w_other_ref, part_ref, gate_ref):
    feats = w_ref.shape[1]
    hidden = w_ref.shape[0] // 2
    groups = rows_ref.shape[0] // (2 * capacity)
    gate = rows_ref[:, feats:].astype(F32).reshape(groups, 2 * capacity, LANES)
    gate_ref[...] = gate[:, :capacity].reshape(groups * capacity, LANES)
    rows = rows_ref[:, :feats]
    pre = []
    back = []
    for ref in (w_ref, w_other_ref):
        pre.append(
            sum(
                jnp.dot(
                    rows[:, block : block + hidden],
                    ref[hidden:, block : block + hidden],
                    preferred_element_type=F32,
                )
                for block in range(0, feats, hidden)
            )
        )
        back.append(
            lax.dot_general(rows, ref[:hidden], COLS_BY_COLS, preferred_element_type=F32)
        )
    pair = []
    for values, span in ((pre, slice(0, capacity)), (back, slice(capacity, 2 * capacity))):
        values = jnp.concatenate(values, axis=1).reshape(groups, 2 * capacity, 2 * hidden)
        pair.append(values[:, span].reshape(groups * capacity, 2 * hidden))
    store_codes(part_ref, pair)


def add_codes_kernel(first_ref, second_ref, out_ref):
    pairs = zip(load_codes(first_ref), load_codes(second_ref))
    store_codes(out_ref, [first + second for first, second in pairs])


def deal(total, refs):
    each, wide = refs[0].shape
    feats = wide - LANES
    gate = split_value(jnp.sum(total[:, feats:], axis=1, keepdims=True))
    for index, ref in enumerate(refs):
        span = slice(index * each, (index + 1) * each)
        ref[:, :feats] = total[span, :feats].astype(ref.dtype)
        ref[:, feats:] = gate[span].astype(ref.dtype)


def slot_kernel(capacity, before, first_ref, second_ref, gate_ref, w_ref, w_other_ref, *refs):
    before_refs, (mine_ref, theirs_ref, *slot_refs) = refs[:before], refs[before:]
    hidden = w_ref.shape[0] // 2
    pairs = zip(load_codes(first_ref), load_codes(second_ref))
    pre, back = [first + second for first, second in pairs]
    gate = gate_ref[:, :1]
    activation, slopes = gelu_pair(pre)
    dpre = (gate * back * slopes).astype(BF16)
    act = gate * activation
    slot = []
    for block in range(0, w_ref.shape[1], hidden):
        span = slice(block, block + hidden)
        slot.append(
            sum(
                lax.dot_general(
                    part, ref[hidden:, span], COLS_BY_COLS, preferred_element_type=F32
                )
                for part, ref in ((dpre[:, :hidden], w_ref), (dpre[:, hidden:], w_other_ref))
            )
        )
    slot_gate = split_value(jnp.sum(activation * back, axis=1, keepdims=True))
    total = jnp.concatenate(slot + [slot_gate], axis=1)
    if len(slot_refs) == 1:
        slot_refs[0][...] = total
    else:
        deal(total, slot_refs)
    rows = dpre.shape[0]
    both = [
        value.reshape(rows // capacity, capacity, 2 * hidden) for value in (dpre.astype(F32), act)
    ]
    both = jnp.concatenate(both, axis=1).reshape(2 * rows, 2 * hidden).astype(BF16)
    mine_ref[...] = both[:, :hidden]
    count = 2 * rows
    for index, ref in enumerate(before_refs):
        theirs_ref[index * count : (index + 1) * count] = ref[...]
    theirs_ref[before * count :] = both[:, hidden:]


def halve_kernel(kept_ref, came_ref, keep_ref, send_ref):
    half = keep_ref.shape[0]
    total = kept_ref[...] + came_ref[...]
    keep_ref[...] = total[:half]
    send_ref[...] = total[half:]


def deal_kernel(kept_ref, came_ref, *refs):
    deal(kept_ref[...] + came_ref[...], refs)


def weight_kernel(capacity, *refs):
    rows_refs, both_refs = refs[:4], refs[4:7]
    w_in_hbm, w_out_hbm, written_ref, w_in_ref, w_out_ref, sems = refs[7:]
    feats, hidden = w_in_ref.shape
    rows = jnp.concatenate([ref[:, :feats] for ref in rows_refs], axis=0)
    both = jnp.concatenate([ref[...] for ref in both_refs], axis=0).astype(F32)
    of_x = lax.broadcasted_iota(jnp.int32, both.shape, 0) % (2 * capacity) < capacity
    dpre = jnp.where(of_x, both, 0.0).astype(BF16)
    act = jnp.where(of_x, 0.0, both).astype(BF16)
    count = feats // PIECES
    copies = []
    for piece in range(PIECES):
        span = slice(piece * count, (piece + 1) * count)
        part = rows[:, span]
        w_in_ref[span] = lax.dot_general(part, dpre, ROWS_BY_ROWS, preferred_element_type=F32)
        w_out_ref[:, span] = lax.dot_general(act, part, ROWS_BY_ROWS, preferred_element_type=F32)
        span = pl.ds(piece * count, count)
        for source, target in (
            (w_in_ref.at[span], w_in_hbm.at[span]),
            (w_out_ref.at[:, span], w_out_hbm.at[:, span]),
        ):
            copy = pltpu.make_async_copy(source, target, sems.at[len(copies)])
            copy.start()
            copies.append(copy)
    for copy in copies:
        copy.wait()
    written_ref[...] = jnp.zeros(written_ref.shape, F32)


def combine_kernel(steps, *refs):
    kept_ref, came_refs = refs[0], refs[1:steps]
    place_ref, spread_ref, masks_ref, tokens_ref, gate_out_ref = refs[steps:]
    feats = tokens_ref.shape[1]
    capacity = kept_ref.shape[0]
    came = [ref[...].astype(F32) for ref in came_refs]
    half = steps // WINDOW
    own = sum(came[: half - 1], kept_ref[...])
    other = sum(came[half:], came[half - 1])
    slots = jnp.concatenate([own, other], axis=0)
    grads = slots[:, :feats]
    high = grads.astype(BF16)
    low = (grads - high.astype(F32)).astype(BF16)
    both = jnp.concatenate([high, low], axis=0)
    tokens_ref[...] = jnp.dot(spread_ref[...], both, preferred_element_type=F32).astype(BF16)
    slot_gate = jnp.sum(slots[:, feats:], axis=1, keepdims=True)
    picked = place_ref[...].astype(F32) * slot_gate
    masks = masks_ref[...]
    result = jnp.zeros(gate_out_ref.shape, F32)
    for index in range(WINDOW):
        span = slice(index * capacity, (index + 1) * capacity)
        value = jnp.sum(picked[span], axis=0, keepdims=True)
        result = result + masks[2 * index : 2 * index + 2] * value
    gate_out_ref[...] = result


def swap(array, axes, bit):
    size = lax.axis_size(axes)
    return lax.ppermute(array, axes, [(index, index ^ bit) for index in range(size)])


def swap_nodes(array, step):
    return swap(array, ("node", "local"), step * lax.axis_size("local") + 1)


def join(pieces, after=()):
    rows, wide = pieces[0].shape
    rows *= len(pieces)
    shape = jax.ShapeDtypeStruct((rows, wide), BF16)
    return call(join_kernel, shape, 0, 4 * rows * wide, after=after)(*pieces)


def body(tokens, grad_out, routes, gates, w_in, w_out):
    nodes = lax.axis_size("node")
    locals_ = lax.axis_size("local")
    edatas = lax.axis_size("edata")
    tok_rows, feats = tokens.shape
    hidden = w_in.shape[1]
    capacity = 2 * tok_rows // EXPERTS
    slots = WINDOW * capacity
    wide = feats + LANES
    coded = 4 * hidden + LANES
    shape = jax.ShapeDtypeStruct
    hbm = pl.BlockSpec(memory_space=pltpu.HBM)
    vmem = pl.BlockSpec(memory_space=pltpu.VMEM)

    inputs = [
        pltpu.with_memory_space_constraint(value, pltpu.HBM)
        for value in (routes.T, gates.T, tokens, grad_out, w_in, w_out)
    ]
    own_rows, other_rows, place, routes, weights = call(
        gather_kernel,
        (
            pltpu.VMEM((2 * capacity, wide), BF16),
            pltpu.VMEM((2 * capacity, wide), BF16),
            pltpu.VMEM((slots, tok_rows), BF16),
            pltpu.VMEM((2, tok_rows), jnp.int32),
            pltpu.VMEM((2 * hidden, feats), BF16),
        ),
        4 * slots * tok_rows * feats,
        4 * tok_rows * feats + 4 * hidden * feats,
        in_specs=[hbm] * 6,
        scratch_shapes=[
            pltpu.VMEM((2, tok_rows), BF16),
            pltpu.VMEM((tok_rows, feats), BF16),
            pltpu.VMEM((tok_rows, feats), BF16),
            pltpu.SemaphoreType.DMA((3 + 2 * PIECES + feats // hidden,)),
        ],
    )(*inputs)

    other_weights = swap(weights, "local", 1)

    quarter = nodes // 4
    near = list(range(quarter, nodes - quarter))
    far = [*range(quarter), *range(nodes - quarter, nodes)]
    half_nodes = nodes // WINDOW
    pieces = [own_rows]
    for step in range(1, nodes):
        pieces.append(swap_nodes(own_rows if step < half_nodes else other_rows, step))
    rows = half_nodes * (locals_ // 2) * capacity
    last = ()
    chains = []
    held = []
    for steps in (near, far):
        chunk = join([pieces[step] for step in steps], last)
        bit = 2
        while bit < locals_:
            chunk = join([chunk, swap(chunk, "local", bit)])
            bit *= 2
        held.append(chunk)
        part, gate_rows = call(
            functools.partial(part_kernel, capacity),
            (shape((rows, coded), I16), shape((rows, LANES), F32)),
            16 * rows * feats * hidden,
            4 * rows * feats + 8 * feats * hidden,
            after=last,
        )(chunk, weights, other_weights)
        last = (part,)
        chains.append((part, swap(part, "edata", edatas // 2), gate_rows))
    bit = edatas // 4
    while bit:
        for index, (part, other, gate_rows) in enumerate(chains):
            part = call(
                add_codes_kernel,
                shape((rows, coded), I16),
                16 * rows * hidden,
                6 * rows * coded,
                after=last,
            )(part, other)
            last = (part,)
            chains[index] = (part, swap(part, "edata", bit), gate_rows)
        bit //= 2

    mine = []
    theirs = ()
    slots_back = {}
    for index, (part, other, gate_rows) in enumerate(chains):
        dealt = [
            shape((capacity, wide), BF16 if index and step else F32)
            for step in (far if index else near)
        ]
        own, packed, *slot_parts = call(
            functools.partial(slot_kernel, capacity, len(theirs)),
            [
                shape((2 * rows, hidden), BF16),
                shape(((1 + len(theirs)) * 2 * rows, hidden), BF16),
                *(dealt if locals_ == 2 else [shape((rows, wide), F32)]),
            ],
            4 * rows * feats * hidden,
            4 * feats * hidden + 4 * rows * feats,
            after=last,
        )(part, other, gate_rows, weights, other_weights, *theirs)
        last = (own,)
        if index == 0:
            spread, masks = call(
                plan_kernel,
                (shape((tok_rows, 2 * slots), BF16), shape((2 * WINDOW, tok_rows), F32)),
                0,
                8 * slots * tok_rows,
                after=last,
            )(place, routes)
            last = (spread,)
        mine.append(own)
        theirs = (packed,)
        if locals_ > 2:
            half = rows // 2
            keep, send = slot_parts[0][:half], slot_parts[0][half:]
            bit = locals_ // 2
            while bit > 2:
                half //= 2
                keep, send = call(
                    halve_kernel,
                    (shape((half, wide), F32),) * 2,
                    4 * half * wide,
                    24 * half * wide,
                )(keep, swap(send, "local", bit))
                bit //= 2
            slot_parts = call(deal_kernel, dealt, 4 * half * wide, 12 * half * wide)(
                keep, swap(send, "local", bit)
            )
        for step, send in zip(far if index else near, slot_parts):
            slots_back[step] = swap_nodes(send, step) if step else send
    came = [swap(chunk, "local", 1) for chunk in held]
    back = swap(theirs[0], "local", 1)
    grad_w_in, grad_w_out, written = call(
        functools.partial(weight_kernel, capacity),
        (shape((feats, hidden), F32), shape((hidden, feats), F32), shape((8, LANES), F32)),
        32 * rows * feats * hidden,
        8 * feats * hidden,
        in_specs=[vmem] * 7,
        after=[slots_back[step] for step in near],
        out_specs=[hbm, hbm, vmem],
        scratch_shapes=[
            pltpu.VMEM((feats, hidden), F32),
            pltpu.VMEM((hidden, feats), F32),
            pltpu.SemaphoreType.DMA((2 * PIECES,)),
        ],
    )(*held, *came, *mine, back)
    grad_tokens, grad_gates = call(
        functools.partial(combine_kernel, nodes),
        (shape((tok_rows, feats), BF16), shape((2, tok_rows), F32)),
        4 * slots * tok_rows * feats,
        2 * tok_rows * feats,
        after=(written,),
    )(*[slots_back[step] for step in range(nodes)], place, spread, masks)
    return (grad_tokens, grad_gates.T, grad_w_in, grad_w_out)


def solution(mesh):
    in_specs = (
        P(("node", "local"), "edata"),
        P(("node", "local"), "edata"),
        P(("node", "local"), None),
        P(("node", "local"), None),
        P("edata", ("node", "local")),
        P(("node", "local"), "edata"),
    )
    out_specs = (
        P(("node", "local"), "edata"),
        P(("node", "local"), None),
        P("edata", ("node", "local")),
        P(("node", "local"), "edata"),
    )
    return jax.shard_map(body, mesh=mesh, in_specs=in_specs, out_specs=out_specs, check_vma=False)
```

```python
import functools

import jax
import jax.numpy as jnp
from jax import lax
from jax.experimental import pallas as pl
from jax.experimental.pallas import tpu as pltpu
from jax.sharding import PartitionSpec as P

EXPERTS = 64
WINDOW = 2
LANES = 128
PIECES = 4
VMEM_LIMIT = 40 * 1024 * 1024

BF16 = jnp.bfloat16
F32 = jnp.float32
I16 = jnp.int16
ROWS_BY_ROWS = (((0,), (0,)), ((), ()))
COLS_BY_COLS = (((1,), (1,)), ((), ()))


def gelu_pair(pre_act):
    coefficient = 0.7978845608028654
    square = pre_act * pre_act
    tanh_val = jnp.tanh(coefficient * (pre_act + 0.044715 * pre_act * square))
    half = 0.5 * (1.0 + tanh_val)
    activation = pre_act * half
    slopes = half + 0.5 * pre_act * (1.0 - tanh_val * tanh_val) * coefficient * (
        1.0 + 3.0 * 0.044715 * square
    )
    return (activation, slopes)


def call(kernel, out_shape, flops, moved, limit=VMEM_LIMIT, in_specs=None, after=(), **more):
    def run(*operands):
        given = in_specs or [pl.BlockSpec(memory_space=pltpu.VMEM)] * len(operands)
        return pl.pallas_call(
            lambda *refs: kernel(*refs[len(after) :]),
            out_shape=out_shape,
            in_specs=[pl.BlockSpec(memory_space=pl.ANY)] * len(after) + list(given),
            compiler_params=pltpu.CompilerParams(vmem_limit_bytes=limit),
            cost_estimate=pl.CostEstimate(flops=flops, bytes_accessed=moved, transcendentals=0),
            **more,
        )(*after, *operands)

    return run


def own_expert():
    half_nodes = lax.axis_size("node") // WINDOW
    return lax.axis_index("node") // half_nodes


def split_value(value):
    high = value.astype(BF16).astype(F32)
    lane = lax.broadcasted_iota(jnp.int32, (value.shape[0], LANES), 1)
    return jnp.where(lane == 0, high, jnp.where(lane == 1, value - high, 0.0))


def encode(values):
    top = jnp.max(jnp.abs(values), axis=1, keepdims=True)
    power = jnp.ceil(jnp.log2(jnp.maximum(top, 1e-30)))
    codes = jnp.round(values * (1.999 * jnp.exp2(14.0 - power)))
    return codes.astype(jnp.int32).astype(I16), power


def decode(codes, power):
    return codes.astype(jnp.int32).astype(F32) * (jnp.exp2(power - 14.0) / 1.999)


def store_codes(out_ref, pair):
    hidden = pair[0].shape[1]
    lane = lax.broadcasted_iota(jnp.int32, (pair[0].shape[0], LANES), 1)
    powers = []
    for index, values in enumerate(pair):
        codes, power = encode(values)
        out_ref[:, index * hidden : (index + 1) * hidden] = codes
        powers.append(power)
    powers = jnp.where(lane == 0, powers[0], powers[1])
    out_ref[:, 2 * hidden :] = powers.astype(jnp.int32).astype(I16)


def load_codes(ref):
    hidden = (ref.shape[1] - LANES) // 2
    powers = ref[:, 2 * hidden :].astype(jnp.int32).astype(F32)
    return [
        decode(ref[:, index * hidden : (index + 1) * hidden], powers[:, index : index + 1])
        for index in range(2)
    ]


def gather_kernel(routes_hbm, gates_hbm, tokens_hbm, grads_hbm, w_in_hbm, w_out_hbm, own_ref,
                  other_ref, place_ref, routes_ref, w_ref, gates_ref, tokens_ref, grads_ref, sems):
    tok_rows, feats = tokens_ref.shape
    capacity = own_ref.shape[0] // 2
    slots = WINDOW * capacity
    copies = [
        pltpu.make_async_copy(routes_hbm, routes_ref, sems.at[0]),
        pltpu.make_async_copy(gates_hbm, gates_ref, sems.at[1]),
    ]
    count = tok_rows // PIECES
    for source, target in ((tokens_hbm, tokens_ref), (grads_hbm, grads_ref)):
        for piece in range(PIECES):
            span = pl.ds(piece * count, count)
            copies.append(
                pltpu.make_async_copy(source.at[span], target.at[span], sems.at[len(copies)])
            )
    hidden = w_out_hbm.shape[0]
    upper, lower = pl.ds(0, hidden), pl.ds(hidden, hidden)
    moves = [(w_out_hbm, w_ref.at[upper])]
    for block in range(0, feats, hidden):
        span = pl.ds(block, hidden)
        moves.append((w_in_hbm.at[span], w_ref.at[lower, span]))
    for source, target in moves:
        copies.append(pltpu.make_async_copy(source, target, sems.at[len(copies)]))
    for copy in copies:
        copy.start()
    earlier = lax.broadcasted_iota(jnp.int32, (tok_rows, tok_rows), 0) < lax.broadcasted_iota(
        jnp.int32, (tok_rows, tok_rows), 1
    )
    earlier = earlier.astype(F32).astype(BF16)
    slot_of = lax.broadcasted_iota(jnp.int32, (capacity, tok_rows), 0).astype(F32)
    row_of = lax.broadcasted_iota(jnp.int32, (8, tok_rows), 0)
    own = own_expert()
    copies[0].wait()
    copies[1].wait()
    routes = routes_ref[...]
    gates = gates_ref[...].astype(F32)
    hits = [(routes == expert).astype(F32) for expert in (own, 1 - own)]
    named = [hit[0:1] + hit[1:2] for hit in hits]
    weight = [hit * gates for hit in hits]
    weight = [value[0:1] + value[1:2] for value in weight]
    names = jnp.where(row_of == 0, named[0], jnp.where(row_of == 1, named[1], 0.0)).astype(BF16)
    before = jnp.dot(names, earlier, preferred_element_type=F32)
    parts = [jnp.where(before[e : e + 1] == slot_of, named[e], 0.0) for e in range(WINDOW)]
    place = jnp.concatenate(parts, axis=0).astype(BF16)
    place_ref[...] = place
    for copy in copies[2 : 2 + PIECES]:
        copy.wait()
    rows_x = jnp.dot(place, tokens_ref[...], preferred_element_type=F32)
    for copy in copies[2 + PIECES : 2 + 2 * PIECES]:
        copy.wait()
    rows_dy = jnp.dot(place, grads_ref[...], preferred_element_type=F32)
    for expert, out_ref in ((0, own_ref), (1, other_ref)):
        span = slice(expert * capacity, (expert + 1) * capacity)
        out_ref[:, :feats] = jnp.concatenate([rows_x[span], rows_dy[span]], axis=0).astype(BF16)
        gate = jnp.sum(parts[expert] * weight[expert], axis=1, keepdims=True)
        gate = jnp.concatenate([gate, gate], axis=0)
        out_ref[:, feats:] = jnp.broadcast_to(gate, (2 * capacity, LANES)).astype(BF16)
    for copy in copies[2 + 2 * PIECES :]:
        copy.wait()


def plan_kernel(place_ref, routes_ref, spread_ref, masks_ref):
    place = place_ref[...].astype(F32)
    spread_ref[...] = jnp.concatenate([place, place], axis=0).T.astype(BF16)
    routes = routes_ref[...]
    own = own_expert()
    for index, expert in enumerate((own, 1 - own)):
        masks_ref[2 * index : 2 * index + 2] = (routes == expert).astype(F32)


def join_kernel(*refs):
    *pieces, out_ref = refs
    rows = pieces[0].shape[0]
    for index, ref in enumerate(pieces):
        out_ref[index * rows : (index + 1) * rows] = ref[...]


def part_kernel(capacity, rows_ref, w_ref, w_other_ref, part_ref, gate_ref):
    feats = w_ref.shape[1]
    hidden = w_ref.shape[0] // 2
    groups = rows_ref.shape[0] // (2 * capacity)
    gate = rows_ref[:, feats:].astype(F32).reshape(groups, 2 * capacity, LANES)
    gate_ref[...] = gate[:, :capacity].reshape(groups * capacity, LANES)
    rows = rows_ref[:, :feats]
    pre = []
    back = []
    for ref in (w_ref, w_other_ref):
        pre.append(
            sum(
                jnp.dot(
                    rows[:, block : block + hidden],
                    ref[hidden:, block : block + hidden],
                    preferred_element_type=F32,
                )
                for block in range(0, feats, hidden)
            )
        )
        back.append(
            lax.dot_general(rows, ref[:hidden], COLS_BY_COLS, preferred_element_type=F32)
        )
    pair = []
    for values, span in ((pre, slice(0, capacity)), (back, slice(capacity, 2 * capacity))):
        values = jnp.concatenate(values, axis=1).reshape(groups, 2 * capacity, 2 * hidden)
        pair.append(values[:, span].reshape(groups * capacity, 2 * hidden))
    store_codes(part_ref, pair)


def add_codes_kernel(first_ref, second_ref, out_ref):
    pairs = zip(load_codes(first_ref), load_codes(second_ref))
    store_codes(out_ref, [first + second for first, second in pairs])


def deal(total, refs):
    each, wide = refs[0].shape
    feats = wide - LANES
    gate = split_value(jnp.sum(total[:, feats:], axis=1, keepdims=True))
    for index, ref in enumerate(refs):
        span = slice(index * each, (index + 1) * each)
        ref[:, :feats] = total[span, :feats].astype(ref.dtype)
        ref[:, feats:] = gate[span].astype(ref.dtype)


def slot_kernel(capacity, before, first_ref, second_ref, gate_ref, w_ref, w_other_ref, *refs):
    before_refs, (mine_ref, theirs_ref, *slot_refs) = refs[:before], refs[before:]
    hidden = w_ref.shape[0] // 2
    pairs = zip(load_codes(first_ref), load_codes(second_ref))
    pre, back = [first + second for first, second in pairs]
    gate = gate_ref[:, :1]
    activation, slopes = gelu_pair(pre)
    dpre = (gate * back * slopes).astype(BF16)
    act = gate * activation
    slot = []
    for block in range(0, w_ref.shape[1], hidden):
        span = slice(block, block + hidden)
        slot.append(
            sum(
                lax.dot_general(
                    part, ref[hidden:, span], COLS_BY_COLS, preferred_element_type=F32
                )
                for part, ref in ((dpre[:, :hidden], w_ref), (dpre[:, hidden:], w_other_ref))
            )
        )
    slot_gate = split_value(jnp.sum(activation * back, axis=1, keepdims=True))
    total = jnp.concatenate(slot + [slot_gate], axis=1)
    if len(slot_refs) == 1:
        slot_refs[0][...] = total
    else:
        deal(total, slot_refs)
    rows = dpre.shape[0]
    both = [
        value.reshape(rows // capacity, capacity, 2 * hidden) for value in (dpre.astype(F32), act)
    ]
    both = jnp.concatenate(both, axis=1).reshape(2 * rows, 2 * hidden).astype(BF16)
    mine_ref[...] = both[:, :hidden]
    count = 2 * rows
    for index, ref in enumerate(before_refs):
        theirs_ref[index * count : (index + 1) * count] = ref[...]
    theirs_ref[before * count :] = both[:, hidden:]


def halve_kernel(kept_ref, came_ref, keep_ref, send_ref):
    half = keep_ref.shape[0]
    total = kept_ref[...] + came_ref[...]
    keep_ref[...] = total[:half]
    send_ref[...] = total[half:]


def deal_kernel(kept_ref, came_ref, *refs):
    deal(kept_ref[...] + came_ref[...], refs)


def weight_kernel(capacity, *refs):
    rows_refs, both_refs = refs[:4], refs[4:7]
    w_in_hbm, w_out_hbm, written_ref, w_in_ref, w_out_ref, sems = refs[7:]
    feats, hidden = w_in_ref.shape
    rows = jnp.concatenate([ref[:, :feats] for ref in rows_refs], axis=0)
    both = jnp.concatenate([ref[...] for ref in both_refs], axis=0).astype(F32)
    of_x = lax.broadcasted_iota(jnp.int32, both.shape, 0) % (2 * capacity) < capacity
    dpre = jnp.where(of_x, both, 0.0).astype(BF16)
    act = jnp.where(of_x, 0.0, both).astype(BF16)
    count = feats // PIECES
    copies = []
    for piece in range(PIECES):
        span = slice(piece * count, (piece + 1) * count)
        part = rows[:, span]
        w_in_ref[span] = lax.dot_general(part, dpre, ROWS_BY_ROWS, preferred_element_type=F32)
        w_out_ref[:, span] = lax.dot_general(act, part, ROWS_BY_ROWS, preferred_element_type=F32)
        span = pl.ds(piece * count, count)
        for source, target in (
            (w_in_ref.at[span], w_in_hbm.at[span]),
            (w_out_ref.at[:, span], w_out_hbm.at[:, span]),
        ):
            copy = pltpu.make_async_copy(source, target, sems.at[len(copies)])
            copy.start()
            copies.append(copy)
    for copy in copies:
        copy.wait()
    written_ref[...] = jnp.zeros(written_ref.shape, F32)


def combine_kernel(steps, *refs):
    kept_ref, came_refs = refs[0], refs[1:steps]
    place_ref, spread_ref, masks_ref, tokens_ref, gate_out_ref = refs[steps:]
    feats = tokens_ref.shape[1]
    capacity = kept_ref.shape[0]
    came = [ref[...].astype(F32) for ref in came_refs]
    half = steps // WINDOW
    own = sum(came[: half - 1], kept_ref[...])
    other = sum(came[half:], came[half - 1])
    slots = jnp.concatenate([own, other], axis=0)
    grads = slots[:, :feats]
    high = grads.astype(BF16)
    low = (grads - high.astype(F32)).astype(BF16)
    both = jnp.concatenate([high, low], axis=0)
    tokens_ref[...] = jnp.dot(spread_ref[...], both, preferred_element_type=F32).astype(BF16)
    slot_gate = jnp.sum(slots[:, feats:], axis=1, keepdims=True)
    picked = place_ref[...].astype(F32) * slot_gate
    masks = masks_ref[...]
    result = jnp.zeros(gate_out_ref.shape, F32)
    for index in range(WINDOW):
        span = slice(index * capacity, (index + 1) * capacity)
        value = jnp.sum(picked[span], axis=0, keepdims=True)
        result = result + masks[2 * index : 2 * index + 2] * value
    gate_out_ref[...] = result


def swap(array, axes, bit):
    size = lax.axis_size(axes)
    return lax.ppermute(array, axes, [(index, index ^ bit) for index in range(size)])


def swap_nodes(array, step):
    return swap(array, ("node", "local"), step * lax.axis_size("local") + 1)


def join(pieces, after=()):
    rows, wide = pieces[0].shape
    rows *= len(pieces)
    shape = jax.ShapeDtypeStruct((rows, wide), BF16)
    return call(join_kernel, shape, 0, 4 * rows * wide, after=after)(*pieces)


def body(tokens, grad_out, routes, gates, w_in, w_out):
    nodes = lax.axis_size("node")
    locals_ = lax.axis_size("local")
    edatas = lax.axis_size("edata")
    tok_rows, feats = tokens.shape
    hidden = w_in.shape[1]
    capacity = 2 * tok_rows // EXPERTS
    slots = WINDOW * capacity
    wide = feats + LANES
    coded = 4 * hidden + LANES
    shape = jax.ShapeDtypeStruct
    hbm = pl.BlockSpec(memory_space=pltpu.HBM)
    vmem = pl.BlockSpec(memory_space=pltpu.VMEM)

    inputs = [
        pltpu.with_memory_space_constraint(value, pltpu.HBM)
        for value in (routes.T, gates.T, tokens, grad_out, w_in, w_out)
    ]
    own_rows, other_rows, place, routes, weights = call(
        gather_kernel,
        (
            pltpu.VMEM((2 * capacity, wide), BF16),
            pltpu.VMEM((2 * capacity, wide), BF16),
            pltpu.VMEM((slots, tok_rows), BF16),
            pltpu.VMEM((2, tok_rows), jnp.int32),
            pltpu.VMEM((2 * hidden, feats), BF16),
        ),
        4 * slots * tok_rows * feats,
        4 * tok_rows * feats + 4 * hidden * feats,
        in_specs=[hbm] * 6,
        scratch_shapes=[
            pltpu.VMEM((2, tok_rows), BF16),
            pltpu.VMEM((tok_rows, feats), BF16),
            pltpu.VMEM((tok_rows, feats), BF16),
            pltpu.SemaphoreType.DMA((3 + 2 * PIECES + feats // hidden,)),
        ],
    )(*inputs)

    other_weights = swap(weights, "local", 1)

    half_nodes = nodes // WINDOW
    pieces = [own_rows]
    for step in range(1, nodes):
        pieces.append(swap_nodes(own_rows if step < half_nodes else other_rows, step))
    rows = half_nodes * (locals_ // 2) * capacity
    bits = [1 << place for place in range(edatas.bit_length() - 1)]
    orders = (bits[::-1], bits)
    last = ()
    chains = []
    held = []
    for chunk, order in zip((pieces[:half_nodes], pieces[half_nodes:]), orders):
        chunk = join(chunk, last)
        bit = 2
        while bit < locals_:
            chunk = join([chunk, swap(chunk, "local", bit)])
            bit *= 2
        held.append(chunk)
        part, gate_rows = call(
            functools.partial(part_kernel, capacity),
            (shape((rows, coded), I16), shape((rows, LANES), F32)),
            16 * rows * feats * hidden,
            4 * rows * feats + 8 * feats * hidden,
            after=last,
        )(chunk, weights, other_weights)
        last = (part,)
        chains.append((part, swap(part, "edata", order[0]), gate_rows))
    for stage in range(1, len(bits)):
        for index, (part, other, gate_rows) in enumerate(chains):
            part = call(
                add_codes_kernel,
                shape((rows, coded), I16),
                16 * rows * hidden,
                6 * rows * coded,
                after=last,
            )(part, other)
            last = (part,)
            chains[index] = (part, swap(part, "edata", orders[index][stage]), gate_rows)

    mine = []
    theirs = ()
    slots_back = []
    for index, (part, other, gate_rows) in enumerate(chains):
        dealt = [shape((capacity, wide), BF16 if index else F32)] * half_nodes
        own, packed, *slot_parts = call(
            functools.partial(slot_kernel, capacity, len(theirs)),
            [
                shape((2 * rows, hidden), BF16),
                shape(((1 + len(theirs)) * 2 * rows, hidden), BF16),
                *(dealt if locals_ == 2 else [shape((rows, wide), F32)]),
            ],
            4 * rows * feats * hidden,
            4 * feats * hidden + 4 * rows * feats,
            after=last,
        )(part, other, gate_rows, weights, other_weights, *theirs)
        last = (own,)
        if index == 0:
            spread, masks = call(
                plan_kernel,
                (shape((tok_rows, 2 * slots), BF16), shape((2 * WINDOW, tok_rows), F32)),
                0,
                8 * slots * tok_rows,
                after=last,
            )(place, routes)
            last = (spread,)
        mine.append(own)
        theirs = (packed,)
        if locals_ > 2:
            half = rows // 2
            keep, send = slot_parts[0][:half], slot_parts[0][half:]
            bit = locals_ // 2
            while bit > 2:
                half //= 2
                keep, send = call(
                    halve_kernel,
                    (shape((half, wide), F32),) * 2,
                    4 * half * wide,
                    24 * half * wide,
                )(keep, swap(send, "local", bit))
                bit //= 2
            slot_parts = call(deal_kernel, dealt, 4 * half * wide, 12 * half * wide)(
                keep, swap(send, "local", bit)
            )
        for step, send in enumerate(slot_parts, index * half_nodes):
            slots_back.append(swap_nodes(send, step) if step else send)
    came = [swap(chunk, "local", 1) for chunk in held]
    back = swap(theirs[0], "local", 1)
    grad_w_in, grad_w_out, written = call(
        functools.partial(weight_kernel, capacity),
        (shape((feats, hidden), F32), shape((hidden, feats), F32), shape((8, LANES), F32)),
        32 * rows * feats * hidden,
        8 * feats * hidden,
        in_specs=[vmem] * 7,
        after=slots_back[1:half_nodes],
        out_specs=[hbm, hbm, vmem],
        scratch_shapes=[
            pltpu.VMEM((feats, hidden), F32),
            pltpu.VMEM((hidden, feats), F32),
            pltpu.SemaphoreType.DMA((2 * PIECES,)),
        ],
    )(*held, *came, *mine, back)
    grad_tokens, grad_gates = call(
        functools.partial(combine_kernel, nodes),
        (shape((tok_rows, feats), BF16), shape((2, tok_rows), F32)),
        4 * slots * tok_rows * feats,
        2 * tok_rows * feats,
        after=(written,),
    )(*slots_back[:half_nodes], *reversed(slots_back[half_nodes:]), place, spread, masks)
    return (grad_tokens, grad_gates.T, grad_w_in, grad_w_out)


def solution(mesh):
    in_specs = (
        P(("node", "local"), "edata"),
        P(("node", "local"), "edata"),
        P(("node", "local"), None),
        P(("node", "local"), None),
        P("edata", ("node", "local")),
        P(("node", "local"), "edata"),
    )
    out_specs = (
        P(("node", "local"), "edata"),
        P(("node", "local"), None),
        P("edata", ("node", "local")),
        P(("node", "local"), "edata"),
    )
    return jax.shard_map(body, mesh=mesh, in_specs=in_specs, out_specs=out_specs, check_vma=False)
```

```python
import functools

import jax
import jax.numpy as jnp
from jax import lax
from jax.experimental import pallas as pl
from jax.experimental.pallas import tpu as pltpu
from jax.sharding import PartitionSpec as P

EXPERTS = 64
WINDOW = 2
LANES = 128
PIECES = 4
VMEM_LIMIT = 40 * 1024 * 1024

BF16 = jnp.bfloat16
F32 = jnp.float32
I16 = jnp.int16
ROWS_BY_ROWS = (((0,), (0,)), ((), ()))
COLS_BY_COLS = (((1,), (1,)), ((), ()))


def gelu_pair(pre_act):
    coefficient = 0.7978845608028654
    square = pre_act * pre_act
    tanh_val = jnp.tanh(coefficient * (pre_act + 0.044715 * pre_act * square))
    half = 0.5 * (1.0 + tanh_val)
    activation = pre_act * half
    slopes = half + 0.5 * pre_act * (1.0 - tanh_val * tanh_val) * coefficient * (
        1.0 + 3.0 * 0.044715 * square
    )
    return (activation, slopes)


def call(kernel, out_shape, flops, moved, limit=VMEM_LIMIT, in_specs=None, after=(), **more):
    def run(*operands):
        given = in_specs or [pl.BlockSpec(memory_space=pltpu.VMEM)] * len(operands)
        return pl.pallas_call(
            lambda *refs: kernel(*refs[len(after) :]),
            out_shape=out_shape,
            in_specs=[pl.BlockSpec(memory_space=pl.ANY)] * len(after) + list(given),
            compiler_params=pltpu.CompilerParams(vmem_limit_bytes=limit),
            cost_estimate=pl.CostEstimate(flops=flops, bytes_accessed=moved, transcendentals=0),
            **more,
        )(*after, *operands)

    return run


def own_expert():
    half_nodes = lax.axis_size("node") // WINDOW
    return lax.axis_index("node") // half_nodes


def split_value(value):
    high = value.astype(BF16).astype(F32)
    lane = lax.broadcasted_iota(jnp.int32, (value.shape[0], LANES), 1)
    return jnp.where(lane == 0, high, jnp.where(lane == 1, value - high, 0.0))


def encode(values):
    top = jnp.max(jnp.abs(values), axis=1, keepdims=True)
    power = jnp.ceil(jnp.log2(jnp.maximum(top, 1e-30)))
    codes = jnp.round(values * (1.999 * jnp.exp2(14.0 - power)))
    return codes.astype(jnp.int32).astype(I16), power


def decode(codes, power):
    return codes.astype(jnp.int32).astype(F32) * (jnp.exp2(power - 14.0) / 1.999)


def store_codes(out_ref, pair):
    hidden = pair[0].shape[1]
    lane = lax.broadcasted_iota(jnp.int32, (pair[0].shape[0], LANES), 1)
    powers = []
    for index, values in enumerate(pair):
        codes, power = encode(values)
        out_ref[:, index * hidden : (index + 1) * hidden] = codes
        powers.append(power)
    powers = jnp.where(lane == 0, powers[0], powers[1])
    out_ref[:, 2 * hidden :] = powers.astype(jnp.int32).astype(I16)


def load_codes(ref):
    hidden = (ref.shape[1] - LANES) // 2
    powers = ref[:, 2 * hidden :].astype(jnp.int32).astype(F32)
    return [
        decode(ref[:, index * hidden : (index + 1) * hidden], powers[:, index : index + 1])
        for index in range(2)
    ]


def gather_kernel(routes_hbm, gates_hbm, tokens_hbm, grads_hbm, w_in_hbm, w_out_hbm, own_ref,
                  other_ref, place_ref, routes_ref, w_ref, gates_ref, tokens_ref, grads_ref, sems):
    tok_rows, feats = tokens_ref.shape
    capacity = own_ref.shape[0] // 2
    slots = WINDOW * capacity
    copies = [
        pltpu.make_async_copy(routes_hbm, routes_ref, sems.at[0]),
        pltpu.make_async_copy(gates_hbm, gates_ref, sems.at[1]),
    ]
    count = tok_rows // PIECES
    for source, target in ((tokens_hbm, tokens_ref), (grads_hbm, grads_ref)):
        for piece in range(PIECES):
            span = pl.ds(piece * count, count)
            copies.append(
                pltpu.make_async_copy(source.at[span], target.at[span], sems.at[len(copies)])
            )
    hidden = w_out_hbm.shape[0]
    upper, lower = pl.ds(0, hidden), pl.ds(hidden, hidden)
    moves = [(w_out_hbm, w_ref.at[upper])]
    for block in range(0, feats, hidden):
        span = pl.ds(block, hidden)
        moves.append((w_in_hbm.at[span], w_ref.at[lower, span]))
    for source, target in moves:
        copies.append(pltpu.make_async_copy(source, target, sems.at[len(copies)]))
    for copy in copies:
        copy.start()
    earlier = lax.broadcasted_iota(jnp.int32, (tok_rows, tok_rows), 0) < lax.broadcasted_iota(
        jnp.int32, (tok_rows, tok_rows), 1
    )
    earlier = earlier.astype(F32).astype(BF16)
    slot_of = lax.broadcasted_iota(jnp.int32, (capacity, tok_rows), 0).astype(F32)
    row_of = lax.broadcasted_iota(jnp.int32, (8, tok_rows), 0)
    own = own_expert()
    copies[0].wait()
    copies[1].wait()
    routes = routes_ref[...]
    gates = gates_ref[...].astype(F32)
    hits = [(routes == expert).astype(F32) for expert in (own, 1 - own)]
    named = [hit[0:1] + hit[1:2] for hit in hits]
    weight = [hit * gates for hit in hits]
    weight = [value[0:1] + value[1:2] for value in weight]
    names = jnp.where(row_of == 0, named[0], jnp.where(row_of == 1, named[1], 0.0)).astype(BF16)
    before = jnp.dot(names, earlier, preferred_element_type=F32)
    parts = [jnp.where(before[e : e + 1] == slot_of, named[e], 0.0) for e in range(WINDOW)]
    place = jnp.concatenate(parts, axis=0).astype(BF16)
    place_ref[...] = place
    for copy in copies[2 : 2 + PIECES]:
        copy.wait()
    rows_x = jnp.dot(place, tokens_ref[...], preferred_element_type=F32)
    for copy in copies[2 + PIECES : 2 + 2 * PIECES]:
        copy.wait()
    rows_dy = jnp.dot(place, grads_ref[...], preferred_element_type=F32)
    for expert, out_ref in ((0, own_ref), (1, other_ref)):
        span = slice(expert * capacity, (expert + 1) * capacity)
        out_ref[:, :feats] = jnp.concatenate([rows_x[span], rows_dy[span]], axis=0).astype(BF16)
        gate = jnp.sum(parts[expert] * weight[expert], axis=1, keepdims=True)
        gate = jnp.concatenate([gate, gate], axis=0)
        out_ref[:, feats:] = jnp.broadcast_to(gate, (2 * capacity, LANES)).astype(BF16)
    for copy in copies[2 + 2 * PIECES :]:
        copy.wait()


def plan_kernel(place_ref, routes_ref, spread_ref, masks_ref):
    place = place_ref[...].astype(F32)
    spread_ref[...] = jnp.concatenate([place, place], axis=0).T.astype(BF16)
    routes = routes_ref[...]
    own = own_expert()
    for index, expert in enumerate((own, 1 - own)):
        masks_ref[2 * index : 2 * index + 2] = (routes == expert).astype(F32)


def join_kernel(*refs):
    *pieces, out_ref = refs
    rows = pieces[0].shape[0]
    for index, ref in enumerate(pieces):
        out_ref[index * rows : (index + 1) * rows] = ref[...]


def part_kernel(capacity, rows_ref, w_ref, w_other_ref, part_ref, gate_ref):
    feats = w_ref.shape[1]
    hidden = w_ref.shape[0] // 2
    groups = rows_ref.shape[0] // (2 * capacity)
    gate = rows_ref[:, feats:].astype(F32).reshape(groups, 2 * capacity, LANES)
    gate_ref[...] = gate[:, :capacity].reshape(groups * capacity, LANES)
    rows = rows_ref[:, :feats]
    pre = []
    back = []
    for ref in (w_ref, w_other_ref):
        pre.append(
            sum(
                jnp.dot(
                    rows[:, block : block + hidden],
                    ref[hidden:, block : block + hidden],
                    preferred_element_type=F32,
                )
                for block in range(0, feats, hidden)
            )
        )
        back.append(
            lax.dot_general(rows, ref[:hidden], COLS_BY_COLS, preferred_element_type=F32)
        )
    pair = []
    for values, span in ((pre, slice(0, capacity)), (back, slice(capacity, 2 * capacity))):
        values = jnp.concatenate(values, axis=1).reshape(groups, 2 * capacity, 2 * hidden)
        pair.append(values[:, span].reshape(groups * capacity, 2 * hidden))
    store_codes(part_ref, pair)


def add_codes_kernel(first_ref, second_ref, out_ref):
    pairs = zip(load_codes(first_ref), load_codes(second_ref))
    store_codes(out_ref, [first + second for first, second in pairs])


def deal(total, refs):
    each, wide = refs[0].shape
    feats = wide - LANES
    gate = split_value(jnp.sum(total[:, feats:], axis=1, keepdims=True))
    for index, ref in enumerate(refs):
        span = slice(index * each, (index + 1) * each)
        ref[:, :feats] = total[span, :feats].astype(ref.dtype)
        ref[:, feats:] = gate[span].astype(ref.dtype)


def slot_kernel(capacity, before, first_ref, second_ref, gate_ref, w_ref, w_other_ref, *refs):
    before_refs, (mine_ref, theirs_ref, *slot_refs) = refs[:before], refs[before:]
    hidden = w_ref.shape[0] // 2
    pairs = zip(load_codes(first_ref), load_codes(second_ref))
    pre, back = [first + second for first, second in pairs]
    gate = gate_ref[:, :1]
    activation, slopes = gelu_pair(pre)
    dpre = (gate * back * slopes).astype(BF16)
    act = gate * activation
    slot = []
    for block in range(0, w_ref.shape[1], hidden):
        span = slice(block, block + hidden)
        slot.append(
            sum(
                lax.dot_general(
                    part, ref[hidden:, span], COLS_BY_COLS, preferred_element_type=F32
                )
                for part, ref in ((dpre[:, :hidden], w_ref), (dpre[:, hidden:], w_other_ref))
            )
        )
    slot_gate = split_value(jnp.sum(activation * back, axis=1, keepdims=True))
    total = jnp.concatenate(slot + [slot_gate], axis=1)
    if len(slot_refs) == 1:
        slot_refs[0][...] = total
    else:
        deal(total, slot_refs)
    rows = dpre.shape[0]
    both = [
        value.reshape(rows // capacity, capacity, 2 * hidden) for value in (dpre.astype(F32), act)
    ]
    both = jnp.concatenate(both, axis=1).reshape(2 * rows, 2 * hidden).astype(BF16)
    mine_ref[...] = both[:, :hidden]
    count = 2 * rows
    for index, ref in enumerate(before_refs):
        theirs_ref[index * count : (index + 1) * count] = ref[...]
    theirs_ref[before * count :] = both[:, hidden:]


def halve_kernel(kept_ref, came_ref, keep_ref, send_ref):
    half = keep_ref.shape[0]
    total = kept_ref[...] + came_ref[...]
    keep_ref[...] = total[:half]
    send_ref[...] = total[half:]


def deal_kernel(kept_ref, came_ref, *refs):
    deal(kept_ref[...] + came_ref[...], refs)


def weight_kernel(capacity, *refs):
    rows_refs, both_refs = refs[:4], refs[4:8]
    w_in_hbm, w_out_hbm, written_ref, w_in_ref, w_out_ref, sems = refs[8:]
    feats, hidden = w_in_ref.shape
    rows = jnp.concatenate([ref[:, :feats] for ref in rows_refs], axis=0)
    both = jnp.concatenate([ref[...] for ref in both_refs], axis=0).astype(F32)
    of_x = lax.broadcasted_iota(jnp.int32, both.shape, 0) % (2 * capacity) < capacity
    dpre = jnp.where(of_x, both, 0.0).astype(BF16)
    act = jnp.where(of_x, 0.0, both).astype(BF16)
    count = feats // PIECES
    copies = []
    for piece in range(PIECES):
        span = slice(piece * count, (piece + 1) * count)
        part = rows[:, span]
        w_in_ref[span] = lax.dot_general(part, dpre, ROWS_BY_ROWS, preferred_element_type=F32)
        w_out_ref[:, span] = lax.dot_general(act, part, ROWS_BY_ROWS, preferred_element_type=F32)
        span = pl.ds(piece * count, count)
        for source, target in (
            (w_in_ref.at[span], w_in_hbm.at[span]),
            (w_out_ref.at[:, span], w_out_hbm.at[:, span]),
        ):
            copy = pltpu.make_async_copy(source, target, sems.at[len(copies)])
            copy.start()
            copies.append(copy)
    for copy in copies:
        copy.wait()
    written_ref[...] = jnp.zeros(written_ref.shape, F32)


def combine_kernel(steps, *refs):
    kept_ref, came_refs = refs[0], refs[1:steps]
    place_ref, spread_ref, masks_ref, tokens_ref, gate_out_ref = refs[steps:]
    feats = tokens_ref.shape[1]
    capacity = kept_ref.shape[0]
    came = [ref[...].astype(F32) for ref in came_refs]
    half = steps // WINDOW
    own = sum(came[: half - 1], kept_ref[...])
    other = sum(came[half:], came[half - 1])
    slots = jnp.concatenate([own, other], axis=0)
    grads = slots[:, :feats]
    high = grads.astype(BF16)
    low = (grads - high.astype(F32)).astype(BF16)
    both = jnp.concatenate([high, low], axis=0)
    tokens_ref[...] = jnp.dot(spread_ref[...], both, preferred_element_type=F32).astype(BF16)
    slot_gate = jnp.sum(slots[:, feats:], axis=1, keepdims=True)
    picked = place_ref[...].astype(F32) * slot_gate
    masks = masks_ref[...]
    result = jnp.zeros(gate_out_ref.shape, F32)
    for index in range(WINDOW):
        span = slice(index * capacity, (index + 1) * capacity)
        value = jnp.sum(picked[span], axis=0, keepdims=True)
        result = result + masks[2 * index : 2 * index + 2] * value
    gate_out_ref[...] = result


def swap(array, axes, bit):
    size = lax.axis_size(axes)
    return lax.ppermute(array, axes, [(index, index ^ bit) for index in range(size)])


def swap_nodes(array, step):
    return swap(array, ("node", "local"), step * lax.axis_size("local") + 1)


def join(pieces, after=()):
    rows, wide = pieces[0].shape
    rows *= len(pieces)
    shape = jax.ShapeDtypeStruct((rows, wide), BF16)
    return call(join_kernel, shape, 0, 4 * rows * wide, after=after)(*pieces)


def body(tokens, grad_out, routes, gates, w_in, w_out):
    nodes = lax.axis_size("node")
    locals_ = lax.axis_size("local")
    edatas = lax.axis_size("edata")
    tok_rows, feats = tokens.shape
    hidden = w_in.shape[1]
    capacity = 2 * tok_rows // EXPERTS
    slots = WINDOW * capacity
    wide = feats + LANES
    coded = 4 * hidden + LANES
    shape = jax.ShapeDtypeStruct
    hbm = pl.BlockSpec(memory_space=pltpu.HBM)
    vmem = pl.BlockSpec(memory_space=pltpu.VMEM)

    inputs = [
        pltpu.with_memory_space_constraint(value, pltpu.HBM)
        for value in (routes.T, gates.T, tokens, grad_out, w_in, w_out)
    ]
    own_rows, other_rows, place, routes, weights = call(
        gather_kernel,
        (
            pltpu.VMEM((2 * capacity, wide), BF16),
            pltpu.VMEM((2 * capacity, wide), BF16),
            pltpu.VMEM((slots, tok_rows), BF16),
            pltpu.VMEM((2, tok_rows), jnp.int32),
            pltpu.VMEM((2 * hidden, feats), BF16),
        ),
        4 * slots * tok_rows * feats,
        4 * tok_rows * feats + 4 * hidden * feats,
        in_specs=[hbm] * 6,
        scratch_shapes=[
            pltpu.VMEM((2, tok_rows), BF16),
            pltpu.VMEM((tok_rows, feats), BF16),
            pltpu.VMEM((tok_rows, feats), BF16),
            pltpu.SemaphoreType.DMA((3 + 2 * PIECES + feats // hidden,)),
        ],
    )(*inputs)

    other_weights = swap(weights, "local", 1)

    half_nodes = nodes // WINDOW
    pieces = [own_rows]
    for step in range(1, nodes):
        pieces.append(swap_nodes(own_rows if step < half_nodes else other_rows, step))
    rows = half_nodes * (locals_ // 2) * capacity
    last = ()
    chains = []
    held = []
    for chunk in (pieces[:half_nodes], pieces[half_nodes:]):
        chunk = join(chunk, last)
        bit = 2
        while bit < locals_:
            chunk = join([chunk, swap(chunk, "local", bit)])
            bit *= 2
        held.append(chunk)
        part, gate_rows = call(
            functools.partial(part_kernel, capacity),
            (shape((rows, coded), I16), shape((rows, LANES), F32)),
            16 * rows * feats * hidden,
            4 * rows * feats + 8 * feats * hidden,
            after=last,
        )(chunk, weights, other_weights)
        last = (part,)
        chains.append((part, swap(part, "edata", edatas // 2), gate_rows))
    bit = edatas // 4
    while bit:
        for index, (part, other, gate_rows) in enumerate(chains):
            part = call(
                add_codes_kernel,
                shape((rows, coded), I16),
                16 * rows * hidden,
                6 * rows * coded,
                after=last,
            )(part, other)
            last = (part,)
            chains[index] = (part, swap(part, "edata", bit), gate_rows)
        bit //= 2

    mine = []
    theirs = ()
    slots_back = []
    for index, (part, other, gate_rows) in enumerate(chains):
        dealt = [shape((capacity, wide), BF16 if index else F32)] * half_nodes
        own, packed, *slot_parts = call(
            functools.partial(slot_kernel, capacity, 0),
            [
                shape((2 * rows, hidden), BF16),
                shape((2 * rows, hidden), BF16),
                *(dealt if locals_ == 2 else [shape((rows, wide), F32)]),
            ],
            4 * rows * feats * hidden,
            4 * feats * hidden + 4 * rows * feats,
            after=last,
        )(part, other, gate_rows, weights, other_weights)
        last = (own,)
        if index == 0:
            spread, masks = call(
                plan_kernel,
                (shape((tok_rows, 2 * slots), BF16), shape((2 * WINDOW, tok_rows), F32)),
                0,
                8 * slots * tok_rows,
                after=last,
            )(place, routes)
            last = (spread,)
        mine.append(own)
        theirs += (packed,)
        if locals_ > 2:
            half = rows // 2
            keep, send = slot_parts[0][:half], slot_parts[0][half:]
            bit = locals_ // 2
            while bit > 2:
                half //= 2
                keep, send = call(
                    halve_kernel,
                    (shape((half, wide), F32),) * 2,
                    4 * half * wide,
                    24 * half * wide,
                )(keep, swap(send, "local", bit))
                bit //= 2
            slot_parts = call(deal_kernel, dealt, 4 * half * wide, 12 * half * wide)(
                keep, swap(send, "local", bit)
            )
        for step, send in enumerate(slot_parts, index * half_nodes):
            slots_back.append(swap_nodes(send, step) if step else send)
    came = [swap(chunk, "local", 1) for chunk in held]
    back = [swap(packed, "local", 1) for packed in theirs]
    grad_w_in, grad_w_out, written = call(
        functools.partial(weight_kernel, capacity),
        (shape((feats, hidden), F32), shape((hidden, feats), F32), shape((8, LANES), F32)),
        0,
        0,
        in_specs=[vmem] * 8,
        after=slots_back[1:half_nodes],
        out_specs=[hbm, hbm, vmem],
        scratch_shapes=[
            pltpu.VMEM((feats, hidden), F32),
            pltpu.VMEM((hidden, feats), F32),
            pltpu.SemaphoreType.DMA((2 * PIECES,)),
        ],
    )(*held, *came, *mine, *back)
    grad_tokens, grad_gates = call(
        functools.partial(combine_kernel, nodes),
        (shape((tok_rows, feats), BF16), shape((2, tok_rows), F32)),
        4 * slots * tok_rows * feats,
        2 * tok_rows * feats,
        after=(written,),
    )(*slots_back[:half_nodes], *reversed(slots_back[half_nodes:]), place, spread, masks)
    return (grad_tokens, grad_gates.T, grad_w_in, grad_w_out)


def solution(mesh):
    in_specs = (
        P(("node", "local"), "edata"),
        P(("node", "local"), "edata"),
        P(("node", "local"), None),
        P(("node", "local"), None),
        P("edata", ("node", "local")),
        P(("node", "local"), "edata"),
    )
    out_specs = (
        P(("node", "local"), "edata"),
        P(("node", "local"), None),
        P("edata", ("node", "local")),
        P(("node", "local"), "edata"),
    )
    return jax.shard_map(body, mesh=mesh, in_specs=in_specs, out_specs=out_specs, check_vma=False)
```

```python
import functools

import jax
import jax.numpy as jnp
from jax import lax
from jax.experimental import pallas as pl
from jax.experimental.pallas import tpu as pltpu
from jax.sharding import PartitionSpec as P

EXPERTS = 64
WINDOW = 2
LANES = 128
PIECES = 4
LOADS = 2
VMEM_LIMIT = 40 * 1024 * 1024

BF16 = jnp.bfloat16
F32 = jnp.float32
I16 = jnp.int16
ROWS_BY_ROWS = (((0,), (0,)), ((), ()))
COLS_BY_COLS = (((1,), (1,)), ((), ()))


def gelu_pair(pre_act):
    coefficient = 0.7978845608028654
    square = pre_act * pre_act
    tanh_val = jnp.tanh(coefficient * (pre_act + 0.044715 * pre_act * square))
    half = 0.5 * (1.0 + tanh_val)
    activation = pre_act * half
    slopes = half + 0.5 * pre_act * (1.0 - tanh_val * tanh_val) * coefficient * (
        1.0 + 3.0 * 0.044715 * square
    )
    return (activation, slopes)


def call(kernel, out_shape, flops, moved, limit=VMEM_LIMIT, in_specs=None, after=(), **more):
    def run(*operands):
        given = in_specs or [pl.BlockSpec(memory_space=pltpu.VMEM)] * len(operands)
        return pl.pallas_call(
            lambda *refs: kernel(*refs[len(after) :]),
            out_shape=out_shape,
            in_specs=[pl.BlockSpec(memory_space=pl.ANY)] * len(after) + list(given),
            compiler_params=pltpu.CompilerParams(vmem_limit_bytes=limit),
            cost_estimate=pl.CostEstimate(flops=flops, bytes_accessed=moved, transcendentals=0),
            **more,
        )(*after, *operands)

    return run


def own_expert():
    half_nodes = lax.axis_size("node") // WINDOW
    return lax.axis_index("node") // half_nodes


def split_value(value):
    high = value.astype(BF16).astype(F32)
    lane = lax.broadcasted_iota(jnp.int32, (value.shape[0], LANES), 1)
    return jnp.where(lane == 0, high, jnp.where(lane == 1, value - high, 0.0))


def encode(values):
    top = jnp.max(jnp.abs(values), axis=1, keepdims=True)
    power = jnp.ceil(jnp.log2(jnp.maximum(top, 1e-30)))
    codes = jnp.round(values * (1.999 * jnp.exp2(14.0 - power)))
    return codes.astype(jnp.int32).astype(I16), power


def decode(codes, power):
    return codes.astype(jnp.int32).astype(F32) * (jnp.exp2(power - 14.0) / 1.999)


def store_codes(out_ref, pair):
    hidden = pair[0].shape[1]
    lane = lax.broadcasted_iota(jnp.int32, (pair[0].shape[0], LANES), 1)
    powers = []
    for index, values in enumerate(pair):
        codes, power = encode(values)
        out_ref[:, index * hidden : (index + 1) * hidden] = codes
        powers.append(power)
    powers = jnp.where(lane == 0, powers[0], powers[1])
    out_ref[:, 2 * hidden :] = powers.astype(jnp.int32).astype(I16)


def load_codes(ref):
    hidden = (ref.shape[1] - LANES) // 2
    powers = ref[:, 2 * hidden :].astype(jnp.int32).astype(F32)
    return [
        decode(ref[:, index * hidden : (index + 1) * hidden], powers[:, index : index + 1])
        for index in range(2)
    ]


def gather_kernel(routes_hbm, gates_hbm, tokens_hbm, grads_hbm, w_in_hbm, w_out_hbm, own_ref,
                  other_ref, place_ref, spread_ref, w_ref, routes_ref, gates_ref, tokens_ref,
                  grads_ref, sems):
    tok_rows, feats = tokens_ref.shape
    capacity = own_ref.shape[0] // 2
    slots = WINDOW * capacity
    copies = [
        pltpu.make_async_copy(routes_hbm, routes_ref, sems.at[0]),
        pltpu.make_async_copy(gates_hbm, gates_ref, sems.at[1]),
    ]
    count = tok_rows // LOADS
    for source, target in ((tokens_hbm, tokens_ref), (grads_hbm, grads_ref)):
        for piece in range(LOADS):
            span = pl.ds(piece * count, count)
            copies.append(
                pltpu.make_async_copy(source.at[span], target.at[span], sems.at[len(copies)])
            )
    hidden = w_out_hbm.shape[0]
    upper, lower = pl.ds(0, hidden), pl.ds(hidden, hidden)
    moves = [(w_out_hbm, w_ref.at[upper])]
    for block in range(0, feats, hidden):
        span = pl.ds(block, hidden)
        moves.append((w_in_hbm.at[span], w_ref.at[lower, span]))
    for source, target in moves:
        copies.append(pltpu.make_async_copy(source, target, sems.at[len(copies)]))
    for copy in copies:
        copy.start()
    earlier = lax.broadcasted_iota(jnp.int32, (tok_rows, tok_rows), 0) < lax.broadcasted_iota(
        jnp.int32, (tok_rows, tok_rows), 1
    )
    earlier = earlier.astype(F32).astype(BF16)
    slot_of = lax.broadcasted_iota(jnp.int32, (capacity, tok_rows), 0).astype(F32)
    row_of = lax.broadcasted_iota(jnp.int32, (8, tok_rows), 0)
    own = own_expert()
    copies[0].wait()
    copies[1].wait()
    routes = routes_ref[...]
    gates = gates_ref[...].astype(F32)
    hits = [(routes == expert).astype(F32) for expert in (own, 1 - own)]
    named = [hit[0:1] + hit[1:2] for hit in hits]
    weight = [hit * gates for hit in hits]
    weight = [value[0:1] + value[1:2] for value in weight]
    names = jnp.where(row_of == 0, named[0], jnp.where(row_of == 1, named[1], 0.0)).astype(BF16)
    before = jnp.dot(names, earlier, preferred_element_type=F32)
    parts = [jnp.where(before[e : e + 1] == slot_of, named[e], 0.0) for e in range(WINDOW)]
    place = jnp.concatenate(parts, axis=0).astype(BF16)
    place_ref[:slots] = place
    spread_ref[...] = jnp.concatenate(parts + parts, axis=0).T.astype(BF16)
    masks = jnp.zeros((16, tok_rows), F32)
    row_of = lax.broadcasted_iota(jnp.int32, masks.shape, 0)
    for index, hit in enumerate(hits):
        for k in range(2):
            masks = jnp.where(row_of == 2 * index + k, hit[k : k + 1], masks)
    place_ref[slots:] = masks.astype(BF16)
    for copy in copies[2 : 2 + LOADS]:
        copy.wait()
    rows_x = jnp.dot(place, tokens_ref[...], preferred_element_type=F32)
    for copy in copies[2 + LOADS : 2 + 2 * LOADS]:
        copy.wait()
    rows_dy = jnp.dot(place, grads_ref[...], preferred_element_type=F32)
    for expert, out_ref in ((0, own_ref), (1, other_ref)):
        span = slice(expert * capacity, (expert + 1) * capacity)
        out_ref[:, :feats] = jnp.concatenate([rows_x[span], rows_dy[span]], axis=0).astype(BF16)
        gate = jnp.sum(parts[expert] * weight[expert], axis=1, keepdims=True)
        gate = jnp.concatenate([gate, gate], axis=0)
        out_ref[:, feats:] = jnp.broadcast_to(gate, (2 * capacity, LANES)).astype(BF16)
    for copy in copies[2 + 2 * LOADS :]:
        copy.wait()


def join_kernel(*refs):
    *pieces, out_ref = refs
    rows = pieces[0].shape[0]
    for index, ref in enumerate(pieces):
        out_ref[index * rows : (index + 1) * rows] = ref[...]


def part_kernel(capacity, rows_ref, w_ref, w_other_ref, part_ref, gate_ref):
    feats = w_ref.shape[1]
    hidden = w_ref.shape[0] // 2
    groups = rows_ref.shape[0] // (2 * capacity)
    gate = rows_ref[:, feats:].astype(F32).reshape(groups, 2 * capacity, LANES)
    gate_ref[...] = gate[:, :capacity].reshape(groups * capacity, LANES)
    rows = rows_ref[:, :feats]
    pre = []
    back = []
    for ref in (w_ref, w_other_ref):
        pre.append(
            sum(
                jnp.dot(
                    rows[:, block : block + hidden],
                    ref[hidden:, block : block + hidden],
                    preferred_element_type=F32,
                )
                for block in range(0, feats, hidden)
            )
        )
        back.append(
            lax.dot_general(rows, ref[:hidden], COLS_BY_COLS, preferred_element_type=F32)
        )
    pair = []
    for values, span in ((pre, slice(0, capacity)), (back, slice(capacity, 2 * capacity))):
        values = jnp.concatenate(values, axis=1).reshape(groups, 2 * capacity, 2 * hidden)
        pair.append(values[:, span].reshape(groups * capacity, 2 * hidden))
    store_codes(part_ref, pair)


def add_codes_kernel(first_ref, second_ref, out_ref):
    pairs = zip(load_codes(first_ref), load_codes(second_ref))
    store_codes(out_ref, [first + second for first, second in pairs])


def deal(total, refs):
    each, wide = refs[0].shape
    feats = wide - LANES
    gate = split_value(jnp.sum(total[:, feats:], axis=1, keepdims=True))
    for index, ref in enumerate(refs):
        span = slice(index * each, (index + 1) * each)
        ref[:, :feats] = total[span, :feats].astype(ref.dtype)
        ref[:, feats:] = gate[span].astype(ref.dtype)


def slot_kernel(capacity, before, first_ref, second_ref, gate_ref, w_ref, w_other_ref, *refs):
    before_refs, (mine_ref, theirs_ref, *slot_refs) = refs[:before], refs[before:]
    hidden = w_ref.shape[0] // 2
    pairs = zip(load_codes(first_ref), load_codes(second_ref))
    pre, back = [first + second for first, second in pairs]
    gate = gate_ref[:, :1]
    activation, slopes = gelu_pair(pre)
    dpre = (gate * back * slopes).astype(BF16)
    act = gate * activation
    slot = []
    for block in range(0, w_ref.shape[1], hidden):
        span = slice(block, block + hidden)
        slot.append(
            sum(
                lax.dot_general(
                    part, ref[hidden:, span], COLS_BY_COLS, preferred_element_type=F32
                )
                for part, ref in ((dpre[:, :hidden], w_ref), (dpre[:, hidden:], w_other_ref))
            )
        )
    slot_gate = split_value(jnp.sum(activation * back, axis=1, keepdims=True))
    total = jnp.concatenate(slot + [slot_gate], axis=1)
    if len(slot_refs) == 1:
        slot_refs[0][...] = total
    else:
        deal(total, slot_refs)
    rows = dpre.shape[0]
    both = [
        value.reshape(rows // capacity, capacity, 2 * hidden) for value in (dpre.astype(F32), act)
    ]
    both = jnp.concatenate(both, axis=1).reshape(2 * rows, 2 * hidden).astype(BF16)
    mine_ref[...] = both[:, :hidden]
    count = 2 * rows
    for index, ref in enumerate(before_refs):
        theirs_ref[index * count : (index + 1) * count] = ref[...]
    theirs_ref[before * count :] = both[:, hidden:]


def halve_kernel(kept_ref, came_ref, keep_ref, send_ref):
    half = keep_ref.shape[0]
    total = kept_ref[...] + came_ref[...]
    keep_ref[...] = total[:half]
    send_ref[...] = total[half:]


def deal_kernel(kept_ref, came_ref, *refs):
    deal(kept_ref[...] + came_ref[...], refs)


def weight_kernel(capacity, *refs):
    rows_refs, both_refs = refs[:4], refs[4:7]
    w_in_hbm, w_out_hbm, written_ref, w_in_ref, w_out_ref, sems = refs[7:]
    feats, hidden = w_in_ref.shape
    rows = jnp.concatenate([ref[:, :feats] for ref in rows_refs], axis=0)
    both = jnp.concatenate([ref[...] for ref in both_refs], axis=0).astype(F32)
    of_x = lax.broadcasted_iota(jnp.int32, both.shape, 0) % (2 * capacity) < capacity
    dpre = jnp.where(of_x, both, 0.0).astype(BF16)
    act = jnp.where(of_x, 0.0, both).astype(BF16)
    count = feats // PIECES
    copies = []
    for piece in range(PIECES):
        span = slice(piece * count, (piece + 1) * count)
        part = rows[:, span]
        w_in_ref[span] = lax.dot_general(part, dpre, ROWS_BY_ROWS, preferred_element_type=F32)
        w_out_ref[:, span] = lax.dot_general(act, part, ROWS_BY_ROWS, preferred_element_type=F32)
        span = pl.ds(piece * count, count)
        for source, target in (
            (w_in_ref.at[span], w_in_hbm.at[span]),
            (w_out_ref.at[:, span], w_out_hbm.at[:, span]),
        ):
            copy = pltpu.make_async_copy(source, target, sems.at[len(copies)])
            copy.start()
            copies.append(copy)
    for copy in copies:
        copy.wait()
    written_ref[...] = jnp.zeros(written_ref.shape, F32)


def combine_kernel(steps, *refs):
    kept_ref, came_refs = refs[0], refs[1:steps]
    place_ref, spread_ref, tokens_ref, gate_out_ref = refs[steps:]
    feats = tokens_ref.shape[1]
    capacity = kept_ref.shape[0]
    came = [ref[...].astype(F32) for ref in came_refs]
    half = steps // WINDOW
    own = sum(came[: half - 1], kept_ref[...])
    other = sum(came[half:], came[half - 1])
    slots = jnp.concatenate([own, other], axis=0)
    grads = slots[:, :feats]
    high = grads.astype(BF16)
    low = (grads - high.astype(F32)).astype(BF16)
    both = jnp.concatenate([high, low], axis=0)
    tokens_ref[...] = jnp.dot(spread_ref[...], both, preferred_element_type=F32).astype(BF16)
    slot_gate = jnp.sum(slots[:, feats:], axis=1, keepdims=True)
    picked = place_ref[: WINDOW * capacity].astype(F32) * slot_gate
    masks = place_ref[WINDOW * capacity :].astype(F32)
    result = jnp.zeros(gate_out_ref.shape, F32)
    for index in range(WINDOW):
        span = slice(index * capacity, (index + 1) * capacity)
        value = jnp.sum(picked[span], axis=0, keepdims=True)
        result = result + masks[2 * index : 2 * index + 2] * value
    gate_out_ref[...] = result


def swap(array, axes, bit):
    size = lax.axis_size(axes)
    return lax.ppermute(array, axes, [(index, index ^ bit) for index in range(size)])


def swap_nodes(array, step):
    return swap(array, ("node", "local"), step * lax.axis_size("local") + 1)


def join(pieces, after=()):
    rows, wide = pieces[0].shape
    rows *= len(pieces)
    shape = jax.ShapeDtypeStruct((rows, wide), BF16)
    return call(join_kernel, shape, 0, 4 * rows * wide, after=after)(*pieces)


def body(tokens, grad_out, routes, gates, w_in, w_out):
    nodes = lax.axis_size("node")
    locals_ = lax.axis_size("local")
    edatas = lax.axis_size("edata")
    tok_rows, feats = tokens.shape
    hidden = w_in.shape[1]
    capacity = 2 * tok_rows // EXPERTS
    slots = WINDOW * capacity
    wide = feats + LANES
    coded = 4 * hidden + LANES
    shape = jax.ShapeDtypeStruct
    hbm = pl.BlockSpec(memory_space=pltpu.HBM)
    vmem = pl.BlockSpec(memory_space=pltpu.VMEM)

    inputs = [
        pltpu.with_memory_space_constraint(value, pltpu.HBM)
        for value in (routes.T, gates.T, tokens, grad_out, w_in, w_out)
    ]
    own_rows, other_rows, place, spread, weights = call(
        gather_kernel,
        (
            pltpu.VMEM((2 * capacity, wide), BF16),
            pltpu.VMEM((2 * capacity, wide), BF16),
            pltpu.VMEM((slots + 16, tok_rows), BF16),
            pltpu.VMEM((tok_rows, 2 * slots), BF16),
            pltpu.VMEM((2 * hidden, feats), BF16),
        ),
        4 * slots * tok_rows * feats,
        4 * tok_rows * feats + 4 * hidden * feats,
        in_specs=[hbm] * 6,
        scratch_shapes=[
            pltpu.VMEM((2, tok_rows), jnp.int32),
            pltpu.VMEM((2, tok_rows), BF16),
            pltpu.VMEM((tok_rows, feats), BF16),
            pltpu.VMEM((tok_rows, feats), BF16),
            pltpu.SemaphoreType.DMA((3 + 2 * LOADS + feats // hidden,)),
        ],
    )(*inputs)

    other_weights = swap(weights, "local", 1)

    half_nodes = nodes // WINDOW
    pieces = [own_rows]
    for step in range(1, nodes):
        pieces.append(swap_nodes(own_rows if step < half_nodes else other_rows, step))
    rows = half_nodes * (locals_ // 2) * capacity
    last = ()
    chains = []
    held = []
    for chunk in (pieces[:half_nodes], pieces[half_nodes:]):
        chunk = join(chunk, last)
        bit = 2
        while bit < locals_:
            chunk = join([chunk, swap(chunk, "local", bit)])
            bit *= 2
        held.append(chunk)
        part, gate_rows = call(
            functools.partial(part_kernel, capacity),
            (shape((rows, coded), I16), shape((rows, LANES), F32)),
            16 * rows * feats * hidden,
            4 * rows * feats + 8 * feats * hidden,
            after=last,
        )(chunk, weights, other_weights)
        last = (part,)
        chains.append((part, swap(part, "edata", edatas // 2), gate_rows))
    bit = edatas // 4
    while bit:
        for index, (part, other, gate_rows) in enumerate(chains):
            part = call(
                add_codes_kernel,
                shape((rows, coded), I16),
                16 * rows * hidden,
                6 * rows * coded,
                after=last,
            )(part, other)
            last = (part,)
            chains[index] = (part, swap(part, "edata", bit), gate_rows)
        bit //= 2

    mine = []
    theirs = ()
    slots_back = []
    for index, (part, other, gate_rows) in enumerate(chains):
        dealt = [shape((capacity, wide), BF16 if index else F32)] * half_nodes
        own, packed, *slot_parts = call(
            functools.partial(slot_kernel, capacity, len(theirs)),
            [
                shape((2 * rows, hidden), BF16),
                shape(((1 + len(theirs)) * 2 * rows, hidden), BF16),
                *(dealt if locals_ == 2 else [shape((rows, wide), F32)]),
            ],
            4 * rows * feats * hidden,
            4 * feats * hidden + 4 * rows * feats,
            after=last,
        )(part, other, gate_rows, weights, other_weights, *theirs)
        last = (own,)
        mine.append(own)
        theirs = (packed,)
        if locals_ > 2:
            half = rows // 2
            keep, send = slot_parts[0][:half], slot_parts[0][half:]
            bit = locals_ // 2
            while bit > 2:
                half //= 2
                keep, send = call(
                    halve_kernel,
                    (shape((half, wide), F32),) * 2,
                    4 * half * wide,
                    24 * half * wide,
                )(keep, swap(send, "local", bit))
                bit //= 2
            slot_parts = call(deal_kernel, dealt, 4 * half * wide, 12 * half * wide)(
                keep, swap(send, "local", bit)
            )
        for step, send in enumerate(slot_parts, index * half_nodes):
            slots_back.append(swap_nodes(send, step) if step else send)
    came = [swap(chunk, "local", 1) for chunk in held]
    back = swap(theirs[0], "local", 1)
    grad_w_in, grad_w_out, written = call(
        functools.partial(weight_kernel, capacity),
        (shape((feats, hidden), F32), shape((hidden, feats), F32), shape((8, LANES), F32)),
        32 * rows * feats * hidden,
        8 * feats * hidden,
        in_specs=[vmem] * 7,
        after=slots_back[1:half_nodes],
        out_specs=[hbm, hbm, vmem],
        scratch_shapes=[
            pltpu.VMEM((feats, hidden), F32),
            pltpu.VMEM((hidden, feats), F32),
            pltpu.SemaphoreType.DMA((2 * PIECES,)),
        ],
    )(*held, *came, *mine, back)
    grad_tokens, grad_gates = call(
        functools.partial(combine_kernel, nodes),
        (shape((tok_rows, feats), BF16), shape((2, tok_rows), F32)),
        4 * slots * tok_rows * feats,
        2 * tok_rows * feats,
        after=(written,),
    )(*slots_back[:half_nodes], *reversed(slots_back[half_nodes:]), place, spread)
    return (grad_tokens, grad_gates.T, grad_w_in, grad_w_out)


def solution(mesh):
    in_specs = (
        P(("node", "local"), "edata"),
        P(("node", "local"), "edata"),
        P(("node", "local"), None),
        P(("node", "local"), None),
        P("edata", ("node", "local")),
        P(("node", "local"), "edata"),
    )
    out_specs = (
        P(("node", "local"), "edata"),
        P(("node", "local"), None),
        P("edata", ("node", "local")),
        P(("node", "local"), "edata"),
    )
    return jax.shard_map(body, mesh=mesh, in_specs=in_specs, out_specs=out_specs, check_vma=False)
```

```python
import functools

import jax
import jax.numpy as jnp
from jax import lax
from jax.experimental import pallas as pl
from jax.experimental.pallas import tpu as pltpu
from jax.sharding import PartitionSpec as P

EXPERTS = 64
WINDOW = 2
LANES = 128
PIECES = 4
LOADS = 1
VMEM_LIMIT = 40 * 1024 * 1024

BF16 = jnp.bfloat16
F32 = jnp.float32
I16 = jnp.int16
ROWS_BY_ROWS = (((0,), (0,)), ((), ()))
COLS_BY_COLS = (((1,), (1,)), ((), ()))


def gelu_pair(pre_act):
    coefficient = 0.7978845608028654
    square = pre_act * pre_act
    tanh_val = jnp.tanh(coefficient * (pre_act + 0.044715 * pre_act * square))
    half = 0.5 * (1.0 + tanh_val)
    activation = pre_act * half
    slopes = half + 0.5 * pre_act * (1.0 - tanh_val * tanh_val) * coefficient * (
        1.0 + 3.0 * 0.044715 * square
    )
    return (activation, slopes)


def call(kernel, out_shape, flops, moved, limit=VMEM_LIMIT, in_specs=None, after=(), **more):
    def run(*operands):
        given = in_specs or [pl.BlockSpec(memory_space=pltpu.VMEM)] * len(operands)
        return pl.pallas_call(
            lambda *refs: kernel(*refs[len(after) :]),
            out_shape=out_shape,
            in_specs=[pl.BlockSpec(memory_space=pl.ANY)] * len(after) + list(given),
            compiler_params=pltpu.CompilerParams(vmem_limit_bytes=limit),
            cost_estimate=pl.CostEstimate(flops=flops, bytes_accessed=moved, transcendentals=0),
            **more,
        )(*after, *operands)

    return run


def own_expert():
    half_nodes = lax.axis_size("node") // WINDOW
    return lax.axis_index("node") // half_nodes


def split_value(value):
    high = value.astype(BF16).astype(F32)
    lane = lax.broadcasted_iota(jnp.int32, (value.shape[0], LANES), 1)
    return jnp.where(lane == 0, high, jnp.where(lane == 1, value - high, 0.0))


def encode(values):
    top = jnp.max(jnp.abs(values), axis=1, keepdims=True)
    power = jnp.ceil(jnp.log2(jnp.maximum(top, 1e-30)))
    codes = jnp.round(values * (1.999 * jnp.exp2(14.0 - power)))
    return codes.astype(jnp.int32).astype(I16), power


def decode(codes, power):
    return codes.astype(jnp.int32).astype(F32) * (jnp.exp2(power - 14.0) / 1.999)


def store_codes(out_ref, pair):
    hidden = pair[0].shape[1]
    lane = lax.broadcasted_iota(jnp.int32, (pair[0].shape[0], LANES), 1)
    powers = []
    for index, values in enumerate(pair):
        codes, power = encode(values)
        out_ref[:, index * hidden : (index + 1) * hidden] = codes
        powers.append(power)
    powers = jnp.where(lane == 0, powers[0], powers[1])
    out_ref[:, 2 * hidden :] = powers.astype(jnp.int32).astype(I16)


def load_codes(ref):
    hidden = (ref.shape[1] - LANES) // 2
    powers = ref[:, 2 * hidden :].astype(jnp.int32).astype(F32)
    return [
        decode(ref[:, index * hidden : (index + 1) * hidden], powers[:, index : index + 1])
        for index in range(2)
    ]


def gather_kernel(routes_hbm, gates_hbm, tokens_hbm, grads_hbm, w_in_hbm, w_out_hbm, own_ref,
                  other_ref, place_ref, spread_ref, w_ref, routes_ref, gates_ref, tokens_ref,
                  grads_ref, sems):
    tok_rows, feats = tokens_ref.shape
    capacity = own_ref.shape[0] // 2
    slots = WINDOW * capacity
    copies = [
        pltpu.make_async_copy(routes_hbm, routes_ref, sems.at[0]),
        pltpu.make_async_copy(gates_hbm, gates_ref, sems.at[1]),
    ]
    count = tok_rows // LOADS
    for source, target in ((tokens_hbm, tokens_ref), (grads_hbm, grads_ref)):
        for piece in range(LOADS):
            span = pl.ds(piece * count, count)
            copies.append(
                pltpu.make_async_copy(source.at[span], target.at[span], sems.at[len(copies)])
            )
    hidden = w_out_hbm.shape[0]
    upper, lower = pl.ds(0, hidden), pl.ds(hidden, hidden)
    moves = [(w_out_hbm, w_ref.at[upper])]
    for block in range(0, feats, hidden):
        span = pl.ds(block, hidden)
        moves.append((w_in_hbm.at[span], w_ref.at[lower, span]))
    for source, target in moves:
        copies.append(pltpu.make_async_copy(source, target, sems.at[len(copies)]))
    for copy in copies:
        copy.start()
    earlier = lax.broadcasted_iota(jnp.int32, (tok_rows, tok_rows), 0) < lax.broadcasted_iota(
        jnp.int32, (tok_rows, tok_rows), 1
    )
    earlier = earlier.astype(F32).astype(BF16)
    slot_of = lax.broadcasted_iota(jnp.int32, (capacity, tok_rows), 0).astype(F32)
    row_of = lax.broadcasted_iota(jnp.int32, (8, tok_rows), 0)
    own = own_expert()
    copies[0].wait()
    copies[1].wait()
    routes = routes_ref[...]
    gates = gates_ref[...].astype(F32)
    hits = [(routes == expert).astype(F32) for expert in (own, 1 - own)]
    named = [hit[0:1] + hit[1:2] for hit in hits]
    weight = [hit * gates for hit in hits]
    weight = [value[0:1] + value[1:2] for value in weight]
    names = jnp.where(row_of == 0, named[0], jnp.where(row_of == 1, named[1], 0.0)).astype(BF16)
    before = jnp.dot(names, earlier, preferred_element_type=F32)
    parts = [jnp.where(before[e : e + 1] == slot_of, named[e], 0.0) for e in range(WINDOW)]
    place = jnp.concatenate(parts, axis=0).astype(BF16)
    place_ref[:slots] = place
    spread_ref[...] = jnp.concatenate(parts + parts, axis=0).T.astype(BF16)
    masks = jnp.zeros((16, tok_rows), F32)
    row_of = lax.broadcasted_iota(jnp.int32, masks.shape, 0)
    for index, hit in enumerate(hits):
        for k in range(2):
            masks = jnp.where(row_of == 2 * index + k, hit[k : k + 1], masks)
    place_ref[slots:] = masks.astype(BF16)
    for copy in copies[2 : 2 + LOADS]:
        copy.wait()
    rows_x = jnp.dot(place, tokens_ref[...], preferred_element_type=F32)
    for copy in copies[2 + LOADS : 2 + 2 * LOADS]:
        copy.wait()
    rows_dy = jnp.dot(place, grads_ref[...], preferred_element_type=F32)
    for expert, out_ref in ((0, own_ref), (1, other_ref)):
        span = slice(expert * capacity, (expert + 1) * capacity)
        out_ref[:, :feats] = jnp.concatenate([rows_x[span], rows_dy[span]], axis=0).astype(BF16)
        gate = jnp.sum(parts[expert] * weight[expert], axis=1, keepdims=True)
        gate = jnp.concatenate([gate, gate], axis=0)
        out_ref[:, feats:] = jnp.broadcast_to(gate, (2 * capacity, LANES)).astype(BF16)
    for copy in copies[2 + 2 * LOADS :]:
        copy.wait()


def join_kernel(*refs):
    *pieces, out_ref = refs
    rows = pieces[0].shape[0]
    for index, ref in enumerate(pieces):
        out_ref[index * rows : (index + 1) * rows] = ref[...]


def part_kernel(capacity, rows_ref, w_ref, w_other_ref, part_ref, gate_ref):
    feats = w_ref.shape[1]
    hidden = w_ref.shape[0] // 2
    groups = rows_ref.shape[0] // (2 * capacity)
    gate = rows_ref[:, feats:].astype(F32).reshape(groups, 2 * capacity, LANES)
    gate_ref[...] = gate[:, :capacity].reshape(groups * capacity, LANES)
    rows = rows_ref[:, :feats]
    pre = []
    back = []
    for ref in (w_ref, w_other_ref):
        pre.append(
            sum(
                jnp.dot(
                    rows[:, block : block + hidden],
                    ref[hidden:, block : block + hidden],
                    preferred_element_type=F32,
                )
                for block in range(0, feats, hidden)
            )
        )
        back.append(
            lax.dot_general(rows, ref[:hidden], COLS_BY_COLS, preferred_element_type=F32)
        )
    pair = []
    for values, span in ((pre, slice(0, capacity)), (back, slice(capacity, 2 * capacity))):
        values = jnp.concatenate(values, axis=1).reshape(groups, 2 * capacity, 2 * hidden)
        pair.append(values[:, span].reshape(groups * capacity, 2 * hidden))
    store_codes(part_ref, pair)


def add_codes_kernel(first_ref, second_ref, out_ref):
    pairs = zip(load_codes(first_ref), load_codes(second_ref))
    store_codes(out_ref, [first + second for first, second in pairs])


def deal(total, refs):
    each, wide = refs[0].shape
    feats = wide - LANES
    gate = split_value(jnp.sum(total[:, feats:], axis=1, keepdims=True))
    for index, ref in enumerate(refs):
        span = slice(index * each, (index + 1) * each)
        ref[:, :feats] = total[span, :feats].astype(ref.dtype)
        ref[:, feats:] = gate[span].astype(ref.dtype)


def slot_kernel(capacity, before, first_ref, second_ref, gate_ref, w_ref, w_other_ref, *refs):
    before_refs, (mine_ref, theirs_ref, *slot_refs) = refs[:before], refs[before:]
    hidden = w_ref.shape[0] // 2
    pairs = zip(load_codes(first_ref), load_codes(second_ref))
    pre, back = [first + second for first, second in pairs]
    gate = gate_ref[:, :1]
    activation, slopes = gelu_pair(pre)
    dpre = (gate * back * slopes).astype(BF16)
    act = gate * activation
    slot = []
    for block in range(0, w_ref.shape[1], hidden):
        span = slice(block, block + hidden)
        slot.append(
            sum(
                lax.dot_general(
                    part, ref[hidden:, span], COLS_BY_COLS, preferred_element_type=F32
                )
                for part, ref in ((dpre[:, :hidden], w_ref), (dpre[:, hidden:], w_other_ref))
            )
        )
    slot_gate = split_value(jnp.sum(activation * back, axis=1, keepdims=True))
    total = jnp.concatenate(slot + [slot_gate], axis=1)
    if len(slot_refs) == 1:
        slot_refs[0][...] = total
    else:
        deal(total, slot_refs)
    rows = dpre.shape[0]
    both = [
        value.reshape(rows // capacity, capacity, 2 * hidden) for value in (dpre.astype(F32), act)
    ]
    both = jnp.concatenate(both, axis=1).reshape(2 * rows, 2 * hidden).astype(BF16)
    mine_ref[...] = both[:, :hidden]
    count = 2 * rows
    for index, ref in enumerate(before_refs):
        theirs_ref[index * count : (index + 1) * count] = ref[...]
    theirs_ref[before * count :] = both[:, hidden:]


def halve_kernel(kept_ref, came_ref, keep_ref, send_ref):
    half = keep_ref.shape[0]
    total = kept_ref[...] + came_ref[...]
    keep_ref[...] = total[:half]
    send_ref[...] = total[half:]


def deal_kernel(kept_ref, came_ref, *refs):
    deal(kept_ref[...] + came_ref[...], refs)


def weight_kernel(capacity, *refs):
    rows_refs, both_refs = refs[:4], refs[4:7]
    w_in_hbm, w_out_hbm, written_ref, w_in_ref, w_out_ref, sems = refs[7:]
    feats, hidden = w_in_ref.shape
    rows = jnp.concatenate([ref[:, :feats] for ref in rows_refs], axis=0)
    both = jnp.concatenate([ref[...] for ref in both_refs], axis=0).astype(F32)
    of_x = lax.broadcasted_iota(jnp.int32, both.shape, 0) % (2 * capacity) < capacity
    dpre = jnp.where(of_x, both, 0.0).astype(BF16)
    act = jnp.where(of_x, 0.0, both).astype(BF16)
    count = feats // PIECES
    copies = []
    for piece in range(PIECES):
        span = slice(piece * count, (piece + 1) * count)
        part = rows[:, span]
        w_in_ref[span] = lax.dot_general(part, dpre, ROWS_BY_ROWS, preferred_element_type=F32)
        w_out_ref[:, span] = lax.dot_general(act, part, ROWS_BY_ROWS, preferred_element_type=F32)
        span = pl.ds(piece * count, count)
        for source, target in (
            (w_in_ref.at[span], w_in_hbm.at[span]),
            (w_out_ref.at[:, span], w_out_hbm.at[:, span]),
        ):
            copy = pltpu.make_async_copy(source, target, sems.at[len(copies)])
            copy.start()
            copies.append(copy)
    for copy in copies:
        copy.wait()
    written_ref[...] = jnp.zeros(written_ref.shape, F32)


def combine_kernel(steps, *refs):
    kept_ref, came_refs = refs[0], refs[1:steps]
    place_ref, spread_ref, tokens_ref, gate_out_ref = refs[steps:]
    feats = tokens_ref.shape[1]
    capacity = kept_ref.shape[0]
    came = [ref[...].astype(F32) for ref in came_refs]
    half = steps // WINDOW
    own = sum(came[: half - 1], kept_ref[...])
    other = sum(came[half:], came[half - 1])
    slots = jnp.concatenate([own, other], axis=0)
    grads = slots[:, :feats]
    high = grads.astype(BF16)
    low = (grads - high.astype(F32)).astype(BF16)
    both = jnp.concatenate([high, low], axis=0)
    tokens_ref[...] = jnp.dot(spread_ref[...], both, preferred_element_type=F32).astype(BF16)
    slot_gate = jnp.sum(slots[:, feats:], axis=1, keepdims=True)
    picked = place_ref[: WINDOW * capacity].astype(F32) * slot_gate
    masks = place_ref[WINDOW * capacity :].astype(F32)
    result = jnp.zeros(gate_out_ref.shape, F32)
    for index in range(WINDOW):
        span = slice(index * capacity, (index + 1) * capacity)
        value = jnp.sum(picked[span], axis=0, keepdims=True)
        result = result + masks[2 * index : 2 * index + 2] * value
    gate_out_ref[...] = result


def swap(array, axes, bit):
    size = lax.axis_size(axes)
    return lax.ppermute(array, axes, [(index, index ^ bit) for index in range(size)])


def swap_nodes(array, step):
    return swap(array, ("node", "local"), step * lax.axis_size("local") + 1)


def join(pieces, after=()):
    rows, wide = pieces[0].shape
    rows *= len(pieces)
    shape = jax.ShapeDtypeStruct((rows, wide), BF16)
    return call(join_kernel, shape, 0, 4 * rows * wide, after=after)(*pieces)


def body(tokens, grad_out, routes, gates, w_in, w_out):
    nodes = lax.axis_size("node")
    locals_ = lax.axis_size("local")
    edatas = lax.axis_size("edata")
    tok_rows, feats = tokens.shape
    hidden = w_in.shape[1]
    capacity = 2 * tok_rows // EXPERTS
    slots = WINDOW * capacity
    wide = feats + LANES
    coded = 4 * hidden + LANES
    shape = jax.ShapeDtypeStruct
    hbm = pl.BlockSpec(memory_space=pltpu.HBM)
    vmem = pl.BlockSpec(memory_space=pltpu.VMEM)

    inputs = [
        pltpu.with_memory_space_constraint(value, pltpu.HBM)
        for value in (routes.T, gates.T, tokens, grad_out, w_in, w_out)
    ]
    own_rows, other_rows, place, spread, weights = call(
        gather_kernel,
        (
            pltpu.VMEM((2 * capacity, wide), BF16),
            pltpu.VMEM((2 * capacity, wide), BF16),
            pltpu.VMEM((slots + 16, tok_rows), BF16),
            pltpu.VMEM((tok_rows, 2 * slots), BF16),
            pltpu.VMEM((2 * hidden, feats), BF16),
        ),
        4 * slots * tok_rows * feats,
        4 * tok_rows * feats + 4 * hidden * feats,
        in_specs=[hbm] * 6,
        scratch_shapes=[
            pltpu.VMEM((2, tok_rows), jnp.int32),
            pltpu.VMEM((2, tok_rows), BF16),
            pltpu.VMEM((tok_rows, feats), BF16),
            pltpu.VMEM((tok_rows, feats), BF16),
            pltpu.SemaphoreType.DMA((3 + 2 * LOADS + feats // hidden,)),
        ],
    )(*inputs)

    other_weights = swap(weights, "local", 1)

    half_nodes = nodes // WINDOW
    pieces = [own_rows]
    for step in range(1, nodes):
        pieces.append(swap_nodes(own_rows if step < half_nodes else other_rows, step))
    rows = half_nodes * (locals_ // 2) * capacity
    last = ()
    chains = []
    held = []
    for chunk in (pieces[:half_nodes], pieces[half_nodes:]):
        chunk = join(chunk, last)
        bit = 2
        while bit < locals_:
            chunk = join([chunk, swap(chunk, "local", bit)])
            bit *= 2
        held.append(chunk)
        part, gate_rows = call(
            functools.partial(part_kernel, capacity),
            (shape((rows, coded), I16), shape((rows, LANES), F32)),
            16 * rows * feats * hidden,
            4 * rows * feats + 8 * feats * hidden,
            after=last,
        )(chunk, weights, other_weights)
        last = (part,)
        chains.append((part, swap(part, "edata", edatas // 2), gate_rows))
    bit = edatas // 4
    while bit:
        for index, (part, other, gate_rows) in enumerate(chains):
            part = call(
                add_codes_kernel,
                shape((rows, coded), I16),
                16 * rows * hidden,
                6 * rows * coded,
                after=last,
            )(part, other)
            last = (part,)
            chains[index] = (part, swap(part, "edata", bit), gate_rows)
        bit //= 2

    mine = []
    theirs = ()
    slots_back = []
    for index, (part, other, gate_rows) in enumerate(chains):
        dealt = [shape((capacity, wide), BF16 if index else F32)] * half_nodes
        own, packed, *slot_parts = call(
            functools.partial(slot_kernel, capacity, len(theirs)),
            [
                shape((2 * rows, hidden), BF16),
                shape(((1 + len(theirs)) * 2 * rows, hidden), BF16),
                *(dealt if locals_ == 2 else [shape((rows, wide), F32)]),
            ],
            4 * rows * feats * hidden,
            4 * feats * hidden + 4 * rows * feats,
            after=last,
        )(part, other, gate_rows, weights, other_weights, *theirs)
        last = (own,)
        mine.append(own)
        theirs = (packed,)
        if locals_ > 2:
            half = rows // 2
            keep, send = slot_parts[0][:half], slot_parts[0][half:]
            bit = locals_ // 2
            while bit > 2:
                half //= 2
                keep, send = call(
                    halve_kernel,
                    (shape((half, wide), F32),) * 2,
                    4 * half * wide,
                    24 * half * wide,
                )(keep, swap(send, "local", bit))
                bit //= 2
            slot_parts = call(deal_kernel, dealt, 4 * half * wide, 12 * half * wide)(
                keep, swap(send, "local", bit)
            )
        for step, send in enumerate(slot_parts, index * half_nodes):
            slots_back.append(swap_nodes(send, step) if step else send)
    came = [swap(chunk, "local", 1) for chunk in held]
    back = swap(theirs[0], "local", 1)
    grad_w_in, grad_w_out, written = call(
        functools.partial(weight_kernel, capacity),
        (shape((feats, hidden), F32), shape((hidden, feats), F32), shape((8, LANES), F32)),
        32 * rows * feats * hidden,
        8 * feats * hidden,
        in_specs=[vmem] * 7,
        after=slots_back[1:half_nodes],
        out_specs=[hbm, hbm, vmem],
        scratch_shapes=[
            pltpu.VMEM((feats, hidden), F32),
            pltpu.VMEM((hidden, feats), F32),
            pltpu.SemaphoreType.DMA((2 * PIECES,)),
        ],
    )(*held, *came, *mine, back)
    grad_tokens, grad_gates = call(
        functools.partial(combine_kernel, nodes),
        (shape((tok_rows, feats), BF16), shape((2, tok_rows), F32)),
        4 * slots * tok_rows * feats,
        2 * tok_rows * feats,
        after=(written,),
    )(*slots_back[:half_nodes], *reversed(slots_back[half_nodes:]), place, spread)
    return (grad_tokens, grad_gates.T, grad_w_in, grad_w_out)


def solution(mesh):
    in_specs = (
        P(("node", "local"), "edata"),
        P(("node", "local"), "edata"),
        P(("node", "local"), None),
        P(("node", "local"), None),
        P("edata", ("node", "local")),
        P(("node", "local"), "edata"),
    )
    out_specs = (
        P(("node", "local"), "edata"),
        P(("node", "local"), None),
        P("edata", ("node", "local")),
        P(("node", "local"), "edata"),
    )
    return jax.shard_map(body, mesh=mesh, in_specs=in_specs, out_specs=out_specs, check_vma=False)
```
